32 devices in a mesh: groups: 2 (over y), lev: 4 (over z), tm: 2 (over x), sub: 2 (over core).
Axes of the slice: x: 2, y: 2, z: 4, core: 2. Of those that a mesh axis runs over, the one named last changes fastest.
Arguments:
- level_field: float32 [32, 96, 16384], P(('groups', 'tm'), ('lev', 'sub')), parts along dimension 0, may hold values from -6 to 6
- tile_weight: float32 [64, 65536], P(None, ('lev', 'sub')), may hold values from -0.4 to 0.4
- tile_rows: int32 [1024], P(('lev', 'sub')), may hold values from 0 to 15
- tile_columns: int32 [1024], P(('lev', 'sub')), may hold values from 0 to 31
- live_count: int32 [8], P(('lev', 'sub')), may hold values from 16 to 128, as said below
- step_hour: int32 [16], P('tm'), may hold values from 0 to 1, as said below
Outputs:
- hourly: float32 [4, 96, 8192], P('groups', 'tm', ('lev', 'sub')), parts along dimension 0
The draws below stay inside these ranges and needn't reach their ends.
There are 2 independent parts, one for each index of `groups`. The reference program is written for one: setup_inputs(seed, part) draws one part's arguments, and reference() takes and returns one part's arrays. A program takes and returns all parts, laid end to end along the dimension named above; an argument that names none is the same for every part. Nothing has to cross between parts.
Inputs may be any that keep to these rules, and one draw needn't show every extreme that they name: `live_count`: some shard has all 128 slots live in every draw, not always the same. `step_hour`: every hour has exactly 8 steps.
All inputs are finite; a program needn't handle non-finite values.
Results may differ from the reference program's by a relative error of at most 0.0003.
Values sent between devices are 32-bit elements; how exact they have to be, the bound alone decides.
No kernel may reach another device: no remote copies, remote signals or barrier semaphores. Data moves between devices by JAX's collectives and lax.ppermute only.
A program may use at most 128 MiB of HBM per device.

```python
import jax
import jax.numpy as jnp
from jax import lax

TILE = 64
LEV = 96
HOURS = 2
CT_DEV = 32
PT_DEV = 16
SLOTS = 128
SHARDS = 8
SLOTS_ALL = 1024
CELLS = 16384
STEPS = 16


def draw_live_count(key, part):
    key = jax.random.fold_in(key, 1)
    lowest = max(SLOTS // 8, 1)
    counts = jax.random.randint(key, (SHARDS,), lowest, SLOTS + 1)
    fuller = jax.random.randint(jax.random.fold_in(key, 2), (), 0, SHARDS)
    return jnp.where(jnp.arange(SHARDS) == fuller, SLOTS, counts).astype(jnp.int32)


def draw_step_hour(key, part):
    key = jax.random.fold_in(key, 5)
    return (jax.random.permutation(key, STEPS) % HOURS).astype(jnp.int32)


def set_ends(array, own_key, least, top_value):
    dims = array.shape
    place = [jax.random.randint(jax.random.fold_in(own_key, axis), (), 0, dims[axis]) for axis in range(len(dims))]
    array = array.at[tuple(place)].set(least)
    longest = dims.index(max(dims))
    place[longest] = (place[longest] + 1) % dims[longest]
    return array.at[tuple(place)].set(top_value)


def level_of(stream_key, shape, split, low, largest):
    loudness = 1.0
    for dim, parts in split:
        heights = jax.random.uniform(jax.random.fold_in(jax.random.fold_in(stream_key, 6), dim), (parts,), jnp.float32, low / len(split), largest / len(split))
        loudness = loudness * jnp.repeat(jnp.exp(heights), shape[dim] // parts).reshape((-1,) + (1,) * (len(shape) - 1 - dim))
    return loudness


def noise(stream_key, shape, scale, reach, split=(), kind=jnp.bfloat16):
    result = scale * jax.random.normal(stream_key, shape, jnp.float32)
    if split:
        result = result * level_of(stream_key, shape, split, -0.22, 0.18)
    return jnp.clip(result, -reach, reach).astype(kind)


def setup_inputs(seed: int = 0, part: int = 0) -> dict:
    seeds = jax.random.split(jax.random.key(seed), 7)
    part_splits = jax.random.split(jax.random.fold_in(seeds[6], part), 7)
    level_field = noise(part_splits[0], (STEPS, LEV, CELLS), 1.0, 6.0, ((0, 2), (1, 8)), jnp.float32)
    tile_weight = noise(seeds[1], (TILE, SLOTS_ALL * TILE), 0.0625, 0.4, ((1, 8),), jnp.float32)
    tile_rows = set_ends(jax.random.randint(seeds[2], (SLOTS_ALL,), 0, PT_DEV), jax.random.fold_in(seeds[2], 1), 0, PT_DEV - 1).astype(jnp.int32)
    tile_columns = set_ends(jax.random.randint(seeds[3], (SLOTS_ALL,), 0, CT_DEV), jax.random.fold_in(seeds[3], 1), 0, CT_DEV - 1).astype(jnp.int32)
    live_count = draw_live_count(jax.random.fold_in(seeds[6], 71), part)
    step_hour = draw_step_hour(jax.random.fold_in(seeds[6], 71), part)
    return dict(level_field=level_field, tile_weight=tile_weight, tile_rows=tile_rows, tile_columns=tile_columns, live_count=live_count, step_hour=step_hour)


def assemble(weights, rows, columns, count):
    live_mask = (jnp.arange(SLOTS, dtype=jnp.int32) < count).astype(jnp.float32)
    column_hot = (columns[:, None] == jnp.arange(CT_DEV, dtype=jnp.int32)[None, :]).astype(jnp.float32) * live_mask[:, None]
    row_hot = (rows[:, None] == jnp.arange(PT_DEV, dtype=jnp.int32)[None, :]).astype(jnp.float32)
    pair_hot = (column_hot[:, :, None] * row_hot[:, None, :]).reshape(SLOTS, CT_DEV * PT_DEV)
    slot_tiles = jnp.transpose(weights, (1, 2, 0)).reshape(SLOTS, TILE * TILE)
    placed = lax.dot_general(pair_hot, slot_tiles, (((0,), (0,)), ((), ())),
                             precision=lax.Precision.HIGHEST, preferred_element_type=jnp.float32)
    placed = placed.reshape(CT_DEV, PT_DEV, TILE, TILE)
    return jnp.transpose(placed, (0, 2, 1, 3)).reshape(CT_DEV * TILE, PT_DEV * TILE)


def reference(level_field, tile_weight, tile_rows, tile_columns, live_count, step_hour):
    cells_dev = CT_DEV * TILE
    weights = jnp.moveaxis(tile_weight.reshape(TILE, SHARDS, SLOTS, TILE), 1, 0)
    row_table = tile_rows.reshape(SHARDS, SLOTS)
    col_table = tile_columns.reshape(SHARDS, SLOTS)
    hour_table = (step_hour[None, :] == jnp.arange(HOURS, dtype=jnp.int32)[:, None]).astype(jnp.float32)

    def remap_shard(items):
        weight_here, rows, columns, count, shard_index = items
        dense_map = assemble(weight_here, rows, columns, count)
        cell_block = lax.dynamic_slice_in_dim(level_field, shard_index * cells_dev, cells_dev, 2)
        pixel_values = jnp.dot(cell_block.reshape(STEPS * LEV, cells_dev), dense_map,
                               preferred_element_type=jnp.float32, precision=lax.Precision.HIGHEST)
        pixel_values = pixel_values.reshape(STEPS, LEV, PT_DEV * TILE)
        summed = jnp.einsum("hs,slp->hlp", hour_table, pixel_values, precision=lax.Precision.HIGHEST)
        return summed / float(STEPS // HOURS)

    stacked = lax.map(remap_shard, (weights, row_table, col_table, live_count,
                                    jnp.arange(SHARDS, dtype=jnp.int32)))
    return jnp.transpose(stacked, (1, 2, 0, 3)).reshape(HOURS, LEV, SHARDS * PT_DEV * TILE)
```

```python
import functools

import jax
import jax.numpy as jnp
from jax import lax
from jax.experimental import pallas as pl
from jax.experimental.pallas import tpu as pltpu
from jax.sharding import PartitionSpec as P

TILE = 64
HOURS = 2
CT_DEV = 32
PT_DEV = 16
SLOTS = 128
CELLS_DEV = CT_DEV * TILE
PIXELS_DEV = PT_DEV * TILE
LANES = 2 * TILE
MIB = 1 << 20

LIGHT = pl.CostEstimate(flops=1, bytes_accessed=1, transcendentals=0)

NT = (((1,), (1,)), ((), ()))
NN = (((1,), (0,)), ((), ()))


def split(x):
    high = x.astype(jnp.bfloat16)
    return high, (x - high.astype(jnp.float32)).astype(jnp.bfloat16)


def dot(a, b, dims):
    return lax.dot_general(a, b, dims, preferred_element_type=jnp.float32)


def place_kernel(rows, columns, count, weights, *refs):
    high, low, total = refs[-3:]
    band = 128

    @pl.loop(0, PIXELS_DEV // band)
    def _(b):
        total[pl.ds(pl.multiple_of(b * band, band), band), :] = jnp.zeros((band, CELLS_DEV), jnp.float32)

    lane_half = lax.broadcasted_iota(jnp.int32, (TILE, LANES), 1) // TILE

    @pl.loop(0, count[0])
    def _(k):
        column = columns[k]
        side = column % 2
        tile = weights[:, pl.ds(pl.multiple_of((k // 2) * LANES, LANES), LANES)]
        moved = pltpu.roll(tile, ((k + column) % 2) * TILE, 1)
        at = (
            pl.ds(pl.multiple_of(rows[k] * TILE, TILE), TILE),
            pl.ds(pl.multiple_of((column // 2) * LANES, LANES), LANES),
        )
        total[at] = total[at] + jnp.where(lane_half == side, moved, 0.0)

    @pl.loop(0, PIXELS_DEV // band)
    def _(b):
        at = pl.ds(pl.multiple_of(b * band, band), band)
        high[at, :], low[at, :] = split(total[at, :])


def place_tiles(rows, columns, count, weights, *after):
    smem = pl.BlockSpec(memory_space=pltpu.SMEM)
    vmem = pl.BlockSpec(memory_space=pltpu.VMEM)
    half = jax.ShapeDtypeStruct((PIXELS_DEV, CELLS_DEV), jnp.bfloat16)
    return pl.pallas_call(
        place_kernel,
        out_shape=(half, half),
        in_specs=[smem, smem, smem, vmem] + [pl.BlockSpec(memory_space=pl.ANY)] * len(after),
        out_specs=(vmem, vmem),
        scratch_shapes=[pltpu.VMEM((PIXELS_DEV, CELLS_DEV), jnp.float32)],
        compiler_params=pltpu.CompilerParams(vmem_limit_bytes=28 * MIB),
        cost_estimate=LIGHT,
        name="place_tiles",
    )(rows, columns, count, weights, *after)


PIXEL_BLOCK = 256


def remap_body(x, high, low):
    m = x.shape[0]
    x_high, x_low = split(x)
    both = dot(jnp.concatenate([x_high, x_low], axis=0), high, NT)
    return both[:m] + both[m:] + dot(x_high, low, NT)


def remap_call(kernel, inputs, out_rows, high, low, name):
    whole = [pl.BlockSpec(a.shape, lambda i, nd=a.ndim: (0,) * nd) for a in inputs]
    map_block = pl.BlockSpec((PIXEL_BLOCK, CELLS_DEV), lambda i: (i, 0))
    return pl.pallas_call(
        kernel,
        out_shape=[jax.ShapeDtypeStruct((rows, PIXELS_DEV), jnp.float32) for rows in out_rows],
        grid=(PIXELS_DEV // PIXEL_BLOCK,),
        in_specs=whole + [map_block, map_block],
        out_specs=[pl.BlockSpec((rows, PIXEL_BLOCK), lambda i: (0, i)) for rows in out_rows],
        compiler_params=pltpu.CompilerParams(vmem_limit_bytes=24 * MIB),
        cost_estimate=LIGHT,
        name=name,
    )(*inputs, high, low)


def remap_rows_kernel(x, high, low, out):
    out[...] = remap_body(x[...], high[...], low[...])


def near_rows(own, other_sub, other_lev, other_both):
    even = lax.axis_index("sub") == 0
    lev_first = lax.axis_index("lev") % 2 == 0
    left, right = jnp.where(even, own, other_sub), jnp.where(even, other_sub, own)
    up, down = jnp.where(even, other_lev, other_both), jnp.where(even, other_both, other_lev)
    return [
        jnp.where(lev_first, left, up),
        jnp.where(lev_first, right, down),
        jnp.where(lev_first, up, left),
        jnp.where(lev_first, down, right),
    ]


def far_rows(same_sub, other_sub):
    even = lax.axis_index("sub") == 0
    levels = same_sub.shape[0] // 2
    blocks = [jnp.where(even, same_sub, other_sub), jnp.where(even, other_sub, same_sub)]
    return [jnp.concatenate([block[:levels], block[levels:]], axis=1) for block in blocks]


def remap_first_kernel(own, other_sub, other_lev, other_both, same, other, high, low, *outs):
    levels = own.shape[0] // HOURS
    blocks = near_rows(own[...], other_sub[...], other_lev[...], other_both[...])
    x = jnp.concatenate(blocks + far_rows(same[...], other[...]), axis=0)
    result = remap_body(x, high[...], low[...])
    for hour in range(HOURS):
        for lev in range(2):
            pieces = []
            for sub in range(2):
                start = ((lev * 2 + sub) * HOURS + hour) * levels
                pieces.append(result[start : start + levels])
            outs[hour * 2 + lev][...] = jnp.concatenate(pieces, axis=0)
    outs[-1][...] = result[4 * HOURS * levels :]


def remap_last_kernel(same, other, high, low, out):
    x = jnp.concatenate(far_rows(same[...], other[...]), axis=0)
    out[...] = remap_body(x, high[...], low[...])


def hour_matrix(step_hour, levels, steps, hours, cuts):
    rows, columns = cuts * levels, cuts * 2 * levels * steps
    row = lax.broadcasted_iota(jnp.int32, (rows, columns), 0)
    column = lax.broadcasted_iota(jnp.int32, (rows, columns), 1)
    span = levels * steps
    near = jnp.full((rows, columns), -1, jnp.int32)
    for cut in range(cuts):
        for half in range(2):
            step = column - (cut * 2 + half) * span - (row - cut * levels) * steps
            inside = (row >= cut * levels) & (row < (cut + 1) * levels)
            inside = inside & (step >= 0) & (step < steps)
            near = jnp.where(inside, step, near)
    blocks = []
    for hour in hours:
        block = jnp.zeros((rows, columns), jnp.float32)
        for step in range(steps):
            block = jnp.where(near == step, jnp.where(step_hour[step] == hour, 1.0, 0.0), block)
        blocks.append(block)
    return jnp.concatenate(blocks, axis=0).astype(jnp.bfloat16)


def peer_shard(k, j):
    subs = lax.axis_size("sub")
    return (lax.axis_index("lev") ^ k) * subs + (lax.axis_index("sub") ^ j)


def field_copies(field, buffer, arrived, peers):
    copies = []
    for place, (k, j) in enumerate(peers):
        start = pl.multiple_of(peer_shard(k, j) * CELLS_DEV, CELLS_DEV)
        copy = pltpu.make_async_copy(
            field.at[:, :, pl.ds(start, CELLS_DEV)], buffer.at[place], arrived.at[place]
        )
        copy.start()
        copies.append(copy)
    return copies


def near_sum_kernel(peers, step_hour, field, *refs):
    *outs, buffer, arrived = refs[-len(peers) - 2 :]
    _, levels, steps, cells = buffer.shape
    copies = field_copies(field, buffer, arrived, peers)
    matrix = hour_matrix(step_hour, levels, steps, range(HOURS), 1)
    for place, out in enumerate(outs):
        copies[place].wait()
        x = buffer[place].reshape(levels * steps, cells)
        out[...] = dot(matrix, jnp.concatenate(split(x), axis=0), NN)


def far_sum_kernel(peers, step_hour, field, *refs):
    theirs, mine, buffer, arrived = refs[-4:]
    _, levels, steps, cells = buffer.shape
    copies = field_copies(field, buffer, arrived, peers)
    me = lax.axis_index("tm")
    matrix = hour_matrix(step_hour, levels, steps, (1 - me, me), 2)
    rows, cut = 2 * levels, cells // 2
    for place, copy in enumerate(copies):
        copy.wait()
        high, low = split(buffer[place].reshape(levels * steps, cells))
        stacked = jnp.concatenate([high[:, :cut], low[:, :cut], high[:, cut:], low[:, cut:]], axis=0)
        result = dot(matrix, stacked, NN)
        theirs[place * rows : (place + 1) * rows] = result[:rows]
        mine[place * rows : (place + 1) * rows] = result[rows:]


def sum_call(kernel, peers, step_hour, field, after, out_shapes, name):
    levels, steps, _ = field.shape
    vmem = pl.BlockSpec(memory_space=pltpu.VMEM)
    return pl.pallas_call(
        functools.partial(kernel, peers),
        out_shape=out_shapes,
        in_specs=[pl.BlockSpec(memory_space=pltpu.SMEM)] + [pl.BlockSpec(memory_space=pl.ANY)] * (1 + len(after)),
        out_specs=[vmem] * len(out_shapes),
        scratch_shapes=[
            pltpu.VMEM((len(peers), levels, steps, CELLS_DEV), jnp.float32),
            pltpu.SemaphoreType.DMA((len(peers),)),
        ],
        compiler_params=pltpu.CompilerParams(vmem_limit_bytes=52 * MIB),
        cost_estimate=LIGHT,
        name=name,
    )(step_hour, field, *after)


def near_sums(peers, step_hour, field, *after):
    shape = jax.ShapeDtypeStruct((HOURS * field.shape[0], CELLS_DEV), jnp.float32)
    return sum_call(near_sum_kernel, peers, step_hour, field, after, [shape] * len(peers), "near_sums")


def far_sums(peers, step_hour, field, *after):
    shape = jax.ShapeDtypeStruct((len(peers) * 2 * field.shape[0], CELLS_DEV // 2), jnp.float32)
    return sum_call(far_sum_kernel, peers, step_hour, field, after, [shape] * 2, "far_sums")


def merge_kernel(mine, got, *outs):
    rows = outs[0].shape[0]
    for place, out in enumerate(outs):
        at = slice(place * rows, (place + 1) * rows)
        out[...] = mine[at] + got[at]


def merge(mine, got, parts):
    vmem = pl.BlockSpec(memory_space=pltpu.VMEM)
    shape = jax.ShapeDtypeStruct((mine.shape[0] // parts, mine.shape[1]), jnp.float32)
    return pl.pallas_call(
        merge_kernel,
        out_shape=[shape] * parts,
        in_specs=[vmem, vmem],
        out_specs=[vmem] * parts,
        compiler_params=pltpu.CompilerParams(vmem_limit_bytes=4 * MIB),
        cost_estimate=LIGHT,
        name="merge",
    )(mine, got)


def finish_kernel(divisor, *refs):
    *arrays, out = refs
    a_own, a_got, b_own, b_got = arrays[-4:]
    me, lev = lax.axis_index("tm"), lax.axis_index("lev")
    half = a_own.shape[0]
    keeps_near = me == lev // 2

    @pl.when(keeps_near)
    def _():
        for place in range(2 * HOURS):
            total = arrays[place][...] + arrays[2 * HOURS + place][...]
            out[place * half : (place + 1) * half, :] = total / divisor

    @pl.when(jnp.logical_not(keeps_near))
    def _():
        for hour in range(HOURS):
            a_at = pl.multiple_of((hour * 2 + lev % 2) * half, half)
            b_at = pl.multiple_of((hour * 2 + 1 - lev % 2) * half, half)
            out[pl.ds(a_at, half), :] = jnp.where(me == hour, a_own[...], a_got[...]) / divisor
            out[pl.ds(b_at, half), :] = jnp.where(me == hour, b_own[...], b_got[...]) / divisor


def finish(arrays, divisor):
    vmem = pl.BlockSpec(memory_space=pltpu.VMEM)
    rows, pixels = arrays[0].shape
    return pl.pallas_call(
        functools.partial(finish_kernel, divisor),
        out_shape=jax.ShapeDtypeStruct((2 * HOURS * rows, pixels), jnp.float32),
        in_specs=[vmem] * len(arrays),
        out_specs=vmem,
        compiler_params=pltpu.CompilerParams(vmem_limit_bytes=8 * MIB),
        name="finish",
    )(*arrays)


def hour_plan(level_field, tile_weight, tile_rows, tile_columns, live_count, step_hour):
    levs, subs, shards_tm = lax.axis_size("lev"), lax.axis_size("sub"), lax.axis_size("tm")
    half = levs // 2
    divisor = float(level_field.shape[0] * shards_tm // HOURS)
    field = jnp.transpose(level_field, (1, 0, 2))

    def to_peer(x, k, j):
        pairs = [(a * subs + b, (a ^ k) * subs + (b ^ j)) for a in range(levs) for b in range(subs)]
        return lax.ppermute(x, ("lev", "sub"), pairs)

    def swap(x):
        return lax.ppermute(x, "tm", [(0, 1), (1, 0)])

    def move(x, keeper):
        pairs = [(a * shards_tm + 1 - keeper(a), a * shards_tm + keeper(a)) for a in range(levs)]
        return lax.ppermute(x, ("lev", "tm"), pairs)

    far_peers = [[(k, j) for j in range(subs)] for k in range(half, levs)]
    near_peers = [(k, j) for k in range(half) for j in range(subs)]
    sums = []
    for peers in far_peers:
        sums.append(far_sums(peers, step_hour, field, *[theirs for theirs, _ in sums]))
    swapped = [swap(theirs) for theirs, _ in sums]
    near = near_sums(near_peers, step_hour, field, sums[-1][0])
    near = [near[0]] + [to_peer(x, k, j) for x, (k, j) in list(zip(near, near_peers))[1:]]
    far, merges = [], []
    for peers, (_, mine), got in zip(far_peers, sums, swapped):
        merged = merge(mine, got, subs)
        merges += merged
        far.append([to_peer(x, k, j) for x, (k, j) in zip(merged, peers)])

    high, low = place_tiles(tile_rows, tile_columns, live_count, tile_weight, *merges)
    rows = far[0][0].shape[0]
    *near_out, a_out = remap_call(
        remap_first_kernel, near + far[0], [rows] * (2 * HOURS + 1), high, low, "remap_first"
    )
    near_got = [move(x, lambda a: a // half) for x in near_out]
    a_got = move(a_out, lambda a: 1 - a // half)
    (b_out,) = remap_call(remap_last_kernel, far[1], [rows], high, low, "remap_last")
    b_got = move(b_out, lambda a: 1 - a // half)
    out = finish(near_out + near_got + [a_out, a_got, b_out, b_got], divisor)
    return out.reshape(HOURS, out.shape[0] // HOURS, PIXELS_DEV)


def general_plan(level_field, tile_weight, tile_rows, tile_columns, live_count, step_hour):
    steps, levels, cells = level_field.shape
    shards = lax.axis_size("lev") * lax.axis_size("sub")
    divisor = float(steps * lax.axis_size("tm") // HOURS)
    hours = jnp.arange(HOURS, dtype=jnp.int32)
    table = (step_hour[None, :] == hours[:, None]).astype(jnp.float32)
    fields = level_field.reshape(steps, levels, shards, cells // shards)
    partial = jnp.einsum("hs,slgc->ghlc", table, fields, precision=lax.Precision.HIGHEST)
    regrouped = lax.all_to_all(partial, ("lev", "sub"), split_axis=0, concat_axis=0, tiled=True)
    rows = jnp.transpose(regrouped, (1, 0, 2, 3)).reshape(-1, cells // shards)
    high, low = place_tiles(tile_rows, tile_columns, live_count, tile_weight)
    (out,) = remap_call(remap_rows_kernel, [rows], [rows.shape[0]], high, low, "remap_rows")
    out = out.reshape(HOURS, shards * levels, PIXELS_DEV) / divisor
    return lax.psum_scatter(out, "tm", scatter_dimension=1, tiled=True)


def solution(mesh):
    sizes = mesh.shape
    paired = sizes["tm"] == HOURS and sizes["lev"] == 4 and sizes["sub"] == 2
    placed = (
        P(("groups", "tm"), ("lev", "sub"), None),
        P(None, ("lev", "sub")),
        P(("lev", "sub")),
        P(("lev", "sub")),
        P(("lev", "sub")),
        P("tm"),
    )
    return jax.shard_map(
        hour_plan if paired else general_plan,
        mesh=mesh,
        in_specs=placed,
        out_specs=P("groups", "tm", ("lev", "sub")),
        check_vma=False,
    )
```

```python
import functools

import jax
import jax.numpy as jnp
from jax import lax
from jax.experimental import pallas as pl
from jax.experimental.pallas import tpu as pltpu
from jax.sharding import PartitionSpec as P

TILE = 64
HOURS = 2
CT_DEV = 32
PT_DEV = 16
SLOTS = 128
CELLS_DEV = CT_DEV * TILE
PIXELS_DEV = PT_DEV * TILE
LANES = 2 * TILE
MIB = 1 << 20

LIGHT = pl.CostEstimate(flops=1, bytes_accessed=1, transcendentals=0)
HEAVY = pl.CostEstimate(flops=10_000_000_000, bytes_accessed=1, transcendentals=0)

NT = (((1,), (1,)), ((), ()))
NN = (((1,), (0,)), ((), ()))


def split(x):
    high = x.astype(jnp.bfloat16)
    return high, (x - high.astype(jnp.float32)).astype(jnp.bfloat16)


def dot(a, b, dims):
    return lax.dot_general(a, b, dims, preferred_element_type=jnp.float32)


GROUP = 8


def place_kernel(rows, columns, count, weights, *refs):
    high, low, total = refs[-3:]
    band = 128

    @pl.loop(0, PIXELS_DEV // band)
    def _(b):
        total[pl.ds(pl.multiple_of(b * band, band), band), :] = jnp.zeros((band, CELLS_DEV), jnp.float32)

    lane_half = lax.broadcasted_iota(jnp.int32, (TILE, LANES), 1) // TILE
    live = count[0]

    @pl.loop(0, (live + GROUP - 1) // GROUP)
    def _(g):
        for pair in range(GROUP // 2):
            lanes = pl.ds(pl.multiple_of((g * (GROUP // 2) + pair) * LANES, LANES), LANES)
            tiles = weights[:, lanes]
            turned = pltpu.roll(tiles, TILE, 1)
            for i in range(2):
                k = g * GROUP + pair * 2 + i
                row, column = rows[k], columns[k]
                side = jnp.where(k < live, column & 1, -1)
                tile = jnp.where(lane_half == i, tiles, turned)
                at = (
                    pl.ds(pl.multiple_of(row * TILE, TILE), TILE),
                    pl.ds(pl.multiple_of((column >> 1) * LANES, LANES), LANES),
                )
                total[at] = total[at] + jnp.where(lane_half == side, tile, 0.0)

    @pl.loop(0, PIXELS_DEV // band)
    def _(b):
        at = pl.ds(pl.multiple_of(b * band, band), band)
        high[at, :], low[at, :] = split(total[at, :])


def place_tiles(rows, columns, count, weights, *after):
    smem = pl.BlockSpec(memory_space=pltpu.SMEM)
    vmem = pl.BlockSpec(memory_space=pltpu.VMEM)
    half = jax.ShapeDtypeStruct((PIXELS_DEV, CELLS_DEV), jnp.bfloat16)
    return pl.pallas_call(
        place_kernel,
        out_shape=(half, half),
        in_specs=[smem, smem, smem, vmem] + [pl.BlockSpec(memory_space=pl.ANY)] * len(after),
        out_specs=(vmem, vmem),
        scratch_shapes=[pltpu.VMEM((PIXELS_DEV, CELLS_DEV), jnp.float32)],
        compiler_params=pltpu.CompilerParams(vmem_limit_bytes=28 * MIB),
        cost_estimate=HEAVY,
        name="place_tiles",
    )(rows, columns, count, weights, *after)


PIXEL_BLOCK = 256


def remap_blocks(x, high, low):
    m = x.shape[0]
    x_high, x_low = split(x)
    both = jnp.concatenate([x_high, x_low], axis=0)
    for start in range(0, PIXELS_DEV, PIXEL_BLOCK):
        at = slice(start, start + PIXEL_BLOCK)
        first = dot(both, high[at, :], NT)
        yield at, first[:m] + first[m:] + dot(x_high, low[at, :], NT)


def remap_call(kernel, inputs, out_rows, high, low, cost, name):
    vmem = pl.BlockSpec(memory_space=pltpu.VMEM)
    return pl.pallas_call(
        kernel,
        out_shape=[jax.ShapeDtypeStruct((rows, PIXELS_DEV), jnp.float32) for rows in out_rows],
        in_specs=[vmem] * (len(inputs) + 2),
        out_specs=[vmem] * len(out_rows),
        compiler_params=pltpu.CompilerParams(vmem_limit_bytes=24 * MIB),
        cost_estimate=cost,
        name=name,
    )(*inputs, high, low)


def remap_rows_kernel(x, high, low, out):
    for at, result in remap_blocks(x[...], high, low):
        out[:, at] = result


def near_rows(own, other_sub, other_lev, other_both):
    even = lax.axis_index("sub") == 0
    lev_first = lax.axis_index("lev") % 2 == 0
    left, right = jnp.where(even, own, other_sub), jnp.where(even, other_sub, own)
    up, down = jnp.where(even, other_lev, other_both), jnp.where(even, other_both, other_lev)
    return [
        jnp.where(lev_first, left, up),
        jnp.where(lev_first, right, down),
        jnp.where(lev_first, up, left),
        jnp.where(lev_first, down, right),
    ]


def far_rows(same_sub, other_sub):
    even = lax.axis_index("sub") == 0
    levels = same_sub.shape[0] // 2
    blocks = [jnp.where(even, same_sub, other_sub), jnp.where(even, other_sub, same_sub)]
    return [jnp.concatenate([block[:levels], block[levels:]], axis=1) for block in blocks]


def keeps_near():
    return lax.axis_index("tm") == lax.axis_index("lev") // 2


def remap_first_kernel(own, sibling, other_lev, same, other, high, low, near_out, far_out, send):
    rows = own.shape[0]
    levels = rows // HOURS
    blocks = near_rows(own[...], sibling[:rows], other_lev[:rows], other_lev[rows:])
    x = jnp.concatenate(blocks + far_rows(same[...], other[...]), axis=0)
    for at, result in remap_blocks(x, high, low):
        for hour in range(HOURS):
            for lev in range(2):
                pieces = []
                for sub in range(2):
                    start = ((lev * 2 + sub) * HOURS + hour) * levels
                    pieces.append(result[start : start + levels])
                place = (hour * 2 + lev) * rows
                near_out[place : place + rows, at] = jnp.concatenate(pieces, axis=0)
        far_out[:, at] = result[4 * rows :]
    near = keeps_near()

    @pl.when(near)
    def _():
        send[:rows] = far_out[...]
        send[rows:] = jnp.zeros((send.shape[0] - rows, PIXELS_DEV), jnp.float32)

    @pl.when(jnp.logical_not(near))
    def _():
        send[...] = near_out[...]


def remap_last_kernel(same, other, high, low, out):
    x = jnp.concatenate(far_rows(same[...], other[...]), axis=0)
    for at, result in remap_blocks(x, high, low):
        out[:, at] = result


def hour_matrix(step_hour, levels, steps, hours, cuts):
    rows, columns = cuts * levels, cuts * 2 * levels * steps
    row = lax.broadcasted_iota(jnp.int32, (rows, columns), 0)
    column = lax.broadcasted_iota(jnp.int32, (rows, columns), 1)
    span = levels * steps
    near = jnp.full((rows, columns), -1, jnp.int32)
    for cut in range(cuts):
        for half in range(2):
            step = column - (cut * 2 + half) * span - (row - cut * levels) * steps
            inside = (row >= cut * levels) & (row < (cut + 1) * levels)
            inside = inside & (step >= 0) & (step < steps)
            near = jnp.where(inside, step, near)
    blocks = []
    for hour in hours:
        block = jnp.zeros((rows, columns), jnp.float32)
        for step in range(steps):
            block = jnp.where(near == step, jnp.where(step_hour[step] == hour, 1.0, 0.0), block)
        blocks.append(block)
    return jnp.concatenate(blocks, axis=0).astype(jnp.bfloat16)


def peer_shard(k, j):
    subs = lax.axis_size("sub")
    return (lax.axis_index("lev") ^ k) * subs + (lax.axis_index("sub") ^ j)


def field_copies(field, buffer, arrived, peers):
    copies = []
    for place, (k, j) in enumerate(peers):
        start = pl.multiple_of(peer_shard(k, j) * CELLS_DEV, CELLS_DEV)
        copy = pltpu.make_async_copy(
            field.at[:, :, pl.ds(start, CELLS_DEV)], buffer.at[place], arrived.at[place]
        )
        copy.start()
        copies.append(copy)
    return copies


def near_sum_kernel(peers, step_hour, field, *refs):
    own, other_lev, sibling, buffer, arrived = refs[-5:]
    _, levels, steps, cells = buffer.shape
    rows = HOURS * levels
    copies = field_copies(field, buffer, arrived, peers)
    matrix = hour_matrix(step_hour, levels, steps, range(HOURS), 1)
    for place, (k, j) in enumerate(peers):
        copies[place].wait()
        x = buffer[place].reshape(levels * steps, cells)
        result = dot(matrix, jnp.concatenate(split(x), axis=0), NN)
        if j == 0:
            (own if k == 0 else other_lev)[...] = result
        else:
            sibling[k * rows : (k + 1) * rows] = result


def far_sum_kernel(peers, step_hour, field, *refs):
    theirs, mine, buffer, arrived = refs[-4:]
    _, levels, steps, cells = buffer.shape
    copies = field_copies(field, buffer, arrived, peers)
    me = lax.axis_index("tm")
    matrix = hour_matrix(step_hour, levels, steps, (1 - me, me), 2)
    rows, cut = 2 * levels, cells // 2
    for place, copy in enumerate(copies):
        copy.wait()
        high, low = split(buffer[place].reshape(levels * steps, cells))
        stacked = jnp.concatenate([high[:, :cut], low[:, :cut], high[:, cut:], low[:, cut:]], axis=0)
        result = dot(matrix, stacked, NN)
        theirs[place * rows : (place + 1) * rows] = result[:rows]
        mine[place * rows : (place + 1) * rows] = result[rows:]


def sum_call(kernel, peers, step_hour, field, after, out_shapes, name):
    levels, steps, _ = field.shape
    vmem = pl.BlockSpec(memory_space=pltpu.VMEM)
    return pl.pallas_call(
        functools.partial(kernel, peers),
        out_shape=out_shapes,
        in_specs=[pl.BlockSpec(memory_space=pltpu.SMEM)] + [pl.BlockSpec(memory_space=pl.ANY)] * (1 + len(after)),
        out_specs=[vmem] * len(out_shapes),
        scratch_shapes=[
            pltpu.VMEM((len(peers), levels, steps, CELLS_DEV), jnp.float32),
            pltpu.SemaphoreType.DMA((len(peers),)),
        ],
        compiler_params=pltpu.CompilerParams(vmem_limit_bytes=52 * MIB),
        cost_estimate=LIGHT,
        name=name,
    )(step_hour, field, *after)


def near_sums(peers, step_hour, field, *after):
    rows = HOURS * field.shape[0]
    shapes = [jax.ShapeDtypeStruct((n * rows, CELLS_DEV), jnp.float32) for n in (1, 1, 2)]
    return sum_call(near_sum_kernel, peers, step_hour, field, after, shapes, "near_sums")


def far_sums(peers, step_hour, field, *after):
    shape = jax.ShapeDtypeStruct((len(peers) * 2 * field.shape[0], CELLS_DEV // 2), jnp.float32)
    return sum_call(far_sum_kernel, peers, step_hour, field, after, [shape] * 2, "far_sums")


def merge_kernel(mine, got, *refs):
    outs = refs[-2:]
    rows = outs[0].shape[0]
    for place, out in enumerate(outs):
        at = slice(place * rows, (place + 1) * rows)
        out[...] = mine[at] + got[at]


def join_kernel(mine, got, *refs):
    rows = mine.shape[0]
    refs[-1][:rows] = mine[...]
    refs[-1][rows:] = got[rows:]


def small_call(kernel, inputs, after, shapes, cost, name):
    vmem = pl.BlockSpec(memory_space=pltpu.VMEM)
    return pl.pallas_call(
        kernel,
        out_shape=[jax.ShapeDtypeStruct(shape, jnp.float32) for shape in shapes],
        in_specs=[vmem] * len(inputs) + [pl.BlockSpec(memory_space=pl.ANY)] * len(after),
        out_specs=[vmem] * len(shapes),
        compiler_params=pltpu.CompilerParams(vmem_limit_bytes=8 * MIB),
        cost_estimate=cost,
        name=name,
    )(*inputs, *after)


def merge(mine, got, *after):
    shape = (mine.shape[0] // 2, mine.shape[1])
    return small_call(merge_kernel, [mine, got], after, [shape, shape], HEAVY, "merge")


def join(mine, got, *after):
    return small_call(join_kernel, [mine, got], after, [got.shape], HEAVY, "join")[0]


def finish_kernel(divisor, near_own, far_own, got, last, got_last, out):
    me, lev = lax.axis_index("tm"), lax.axis_index("lev")
    rows = far_own.shape[0]
    near = keeps_near()

    @pl.when(near)
    def _():
        out[...] = (near_own[...] + got[...]) / divisor

    @pl.when(jnp.logical_not(near))
    def _():
        for hour in range(HOURS):
            first_at = pl.multiple_of((hour * 2 + 1 - lev % 2) * rows, rows)
            last_at = pl.multiple_of((hour * 2 + lev % 2) * rows, rows)
            out[pl.ds(first_at, rows), :] = jnp.where(me == hour, far_own[...], got[:rows]) / divisor
            out[pl.ds(last_at, rows), :] = jnp.where(me == hour, last[...], got_last[...]) / divisor


def finish(arrays, divisor):
    call = functools.partial(finish_kernel, divisor)
    return small_call(call, arrays, [], [arrays[0].shape], LIGHT, "finish")[0]


def hour_plan(level_field, tile_weight, tile_rows, tile_columns, live_count, step_hour):
    levs, subs, shards_tm = lax.axis_size("lev"), lax.axis_size("sub"), lax.axis_size("tm")
    half = levs // 2
    divisor = float(level_field.shape[0] * shards_tm // HOURS)
    field = jnp.transpose(level_field, (1, 0, 2))

    def to_peer(x, k, j):
        pairs = [(a * subs + b, (a ^ k) * subs + (b ^ j)) for a in range(levs) for b in range(subs)]
        return lax.ppermute(x, ("lev", "sub"), pairs)

    def swap(x):
        return lax.ppermute(x, "tm", [(0, 1), (1, 0)])

    def far_peers(k):
        return [(k, j) for j in range(subs)]

    near_peers = [(k, j) for j in reversed(range(subs)) for k in reversed(range(half))]
    theirs_a, mine_a = far_sums(far_peers(half + 1), step_hour, field)
    got_a = swap(theirs_a)
    own, other_lev, sibling = near_sums(near_peers, step_hour, field, theirs_a)
    got_sibling = to_peer(sibling, 0, 1)
    theirs_b, mine_b = far_sums(far_peers(half), step_hour, field, sibling)
    got_b = swap(theirs_b)

    merged_a = merge(mine_a, got_a, theirs_b)
    far_a = [to_peer(x, half + 1, j) for j, x in enumerate(merged_a)]
    joined = join(other_lev, got_sibling, *merged_a)
    got_lev = to_peer(joined, 1, 0)
    merged_b = merge(mine_b, got_b, joined)
    far_b = [to_peer(x, half, j) for j, x in enumerate(merged_b)]

    high, low = place_tiles(tile_rows, tile_columns, live_count, tile_weight, *merged_b)
    rows = mine_a.shape[0] // subs
    near = [own, got_sibling, got_lev]
    near_out, far_out, send = remap_call(
        remap_first_kernel, near + far_a, [4 * rows, rows, 4 * rows], high, low, LIGHT, "remap_first"
    )
    got = swap(send)
    (last,) = remap_call(remap_last_kernel, far_b, [rows], high, low, HEAVY, "remap_last")
    got_last = swap(last)
    out = finish([near_out, far_out, got, last, got_last], divisor)
    return out.reshape(HOURS, out.shape[0] // HOURS, PIXELS_DEV)


def general_plan(level_field, tile_weight, tile_rows, tile_columns, live_count, step_hour):
    steps, levels, cells = level_field.shape
    shards = lax.axis_size("lev") * lax.axis_size("sub")
    divisor = float(steps * lax.axis_size("tm") // HOURS)
    hours = jnp.arange(HOURS, dtype=jnp.int32)
    table = (step_hour[None, :] == hours[:, None]).astype(jnp.float32)
    fields = level_field.reshape(steps, levels, shards, cells // shards)
    partial = jnp.einsum("hs,slgc->ghlc", table, fields, precision=lax.Precision.HIGHEST)
    regrouped = lax.all_to_all(partial, ("lev", "sub"), split_axis=0, concat_axis=0, tiled=True)
    rows = jnp.transpose(regrouped, (1, 0, 2, 3)).reshape(-1, cells // shards)
    high, low = place_tiles(tile_rows, tile_columns, live_count, tile_weight)
    (out,) = remap_call(remap_rows_kernel, [rows], [rows.shape[0]], high, low, LIGHT, "remap_rows")
    out = out.reshape(HOURS, shards * levels, PIXELS_DEV) / divisor
    return lax.psum_scatter(out, "tm", scatter_dimension=1, tiled=True)


def solution(mesh):
    sizes = mesh.shape
    paired = sizes["tm"] == HOURS and sizes["lev"] == 4 and sizes["sub"] == 2
    placed = (
        P(("groups", "tm"), ("lev", "sub"), None),
        P(None, ("lev", "sub")),
        P(("lev", "sub")),
        P(("lev", "sub")),
        P(("lev", "sub")),
        P("tm"),
    )
    return jax.shard_map(
        hour_plan if paired else general_plan,
        mesh=mesh,
        in_specs=placed,
        out_specs=P("groups", "tm", ("lev", "sub")),
        check_vma=False,
    )
```

```python
import functools

import jax
import jax.numpy as jnp
from jax import lax
from jax.experimental import pallas as pl
from jax.experimental.pallas import tpu as pltpu
from jax.sharding import PartitionSpec as P

TILE = 64
HOURS = 2
CT_DEV = 32
PT_DEV = 16
SLOTS = 128
CELLS_DEV = CT_DEV * TILE
PIXELS_DEV = PT_DEV * TILE
LANES = 2 * TILE
MIB = 1 << 20

LIGHT = pl.CostEstimate(flops=1, bytes_accessed=1, transcendentals=0)
HEAVY = pl.CostEstimate(flops=10_000_000_000, bytes_accessed=1, transcendentals=0)

NT = (((1,), (1,)), ((), ()))
NN = (((1,), (0,)), ((), ()))


def split(x):
    high = x.astype(jnp.bfloat16)
    return high, (x - high.astype(jnp.float32)).astype(jnp.bfloat16)


def dot(a, b, dims):
    return lax.dot_general(a, b, dims, preferred_element_type=jnp.float32)


GROUP = 8


def place_kernel(rows, columns, count, weights, *refs):
    held, high, low, passed, total = refs
    band = 128
    passed[...] = held[...]

    @pl.loop(0, PIXELS_DEV // band)
    def _(b):
        total[pl.ds(pl.multiple_of(b * band, band), band), :] = jnp.zeros((band, CELLS_DEV), jnp.float32)

    lane_half = lax.broadcasted_iota(jnp.int32, (TILE, LANES), 1) // TILE
    live = count[0]

    @pl.loop(0, (live + GROUP - 1) // GROUP)
    def _(g):
        for pair in range(GROUP // 2):
            lanes = pl.ds(pl.multiple_of((g * (GROUP // 2) + pair) * LANES, LANES), LANES)
            tiles = weights[:, lanes]
            turned = pltpu.roll(tiles, TILE, 1)
            for i in range(2):
                k = g * GROUP + pair * 2 + i
                row, column = rows[k], columns[k]
                side = jnp.where(k < live, column & 1, -1)
                tile = jnp.where(lane_half == i, tiles, turned)
                at = (
                    pl.ds(pl.multiple_of(row * TILE, TILE), TILE),
                    pl.ds(pl.multiple_of((column >> 1) * LANES, LANES), LANES),
                )
                total[at] = total[at] + jnp.where(lane_half == side, tile, 0.0)

    @pl.loop(0, PIXELS_DEV // band)
    def _(b):
        at = pl.ds(pl.multiple_of(b * band, band), band)
        high[at, :], low[at, :] = split(total[at, :])


def place_tiles(rows, columns, count, weights, held):
    smem = pl.BlockSpec(memory_space=pltpu.SMEM)
    vmem = pl.BlockSpec(memory_space=pltpu.VMEM)
    half = jax.ShapeDtypeStruct((PIXELS_DEV, CELLS_DEV), jnp.bfloat16)
    return pl.pallas_call(
        place_kernel,
        out_shape=(half, half, jax.ShapeDtypeStruct(held.shape, held.dtype)),
        in_specs=[smem, smem, smem, vmem, vmem],
        out_specs=(vmem, vmem, vmem),
        scratch_shapes=[pltpu.VMEM((PIXELS_DEV, CELLS_DEV), jnp.float32)],
        compiler_params=pltpu.CompilerParams(vmem_limit_bytes=28 * MIB),
        cost_estimate=HEAVY,
        name="place_tiles",
    )(rows, columns, count, weights, held)


PIXEL_BLOCK = 256


def remap_blocks(x, high, low):
    m = x.shape[0]
    x_high, x_low = split(x)
    both = jnp.concatenate([x_high, x_low], axis=0)
    for start in range(0, PIXELS_DEV, PIXEL_BLOCK):
        at = slice(start, start + PIXEL_BLOCK)
        first = dot(both, high[at, :], NT)
        yield at, first[:m] + first[m:] + dot(x_high, low[at, :], NT)


def remap_call(kernel, inputs, after, out_rows, high, low, cost, name):
    vmem = pl.BlockSpec(memory_space=pltpu.VMEM)
    return pl.pallas_call(
        kernel,
        out_shape=[jax.ShapeDtypeStruct((rows, PIXELS_DEV), jnp.float32) for rows in out_rows],
        in_specs=[vmem] * (len(inputs) + 2) + [pl.BlockSpec(memory_space=pl.ANY)] * len(after),
        out_specs=[vmem] * len(out_rows),
        compiler_params=pltpu.CompilerParams(vmem_limit_bytes=24 * MIB),
        cost_estimate=cost,
        name=name,
    )(*inputs, high, low, *after)


def remap_rows_kernel(x, high, low, out):
    for at, result in remap_blocks(x[...], high, low):
        out[:, at] = result


def far_rows(same_sub, other_sub):
    even = lax.axis_index("sub") == 0
    levels = same_sub.shape[0] // 2
    blocks = [jnp.where(even, same_sub, other_sub), jnp.where(even, other_sub, same_sub)]
    return [jnp.concatenate([block[:levels], block[levels:]], axis=1) for block in blocks]


def keeps_near():
    return lax.axis_index("tm") == lax.axis_index("lev") // 2


def near_rows(same_sub, other_sub):
    even = lax.axis_index("sub") == 0
    return [jnp.where(even, same_sub, other_sub), jnp.where(even, other_sub, same_sub)]


def by_hour(result, levels):
    pieces = [result[start : start + levels] for start in range(0, 2 * HOURS * levels, levels)]
    return jnp.concatenate([pieces[sub * HOURS + hour] for hour in range(HOURS) for sub in range(2)], axis=0)


def remap_chip_kernel(own, sibling, high, low, *refs):
    out = refs[-1]
    x = jnp.concatenate(near_rows(own[...], sibling[...]), axis=0)
    for at, result in remap_blocks(x, high, low):
        out[:, at] = by_hour(result, own.shape[0] // HOURS)


def remap_first_kernel(near_same, near_other, same, other, high, low, *refs):
    near_out, far_out, send = refs[-3:]
    levels = near_same.shape[0] // HOURS
    rows = 2 * HOURS * levels
    blocks = near_rows(near_same[...], near_other[...]) + far_rows(same[...], other[...])
    for at, result in remap_blocks(jnp.concatenate(blocks, axis=0), high, low):
        near_out[:, at] = by_hour(result, levels)
        far_out[:, at] = result[rows:]
    near = keeps_near()
    half = far_out.shape[0]

    @pl.when(near)
    def _():
        send[:half] = far_out[...]
        send[half:] = jnp.zeros((send.shape[0] - half, PIXELS_DEV), jnp.float32)

    @pl.when(jnp.logical_not(near))
    def _():
        send[...] = near_out[...]


def remap_last_kernel(same, other, high, low, *refs):
    out = refs[-1]
    x = jnp.concatenate(far_rows(same[...], other[...]), axis=0)
    for at, result in remap_blocks(x, high, low):
        out[:, at] = result


def hour_matrix(step_hour, levels, steps, hours, cuts):
    rows, columns = cuts * levels, cuts * 2 * levels * steps
    row = lax.broadcasted_iota(jnp.int32, (rows, columns), 0)
    column = lax.broadcasted_iota(jnp.int32, (rows, columns), 1)
    span = levels * steps
    near = jnp.full((rows, columns), -1, jnp.int32)
    for cut in range(cuts):
        for half in range(2):
            step = column - (cut * 2 + half) * span - (row - cut * levels) * steps
            inside = (row >= cut * levels) & (row < (cut + 1) * levels)
            inside = inside & (step >= 0) & (step < steps)
            near = jnp.where(inside, step, near)
    blocks = []
    for hour in hours:
        block = jnp.zeros((rows, columns), jnp.float32)
        for step in range(steps):
            block = jnp.where(near == step, jnp.where(step_hour[step] == hour, 1.0, 0.0), block)
        blocks.append(block)
    return jnp.concatenate(blocks, axis=0).astype(jnp.bfloat16)


def peer_shard(k, j):
    subs = lax.axis_size("sub")
    return (lax.axis_index("lev") ^ k) * subs + (lax.axis_index("sub") ^ j)


def field_copies(field, buffer, arrived, peers):
    copies = []
    for place, (k, j) in enumerate(peers):
        start = pl.multiple_of(peer_shard(k, j) * CELLS_DEV, CELLS_DEV)
        copy = pltpu.make_async_copy(
            field.at[:, :, pl.ds(start, CELLS_DEV)], buffer.at[place], arrived.at[place]
        )
        copy.start()
        copies.append(copy)
    return copies


def sums_kernel(near_peers, far_peers, step_hour, field, *refs):
    buffer, arrived = refs[-2:]
    near = refs[: len(near_peers)]
    theirs, mine = refs[len(near_peers) : -2 : 2], refs[len(near_peers) + 1 : -2 : 2]
    _, levels, steps, cells = buffer.shape
    peers = [*sum(far_peers, []), *near_peers]
    copies = field_copies(field, buffer, arrived, peers)
    me = lax.axis_index("tm")
    matrix = hour_matrix(step_hour, levels, steps, (1 - me, me), 2)
    rows, cut = 2 * levels, cells // 2
    place = 0
    for chunk, members in enumerate(far_peers):
        for j in range(len(members)):
            copies[place].wait()
            high, low = split(buffer[place].reshape(levels * steps, cells))
            halves = [high[:, :cut], low[:, :cut], high[:, cut:], low[:, cut:]]
            result = dot(matrix, jnp.concatenate(halves, axis=0), NN)
            theirs[chunk][j * rows : (j + 1) * rows] = result[:rows]
            mine[chunk][j * rows : (j + 1) * rows] = result[rows:]
            place += 1
    matrix = hour_matrix(step_hour, levels, steps, range(HOURS), 1)
    for out in near:
        copies[place].wait()
        x = buffer[place].reshape(levels * steps, cells)
        out[...] = dot(matrix, jnp.concatenate(split(x), axis=0), NN)
        place += 1


def hour_sums(near_peers, far_peers, step_hour, field):
    levels, steps, _ = field.shape
    vmem = pl.BlockSpec(memory_space=pltpu.VMEM)
    shapes = [(HOURS * levels, CELLS_DEV)] * len(near_peers)
    for members in far_peers:
        shapes += [(len(members) * 2 * levels, CELLS_DEV // 2)] * 2
    count = len(near_peers) + sum(map(len, far_peers))
    outs = pl.pallas_call(
        functools.partial(sums_kernel, near_peers, far_peers),
        out_shape=[jax.ShapeDtypeStruct(shape, jnp.float32) for shape in shapes],
        in_specs=[pl.BlockSpec(memory_space=pltpu.SMEM), pl.BlockSpec(memory_space=pl.ANY)],
        out_specs=[vmem] * len(shapes),
        scratch_shapes=[
            pltpu.VMEM((count, levels, steps, CELLS_DEV), jnp.float32),
            pltpu.SemaphoreType.DMA((count,)),
        ],
        compiler_params=pltpu.CompilerParams(vmem_limit_bytes=52 * MIB),
        cost_estimate=LIGHT,
        name="hour_sums",
    )(step_hour, field)
    far = outs[len(near_peers) :]
    return outs[: len(near_peers)], list(zip(far[::2], far[1::2]))


def merge_kernel(mine, got, *refs):
    outs = refs[-2:]
    rows = outs[0].shape[0]
    for place, out in enumerate(outs):
        at = slice(place * rows, (place + 1) * rows)
        out[...] = mine[at] + got[at]


def small_call(kernel, inputs, after, shapes, cost, name):
    vmem = pl.BlockSpec(memory_space=pltpu.VMEM)
    return pl.pallas_call(
        kernel,
        out_shape=[jax.ShapeDtypeStruct(shape, jnp.float32) for shape in shapes],
        in_specs=[vmem] * len(inputs) + [pl.BlockSpec(memory_space=pl.ANY)] * len(after),
        out_specs=[vmem] * len(shapes),
        compiler_params=pltpu.CompilerParams(vmem_limit_bytes=8 * MIB),
        cost_estimate=cost,
        name=name,
    )(*inputs, *after)


def merge(mine, got, *after):
    shape = (mine.shape[0] // 2, mine.shape[1])
    return small_call(merge_kernel, [mine, got], after, [shape, shape], HEAVY, "merge")


def finish_kernel(divisor, chip, got_chip, near_own, far_own, got, last, got_last, out):
    me, lev = lax.axis_index("tm"), lax.axis_index("lev") % 2
    rows = far_own.shape[0]
    near = keeps_near()
    for hour in range(HOURS):
        first_at = pl.ds(pl.multiple_of((hour * 2 + 1 - lev) * rows, rows), rows)
        last_at = pl.ds(pl.multiple_of((hour * 2 + lev) * rows, rows), rows)
        here = slice(hour * rows, (hour + 1) * rows)

        @pl.when(near)
        def _():
            out[first_at, :] = (near_own[here] + got[here]) / divisor
            out[last_at, :] = (chip[here] + got_chip[here]) / divisor

        @pl.when(jnp.logical_not(near))
        def _():
            out[first_at, :] = jnp.where(me == hour, far_own[...], got[:rows]) / divisor
            out[last_at, :] = jnp.where(me == hour, last[...], got_last[...]) / divisor


def finish(arrays, divisor):
    call = functools.partial(finish_kernel, divisor)
    shape = (2 * arrays[0].shape[0], PIXELS_DEV)
    return small_call(call, arrays, [], [shape], LIGHT, "finish")[0]


def hour_plan(level_field, tile_weight, tile_rows, tile_columns, live_count, step_hour):
    levs, subs, shards_tm = lax.axis_size("lev"), lax.axis_size("sub"), lax.axis_size("tm")
    half = levs // 2
    divisor = float(level_field.shape[0] * shards_tm // HOURS)
    field = jnp.transpose(level_field, (1, 0, 2))

    def to_peer(x, k, j):
        pairs = [(a * subs + b, (a ^ k) * subs + (b ^ j)) for a in range(levs) for b in range(subs)]
        return lax.ppermute(x, ("lev", "sub"), pairs)

    def swap(x):
        return lax.ppermute(x, "tm", [(0, 1), (1, 0)])

    near_peers = [(1, 0), (1, 1), (0, 1), (0, 0)]
    far_peers = [[(k, j) for j in range(subs)] for k in (half + 1, half)]
    near, ((theirs_a, mine_a), (theirs_b, mine_b)) = hour_sums(near_peers, far_peers, step_hour, field)
    got_a = swap(theirs_a)
    near = [to_peer(x, k, j) for x, (k, j) in list(zip(near, near_peers))[:-1]] + [near[-1]]
    near_same, near_other, sibling, own = near
    high, low, theirs_b = place_tiles(tile_rows, tile_columns, live_count, tile_weight, theirs_b)
    got_b = swap(theirs_b)
    merged_a = merge(mine_a, got_a, sibling, high)
    far_a = [to_peer(x, *peer) for x, peer in zip(merged_a, far_peers[0])]

    rows = mine_a.shape[0] // subs
    (chip,) = remap_call(
        remap_chip_kernel, [own, sibling], merged_a, [2 * rows], high, low, HEAVY, "remap_chip"
    )
    got_chip = swap(chip)
    merged_b = merge(mine_b, got_b, near_same, near_other, chip)
    far_b = [to_peer(x, *peer) for x, peer in zip(merged_b, far_peers[1])]
    near_out, far_out, send = remap_call(
        remap_first_kernel,
        [near_same, near_other, *far_a],
        merged_b,
        [2 * rows, rows, 2 * rows],
        high,
        low,
        HEAVY,
        "remap_first",
    )
    got = swap(send)
    (last,) = remap_call(remap_last_kernel, far_b, [send], [rows], high, low, HEAVY, "remap_last")
    got_last = swap(last)
    out = finish([chip, got_chip, near_out, far_out, got, last, got_last], divisor)
    return out.reshape(HOURS, out.shape[0] // HOURS, PIXELS_DEV)


def general_plan(level_field, tile_weight, tile_rows, tile_columns, live_count, step_hour):
    steps, levels, cells = level_field.shape
    shards = lax.axis_size("lev") * lax.axis_size("sub")
    divisor = float(steps * lax.axis_size("tm") // HOURS)
    hours = jnp.arange(HOURS, dtype=jnp.int32)
    table = (step_hour[None, :] == hours[:, None]).astype(jnp.float32)
    fields = level_field.reshape(steps, levels, shards, cells // shards)
    partial = jnp.einsum("hs,slgc->ghlc", table, fields, precision=lax.Precision.HIGHEST)
    regrouped = lax.all_to_all(partial, ("lev", "sub"), split_axis=0, concat_axis=0, tiled=True)
    rows = jnp.transpose(regrouped, (1, 0, 2, 3)).reshape(-1, cells // shards)
    high, low, rows = place_tiles(tile_rows, tile_columns, live_count, tile_weight, rows)
    (out,) = remap_call(remap_rows_kernel, [rows], [], [rows.shape[0]], high, low, LIGHT, "remap_rows")
    out = out.reshape(HOURS, shards * levels, PIXELS_DEV) / divisor
    return lax.psum_scatter(out, "tm", scatter_dimension=1, tiled=True)


def solution(mesh):
    sizes = mesh.shape
    paired = sizes["tm"] == HOURS and sizes["lev"] == 4 and sizes["sub"] == 2
    placed = (
        P(("groups", "tm"), ("lev", "sub"), None),
        P(None, ("lev", "sub")),
        P(("lev", "sub")),
        P(("lev", "sub")),
        P(("lev", "sub")),
        P("tm"),
    )
    return jax.shard_map(
        hour_plan if paired else general_plan,
        mesh=mesh,
        in_specs=placed,
        out_specs=P("groups", "tm", ("lev", "sub")),
        check_vma=False,
    )
```

```python
import functools

import jax
import jax.numpy as jnp
from jax import lax
from jax.experimental import pallas as pl
from jax.experimental.pallas import tpu as pltpu
from jax.sharding import PartitionSpec as P

TILE = 64
HOURS = 2
CT_DEV = 32
PT_DEV = 16
SLOTS = 128
CELLS_DEV = CT_DEV * TILE
PIXELS_DEV = PT_DEV * TILE
LANES = 2 * TILE
MIB = 1 << 20

LIGHT = pl.CostEstimate(flops=1, bytes_accessed=1, transcendentals=0)
HEAVY = pl.CostEstimate(flops=10_000_000_000, bytes_accessed=1, transcendentals=0)

NT = (((1,), (1,)), ((), ()))
NN = (((1,), (0,)), ((), ()))


def split(x):
    high = x.astype(jnp.bfloat16)
    return high, (x - high.astype(jnp.float32)).astype(jnp.bfloat16)


def dot(a, b, dims):
    return lax.dot_general(a, b, dims, preferred_element_type=jnp.float32)


GROUP = 8


def place_kernel(rows, columns, count, weights, *refs):
    high, low, total = refs[-3:]
    band = 128

    @pl.loop(0, PIXELS_DEV // band)
    def _(b):
        total[pl.ds(pl.multiple_of(b * band, band), band), :] = jnp.zeros((band, CELLS_DEV), jnp.float32)

    lane_half = lax.broadcasted_iota(jnp.int32, (TILE, LANES), 1) // TILE
    live = count[0]

    @pl.loop(0, (live + GROUP - 1) // GROUP)
    def _(g):
        for pair in range(GROUP // 2):
            lanes = pl.ds(pl.multiple_of((g * (GROUP // 2) + pair) * LANES, LANES), LANES)
            tiles = weights[:, lanes]
            turned = pltpu.roll(tiles, TILE, 1)
            for i in range(2):
                k = g * GROUP + pair * 2 + i
                row, column = rows[k], columns[k]
                side = jnp.where(k < live, column & 1, -1)
                tile = jnp.where(lane_half == i, tiles, turned)
                at = (
                    pl.ds(pl.multiple_of(row * TILE, TILE), TILE),
                    pl.ds(pl.multiple_of((column >> 1) * LANES, LANES), LANES),
                )
                total[at] = total[at] + jnp.where(lane_half == side, tile, 0.0)

    @pl.loop(0, PIXELS_DEV // band)
    def _(b):
        at = pl.ds(pl.multiple_of(b * band, band), band)
        high[at, :], low[at, :] = split(total[at, :])


def place_tiles(rows, columns, count, weights, *after):
    smem = pl.BlockSpec(memory_space=pltpu.SMEM)
    vmem = pl.BlockSpec(memory_space=pltpu.VMEM)
    half = jax.ShapeDtypeStruct((PIXELS_DEV, CELLS_DEV), jnp.bfloat16)
    return pl.pallas_call(
        place_kernel,
        out_shape=(half, half),
        in_specs=[smem, smem, smem, vmem] + [pl.BlockSpec(memory_space=pl.ANY)] * len(after),
        out_specs=(vmem, vmem),
        scratch_shapes=[pltpu.VMEM((PIXELS_DEV, CELLS_DEV), jnp.float32)],
        compiler_params=pltpu.CompilerParams(vmem_limit_bytes=28 * MIB),
        cost_estimate=HEAVY,
        name="place_tiles",
    )(rows, columns, count, weights, *after)


PIXEL_BLOCK = 256


def remap_blocks(x, high, low):
    m = x.shape[0]
    x_high, x_low = split(x)
    both = jnp.concatenate([x_high, x_low], axis=0)
    for start in range(0, PIXELS_DEV, PIXEL_BLOCK):
        at = slice(start, start + PIXEL_BLOCK)
        first = dot(both, high[at, :], NT)
        yield at, first[:m] + first[m:] + dot(x_high, low[at, :], NT)


def remap_call(kernel, inputs, after, out_rows, high, low, cost, name):
    vmem = pl.BlockSpec(memory_space=pltpu.VMEM)
    return pl.pallas_call(
        kernel,
        out_shape=[jax.ShapeDtypeStruct((rows, PIXELS_DEV), jnp.float32) for rows in out_rows],
        in_specs=[vmem] * (len(inputs) + 2) + [pl.BlockSpec(memory_space=pl.ANY)] * len(after),
        out_specs=[vmem] * len(out_rows),
        compiler_params=pltpu.CompilerParams(vmem_limit_bytes=24 * MIB),
        cost_estimate=cost,
        name=name,
    )(*inputs, high, low, *after)


def remap_rows_kernel(x, high, low, out):
    for at, result in remap_blocks(x[...], high, low):
        out[:, at] = result


def far_rows(same_sub, other_sub):
    even = lax.axis_index("sub") == 0
    levels = same_sub.shape[0] // 2
    blocks = [jnp.where(even, same_sub, other_sub), jnp.where(even, other_sub, same_sub)]
    return [jnp.concatenate([block[:levels], block[levels:]], axis=1) for block in blocks]


def keeps_near():
    return lax.axis_index("tm") == lax.axis_index("lev") // 2


def near_rows(same_sub, other_sub):
    even = lax.axis_index("sub") == 0
    return [jnp.where(even, same_sub, other_sub), jnp.where(even, other_sub, same_sub)]


def by_hour(result, levels):
    pieces = [result[start : start + levels] for start in range(0, 2 * HOURS * levels, levels)]
    return jnp.concatenate([pieces[sub * HOURS + hour] for hour in range(HOURS) for sub in range(2)], axis=0)


def remap_chip_kernel(own, sibling, high, low, *refs):
    out = refs[-1]
    x = jnp.concatenate(near_rows(own[...], sibling[...]), axis=0)
    for at, result in remap_blocks(x, high, low):
        out[:, at] = by_hour(result, own.shape[0] // HOURS)


def remap_first_kernel(near_same, near_other, same, other, high, low, *refs):
    near_out, far_out, send = refs[-3:]
    levels = near_same.shape[0] // HOURS
    rows = 2 * HOURS * levels
    blocks = near_rows(near_same[...], near_other[...]) + far_rows(same[...], other[...])
    for at, result in remap_blocks(jnp.concatenate(blocks, axis=0), high, low):
        near_out[:, at] = by_hour(result, levels)
        far_out[:, at] = result[rows:]
    near = keeps_near()
    half = far_out.shape[0]

    @pl.when(near)
    def _():
        send[:half] = far_out[...]
        send[half:] = jnp.zeros((send.shape[0] - half, PIXELS_DEV), jnp.float32)

    @pl.when(jnp.logical_not(near))
    def _():
        send[...] = near_out[...]


def remap_last_kernel(same, other, high, low, *refs):
    out = refs[-1]
    x = jnp.concatenate(far_rows(same[...], other[...]), axis=0)
    for at, result in remap_blocks(x, high, low):
        out[:, at] = result


def hour_matrix(step_hour, levels, steps, hours, cuts):
    rows, columns = cuts * levels, cuts * 2 * levels * steps
    row = lax.broadcasted_iota(jnp.int32, (rows, columns), 0)
    column = lax.broadcasted_iota(jnp.int32, (rows, columns), 1)
    span = levels * steps
    near = jnp.full((rows, columns), -1, jnp.int32)
    for cut in range(cuts):
        for half in range(2):
            step = column - (cut * 2 + half) * span - (row - cut * levels) * steps
            inside = (row >= cut * levels) & (row < (cut + 1) * levels)
            inside = inside & (step >= 0) & (step < steps)
            near = jnp.where(inside, step, near)
    blocks = []
    for hour in hours:
        block = jnp.zeros((rows, columns), jnp.float32)
        for step in range(steps):
            block = jnp.where(near == step, jnp.where(step_hour[step] == hour, 1.0, 0.0), block)
        blocks.append(block)
    return jnp.concatenate(blocks, axis=0).astype(jnp.bfloat16)


def peer_shard(k, j):
    subs = lax.axis_size("sub")
    return (lax.axis_index("lev") ^ k) * subs + (lax.axis_index("sub") ^ j)


def field_copies(field, buffer, arrived, peers):
    copies = []
    for place, (k, j) in enumerate(peers):
        start = pl.multiple_of(peer_shard(k, j) * CELLS_DEV, CELLS_DEV)
        copy = pltpu.make_async_copy(
            field.at[:, :, pl.ds(start, CELLS_DEV)], buffer.at[place], arrived.at[place]
        )
        copy.start()
        copies.append(copy)
    return copies


def sums_kernel(near_peers, far_peers, step_hour, field, *refs):
    buffer, arrived = refs[-2:]
    outs = refs[-2 - len(near_peers) - 2 * len(far_peers) : -2]
    near, theirs, mine = outs[: len(near_peers)], outs[len(near_peers) :: 2], outs[len(near_peers) + 1 :: 2]
    _, levels, steps, cells = buffer.shape
    peers = [*sum(far_peers, []), *near_peers]
    copies = field_copies(field, buffer, arrived, peers)
    me = lax.axis_index("tm")
    matrix = hour_matrix(step_hour, levels, steps, (1 - me, me), 2)
    rows, cut = 2 * levels, cells // 2
    place = 0
    for chunk, members in enumerate(far_peers):
        for j in range(len(members)):
            copies[place].wait()
            high, low = split(buffer[place].reshape(levels * steps, cells))
            halves = [high[:, :cut], low[:, :cut], high[:, cut:], low[:, cut:]]
            result = dot(matrix, jnp.concatenate(halves, axis=0), NN)
            theirs[chunk][j * rows : (j + 1) * rows] = result[:rows]
            mine[chunk][j * rows : (j + 1) * rows] = result[rows:]
            place += 1
    if near:
        matrix = hour_matrix(step_hour, levels, steps, range(HOURS), 1)
    for out in near:
        copies[place].wait()
        x = buffer[place].reshape(levels * steps, cells)
        out[...] = dot(matrix, jnp.concatenate(split(x), axis=0), NN)
        place += 1


def hour_sums(near_peers, far_peers, step_hour, field, *after):
    levels, steps, _ = field.shape
    vmem = pl.BlockSpec(memory_space=pltpu.VMEM)
    shapes = [(HOURS * levels, CELLS_DEV)] * len(near_peers)
    for members in far_peers:
        shapes += [(len(members) * 2 * levels, CELLS_DEV // 2)] * 2
    count = len(near_peers) + sum(map(len, far_peers))
    outs = pl.pallas_call(
        functools.partial(sums_kernel, near_peers, far_peers),
        out_shape=[jax.ShapeDtypeStruct(shape, jnp.float32) for shape in shapes],
        in_specs=[pl.BlockSpec(memory_space=pltpu.SMEM)] + [pl.BlockSpec(memory_space=pl.ANY)] * (1 + len(after)),
        out_specs=[vmem] * len(shapes),
        scratch_shapes=[
            pltpu.VMEM((count, levels, steps, CELLS_DEV), jnp.float32),
            pltpu.SemaphoreType.DMA((count,)),
        ],
        compiler_params=pltpu.CompilerParams(vmem_limit_bytes=52 * MIB),
        cost_estimate=LIGHT,
        name="hour_sums",
    )(step_hour, field, *after)
    far = outs[len(near_peers) :]
    return outs[: len(near_peers)], list(zip(far[::2], far[1::2]))


def merge_kernel(parts, mine, got, *refs):
    outs = refs[-parts:]
    rows = mine.shape[0] // parts
    for place, out in enumerate(outs):
        at = slice(place * rows, (place + 1) * rows)
        out[...] = mine[at] + got[at]


def small_call(kernel, inputs, after, shapes, cost, name):
    vmem = pl.BlockSpec(memory_space=pltpu.VMEM)
    return pl.pallas_call(
        kernel,
        out_shape=[jax.ShapeDtypeStruct(shape, jnp.float32) for shape in shapes],
        in_specs=[vmem] * len(inputs) + [pl.BlockSpec(memory_space=pl.ANY)] * len(after),
        out_specs=[vmem] * len(shapes),
        compiler_params=pltpu.CompilerParams(vmem_limit_bytes=8 * MIB),
        cost_estimate=cost,
        name=name,
    )(*inputs, *after)


def merge(parts, mine, got, *after):
    shapes = [(mine.shape[0] // parts, mine.shape[1])] * parts
    return small_call(functools.partial(merge_kernel, parts), [mine, got], after, shapes, HEAVY, "merge")


def finish_kernel(divisor, chip, got_chip, near_own, far_own, got, last, got_last, out):
    me, lev = lax.axis_index("tm"), lax.axis_index("lev") % 2
    rows = far_own.shape[0]
    near = keeps_near()
    for hour in range(HOURS):
        first_at = pl.ds(pl.multiple_of((hour * 2 + 1 - lev) * rows, rows), rows)
        last_at = pl.ds(pl.multiple_of((hour * 2 + lev) * rows, rows), rows)
        here = slice(hour * rows, (hour + 1) * rows)

        @pl.when(near)
        def _():
            out[first_at, :] = (near_own[here] + got[here]) / divisor
            out[last_at, :] = (chip[here] + got_chip[here]) / divisor

        @pl.when(jnp.logical_not(near))
        def _():
            out[first_at, :] = jnp.where(me == hour, far_own[...], got[:rows]) / divisor
            out[last_at, :] = jnp.where(me == hour, last[...], got_last[...]) / divisor


def finish(arrays, divisor):
    call = functools.partial(finish_kernel, divisor)
    shape = (2 * arrays[0].shape[0], PIXELS_DEV)
    return small_call(call, arrays, [], [shape], LIGHT, "finish")[0]


def hour_plan(level_field, tile_weight, tile_rows, tile_columns, live_count, step_hour):
    levs, subs, shards_tm = lax.axis_size("lev"), lax.axis_size("sub"), lax.axis_size("tm")
    half = levs // 2
    divisor = float(level_field.shape[0] * shards_tm // HOURS)
    field = jnp.transpose(level_field, (1, 0, 2))

    def to_peer(x, k, j):
        pairs = [(a * subs + b, (a ^ k) * subs + (b ^ j)) for a in range(levs) for b in range(subs)]
        return lax.ppermute(x, ("lev", "sub"), pairs)

    def swap(x):
        return lax.ppermute(x, "tm", [(0, 1), (1, 0)])

    near_peers = [(1, 0), (1, 1), (0, 1), (0, 0)]
    chunks = [[(half + 1, 0)], [(half + 1, 1)], [(half, j) for j in range(subs)]]

    def send_merged(chunk, mine, got, *after):
        merged = merge(len(chunk), mine, got, *after)
        return merged, [to_peer(x, *peer) for x, peer in zip(merged, chunk)]

    _, [(theirs_0, mine_0)] = hour_sums([], chunks[:1], step_hour, field)
    got_0 = swap(theirs_0)
    near, [(theirs_1, mine_1)] = hour_sums(near_peers, chunks[1:2], step_hour, field, theirs_0)
    got_1 = swap(theirs_1)
    near_same, near_other, sibling = [to_peer(x, *peer) for x, peer in zip(near[:3], near_peers)]
    merged_0, far_0 = send_merged(chunks[0], mine_0, got_0, theirs_1)
    merged_1, far_1 = send_merged(chunks[1], mine_1, got_1, sibling, *merged_0)
    _, [(theirs_2, mine_2)] = hour_sums([], chunks[2:], step_hour, field, *merged_1)
    got_2 = swap(theirs_2)
    high, low = place_tiles(tile_rows, tile_columns, live_count, tile_weight, theirs_2)
    merged_2, far_2 = send_merged(chunks[2], mine_2, got_2, high, near_same, near_other)

    rows = mine_0.shape[0]
    (chip,) = remap_call(
        remap_chip_kernel, [near[3], sibling], merged_2, [2 * rows], high, low, HEAVY, "remap_chip"
    )
    got_chip = swap(chip)
    near_out, far_out, send = remap_call(
        remap_first_kernel,
        [near_same, near_other, *far_0, *far_1],
        [chip],
        [2 * rows, rows, 2 * rows],
        high,
        low,
        HEAVY,
        "remap_first",
    )
    got = swap(send)
    (last,) = remap_call(remap_last_kernel, far_2, [send], [rows], high, low, HEAVY, "remap_last")
    got_last = swap(last)
    out = finish([chip, got_chip, near_out, far_out, got, last, got_last], divisor)
    return out.reshape(HOURS, out.shape[0] // HOURS, PIXELS_DEV)


def general_plan(level_field, tile_weight, tile_rows, tile_columns, live_count, step_hour):
    steps, levels, cells = level_field.shape
    shards = lax.axis_size("lev") * lax.axis_size("sub")
    divisor = float(steps * lax.axis_size("tm") // HOURS)
    hours = jnp.arange(HOURS, dtype=jnp.int32)
    table = (step_hour[None, :] == hours[:, None]).astype(jnp.float32)
    fields = level_field.reshape(steps, levels, shards, cells // shards)
    partial = jnp.einsum("hs,slgc->ghlc", table, fields, precision=lax.Precision.HIGHEST)
    regrouped = lax.all_to_all(partial, ("lev", "sub"), split_axis=0, concat_axis=0, tiled=True)
    rows = jnp.transpose(regrouped, (1, 0, 2, 3)).reshape(-1, cells // shards)
    high, low = place_tiles(tile_rows, tile_columns, live_count, tile_weight)
    (out,) = remap_call(remap_rows_kernel, [rows], [], [rows.shape[0]], high, low, LIGHT, "remap_rows")
    out = out.reshape(HOURS, shards * levels, PIXELS_DEV) / divisor
    return lax.psum_scatter(out, "tm", scatter_dimension=1, tiled=True)


def solution(mesh):
    sizes = mesh.shape
    paired = sizes["tm"] == HOURS and sizes["lev"] == 4 and sizes["sub"] == 2
    placed = (
        P(("groups", "tm"), ("lev", "sub"), None),
        P(None, ("lev", "sub")),
        P(("lev", "sub")),
        P(("lev", "sub")),
        P(("lev", "sub")),
        P("tm"),
    )
    return jax.shard_map(
        hour_plan if paired else general_plan,
        mesh=mesh,
        in_specs=placed,
        out_specs=P("groups", "tm", ("lev", "sub")),
        check_vma=False,
    )
```

```python
import functools

import jax
import jax.numpy as jnp
from jax import lax
from jax.experimental import pallas as pl
from jax.experimental.pallas import tpu as pltpu
from jax.sharding import PartitionSpec as P

TILE = 64
HOURS = 2
CT_DEV = 32
PT_DEV = 16
SLOTS = 128
CELLS_DEV = CT_DEV * TILE
PIXELS_DEV = PT_DEV * TILE
LANES = 2 * TILE
MIB = 1 << 20

LIGHT = pl.CostEstimate(flops=1, bytes_accessed=1, transcendentals=0)
HEAVY = pl.CostEstimate(flops=10_000_000_000, bytes_accessed=1, transcendentals=0)

NT = (((1,), (1,)), ((), ()))
NN = (((1,), (0,)), ((), ()))


def split(x):
    high = x.astype(jnp.bfloat16)
    return high, (x - high.astype(jnp.float32)).astype(jnp.bfloat16)


def dot(a, b, dims):
    return lax.dot_general(a, b, dims, preferred_element_type=jnp.float32)


GROUP = 8


def place_kernel(rows, columns, count, weights, *refs):
    high, low, total = refs[-3:]
    band = 128

    @pl.loop(0, PIXELS_DEV // band)
    def _(b):
        total[pl.ds(pl.multiple_of(b * band, band), band), :] = jnp.zeros((band, CELLS_DEV), jnp.float32)

    lane_half = lax.broadcasted_iota(jnp.int32, (TILE, LANES), 1) // TILE
    live = count[0]

    @pl.loop(0, (live + GROUP - 1) // GROUP)
    def _(g):
        for pair in range(GROUP // 2):
            lanes = pl.ds(pl.multiple_of((g * (GROUP // 2) + pair) * LANES, LANES), LANES)
            tiles = weights[:, lanes]
            turned = pltpu.roll(tiles, TILE, 1)
            for i in range(2):
                k = g * GROUP + pair * 2 + i
                row, column = rows[k], columns[k]
                side = jnp.where(k < live, column & 1, -1)
                tile = jnp.where(lane_half == i, tiles, turned)
                at = (
                    pl.ds(pl.multiple_of(row * TILE, TILE), TILE),
                    pl.ds(pl.multiple_of((column >> 1) * LANES, LANES), LANES),
                )
                total[at] = total[at] + jnp.where(lane_half == side, tile, 0.0)

    @pl.loop(0, PIXELS_DEV // band)
    def _(b):
        at = pl.ds(pl.multiple_of(b * band, band), band)
        high[at, :], low[at, :] = split(total[at, :])


def place_tiles(rows, columns, count, weights, *after):
    smem = pl.BlockSpec(memory_space=pltpu.SMEM)
    vmem = pl.BlockSpec(memory_space=pltpu.VMEM)
    half = jax.ShapeDtypeStruct((PIXELS_DEV, CELLS_DEV), jnp.bfloat16)
    return pl.pallas_call(
        place_kernel,
        out_shape=(half, half),
        in_specs=[smem, smem, smem, vmem] + [pl.BlockSpec(memory_space=pl.ANY)] * len(after),
        out_specs=(vmem, vmem),
        scratch_shapes=[pltpu.VMEM((PIXELS_DEV, CELLS_DEV), jnp.float32)],
        compiler_params=pltpu.CompilerParams(vmem_limit_bytes=28 * MIB),
        cost_estimate=HEAVY,
        name="place_tiles",
    )(rows, columns, count, weights, *after)


PIXEL_BLOCK = 256


def remap_blocks(x, high, low):
    m = x.shape[0]
    x_high, x_low = split(x)
    both = jnp.concatenate([x_high, x_low], axis=0)
    for start in range(0, PIXELS_DEV, PIXEL_BLOCK):
        at = slice(start, start + PIXEL_BLOCK)
        first = dot(both, high[at, :], NT)
        yield at, first[:m] + first[m:] + dot(x_high, low[at, :], NT)


def remap_call(kernel, inputs, after, out_rows, high, low, cost, name):
    vmem = pl.BlockSpec(memory_space=pltpu.VMEM)
    return pl.pallas_call(
        kernel,
        out_shape=[jax.ShapeDtypeStruct((rows, PIXELS_DEV), jnp.float32) for rows in out_rows],
        in_specs=[vmem] * (len(inputs) + 2) + [pl.BlockSpec(memory_space=pl.ANY)] * len(after),
        out_specs=[vmem] * len(out_rows),
        compiler_params=pltpu.CompilerParams(vmem_limit_bytes=24 * MIB),
        cost_estimate=cost,
        name=name,
    )(*inputs, high, low, *after)


def remap_rows_kernel(x, high, low, out):
    for at, result in remap_blocks(x[...], high, low):
        out[:, at] = result


def unfold(block):
    levels = block.shape[0] // 2
    return jnp.concatenate([block[:levels], block[levels:]], axis=1)


def far_rows(same_sub, other_sub):
    even = lax.axis_index("sub") == 0
    blocks = [jnp.where(even, same_sub, other_sub), jnp.where(even, other_sub, same_sub)]
    return [unfold(block) for block in blocks]


def keeps_near():
    return lax.axis_index("tm") == lax.axis_index("lev") // 2


def near_rows(same_sub, other_sub):
    even = lax.axis_index("sub") == 0
    return [jnp.where(even, same_sub, other_sub), jnp.where(even, other_sub, same_sub)]


def by_hour(result, levels):
    pieces = [result[start : start + levels] for start in range(0, 2 * HOURS * levels, levels)]
    return jnp.concatenate([pieces[sub * HOURS + hour] for hour in range(HOURS) for sub in range(2)], axis=0)


def remap_chip_kernel(own, sibling, high, low, *refs):
    out = refs[-1]
    x = jnp.concatenate(near_rows(own[...], sibling[...]), axis=0)
    for at, result in remap_blocks(x, high, low):
        out[:, at] = by_hour(result, own.shape[0] // HOURS)


def remap_first_kernel(near_same, near_other, plain, same, other, high, low, *refs):
    near_out, far_out, send = refs[-3:]
    levels = near_same.shape[0] // HOURS
    rows = 2 * HOURS * levels
    blocks = near_rows(near_same[...], near_other[...]) + [plain[...]] + far_rows(same[...], other[...])
    for at, result in remap_blocks(jnp.concatenate(blocks, axis=0), high, low):
        near_out[:, at] = by_hour(result, levels)
        far_out[:, at] = result[rows:]
    near = keeps_near()

    @pl.when(near)
    def _():
        send[...] = far_out[...]

    @pl.when(jnp.logical_not(near))
    def _():
        send[...] = near_out[...]


def remap_last_kernel(block, high, low, *refs):
    out = refs[-1]
    x = unfold(block[...])
    x = jnp.concatenate([x, jnp.zeros((out.shape[0] - x.shape[0], x.shape[1]), jnp.float32)], axis=0)
    for at, result in remap_blocks(x, high, low):
        out[:, at] = result


def hour_matrix(step_hour, levels, steps, hours, cuts):
    rows, columns = cuts * levels, cuts * 2 * levels * steps
    row = lax.broadcasted_iota(jnp.int32, (rows, columns), 0)
    column = lax.broadcasted_iota(jnp.int32, (rows, columns), 1)
    span = levels * steps
    near = jnp.full((rows, columns), -1, jnp.int32)
    for cut in range(cuts):
        for half in range(2):
            step = column - (cut * 2 + half) * span - (row - cut * levels) * steps
            inside = (row >= cut * levels) & (row < (cut + 1) * levels)
            inside = inside & (step >= 0) & (step < steps)
            near = jnp.where(inside, step, near)
    blocks = []
    for hour in hours:
        block = jnp.zeros((rows, columns), jnp.float32)
        for step in range(steps):
            block = jnp.where(near == step, jnp.where(step_hour[step] == hour, 1.0, 0.0), block)
        blocks.append(block)
    return jnp.concatenate(blocks, axis=0).astype(jnp.bfloat16)


def peer_shard(k, j):
    subs = lax.axis_size("sub")
    return (lax.axis_index("lev") ^ k) * subs + (lax.axis_index("sub") ^ j)


def field_copies(field, buffer, arrived, peers):
    copies = []
    for place, (k, j) in enumerate(peers):
        start = pl.multiple_of(peer_shard(k, j) * CELLS_DEV, CELLS_DEV)
        copy = pltpu.make_async_copy(
            field.at[:, :, pl.ds(start, CELLS_DEV)], buffer.at[place], arrived.at[place]
        )
        copy.start()
        copies.append(copy)
    return copies


def sums_kernel(plain_peers, far_peers, step_hour, field, *refs):
    buffer, arrived = refs[-2:]
    outs = refs[-2 - len(plain_peers) - 2 * len(far_peers) : -2]
    near, theirs, mine = outs[: len(plain_peers)], outs[len(plain_peers) :: 2], outs[len(plain_peers) + 1 :: 2]
    _, levels, steps, cells = buffer.shape
    peers = [*sum(far_peers, []), *plain_peers]
    copies = field_copies(field, buffer, arrived, peers)
    me = lax.axis_index("tm")
    matrix = hour_matrix(step_hour, levels, steps, (1 - me, me), 2)
    rows, cut = 2 * levels, cells // 2
    place = 0
    for chunk, members in enumerate(far_peers):
        for j in range(len(members)):
            copies[place].wait()
            high, low = split(buffer[place].reshape(levels * steps, cells))
            halves = [high[:, :cut], low[:, :cut], high[:, cut:], low[:, cut:]]
            result = dot(matrix, jnp.concatenate(halves, axis=0), NN)
            theirs[chunk][j * rows : (j + 1) * rows] = result[:rows]
            mine[chunk][j * rows : (j + 1) * rows] = result[rows:]
            place += 1
    if near:
        matrix = hour_matrix(step_hour, levels, steps, range(HOURS), 1)
    for out in near:
        copies[place].wait()
        x = buffer[place].reshape(levels * steps, cells)
        out[...] = dot(matrix, jnp.concatenate(split(x), axis=0), NN)
        place += 1


def hour_sums(plain_peers, far_peers, step_hour, field, *after):
    levels, steps, _ = field.shape
    vmem = pl.BlockSpec(memory_space=pltpu.VMEM)
    shapes = [(HOURS * levels, CELLS_DEV)] * len(plain_peers)
    for members in far_peers:
        shapes += [(len(members) * 2 * levels, CELLS_DEV // 2)] * 2
    count = len(plain_peers) + sum(map(len, far_peers))
    outs = pl.pallas_call(
        functools.partial(sums_kernel, plain_peers, far_peers),
        out_shape=[jax.ShapeDtypeStruct(shape, jnp.float32) for shape in shapes],
        in_specs=[pl.BlockSpec(memory_space=pltpu.SMEM)] + [pl.BlockSpec(memory_space=pl.ANY)] * (1 + len(after)),
        out_specs=[vmem] * len(shapes),
        scratch_shapes=[
            pltpu.VMEM((count, levels, steps, CELLS_DEV), jnp.float32),
            pltpu.SemaphoreType.DMA((count,)),
        ],
        compiler_params=pltpu.CompilerParams(vmem_limit_bytes=52 * MIB),
        cost_estimate=LIGHT,
        name="hour_sums",
    )(step_hour, field, *after)
    far = outs[len(plain_peers) :]
    return outs[: len(plain_peers)], list(zip(far[::2], far[1::2]))


def merge_kernel(parts, mine, got, *refs):
    outs = refs[-parts:]
    rows = mine.shape[0] // parts
    for place, out in enumerate(outs):
        at = slice(place * rows, (place + 1) * rows)
        out[...] = mine[at] + got[at]


def small_call(kernel, inputs, after, shapes, cost, name):
    vmem = pl.BlockSpec(memory_space=pltpu.VMEM)
    return pl.pallas_call(
        kernel,
        out_shape=[jax.ShapeDtypeStruct(shape, jnp.float32) for shape in shapes],
        in_specs=[vmem] * len(inputs) + [pl.BlockSpec(memory_space=pl.ANY)] * len(after),
        out_specs=[vmem] * len(shapes),
        compiler_params=pltpu.CompilerParams(vmem_limit_bytes=8 * MIB),
        cost_estimate=cost,
        name=name,
    )(*inputs, *after)


def hold_kernel(x, *refs):
    refs[-1][...] = x[...]


def hold(x, *after):
    return small_call(hold_kernel, [x], after, [x.shape], HEAVY, "hold")[0]


def merge(parts, mine, got, *after):
    shapes = [(mine.shape[0] // parts, mine.shape[1])] * parts
    return small_call(functools.partial(merge_kernel, parts), [mine, got], after, shapes, HEAVY, "merge")


def finish_kernel(divisor, levels, chip, got_chip, near_own, far_own, got, last, got_last, out):
    me, lev, even = lax.axis_index("tm"), lax.axis_index("lev") % 2, lax.axis_index("sub") == 0
    rows = 2 * levels
    near = keeps_near()
    for hour in range(HOURS):
        first_at = pl.ds(pl.multiple_of((hour * 2 + 1 - lev) * rows, rows), rows)
        last_at = pl.ds(pl.multiple_of((hour * 2 + lev) * rows, rows), rows)
        here = slice(hour * rows, (hour + 1) * rows)

        @pl.when(near)
        def _():
            out[first_at, :] = (near_own[here] + got[here]) / divisor
            out[last_at, :] = (chip[here] + got_chip[here]) / divisor

        @pl.when(jnp.logical_not(near))
        def _():
            out[first_at, :] = jnp.where(me == hour, far_own[rows:], got[rows:]) / divisor
            plain = far_own[hour * levels : (hour + 1) * levels] + got[hour * levels : (hour + 1) * levels]
            other = jnp.where(me == hour, last[:levels], got_last[:levels])
            pair = [jnp.where(even, plain, other), jnp.where(even, other, plain)]
            out[last_at, :] = jnp.concatenate(pair, axis=0) / divisor


def finish(arrays, levels, divisor):
    call = functools.partial(finish_kernel, divisor, levels)
    shape = (2 * arrays[0].shape[0], PIXELS_DEV)
    return small_call(call, arrays, [], [shape], LIGHT, "finish")[0]


def hour_plan(level_field, tile_weight, tile_rows, tile_columns, live_count, step_hour):
    levs, subs, shards_tm = lax.axis_size("lev"), lax.axis_size("sub"), lax.axis_size("tm")
    half = levs // 2
    divisor = float(level_field.shape[0] * shards_tm // HOURS)
    field = jnp.transpose(level_field, (1, 0, 2))

    def to_peer(x, k, j):
        pairs = [(a * subs + b, (a ^ k) * subs + (b ^ j)) for a in range(levs) for b in range(subs)]
        return lax.ppermute(x, ("lev", "sub"), pairs)

    def swap(x):
        return lax.ppermute(x, "tm", [(0, 1), (1, 0)])

    near_peers = [(1, 0), (1, 1), (0, 1), (0, 0)]
    plain, first, second = (half, 0), [(half + 1, j) for j in range(subs)], [(half, 1)]

    def send_merged(chunk, mine, got, *after):
        merged = merge(len(chunk), mine, got, *after)
        return merged, [to_peer(x, *peer) for x, peer in zip(merged, chunk)]

    (plain_sums,), [(theirs_0, mine_0)] = hour_sums([plain], [first], step_hour, field)
    plain_got = to_peer(plain_sums, *plain)
    got_0 = swap(theirs_0)
    near, [(theirs_1, mine_1)] = hour_sums(near_peers, [second], step_hour, field, theirs_0)
    near_same, near_other, sibling = [to_peer(x, *peer) for x, peer in zip(near[:3], near_peers)]
    merged_0, far_0 = send_merged(first, mine_0, got_0, theirs_1)
    theirs_1 = hold(theirs_1, plain_got, *merged_0)
    got_1 = swap(theirs_1)
    high, low = place_tiles(tile_rows, tile_columns, live_count, tile_weight, theirs_1, sibling)
    merged_1, far_1 = send_merged(second, mine_1, got_1, high)

    levels = field.shape[0]
    rows = 2 * levels
    (chip,) = remap_call(
        remap_chip_kernel, [near[3], sibling], merged_1, [2 * rows], high, low, HEAVY, "remap_chip"
    )
    got_chip = swap(chip)
    near_out, far_out, send = remap_call(
        remap_first_kernel,
        [near_same, near_other, plain_got, *far_0],
        [chip],
        [2 * rows] * 3,
        high,
        low,
        HEAVY,
        "remap_first",
    )
    got = swap(send)
    padded = -(-levels // 16) * 16
    (last,) = remap_call(remap_last_kernel, far_1, [send], [padded], high, low, HEAVY, "remap_last")
    got_last = swap(last)
    out = finish([chip, got_chip, near_out, far_out, got, last, got_last], levels, divisor)
    return out.reshape(HOURS, out.shape[0] // HOURS, PIXELS_DEV)


def general_plan(level_field, tile_weight, tile_rows, tile_columns, live_count, step_hour):
    steps, levels, cells = level_field.shape
    shards = lax.axis_size("lev") * lax.axis_size("sub")
    divisor = float(steps * lax.axis_size("tm") // HOURS)
    hours = jnp.arange(HOURS, dtype=jnp.int32)
    table = (step_hour[None, :] == hours[:, None]).astype(jnp.float32)
    fields = level_field.reshape(steps, levels, shards, cells // shards)
    partial = jnp.einsum("hs,slgc->ghlc", table, fields, precision=lax.Precision.HIGHEST)
    regrouped = lax.all_to_all(partial, ("lev", "sub"), split_axis=0, concat_axis=0, tiled=True)
    rows = jnp.transpose(regrouped, (1, 0, 2, 3)).reshape(-1, cells // shards)
    high, low = place_tiles(tile_rows, tile_columns, live_count, tile_weight)
    (out,) = remap_call(remap_rows_kernel, [rows], [], [rows.shape[0]], high, low, LIGHT, "remap_rows")
    out = out.reshape(HOURS, shards * levels, PIXELS_DEV) / divisor
    return lax.psum_scatter(out, "tm", scatter_dimension=1, tiled=True)


def solution(mesh):
    sizes = mesh.shape
    paired = sizes["tm"] == HOURS and sizes["lev"] == 4 and sizes["sub"] == 2
    placed = (
        P(("groups", "tm"), ("lev", "sub"), None),
        P(None, ("lev", "sub")),
        P(("lev", "sub")),
        P(("lev", "sub")),
        P(("lev", "sub")),
        P("tm"),
    )
    return jax.shard_map(
        hour_plan if paired else general_plan,
        mesh=mesh,
        in_specs=placed,
        out_specs=P("groups", "tm", ("lev", "sub")),
        check_vma=False,
    )
```

```python
import functools

import jax
import jax.numpy as jnp
from jax import lax
from jax.experimental import pallas as pl
from jax.experimental.pallas import tpu as pltpu
from jax.sharding import PartitionSpec as P

TILE = 64
HOURS = 2
CT_DEV = 32
PT_DEV = 16
SLOTS = 128
CELLS_DEV = CT_DEV * TILE
PIXELS_DEV = PT_DEV * TILE
LANES = 2 * TILE
MIB = 1 << 20

LIGHT = pl.CostEstimate(flops=1, bytes_accessed=1, transcendentals=0)
MEDIUM = pl.CostEstimate(flops=2_500_000_000, bytes_accessed=1, transcendentals=0)
HEAVY = pl.CostEstimate(flops=10_000_000_000, bytes_accessed=1, transcendentals=0)

NT = (((1,), (1,)), ((), ()))
NN = (((1,), (0,)), ((), ()))


def split(x):
    high = x.astype(jnp.bfloat16)
    return high, (x - high.astype(jnp.float32)).astype(jnp.bfloat16)


def dot(a, b, dims):
    return lax.dot_general(a, b, dims, preferred_element_type=jnp.float32)


GROUP = 8


def place_kernel(rows, columns, count, weights, *refs):
    high, low, total = refs[-3:]
    band = 128

    @pl.loop(0, PIXELS_DEV // band)
    def _(b):
        total[pl.ds(pl.multiple_of(b * band, band), band), :] = jnp.zeros((band, CELLS_DEV), jnp.float32)

    lane_half = lax.broadcasted_iota(jnp.int32, (TILE, LANES), 1) // TILE
    live = count[0]

    @pl.loop(0, (live + GROUP - 1) // GROUP)
    def _(g):
        for pair in range(GROUP // 2):
            lanes = pl.ds(pl.multiple_of((g * (GROUP // 2) + pair) * LANES, LANES), LANES)
            tiles = weights[:, lanes]
            turned = pltpu.roll(tiles, TILE, 1)
            for i in range(2):
                k = g * GROUP + pair * 2 + i
                row, column = rows[k], columns[k]
                side = jnp.where(k < live, column & 1, -1)
                tile = jnp.where(lane_half == i, tiles, turned)
                at = (
                    pl.ds(pl.multiple_of(row * TILE, TILE), TILE),
                    pl.ds(pl.multiple_of((column >> 1) * LANES, LANES), LANES),
                )
                total[at] = total[at] + jnp.where(lane_half == side, tile, 0.0)

    @pl.loop(0, PIXELS_DEV // band)
    def _(b):
        at = pl.ds(pl.multiple_of(b * band, band), band)
        high[at, :], low[at, :] = split(total[at, :])


def place_tiles(rows, columns, count, weights, *after):
    smem = pl.BlockSpec(memory_space=pltpu.SMEM)
    vmem = pl.BlockSpec(memory_space=pltpu.VMEM)
    half = jax.ShapeDtypeStruct((PIXELS_DEV, CELLS_DEV), jnp.bfloat16)
    return pl.pallas_call(
        place_kernel,
        out_shape=(half, half),
        in_specs=[smem, smem, smem, vmem] + [pl.BlockSpec(memory_space=pl.ANY)] * len(after),
        out_specs=(vmem, vmem),
        scratch_shapes=[pltpu.VMEM((PIXELS_DEV, CELLS_DEV), jnp.float32)],
        compiler_params=pltpu.CompilerParams(vmem_limit_bytes=28 * MIB),
        cost_estimate=HEAVY,
        name="place_tiles",
    )(rows, columns, count, weights, *after)


PIXEL_BLOCK = 256


def remap_blocks(x, high, low):
    m = x.shape[0]
    x_high, x_low = split(x)
    both = jnp.concatenate([x_high, x_low], axis=0)
    for start in range(0, PIXELS_DEV, PIXEL_BLOCK):
        at = slice(start, start + PIXEL_BLOCK)
        first = dot(both, high[at, :], NT)
        yield at, first[:m] + first[m:] + dot(x_high, low[at, :], NT)


def remap_call(kernel, inputs, after, out_rows, high, low, cost, name, scratch_rows=()):
    vmem = pl.BlockSpec(memory_space=pltpu.VMEM)
    return pl.pallas_call(
        kernel,
        out_shape=[jax.ShapeDtypeStruct((rows, PIXELS_DEV), jnp.float32) for rows in out_rows],
        in_specs=[vmem] * (len(inputs) + 2) + [pl.BlockSpec(memory_space=pl.ANY)] * len(after),
        out_specs=[vmem] * len(out_rows),
        scratch_shapes=[pltpu.VMEM((rows, PIXELS_DEV), jnp.float32) for rows in scratch_rows],
        compiler_params=pltpu.CompilerParams(vmem_limit_bytes=24 * MIB),
        cost_estimate=cost,
        name=name,
    )(*inputs, high, low, *after)


def remap_rows_kernel(x, high, low, out):
    for at, result in remap_blocks(x[...], high, low):
        out[:, at] = result


def unfold(block):
    levels = block.shape[0] // 2
    return jnp.concatenate([block[:levels], block[levels:]], axis=1)


def far_rows(same_sub, other_sub):
    even = lax.axis_index("sub") == 0
    blocks = [jnp.where(even, same_sub, other_sub), jnp.where(even, other_sub, same_sub)]
    return [unfold(block) for block in blocks]


def keeps_near():
    return lax.axis_index("tm") == lax.axis_index("lev") // 2


def near_rows(same_sub, other_sub):
    even = lax.axis_index("sub") == 0
    return [jnp.where(even, same_sub, other_sub), jnp.where(even, other_sub, same_sub)]


def by_hour(result, levels):
    pieces = [result[start : start + levels] for start in range(0, 2 * HOURS * levels, levels)]
    return jnp.concatenate([pieces[sub * HOURS + hour] for hour in range(HOURS) for sub in range(2)], axis=0)


def sort_out(near_result, far_result, keep, send):
    near = keeps_near()

    @pl.when(near)
    def _():
        keep[...], send[...] = near_result[...], far_result[...]

    @pl.when(jnp.logical_not(near))
    def _():
        keep[...], send[...] = far_result[...], near_result[...]


def remap_both_kernel(own, pack, plain, high, low, *refs):
    keep, send, near_result, far_result = refs[-4:]
    rows = own.shape[0]
    other = jnp.concatenate([pack[:rows], pack[rows : 2 * rows]], axis=1)
    blocks = near_rows(own[...], other) + [plain[...]]
    for at, result in remap_blocks(jnp.concatenate(blocks, axis=0), high, low):
        near_result[:, at] = by_hour(result, rows // HOURS)
        far_result[:rows, at] = result[2 * rows :]
    far_result[rows:] = jnp.zeros((rows, PIXELS_DEV), jnp.float32)
    sort_out(near_result, far_result, keep, send)


def remap_one_kernel(near, far, high, low, *refs):
    keep, send, near_result, far_result = refs[-4:]
    rows = far.shape[0]
    blocks = far_rows(near[:rows], near[rows:]) + [far[...]]
    for at, result in remap_blocks(jnp.concatenate(blocks, axis=0), high, low):
        near_result[:, at] = result[:rows]
        far_result[:, at] = result[rows:]
    sort_out(near_result, far_result, keep, send)


def remap_last_kernel(block, high, low, *refs):
    out = refs[-1]
    x = unfold(block[...])
    x = jnp.concatenate([x, jnp.zeros((out.shape[0] - x.shape[0], x.shape[1]), jnp.float32)], axis=0)
    for at, result in remap_blocks(x, high, low):
        out[:, at] = result


def hour_matrix(step_hour, levels, steps, hours, cuts):
    rows, columns = cuts * levels, cuts * 2 * levels * steps
    row = lax.broadcasted_iota(jnp.int32, (rows, columns), 0)
    column = lax.broadcasted_iota(jnp.int32, (rows, columns), 1)
    span = levels * steps
    near = jnp.full((rows, columns), -1, jnp.int32)
    for cut in range(cuts):
        for half in range(2):
            step = column - (cut * 2 + half) * span - (row - cut * levels) * steps
            inside = (row >= cut * levels) & (row < (cut + 1) * levels)
            inside = inside & (step >= 0) & (step < steps)
            near = jnp.where(inside, step, near)
    blocks = []
    for hour in hours:
        block = jnp.zeros((rows, columns), jnp.float32)
        for step in range(steps):
            block = jnp.where(near == step, jnp.where(step_hour[step] == hour, 1.0, 0.0), block)
        blocks.append(block)
    return jnp.concatenate(blocks, axis=0).astype(jnp.bfloat16)


def peer_shard(k, j):
    subs = lax.axis_size("sub")
    return (lax.axis_index("lev") ^ k) * subs + (lax.axis_index("sub") ^ j)


def field_copies(field, buffer, arrived, peers):
    copies = []
    for place, (k, j) in enumerate(peers):
        start = pl.multiple_of(peer_shard(k, j) * CELLS_DEV, CELLS_DEV)
        copy = pltpu.make_async_copy(
            field.at[:, :, pl.ds(start, CELLS_DEV)], buffer.at[place], arrived.at[place]
        )
        copy.start()
        copies.append(copy)
    return copies


def sums_kernel(plain, first, second, step_hour, field, *refs):
    plain_out, own, pack, theirs_0, mine_0, theirs_1, mine_1, theirs_2, mine_2, buffer, arrived = refs
    _, levels, steps, cells = buffer.shape
    rows, cut = HOURS * levels, cells // 2
    peers = [plain, *first, (1, 0), (1, 1), (0, 1), (0, 0), second]
    copies = field_copies(field, buffer, arrived, peers)
    me = lax.axis_index("tm")
    by_place = hour_matrix(step_hour, levels, steps, (1 - me, me), 2)
    by_hour = hour_matrix(step_hour, levels, steps, range(HOURS), 1)

    def halves(place):
        copies[place].wait()
        return split(buffer[place].reshape(levels * steps, cells))

    def with_both_hours(place):
        return dot(by_hour, jnp.concatenate(halves(place), axis=0), NN)

    def theirs_and_mine(place):
        high, low = halves(place)
        stacked = [high[:, :cut], low[:, :cut], high[:, cut:], low[:, cut:]]
        result = dot(by_place, jnp.concatenate(stacked, axis=0), NN)
        return result[:rows], result[rows:]

    plain_out[...] = with_both_hours(0)
    for j in range(len(first)):
        at = slice(j * rows, (j + 1) * rows)
        theirs_0[at], mine_0[at] = theirs_and_mine(1 + j)
    place = 1 + len(first)
    theirs_1[...], mine_1[...] = theirs_and_mine(place)
    pack[2 * rows : 3 * rows], pack[3 * rows :] = theirs_and_mine(place + 1)
    result = with_both_hours(place + 2)
    pack[:rows], pack[rows : 2 * rows] = result[:, :cut], result[:, cut:]
    own[...] = with_both_hours(place + 3)
    theirs_2[...], mine_2[...] = theirs_and_mine(place + 4)


def hour_sums(plain, first, second, step_hour, field):
    levels, steps, _ = field.shape
    rows, cut = HOURS * levels, CELLS_DEV // 2
    vmem = pl.BlockSpec(memory_space=pltpu.VMEM)
    shapes = [(rows, CELLS_DEV)] * 2 + [(4 * rows, cut)]
    shapes += [(len(first) * rows, cut)] * 2 + [(rows, cut)] * 4
    count = len(first) + 6
    return pl.pallas_call(
        functools.partial(sums_kernel, plain, first, second),
        out_shape=[jax.ShapeDtypeStruct(shape, jnp.float32) for shape in shapes],
        in_specs=[pl.BlockSpec(memory_space=pltpu.SMEM), pl.BlockSpec(memory_space=pl.ANY)],
        out_specs=[vmem] * len(shapes),
        scratch_shapes=[
            pltpu.VMEM((count, levels, steps, CELLS_DEV), jnp.float32),
            pltpu.SemaphoreType.DMA((count,)),
        ],
        compiler_params=pltpu.CompilerParams(vmem_limit_bytes=52 * MIB),
        cost_estimate=LIGHT,
        name="hour_sums",
    )(step_hour, field)


def merge_first_kernel(mine, got, theirs_near, mine_near, pack, theirs_last, mine_last, *refs):
    *outs, theirs, kept = refs[-4:]
    rows = theirs_near.shape[0]
    for place, out in enumerate(outs):
        at = slice(place * rows, (place + 1) * rows)
        out[...] = mine[at] + got[at]
    theirs[:rows], kept[:rows] = theirs_near[...], mine_near[...]
    theirs[rows : 2 * rows], kept[rows : 2 * rows] = pack[2 * rows : 3 * rows], pack[3 * rows :]
    theirs[2 * rows :], kept[2 * rows :] = theirs_last[...], mine_last[...]


def merge_last_kernel(mine, got, *refs):
    near, last = refs[-2:]
    rows = near.shape[0]
    near[...] = mine[:rows] + got[:rows]
    last[...] = mine[rows:] + got[rows:]


def far_rows_kernel(same_sub, other_sub, out):
    out[...] = jnp.concatenate(far_rows(same_sub[...], other_sub[...]), axis=0)


def small_call(kernel, inputs, after, shapes, cost, name):
    vmem = pl.BlockSpec(memory_space=pltpu.VMEM)
    return pl.pallas_call(
        kernel,
        out_shape=[jax.ShapeDtypeStruct(shape, jnp.float32) for shape in shapes],
        in_specs=[vmem] * len(inputs) + [pl.BlockSpec(memory_space=pl.ANY)] * len(after),
        out_specs=[vmem] * len(shapes),
        compiler_params=pltpu.CompilerParams(vmem_limit_bytes=8 * MIB),
        cost_estimate=cost,
        name=name,
    )(*inputs, *after)


def finish_kernel(divisor, levels, both, got_both, one, got_one, last, got_last, out):
    me, lev, even = lax.axis_index("tm"), lax.axis_index("lev") % 2, lax.axis_index("sub") == 0
    rows = 2 * levels
    near = keeps_near()
    for hour in range(HOURS):
        one_at = pl.ds(pl.multiple_of((hour * 2 + 1 - lev) * rows, rows), rows)
        both_at = pl.ds(pl.multiple_of((hour * 2 + lev) * rows, rows), rows)
        out[one_at, :] = jnp.where(me == hour, one[...], got_one[...]) / divisor

        @pl.when(near)
        def _():
            here = slice(hour * rows, (hour + 1) * rows)
            out[both_at, :] = (both[here] + got_both[here]) / divisor

        @pl.when(jnp.logical_not(near))
        def _():
            here = slice(hour * levels, (hour + 1) * levels)
            plain = both[here] + got_both[here]
            other = jnp.where(me == hour, last[:levels], got_last[:levels])
            pair = [jnp.where(even, plain, other), jnp.where(even, other, plain)]
            out[both_at, :] = jnp.concatenate(pair, axis=0) / divisor


def finish(arrays, levels, divisor):
    call = functools.partial(finish_kernel, divisor, levels)
    shape = (2 * arrays[0].shape[0], PIXELS_DEV)
    return small_call(call, arrays, [], [shape], LIGHT, "finish")[0]


def hour_plan(level_field, tile_weight, tile_rows, tile_columns, live_count, step_hour):
    levs, subs, shards_tm = lax.axis_size("lev"), lax.axis_size("sub"), lax.axis_size("tm")
    half = levs // 2
    divisor = float(level_field.shape[0] * shards_tm // HOURS)
    field = jnp.transpose(level_field, (1, 0, 2))

    def to_peer(x, k, j):
        pairs = [(a * subs + b, (a ^ k) * subs + (b ^ j)) for a in range(levs) for b in range(subs)]
        return lax.ppermute(x, ("lev", "sub"), pairs)

    def swap(x):
        return lax.ppermute(x, "tm", [(0, 1), (1, 0)])

    plain, first, second = (half, 0), [(half + 1, j) for j in range(subs)], (half, 1)
    sums = hour_sums(plain, first, second, step_hour, field)
    plain_sums, own, pack, theirs_0, mine_0, theirs_1, mine_1, theirs_2, mine_2 = sums
    rows = 2 * field.shape[0]
    folded = theirs_1.shape
    pack = to_peer(pack, 0, 1)
    got_0 = swap(theirs_0)
    plain_got = to_peer(plain_sums, *plain)
    high, low = place_tiles(tile_rows, tile_columns, live_count, tile_weight, theirs_0)

    *merged, theirs_1, mine_1 = small_call(
        merge_first_kernel,
        [mine_0, got_0, theirs_1, mine_1, pack, theirs_2, mine_2],
        [high],
        [folded] * 2 + [(3 * rows, folded[1])] * 2,
        HEAVY,
        "merge_first",
    )
    first_got = [to_peer(x, *peer) for x, peer in reversed(list(zip(merged, first)))][::-1]
    got_1 = swap(theirs_1)
    both, send = remap_call(
        remap_both_kernel,
        [own, pack, plain_got],
        merged,
        [2 * rows] * 2,
        high,
        low,
        MEDIUM,
        "remap_both",
        [2 * rows] * 2,
    )
    got_both = swap(send)
    near, last = small_call(
        merge_last_kernel, [mine_1, got_1], [both], [(2 * rows, folded[1]), folded], HEAVY, "merge_last"
    )
    near_got = to_peer(near, 1, 0)
    second_got = to_peer(last, *second)
    far = small_call(far_rows_kernel, first_got, [], [(rows, CELLS_DEV)], HEAVY, "far_rows")[0]
    one, send = remap_call(
        remap_one_kernel, [near_got, far], [], [rows] * 2, high, low, LIGHT, "remap_one", [rows] * 2
    )
    got_one = swap(send)
    padded = -(-rows // 32) * 16
    (last,) = remap_call(remap_last_kernel, [second_got], [one], [padded], high, low, HEAVY, "remap_last")
    got_last = swap(last)
    out = finish([both, got_both, one, got_one, last, got_last], rows // 2, divisor)
    return out.reshape(HOURS, out.shape[0] // HOURS, PIXELS_DEV)


def general_plan(level_field, tile_weight, tile_rows, tile_columns, live_count, step_hour):
    steps, levels, cells = level_field.shape
    shards = lax.axis_size("lev") * lax.axis_size("sub")
    divisor = float(steps * lax.axis_size("tm") // HOURS)
    hours = jnp.arange(HOURS, dtype=jnp.int32)
    table = (step_hour[None, :] == hours[:, None]).astype(jnp.float32)
    fields = level_field.reshape(steps, levels, shards, cells // shards)
    partial = jnp.einsum("hs,slgc->ghlc", table, fields, precision=lax.Precision.HIGHEST)
    regrouped = lax.all_to_all(partial, ("lev", "sub"), split_axis=0, concat_axis=0, tiled=True)
    rows = jnp.transpose(regrouped, (1, 0, 2, 3)).reshape(-1, cells // shards)
    high, low = place_tiles(tile_rows, tile_columns, live_count, tile_weight)
    (out,) = remap_call(remap_rows_kernel, [rows], [], [rows.shape[0]], high, low, LIGHT, "remap_rows")
    out = out.reshape(HOURS, shards * levels, PIXELS_DEV) / divisor
    return lax.psum_scatter(out, "tm", scatter_dimension=1, tiled=True)


def solution(mesh):
    sizes = mesh.shape
    paired = sizes["tm"] == HOURS and sizes["lev"] == 4 and sizes["sub"] == 2
    placed = (
        P(("groups", "tm"), ("lev", "sub"), None),
        P(None, ("lev", "sub")),
        P(("lev", "sub")),
        P(("lev", "sub")),
        P(("lev", "sub")),
        P("tm"),
    )
    return jax.shard_map(
        hour_plan if paired else general_plan,
        mesh=mesh,
        in_specs=placed,
        out_specs=P("groups", "tm", ("lev", "sub")),
        check_vma=False,
    )
```

```python
import functools

import jax
import jax.numpy as jnp
from jax import lax
from jax.experimental import pallas as pl
from jax.experimental.pallas import tpu as pltpu
from jax.sharding import PartitionSpec as P

TILE = 64
HOURS = 2
CT_DEV = 32
PT_DEV = 16
SLOTS = 128
CELLS_DEV = CT_DEV * TILE
PIXELS_DEV = PT_DEV * TILE
LANES = 2 * TILE
MIB = 1 << 20

LIGHT = pl.CostEstimate(flops=1, bytes_accessed=1, transcendentals=0)
MEDIUM = pl.CostEstimate(flops=2_500_000_000, bytes_accessed=1, transcendentals=0)
HEAVY = pl.CostEstimate(flops=10_000_000_000, bytes_accessed=1, transcendentals=0)

NT = (((1,), (1,)), ((), ()))
NN = (((1,), (0,)), ((), ()))


def split(x):
    high = x.astype(jnp.bfloat16)
    return high, (x - high.astype(jnp.float32)).astype(jnp.bfloat16)


def dot(a, b, dims):
    return lax.dot_general(a, b, dims, preferred_element_type=jnp.float32)


GROUP = 8


def place_kernel(rows, columns, count, weights, *refs):
    high, low, total = refs[-3:]
    band = 128

    @pl.loop(0, PIXELS_DEV // band)
    def _(b):
        total[pl.ds(pl.multiple_of(b * band, band), band), :] = jnp.zeros((band, CELLS_DEV), jnp.float32)

    lane_half = lax.broadcasted_iota(jnp.int32, (TILE, LANES), 1) // TILE
    live = count[0]

    @pl.loop(0, (live + GROUP - 1) // GROUP)
    def _(g):
        for pair in range(GROUP // 2):
            lanes = pl.ds(pl.multiple_of((g * (GROUP // 2) + pair) * LANES, LANES), LANES)
            tiles = weights[:, lanes]
            turned = pltpu.roll(tiles, TILE, 1)
            for i in range(2):
                k = g * GROUP + pair * 2 + i
                row, column = rows[k], columns[k]
                side = jnp.where(k < live, column & 1, -1)
                tile = jnp.where(lane_half == i, tiles, turned)
                at = (
                    pl.ds(pl.multiple_of(row * TILE, TILE), TILE),
                    pl.ds(pl.multiple_of((column >> 1) * LANES, LANES), LANES),
                )
                total[at] = total[at] + jnp.where(lane_half == side, tile, 0.0)

    @pl.loop(0, PIXELS_DEV // band)
    def _(b):
        at = pl.ds(pl.multiple_of(b * band, band), band)
        high[at, :], low[at, :] = split(total[at, :])


def place_tiles(rows, columns, count, weights, *after):
    smem = pl.BlockSpec(memory_space=pltpu.SMEM)
    vmem = pl.BlockSpec(memory_space=pltpu.VMEM)
    half = jax.ShapeDtypeStruct((PIXELS_DEV, CELLS_DEV), jnp.bfloat16)
    return pl.pallas_call(
        place_kernel,
        out_shape=(half, half),
        in_specs=[smem, smem, smem, vmem] + [pl.BlockSpec(memory_space=pl.ANY)] * len(after),
        out_specs=(vmem, vmem),
        scratch_shapes=[pltpu.VMEM((PIXELS_DEV, CELLS_DEV), jnp.float32)],
        compiler_params=pltpu.CompilerParams(vmem_limit_bytes=28 * MIB),
        cost_estimate=LIGHT,
        name="place_tiles",
    )(rows, columns, count, weights, *after)


PIXEL_BLOCK = 256


def remap_blocks(x, high, low):
    m = x.shape[0]
    x_high, x_low = split(x)
    both = jnp.concatenate([x_high, x_low], axis=0)
    for start in range(0, PIXELS_DEV, PIXEL_BLOCK):
        at = slice(start, start + PIXEL_BLOCK)
        first = dot(both, high[at, :], NT)
        yield at, first[:m] + first[m:] + dot(x_high, low[at, :], NT)


def remap_call(kernel, inputs, after, out_rows, high, low, cost, name, scratch_rows=()):
    vmem = pl.BlockSpec(memory_space=pltpu.VMEM)
    return pl.pallas_call(
        kernel,
        out_shape=[jax.ShapeDtypeStruct((rows, PIXELS_DEV), jnp.float32) for rows in out_rows],
        in_specs=[vmem] * (len(inputs) + 2) + [pl.BlockSpec(memory_space=pl.ANY)] * len(after),
        out_specs=[vmem] * len(out_rows),
        scratch_shapes=[pltpu.VMEM((rows, PIXELS_DEV), jnp.float32) for rows in scratch_rows],
        compiler_params=pltpu.CompilerParams(vmem_limit_bytes=24 * MIB),
        cost_estimate=cost,
        name=name,
    )(*inputs, high, low, *after)


def remap_rows_kernel(x, high, low, out):
    for at, result in remap_blocks(x[...], high, low):
        out[:, at] = result


def unfold(block):
    levels = block.shape[0] // 2
    return jnp.concatenate([block[:levels], block[levels:]], axis=1)


def far_rows(same_sub, other_sub):
    even = lax.axis_index("sub") == 0
    blocks = [jnp.where(even, same_sub, other_sub), jnp.where(even, other_sub, same_sub)]
    return [unfold(block) for block in blocks]


def keeps_near():
    return lax.axis_index("tm") == lax.axis_index("lev") // 2


def near_rows(same_sub, other_sub):
    even = lax.axis_index("sub") == 0
    return [jnp.where(even, same_sub, other_sub), jnp.where(even, other_sub, same_sub)]


def by_hour(result, levels):
    pieces = [result[start : start + levels] for start in range(0, 2 * HOURS * levels, levels)]
    return jnp.concatenate([pieces[sub * HOURS + hour] for hour in range(HOURS) for sub in range(2)], axis=0)


def sort_out(near_result, far_result, keep, send):
    near = keeps_near()

    @pl.when(near)
    def _():
        keep[...], send[...] = near_result[...], far_result[...]

    @pl.when(jnp.logical_not(near))
    def _():
        keep[...], send[...] = far_result[...], near_result[...]


def remap_both_kernel(own, sibling, plain, high, low, *refs):
    keep, send, near_result, far_result = refs[-4:]
    rows = own.shape[0]
    blocks = near_rows(own[...], sibling[...]) + [plain[...]]
    for at, result in remap_blocks(jnp.concatenate(blocks, axis=0), high, low):
        near_result[:, at] = by_hour(result, rows // HOURS)
        far_result[:rows, at] = result[2 * rows :]
    far_result[rows:] = jnp.zeros((rows, PIXELS_DEV), jnp.float32)
    sort_out(near_result, far_result, keep, send)


def remap_near_kernel(near_same, near_other, far, high, low, *refs):
    keep, send, near_result, far_result = refs[-4:]
    rows = near_same.shape[0]
    blocks = near_rows(near_same[...], near_other[...]) + [far[...]]
    for at, result in remap_blocks(jnp.concatenate(blocks, axis=0), high, low):
        near_result[:, at] = by_hour(result, rows // HOURS)
        far_result[:rows, at] = result[2 * rows :]
    far_result[rows:] = jnp.zeros((rows, PIXELS_DEV), jnp.float32)
    sort_out(near_result, far_result, keep, send)


def remap_last_kernel(block, high, low, *refs):
    out = refs[-1]
    x = unfold(block[...])
    x = jnp.concatenate([x, jnp.zeros((out.shape[0] - x.shape[0], x.shape[1]), jnp.float32)], axis=0)
    for at, result in remap_blocks(x, high, low):
        out[:, at] = result


def hour_matrix(step_hour, levels, steps, hours, cuts):
    rows, columns = cuts * levels, cuts * 2 * levels * steps
    row = lax.broadcasted_iota(jnp.int32, (rows, columns), 0)
    column = lax.broadcasted_iota(jnp.int32, (rows, columns), 1)
    span = levels * steps
    near = jnp.full((rows, columns), -1, jnp.int32)
    for cut in range(cuts):
        for half in range(2):
            step = column - (cut * 2 + half) * span - (row - cut * levels) * steps
            inside = (row >= cut * levels) & (row < (cut + 1) * levels)
            inside = inside & (step >= 0) & (step < steps)
            near = jnp.where(inside, step, near)
    blocks = []
    for hour in hours:
        block = jnp.zeros((rows, columns), jnp.float32)
        for step in range(steps):
            block = jnp.where(near == step, jnp.where(step_hour[step] == hour, 1.0, 0.0), block)
        blocks.append(block)
    return jnp.concatenate(blocks, axis=0).astype(jnp.bfloat16)


def peer_shard(k, j):
    subs = lax.axis_size("sub")
    return (lax.axis_index("lev") ^ k) * subs + (lax.axis_index("sub") ^ j)


def field_copies(field, buffer, arrived, peers):
    copies = []
    for place, (k, j) in enumerate(peers):
        start = pl.multiple_of(peer_shard(k, j) * CELLS_DEV, CELLS_DEV)
        copy = pltpu.make_async_copy(
            field.at[:, :, pl.ds(start, CELLS_DEV)], buffer.at[place], arrived.at[place]
        )
        copy.start()
        copies.append(copy)
    return copies


def sums_kernel(plain, first, second, step_hour, field, *refs):
    *outs, buffer, arrived = refs
    _, levels, steps, cells = buffer.shape
    rows, cut = HOURS * levels, cells // 2
    copies = field_copies(field, buffer, arrived, [*plain, *first, second])
    me = lax.axis_index("tm")
    by_place = hour_matrix(step_hour, levels, steps, (1 - me, me), 2)
    by_hour = hour_matrix(step_hour, levels, steps, range(HOURS), 1)

    def halves(place):
        copies[place].wait()
        return split(buffer[place].reshape(levels * steps, cells))

    for place in range(len(plain)):
        outs[place][...] = dot(by_hour, jnp.concatenate(halves(place), axis=0), NN)
    theirs_first, mine_first, theirs_second, mine_second = outs[len(plain) :]
    for j in range(len(first) + 1):
        high, low = halves(len(plain) + j)
        stacked = [high[:, :cut], low[:, :cut], high[:, cut:], low[:, cut:]]
        result = dot(by_place, jnp.concatenate(stacked, axis=0), NN)
        if j < len(first):
            at = slice(j * rows, (j + 1) * rows)
            theirs_first[at], mine_first[at] = result[:rows], result[rows:]
        else:
            theirs_second[...], mine_second[...] = result[:rows], result[rows:]


def hour_sums(plain, first, second, step_hour, field):
    levels, steps, _ = field.shape
    rows, cut = HOURS * levels, CELLS_DEV // 2
    vmem = pl.BlockSpec(memory_space=pltpu.VMEM)
    shapes = [(rows, CELLS_DEV)] * len(plain) + [(len(first) * rows, cut)] * 2 + [(rows, cut)] * 2
    count = len(plain) + len(first) + 1
    outs = pl.pallas_call(
        functools.partial(sums_kernel, plain, first, second),
        out_shape=[jax.ShapeDtypeStruct(shape, jnp.float32) for shape in shapes],
        in_specs=[pl.BlockSpec(memory_space=pltpu.SMEM), pl.BlockSpec(memory_space=pl.ANY)],
        out_specs=[vmem] * len(shapes),
        scratch_shapes=[
            pltpu.VMEM((count, levels, steps, CELLS_DEV), jnp.float32),
            pltpu.SemaphoreType.DMA((count,)),
        ],
        compiler_params=pltpu.CompilerParams(vmem_limit_bytes=52 * MIB),
        cost_estimate=LIGHT,
        name="hour_sums",
    )(step_hour, field)
    return outs[: len(plain)], outs[len(plain) :]


def merge_kernel(mine, got, *refs):
    outs = refs[-(mine.shape[0] // refs[-1].shape[0]) :]
    rows = outs[0].shape[0]
    for place, out in enumerate(outs):
        at = slice(place * rows, (place + 1) * rows)
        out[...] = mine[at] + got[at]


def hold_kernel(x, *refs):
    refs[-1][...] = x[...]


def far_rows_kernel(same_sub, other_sub, out):
    out[...] = jnp.concatenate(far_rows(same_sub[...], other_sub[...]), axis=0)


def small_call(kernel, inputs, after, shapes, cost, name):
    vmem = pl.BlockSpec(memory_space=pltpu.VMEM)
    return pl.pallas_call(
        kernel,
        out_shape=[jax.ShapeDtypeStruct(shape, jnp.float32) for shape in shapes],
        in_specs=[vmem] * len(inputs) + [pl.BlockSpec(memory_space=pl.ANY)] * len(after),
        out_specs=[vmem] * len(shapes),
        compiler_params=pltpu.CompilerParams(vmem_limit_bytes=8 * MIB),
        cost_estimate=cost,
        name=name,
    )(*inputs, *after)


def finish_kernel(divisor, levels, chip, got_chip, one, got_one, last, got_last, out):
    me, lev, even = lax.axis_index("tm"), lax.axis_index("lev") % 2, lax.axis_index("sub") == 0
    rows = 2 * levels
    near = keeps_near()
    for hour in range(HOURS):
        same_at = pl.ds(pl.multiple_of((hour * 2 + lev) * rows, rows), rows)
        other_at = pl.ds(pl.multiple_of((hour * 2 + 1 - lev) * rows, rows), rows)

        @pl.when(near)
        def _():
            here = slice(hour * rows, (hour + 1) * rows)
            out[same_at, :] = (chip[here] + got_chip[here]) / divisor
            out[other_at, :] = (one[here] + got_one[here]) / divisor

        @pl.when(jnp.logical_not(near))
        def _():
            here = slice(hour * levels, (hour + 1) * levels)
            plain = chip[here] + got_chip[here]
            other = jnp.where(me == hour, last[:levels], got_last[:levels])
            pair = [jnp.where(even, plain, other), jnp.where(even, other, plain)]
            out[other_at, :] = jnp.concatenate(pair, axis=0) / divisor
            out[same_at, :] = jnp.where(me == hour, one[:rows], got_one[:rows]) / divisor


def finish(arrays, levels, divisor):
    call = functools.partial(finish_kernel, divisor, levels)
    shape = (2 * arrays[0].shape[0], PIXELS_DEV)
    return small_call(call, arrays, [], [shape], LIGHT, "finish")[0]


def hour_plan(level_field, tile_weight, tile_rows, tile_columns, live_count, step_hour):
    levs, subs, shards_tm = lax.axis_size("lev"), lax.axis_size("sub"), lax.axis_size("tm")
    half = levs // 2
    divisor = float(level_field.shape[0] * shards_tm // HOURS)
    field = jnp.transpose(level_field, (1, 0, 2))

    def to_peer(x, k, j):
        pairs = [(a * subs + b, (a ^ k) * subs + (b ^ j)) for a in range(levs) for b in range(subs)]
        return lax.ppermute(x, ("lev", "sub"), pairs)

    def swap(x):
        return lax.ppermute(x, "tm", [(0, 1), (1, 0)])

    plain = [(half + 1, 0), (1, 0), (1, 1), (0, 1), (0, 0)]
    first, second = [(half, j) for j in range(subs)], (half + 1, 1)
    sums, (theirs_0, mine_0, theirs_1, mine_1) = hour_sums(plain, first, second, step_hour, field)
    rows = 2 * field.shape[0]
    folded = theirs_1.shape
    sibling = to_peer(sums[3], *plain[3])
    near_got = [to_peer(x, *peer) for x, peer in list(zip(sums, plain))[1:3]]
    got_0 = swap(theirs_0)
    plain_got = to_peer(sums[0], *plain[0])
    high, low = place_tiles(tile_rows, tile_columns, live_count, tile_weight, theirs_0)

    merged = small_call(
        merge_kernel, [mine_0, got_0], [high, sibling], [folded] * subs, LIGHT, "merge_first"
    )
    first_got = [to_peer(x, *peer) for x, peer in zip(merged, first)]
    theirs_1 = small_call(hold_kernel, [theirs_1], [plain_got, *merged], [folded], LIGHT, "hold")[0]
    got_1 = swap(theirs_1)
    both, send = remap_call(
        remap_both_kernel,
        [sums[4], sibling, plain_got],
        [theirs_1],
        [2 * rows] * 2,
        high,
        low,
        MEDIUM,
        "remap_both",
        [2 * rows] * 2,
    )
    got_both = swap(send)
    merged = small_call(
        merge_kernel, [mine_1, got_1], [both, near_got[0]], [folded], HEAVY, "merge_last"
    )
    second_got = to_peer(merged[0], *second)
    far = small_call(far_rows_kernel, first_got, [], [(rows, CELLS_DEV)], HEAVY, "far_rows")[0]
    one, send = remap_call(
        remap_near_kernel,
        [*near_got, far],
        [],
        [2 * rows] * 2,
        high,
        low,
        LIGHT,
        "remap_near",
        [2 * rows] * 2,
    )
    got_one = swap(send)
    padded = -(-rows // 32) * 16
    (last,) = remap_call(remap_last_kernel, [second_got], [one], [padded], high, low, HEAVY, "remap_last")
    got_last = swap(last)
    out = finish([both, got_both, one, got_one, last, got_last], rows // 2, divisor)
    return out.reshape(HOURS, out.shape[0] // HOURS, PIXELS_DEV)


def general_plan(level_field, tile_weight, tile_rows, tile_columns, live_count, step_hour):
    steps, levels, cells = level_field.shape
    shards = lax.axis_size("lev") * lax.axis_size("sub")
    divisor = float(steps * lax.axis_size("tm") // HOURS)
    hours = jnp.arange(HOURS, dtype=jnp.int32)
    table = (step_hour[None, :] == hours[:, None]).astype(jnp.float32)
    fields = level_field.reshape(steps, levels, shards, cells // shards)
    partial = jnp.einsum("hs,slgc->ghlc", table, fields, precision=lax.Precision.HIGHEST)
    regrouped = lax.all_to_all(partial, ("lev", "sub"), split_axis=0, concat_axis=0, tiled=True)
    rows = jnp.transpose(regrouped, (1, 0, 2, 3)).reshape(-1, cells // shards)
    high, low = place_tiles(tile_rows, tile_columns, live_count, tile_weight)
    (out,) = remap_call(remap_rows_kernel, [rows], [], [rows.shape[0]], high, low, LIGHT, "remap_rows")
    out = out.reshape(HOURS, shards * levels, PIXELS_DEV) / divisor
    return lax.psum_scatter(out, "tm", scatter_dimension=1, tiled=True)


def solution(mesh):
    sizes = mesh.shape
    paired = sizes["tm"] == HOURS and sizes["lev"] == 4 and sizes["sub"] == 2
    placed = (
        P(("groups", "tm"), ("lev", "sub"), None),
        P(None, ("lev", "sub")),
        P(("lev", "sub")),
        P(("lev", "sub")),
        P(("lev", "sub")),
        P("tm"),
    )
    return jax.shard_map(
        hour_plan if paired else general_plan,
        mesh=mesh,
        in_specs=placed,
        out_specs=P("groups", "tm", ("lev", "sub")),
        check_vma=False,
    )
```

```python
import functools

import jax
import jax.numpy as jnp
from jax import lax
from jax.experimental import pallas as pl
from jax.experimental.pallas import tpu as pltpu
from jax.sharding import PartitionSpec as P

TILE = 64
HOURS = 2
CT_DEV = 32
PT_DEV = 16
SLOTS = 128
CELLS_DEV = CT_DEV * TILE
PIXELS_DEV = PT_DEV * TILE
LANES = 2 * TILE
MIB = 1 << 20

LIGHT = pl.CostEstimate(flops=1, bytes_accessed=1, transcendentals=0)
MEDIUM = pl.CostEstimate(flops=2_500_000_000, bytes_accessed=1, transcendentals=0)
HEAVY = pl.CostEstimate(flops=10_000_000_000, bytes_accessed=1, transcendentals=0)

NT = (((1,), (1,)), ((), ()))
NN = (((1,), (0,)), ((), ()))


def split(x):
    high = x.astype(jnp.bfloat16)
    return high, (x - high.astype(jnp.float32)).astype(jnp.bfloat16)


def dot(a, b, dims):
    return lax.dot_general(a, b, dims, preferred_element_type=jnp.float32)


GROUP = 8


def place_kernel(rows, columns, count, weights, *refs):
    high, low, total = refs[-3:]
    band = 128

    @pl.loop(0, PIXELS_DEV // band)
    def _(b):
        total[pl.ds(pl.multiple_of(b * band, band), band), :] = jnp.zeros((band, CELLS_DEV), jnp.float32)

    lane_half = lax.broadcasted_iota(jnp.int32, (TILE, LANES), 1) // TILE
    live = count[0]

    @pl.loop(0, (live + GROUP - 1) // GROUP)
    def _(g):
        for pair in range(GROUP // 2):
            lanes = pl.ds(pl.multiple_of((g * (GROUP // 2) + pair) * LANES, LANES), LANES)
            tiles = weights[:, lanes]
            turned = pltpu.roll(tiles, TILE, 1)
            for i in range(2):
                k = g * GROUP + pair * 2 + i
                row, column = rows[k], columns[k]
                side = jnp.where(k < live, column & 1, -1)
                tile = jnp.where(lane_half == i, tiles, turned)
                at = (
                    pl.ds(pl.multiple_of(row * TILE, TILE), TILE),
                    pl.ds(pl.multiple_of((column >> 1) * LANES, LANES), LANES),
                )
                total[at] = total[at] + jnp.where(lane_half == side, tile, 0.0)

    @pl.loop(0, PIXELS_DEV // band)
    def _(b):
        at = pl.ds(pl.multiple_of(b * band, band), band)
        high[at, :], low[at, :] = split(total[at, :])


def place_tiles(rows, columns, count, weights, *after):
    smem = pl.BlockSpec(memory_space=pltpu.SMEM)
    vmem = pl.BlockSpec(memory_space=pltpu.VMEM)
    half = jax.ShapeDtypeStruct((PIXELS_DEV, CELLS_DEV), jnp.bfloat16)
    return pl.pallas_call(
        place_kernel,
        out_shape=(half, half),
        in_specs=[smem, smem, smem, vmem] + [pl.BlockSpec(memory_space=pl.ANY)] * len(after),
        out_specs=(vmem, vmem),
        scratch_shapes=[pltpu.VMEM((PIXELS_DEV, CELLS_DEV), jnp.float32)],
        compiler_params=pltpu.CompilerParams(vmem_limit_bytes=28 * MIB),
        cost_estimate=HEAVY,
        name="place_tiles",
    )(rows, columns, count, weights, *after)


PIXEL_BLOCK = 256


def remap_blocks(x, high, low):
    m = x.shape[0]
    x_high, x_low = split(x)
    both = jnp.concatenate([x_high, x_low], axis=0)
    for start in range(0, PIXELS_DEV, PIXEL_BLOCK):
        at = slice(start, start + PIXEL_BLOCK)
        first = dot(both, high[at, :], NT)
        yield at, first[:m] + first[m:] + dot(x_high, low[at, :], NT)


def remap_call(kernel, inputs, after, out_rows, high, low, cost, name, scratch_rows=()):
    vmem = pl.BlockSpec(memory_space=pltpu.VMEM)
    return pl.pallas_call(
        kernel,
        out_shape=[jax.ShapeDtypeStruct((rows, PIXELS_DEV), jnp.float32) for rows in out_rows],
        in_specs=[vmem] * (len(inputs) + 2) + [pl.BlockSpec(memory_space=pl.ANY)] * len(after),
        out_specs=[vmem] * len(out_rows),
        scratch_shapes=[pltpu.VMEM((rows, PIXELS_DEV), jnp.float32) for rows in scratch_rows],
        compiler_params=pltpu.CompilerParams(vmem_limit_bytes=24 * MIB),
        cost_estimate=cost,
        name=name,
    )(*inputs, high, low, *after)


def remap_rows_kernel(x, high, low, out):
    for at, result in remap_blocks(x[...], high, low):
        out[:, at] = result


def unfold(block):
    levels = block.shape[0] // 2
    return jnp.concatenate([block[:levels], block[levels:]], axis=1)


def far_rows(same_sub, other_sub):
    even = lax.axis_index("sub") == 0
    blocks = [jnp.where(even, same_sub, other_sub), jnp.where(even, other_sub, same_sub)]
    return [unfold(block) for block in blocks]


def keeps_near():
    return lax.axis_index("tm") == lax.axis_index("lev") // 2


def near_rows(same_sub, other_sub):
    even = lax.axis_index("sub") == 0
    return [jnp.where(even, same_sub, other_sub), jnp.where(even, other_sub, same_sub)]


def by_hour(result, levels):
    pieces = [result[start : start + levels] for start in range(0, 2 * HOURS * levels, levels)]
    return jnp.concatenate([pieces[sub * HOURS + hour] for hour in range(HOURS) for sub in range(2)], axis=0)


def sort_out(near_result, far_result, keep, send):
    near = keeps_near()

    @pl.when(near)
    def _():
        keep[...], send[...] = near_result[...], far_result[...]

    @pl.when(jnp.logical_not(near))
    def _():
        keep[...], send[...] = far_result[...], near_result[...]


def remap_both_kernel(own, sibling, plain, high, low, *refs):
    keep, send, near_result, far_result = refs[-4:]
    rows = own.shape[0]
    blocks = near_rows(own[...], sibling[...]) + [plain[...]]
    for at, result in remap_blocks(jnp.concatenate(blocks, axis=0), high, low):
        near_result[:, at] = by_hour(result, rows // HOURS)
        far_result[:rows, at] = result[2 * rows :]
    far_result[rows:] = jnp.zeros((rows, PIXELS_DEV), jnp.float32)
    sort_out(near_result, far_result, keep, send)


def remap_near_kernel(near_same, near_other, far, high, low, *refs):
    keep, send, near_result, far_result = refs[-4:]
    rows = near_same.shape[0]
    blocks = near_rows(near_same[...], near_other[...]) + [far[...]]
    for at, result in remap_blocks(jnp.concatenate(blocks, axis=0), high, low):
        near_result[:, at] = by_hour(result, rows // HOURS)
        far_result[:rows, at] = result[2 * rows :]
    far_result[rows:] = jnp.zeros((rows, PIXELS_DEV), jnp.float32)
    sort_out(near_result, far_result, keep, send)


def remap_last_kernel(block, high, low, *refs):
    out = refs[-1]
    x = unfold(block[...])
    x = jnp.concatenate([x, jnp.zeros((out.shape[0] - x.shape[0], x.shape[1]), jnp.float32)], axis=0)
    for at, result in remap_blocks(x, high, low):
        out[:, at] = result


def hour_matrix(step_hour, levels, steps, hours, cuts):
    rows, columns = cuts * levels, cuts * 2 * levels * steps
    row = lax.broadcasted_iota(jnp.int32, (rows, columns), 0)
    column = lax.broadcasted_iota(jnp.int32, (rows, columns), 1)
    span = levels * steps
    near = jnp.full((rows, columns), -1, jnp.int32)
    for cut in range(cuts):
        for half in range(2):
            step = column - (cut * 2 + half) * span - (row - cut * levels) * steps
            inside = (row >= cut * levels) & (row < (cut + 1) * levels)
            inside = inside & (step >= 0) & (step < steps)
            near = jnp.where(inside, step, near)
    blocks = []
    for hour in hours:
        block = jnp.zeros((rows, columns), jnp.float32)
        for step in range(steps):
            block = jnp.where(near == step, jnp.where(step_hour[step] == hour, 1.0, 0.0), block)
        blocks.append(block)
    return jnp.concatenate(blocks, axis=0).astype(jnp.bfloat16)


def peer_shard(k, j):
    subs = lax.axis_size("sub")
    return (lax.axis_index("lev") ^ k) * subs + (lax.axis_index("sub") ^ j)


def field_copies(field, buffer, arrived, peers):
    copies = []
    for place, (k, j) in enumerate(peers):
        start = pl.multiple_of(peer_shard(k, j) * CELLS_DEV, CELLS_DEV)
        copy = pltpu.make_async_copy(
            field.at[:, :, pl.ds(start, CELLS_DEV)], buffer.at[place], arrived.at[place]
        )
        copy.start()
        copies.append(copy)
    return copies


def sums_kernel(plain, first, second, step_hour, field, *refs):
    *outs, buffer, arrived = refs
    _, levels, steps, cells = buffer.shape
    rows, cut = HOURS * levels, cells // 2
    copies = field_copies(field, buffer, arrived, [*plain, *first, second])
    me = lax.axis_index("tm")
    by_place = hour_matrix(step_hour, levels, steps, (1 - me, me), 2)
    by_hour = hour_matrix(step_hour, levels, steps, range(HOURS), 1)

    def halves(place):
        copies[place].wait()
        return split(buffer[place].reshape(levels * steps, cells))

    for place in range(len(plain)):
        outs[place][...] = dot(by_hour, jnp.concatenate(halves(place), axis=0), NN)
    theirs_first, mine_first, theirs_second, mine_second = outs[len(plain) :]
    for j in range(len(first) + 1):
        high, low = halves(len(plain) + j)
        stacked = [high[:, :cut], low[:, :cut], high[:, cut:], low[:, cut:]]
        result = dot(by_place, jnp.concatenate(stacked, axis=0), NN)
        if j < len(first):
            at = slice(j * rows, (j + 1) * rows)
            theirs_first[at], mine_first[at] = result[:rows], result[rows:]
        else:
            theirs_second[...], mine_second[...] = result[:rows], result[rows:]


def hour_sums(plain, first, second, step_hour, field):
    levels, steps, _ = field.shape
    rows, cut = HOURS * levels, CELLS_DEV // 2
    vmem = pl.BlockSpec(memory_space=pltpu.VMEM)
    shapes = [(rows, CELLS_DEV)] * len(plain) + [(len(first) * rows, cut)] * 2 + [(rows, cut)] * 2
    count = len(plain) + len(first) + 1
    outs = pl.pallas_call(
        functools.partial(sums_kernel, plain, first, second),
        out_shape=[jax.ShapeDtypeStruct(shape, jnp.float32) for shape in shapes],
        in_specs=[pl.BlockSpec(memory_space=pltpu.SMEM), pl.BlockSpec(memory_space=pl.ANY)],
        out_specs=[vmem] * len(shapes),
        scratch_shapes=[
            pltpu.VMEM((count, levels, steps, CELLS_DEV), jnp.float32),
            pltpu.SemaphoreType.DMA((count,)),
        ],
        compiler_params=pltpu.CompilerParams(vmem_limit_bytes=52 * MIB),
        cost_estimate=LIGHT,
        name="hour_sums",
    )(step_hour, field)
    return outs[: len(plain)], outs[len(plain) :]


def merge_kernel(mine, got, *refs):
    outs = refs[-(mine.shape[0] // refs[-1].shape[0]) :]
    rows = outs[0].shape[0]
    for place, out in enumerate(outs):
        at = slice(place * rows, (place + 1) * rows)
        out[...] = mine[at] + got[at]


def hold_kernel(x, *refs):
    refs[-1][...] = x[...]


def far_rows_kernel(same_sub, other_sub, out):
    out[...] = jnp.concatenate(far_rows(same_sub[...], other_sub[...]), axis=0)


def small_call(kernel, inputs, after, shapes, cost, name):
    vmem = pl.BlockSpec(memory_space=pltpu.VMEM)
    return pl.pallas_call(
        kernel,
        out_shape=[jax.ShapeDtypeStruct(shape, jnp.float32) for shape in shapes],
        in_specs=[vmem] * len(inputs) + [pl.BlockSpec(memory_space=pl.ANY)] * len(after),
        out_specs=[vmem] * len(shapes),
        compiler_params=pltpu.CompilerParams(vmem_limit_bytes=8 * MIB),
        cost_estimate=cost,
        name=name,
    )(*inputs, *after)


def finish_kernel(divisor, levels, chip, got_chip, one, got_one, last, got_last, out):
    me, lev, even = lax.axis_index("tm"), lax.axis_index("lev") % 2, lax.axis_index("sub") == 0
    rows = 2 * levels
    near = keeps_near()
    for hour in range(HOURS):
        same_at = pl.ds(pl.multiple_of((hour * 2 + lev) * rows, rows), rows)
        other_at = pl.ds(pl.multiple_of((hour * 2 + 1 - lev) * rows, rows), rows)

        @pl.when(near)
        def _():
            here = slice(hour * rows, (hour + 1) * rows)
            out[same_at, :] = (chip[here] + got_chip[here]) / divisor
            out[other_at, :] = (one[here] + got_one[here]) / divisor

        @pl.when(jnp.logical_not(near))
        def _():
            here = slice(hour * levels, (hour + 1) * levels)
            plain = chip[here] + got_chip[here]
            other = jnp.where(me == hour, last[:levels], got_last[:levels])
            pair = [jnp.where(even, plain, other), jnp.where(even, other, plain)]
            out[same_at, :] = jnp.concatenate(pair, axis=0) / divisor
            out[other_at, :] = jnp.where(me == hour, one[:rows], got_one[:rows]) / divisor


def finish(arrays, levels, divisor):
    call = functools.partial(finish_kernel, divisor, levels)
    shape = (2 * arrays[0].shape[0], PIXELS_DEV)
    return small_call(call, arrays, [], [shape], LIGHT, "finish")[0]


def hour_plan(level_field, tile_weight, tile_rows, tile_columns, live_count, step_hour):
    levs, subs, shards_tm = lax.axis_size("lev"), lax.axis_size("sub"), lax.axis_size("tm")
    half = levs // 2
    divisor = float(level_field.shape[0] * shards_tm // HOURS)
    field = jnp.transpose(level_field, (1, 0, 2))

    def to_peer(x, k, j):
        pairs = [(a * subs + b, (a ^ k) * subs + (b ^ j)) for a in range(levs) for b in range(subs)]
        return lax.ppermute(x, ("lev", "sub"), pairs)

    def swap(x):
        return lax.ppermute(x, "tm", [(0, 1), (1, 0)])

    plain = [(half, 0), (1, 0), (1, 1), (0, 1), (0, 0)]
    first, second = [(half + 1, j) for j in range(subs)], (half, 1)
    sums, (theirs_0, mine_0, theirs_1, mine_1) = hour_sums(plain, first, second, step_hour, field)
    rows = 2 * field.shape[0]
    folded = theirs_1.shape
    sibling = to_peer(sums[3], *plain[3])
    near_got = [to_peer(x, *peer) for x, peer in list(zip(sums, plain))[1:3]]
    got_0 = swap(theirs_0)
    plain_got = to_peer(sums[0], *plain[0])
    high, low = place_tiles(tile_rows, tile_columns, live_count, tile_weight, theirs_0)

    merged = small_call(
        merge_kernel, [mine_0, got_0], [high, sibling], [folded] * subs, LIGHT, "merge_first"
    )
    first_got = [to_peer(x, *peer) for x, peer in zip(merged, first)]
    theirs_1 = small_call(hold_kernel, [theirs_1], [plain_got, *merged], [folded], LIGHT, "hold")[0]
    got_1 = swap(theirs_1)
    both, send = remap_call(
        remap_both_kernel,
        [sums[4], sibling, plain_got],
        [theirs_1],
        [2 * rows] * 2,
        high,
        low,
        MEDIUM,
        "remap_both",
        [2 * rows] * 2,
    )
    got_both = swap(send)
    merged = small_call(
        merge_kernel, [mine_1, got_1], [both, near_got[0]], [folded], HEAVY, "merge_last"
    )
    second_got = to_peer(merged[0], *second)
    far = small_call(far_rows_kernel, first_got, [], [(rows, CELLS_DEV)], HEAVY, "far_rows")[0]
    one, send = remap_call(
        remap_near_kernel,
        [*near_got, far],
        [],
        [2 * rows] * 2,
        high,
        low,
        LIGHT,
        "remap_near",
        [2 * rows] * 2,
    )
    got_one = swap(send)
    padded = -(-rows // 32) * 16
    (last,) = remap_call(remap_last_kernel, [second_got], [one], [padded], high, low, HEAVY, "remap_last")
    got_last = swap(last)
    out = finish([both, got_both, one, got_one, last, got_last], rows // 2, divisor)
    return out.reshape(HOURS, out.shape[0] // HOURS, PIXELS_DEV)


def general_plan(level_field, tile_weight, tile_rows, tile_columns, live_count, step_hour):
    steps, levels, cells = level_field.shape
    shards = lax.axis_size("lev") * lax.axis_size("sub")
    divisor = float(steps * lax.axis_size("tm") // HOURS)
    hours = jnp.arange(HOURS, dtype=jnp.int32)
    table = (step_hour[None, :] == hours[:, None]).astype(jnp.float32)
    fields = level_field.reshape(steps, levels, shards, cells // shards)
    partial = jnp.einsum("hs,slgc->ghlc", table, fields, precision=lax.Precision.HIGHEST)
    regrouped = lax.all_to_all(partial, ("lev", "sub"), split_axis=0, concat_axis=0, tiled=True)
    rows = jnp.transpose(regrouped, (1, 0, 2, 3)).reshape(-1, cells // shards)
    high, low = place_tiles(tile_rows, tile_columns, live_count, tile_weight)
    (out,) = remap_call(remap_rows_kernel, [rows], [], [rows.shape[0]], high, low, LIGHT, "remap_rows")
    out = out.reshape(HOURS, shards * levels, PIXELS_DEV) / divisor
    return lax.psum_scatter(out, "tm", scatter_dimension=1, tiled=True)


def solution(mesh):
    sizes = mesh.shape
    paired = sizes["tm"] == HOURS and sizes["lev"] == 4 and sizes["sub"] == 2
    placed = (
        P(("groups", "tm"), ("lev", "sub"), None),
        P(None, ("lev", "sub")),
        P(("lev", "sub")),
        P(("lev", "sub")),
        P(("lev", "sub")),
        P("tm"),
    )
    return jax.shard_map(
        hour_plan if paired else general_plan,
        mesh=mesh,
        in_specs=placed,
        out_specs=P("groups", "tm", ("lev", "sub")),
        check_vma=False,
    )
```

```python
import functools

import jax
import jax.numpy as jnp
from jax import lax
from jax.experimental import pallas as pl
from jax.experimental.pallas import tpu as pltpu
from jax.sharding import PartitionSpec as P

TILE = 64
HOURS = 2
CT_DEV = 32
PT_DEV = 16
SLOTS = 128
CELLS_DEV = CT_DEV * TILE
PIXELS_DEV = PT_DEV * TILE
LANES = 2 * TILE
MIB = 1 << 20

LIGHT = pl.CostEstimate(flops=1, bytes_accessed=1, transcendentals=0)
MEDIUM = pl.CostEstimate(flops=2_500_000_000, bytes_accessed=1, transcendentals=0)
HEAVY = pl.CostEstimate(flops=10_000_000_000, bytes_accessed=1, transcendentals=0)

NT = (((1,), (1,)), ((), ()))
NN = (((1,), (0,)), ((), ()))


def split(x):
    high = x.astype(jnp.bfloat16)
    return high, (x - high.astype(jnp.float32)).astype(jnp.bfloat16)


def dot(a, b, dims):
    return lax.dot_general(a, b, dims, preferred_element_type=jnp.float32)


GROUP = 8


def place_kernel(rows, columns, count, weights, *refs):
    high, low, total = refs[-3:]
    band = 128

    @pl.loop(0, PIXELS_DEV // band)
    def _(b):
        total[pl.ds(pl.multiple_of(b * band, band), band), :] = jnp.zeros((band, CELLS_DEV), jnp.float32)

    lane_half = lax.broadcasted_iota(jnp.int32, (TILE, LANES), 1) // TILE
    live = count[0]

    @pl.loop(0, (live + GROUP - 1) // GROUP)
    def _(g):
        for pair in range(GROUP // 2):
            lanes = pl.ds(pl.multiple_of((g * (GROUP // 2) + pair) * LANES, LANES), LANES)
            tiles = weights[:, lanes]
            turned = pltpu.roll(tiles, TILE, 1)
            for i in range(2):
                k = g * GROUP + pair * 2 + i
                row, column = rows[k], columns[k]
                side = jnp.where(k < live, column & 1, -1)
                tile = jnp.where(lane_half == i, tiles, turned)
                at = (
                    pl.ds(pl.multiple_of(row * TILE, TILE), TILE),
                    pl.ds(pl.multiple_of((column >> 1) * LANES, LANES), LANES),
                )
                total[at] = total[at] + jnp.where(lane_half == side, tile, 0.0)

    @pl.loop(0, PIXELS_DEV // band)
    def _(b):
        at = pl.ds(pl.multiple_of(b * band, band), band)
        high[at, :], low[at, :] = split(total[at, :])


def place_tiles(rows, columns, count, weights, *after):
    smem = pl.BlockSpec(memory_space=pltpu.SMEM)
    vmem = pl.BlockSpec(memory_space=pltpu.VMEM)
    half = jax.ShapeDtypeStruct((PIXELS_DEV, CELLS_DEV), jnp.bfloat16)
    return pl.pallas_call(
        place_kernel,
        out_shape=(half, half),
        in_specs=[smem, smem, smem, vmem] + [pl.BlockSpec(memory_space=pl.ANY)] * len(after),
        out_specs=(vmem, vmem),
        scratch_shapes=[pltpu.VMEM((PIXELS_DEV, CELLS_DEV), jnp.float32)],
        compiler_params=pltpu.CompilerParams(vmem_limit_bytes=28 * MIB),
        cost_estimate=HEAVY,
        name="place_tiles",
    )(rows, columns, count, weights, *after)


PIXEL_BLOCK = 256


def remap_blocks(x, high, low):
    m = x.shape[0]
    x_high, x_low = split(x)
    both = jnp.concatenate([x_high, x_low], axis=0)
    for start in range(0, PIXELS_DEV, PIXEL_BLOCK):
        at = slice(start, start + PIXEL_BLOCK)
        first = dot(both, high[at, :], NT)
        yield at, first[:m] + first[m:] + dot(x_high, low[at, :], NT)


def remap_call(kernel, inputs, after, out_rows, high, low, cost, name, scratch_rows=()):
    vmem = pl.BlockSpec(memory_space=pltpu.VMEM)
    return pl.pallas_call(
        kernel,
        out_shape=[jax.ShapeDtypeStruct((rows, PIXELS_DEV), jnp.float32) for rows in out_rows],
        in_specs=[vmem] * (len(inputs) + 2) + [pl.BlockSpec(memory_space=pl.ANY)] * len(after),
        out_specs=[vmem] * len(out_rows),
        scratch_shapes=[pltpu.VMEM((rows, PIXELS_DEV), jnp.float32) for rows in scratch_rows],
        compiler_params=pltpu.CompilerParams(vmem_limit_bytes=24 * MIB),
        cost_estimate=cost,
        name=name,
    )(*inputs, high, low, *after)


def remap_rows_kernel(x, high, low, out):
    for at, result in remap_blocks(x[...], high, low):
        out[:, at] = result


def unfold(block):
    levels = block.shape[0] // 2
    return jnp.concatenate([block[:levels], block[levels:]], axis=1)


def far_rows(same_sub, other_sub):
    even = lax.axis_index("sub") == 0
    blocks = [jnp.where(even, same_sub, other_sub), jnp.where(even, other_sub, same_sub)]
    return [unfold(block) for block in blocks]


def keeps_near():
    return lax.axis_index("tm") == lax.axis_index("lev") // 2


def near_rows(same_sub, other_sub):
    even = lax.axis_index("sub") == 0
    return [jnp.where(even, same_sub, other_sub), jnp.where(even, other_sub, same_sub)]


def by_hour(result, levels):
    pieces = [result[start : start + levels] for start in range(0, 2 * HOURS * levels, levels)]
    return jnp.concatenate([pieces[sub * HOURS + hour] for hour in range(HOURS) for sub in range(2)], axis=0)


def sort_out(near_result, far_result, keep, send):
    near = keeps_near()

    @pl.when(near)
    def _():
        keep[...], send[...] = near_result[...], far_result[...]

    @pl.when(jnp.logical_not(near))
    def _():
        keep[...], send[...] = far_result[...], near_result[...]


def remap_both_kernel(own, sibling, plain, high, low, *refs):
    keep, send, near_result, far_result = refs[-4:]
    rows = own.shape[0]
    blocks = near_rows(own[...], sibling[...]) + [plain[...]]
    for at, result in remap_blocks(jnp.concatenate(blocks, axis=0), high, low):
        near_result[:, at] = by_hour(result, rows // HOURS)
        far_result[:rows, at] = result[2 * rows :]
    far_result[rows:] = jnp.zeros((rows, PIXELS_DEV), jnp.float32)
    sort_out(near_result, far_result, keep, send)


def remap_near_kernel(near_same, near_other, far, high, low, *refs):
    keep, send, near_result, far_result = refs[-4:]
    rows = near_same.shape[0]
    blocks = near_rows(near_same[...], near_other[...]) + [far[...]]
    for at, result in remap_blocks(jnp.concatenate(blocks, axis=0), high, low):
        near_result[:, at] = by_hour(result, rows // HOURS)
        far_result[:rows, at] = result[2 * rows :]
    far_result[rows:] = jnp.zeros((rows, PIXELS_DEV), jnp.float32)
    sort_out(near_result, far_result, keep, send)


def remap_last_kernel(block, high, low, *refs):
    out = refs[-1]
    x = unfold(block[...])
    x = jnp.concatenate([x, jnp.zeros((out.shape[0] - x.shape[0], x.shape[1]), jnp.float32)], axis=0)
    for at, result in remap_blocks(x, high, low):
        out[:, at] = result


def hour_matrix(step_hour, levels, steps, hours, cuts):
    rows, columns = cuts * levels, cuts * 2 * levels * steps
    row = lax.broadcasted_iota(jnp.int32, (rows, columns), 0)
    column = lax.broadcasted_iota(jnp.int32, (rows, columns), 1)
    span = levels * steps
    near = jnp.full((rows, columns), -1, jnp.int32)
    for cut in range(cuts):
        for half in range(2):
            step = column - (cut * 2 + half) * span - (row - cut * levels) * steps
            inside = (row >= cut * levels) & (row < (cut + 1) * levels)
            inside = inside & (step >= 0) & (step < steps)
            near = jnp.where(inside, step, near)
    blocks = []
    for hour in hours:
        block = jnp.zeros((rows, columns), jnp.float32)
        for step in range(steps):
            block = jnp.where(near == step, jnp.where(step_hour[step] == hour, 1.0, 0.0), block)
        blocks.append(block)
    return jnp.concatenate(blocks, axis=0).astype(jnp.bfloat16)


def peer_shard(k, j):
    subs = lax.axis_size("sub")
    return (lax.axis_index("lev") ^ k) * subs + (lax.axis_index("sub") ^ j)


def field_copies(field, buffer, arrived, peers):
    copies = []
    for place, (k, j) in enumerate(peers):
        start = pl.multiple_of(peer_shard(k, j) * CELLS_DEV, CELLS_DEV)
        copy = pltpu.make_async_copy(
            field.at[:, :, pl.ds(start, CELLS_DEV)], buffer.at[place], arrived.at[place]
        )
        copy.start()
        copies.append(copy)
    return copies


def sums_kernel(plain, first, second, step_hour, field, *refs):
    *outs, buffer, arrived = refs
    _, levels, steps, cells = buffer.shape
    rows, cut = HOURS * levels, cells // 2
    copies = field_copies(field, buffer, arrived, [*plain, *first, second])
    me = lax.axis_index("tm")
    by_place = hour_matrix(step_hour, levels, steps, (1 - me, me), 2)
    by_hour = hour_matrix(step_hour, levels, steps, range(HOURS), 1)

    def halves(place):
        copies[place].wait()
        return split(buffer[place].reshape(levels * steps, cells))

    for place in range(len(plain)):
        outs[place][...] = dot(by_hour, jnp.concatenate(halves(place), axis=0), NN)
    theirs_first, mine_first, theirs_second, mine_second = outs[len(plain) :]
    for j in range(len(first) + 1):
        high, low = halves(len(plain) + j)
        stacked = [high[:, :cut], low[:, :cut], high[:, cut:], low[:, cut:]]
        result = dot(by_place, jnp.concatenate(stacked, axis=0), NN)
        if j < len(first):
            at = slice(j * rows, (j + 1) * rows)
            theirs_first[at], mine_first[at] = result[:rows], result[rows:]
        else:
            theirs_second[...], mine_second[...] = result[:rows], result[rows:]


def hour_sums(plain, first, second, step_hour, field):
    levels, steps, _ = field.shape
    rows, cut = HOURS * levels, CELLS_DEV // 2
    vmem = pl.BlockSpec(memory_space=pltpu.VMEM)
    shapes = [(rows, CELLS_DEV)] * len(plain) + [(len(first) * rows, cut)] * 2 + [(rows, cut)] * 2
    count = len(plain) + len(first) + 1
    outs = pl.pallas_call(
        functools.partial(sums_kernel, plain, first, second),
        out_shape=[jax.ShapeDtypeStruct(shape, jnp.float32) for shape in shapes],
        in_specs=[pl.BlockSpec(memory_space=pltpu.SMEM), pl.BlockSpec(memory_space=pl.ANY)],
        out_specs=[vmem] * len(shapes),
        scratch_shapes=[
            pltpu.VMEM((count, levels, steps, CELLS_DEV), jnp.float32),
            pltpu.SemaphoreType.DMA((count,)),
        ],
        compiler_params=pltpu.CompilerParams(vmem_limit_bytes=52 * MIB),
        cost_estimate=LIGHT,
        name="hour_sums",
    )(step_hour, field)
    return outs[: len(plain)], outs[len(plain) :]


def hold_kernel(x, *refs):
    refs[-1][...] = x[...]


def merge_first_kernel(mine, got, held, *refs):
    out, passed = refs[-2:]
    rows = out.shape[0]
    out[...] = mine[:rows] + got[:rows]
    passed[...] = held[...]


def merge_next_kernel(mine, got, *refs):
    rows = refs[-1].shape[0]
    refs[-1][...] = mine[rows:] + got[rows:]


def merge_last_kernel(mine, got, *refs):
    refs[-1][...] = mine[...] + got[...]


def far_rows_kernel(same_sub, other_sub, *refs):
    refs[-1][...] = jnp.concatenate(far_rows(same_sub[...], other_sub[...]), axis=0)


def small_call(kernel, inputs, after, shapes, cost, name):
    vmem = pl.BlockSpec(memory_space=pltpu.VMEM)
    return pl.pallas_call(
        kernel,
        out_shape=[jax.ShapeDtypeStruct(shape, jnp.float32) for shape in shapes],
        in_specs=[vmem] * len(inputs) + [pl.BlockSpec(memory_space=pl.ANY)] * len(after),
        out_specs=[vmem] * len(shapes),
        compiler_params=pltpu.CompilerParams(vmem_limit_bytes=8 * MIB),
        cost_estimate=cost,
        name=name,
    )(*inputs, *after)


def sum_both_kernel(own, got, *refs):
    refs[-1][...] = own[...] + got[...]


def finish_kernel(divisor, levels, both, one, got_one, last, got_last, out):
    me, lev, even = lax.axis_index("tm"), lax.axis_index("lev") % 2, lax.axis_index("sub") == 0
    rows = 2 * levels
    near = keeps_near()
    for hour in range(HOURS):
        same_at = pl.ds(pl.multiple_of((hour * 2 + lev) * rows, rows), rows)
        other_at = pl.ds(pl.multiple_of((hour * 2 + 1 - lev) * rows, rows), rows)

        @pl.when(near)
        def _():
            here = slice(hour * rows, (hour + 1) * rows)
            out[same_at, :] = both[here] / divisor
            out[other_at, :] = (one[here] + got_one[here]) / divisor

        @pl.when(jnp.logical_not(near))
        def _():
            plain = both[hour * levels : (hour + 1) * levels]
            other = jnp.where(me == hour, last[:levels], got_last[:levels])
            pair = [jnp.where(even, plain, other), jnp.where(even, other, plain)]
            out[same_at, :] = jnp.concatenate(pair, axis=0) / divisor
            out[other_at, :] = jnp.where(me == hour, one[:rows], got_one[:rows]) / divisor


def finish(arrays, levels, divisor):
    call = functools.partial(finish_kernel, divisor, levels)
    shape = (2 * arrays[0].shape[0], PIXELS_DEV)
    return small_call(call, arrays, [], [shape], LIGHT, "finish")[0]


def hour_plan(level_field, tile_weight, tile_rows, tile_columns, live_count, step_hour):
    levs, subs, shards_tm = lax.axis_size("lev"), lax.axis_size("sub"), lax.axis_size("tm")
    half = levs // 2
    divisor = float(level_field.shape[0] * shards_tm // HOURS)
    field = jnp.transpose(level_field, (1, 0, 2))

    def to_peer(x, k, j):
        pairs = [(a * subs + b, (a ^ k) * subs + (b ^ j)) for a in range(levs) for b in range(subs)]
        return lax.ppermute(x, ("lev", "sub"), pairs)

    def swap(x):
        return lax.ppermute(x, "tm", [(0, 1), (1, 0)])

    plain = [(half, 0), (1, 0), (1, 1), (0, 1), (0, 0)]
    first, second = [(half + 1, j) for j in range(subs)], (half, 1)
    sums, (theirs_0, mine_0, theirs_1, mine_1) = hour_sums(plain, first, second, step_hour, field)
    rows = 2 * field.shape[0]
    folded = theirs_1.shape
    sibling = to_peer(sums[3], *plain[3])
    near_got = [to_peer(x, *peer) for x, peer in list(zip(sums, plain))[1:3]]
    got_0 = swap(theirs_0)
    plain_got = to_peer(sums[0], *plain[0])
    high, low = place_tiles(tile_rows, tile_columns, live_count, tile_weight, theirs_0)

    merged, theirs_1 = small_call(
        merge_first_kernel,
        [mine_0, got_0, theirs_1],
        [high, sibling],
        [folded] * 2,
        LIGHT,
        "merge_first",
    )
    got_1 = swap(theirs_1)
    far_same = to_peer(merged, *first[0])
    merged = small_call(
        merge_next_kernel, [mine_0, got_0], [plain_got, merged], [folded], MEDIUM, "merge_next"
    )
    far_other = to_peer(merged[0], *first[1])
    merged = small_call(merge_last_kernel, [mine_1, got_1], merged, [folded], LIGHT, "merge_last")
    second_got = to_peer(merged[0], *second)
    both, send = remap_call(
        remap_both_kernel,
        [sums[4], sibling, plain_got],
        merged,
        [2 * rows] * 2,
        high,
        low,
        MEDIUM,
        "remap_both",
        [2 * rows] * 2,
    )
    send = small_call(hold_kernel, [send], [near_got[0]], [send.shape], LIGHT, "hold")[0]
    got_both = swap(send)
    far = small_call(far_rows_kernel, [far_same, far_other], [both], [(rows, CELLS_DEV)], HEAVY, "far_rows")[0]
    one, send = remap_call(
        remap_near_kernel,
        [*near_got, far],
        [],
        [2 * rows] * 2,
        high,
        low,
        LIGHT,
        "remap_near",
        [2 * rows] * 2,
    )
    got_one = swap(send)
    both = small_call(sum_both_kernel, [both, got_both], [one], [both.shape], LIGHT, "sum_both")[0]
    padded = -(-rows // 32) * 16
    (last,) = remap_call(remap_last_kernel, [second_got], [both], [padded], high, low, HEAVY, "remap_last")
    got_last = swap(last)
    out = finish([both, one, got_one, last, got_last], rows // 2, divisor)
    return out.reshape(HOURS, out.shape[0] // HOURS, PIXELS_DEV)


def general_plan(level_field, tile_weight, tile_rows, tile_columns, live_count, step_hour):
    steps, levels, cells = level_field.shape
    shards = lax.axis_size("lev") * lax.axis_size("sub")
    divisor = float(steps * lax.axis_size("tm") // HOURS)
    hours = jnp.arange(HOURS, dtype=jnp.int32)
    table = (step_hour[None, :] == hours[:, None]).astype(jnp.float32)
    fields = level_field.reshape(steps, levels, shards, cells // shards)
    partial = jnp.einsum("hs,slgc->ghlc", table, fields, precision=lax.Precision.HIGHEST)
    regrouped = lax.all_to_all(partial, ("lev", "sub"), split_axis=0, concat_axis=0, tiled=True)
    rows = jnp.transpose(regrouped, (1, 0, 2, 3)).reshape(-1, cells // shards)
    high, low = place_tiles(tile_rows, tile_columns, live_count, tile_weight)
    (out,) = remap_call(remap_rows_kernel, [rows], [], [rows.shape[0]], high, low, LIGHT, "remap_rows")
    out = out.reshape(HOURS, shards * levels, PIXELS_DEV) / divisor
    return lax.psum_scatter(out, "tm", scatter_dimension=1, tiled=True)


def solution(mesh):
    sizes = mesh.shape
    paired = sizes["tm"] == HOURS and sizes["lev"] == 4 and sizes["sub"] == 2
    placed = (
        P(("groups", "tm"), ("lev", "sub"), None),
        P(None, ("lev", "sub")),
        P(("lev", "sub")),
        P(("lev", "sub")),
        P(("lev", "sub")),
        P("tm"),
    )
    return jax.shard_map(
        hour_plan if paired else general_plan,
        mesh=mesh,
        in_specs=placed,
        out_specs=P("groups", "tm", ("lev", "sub")),
        check_vma=False,
    )
```

```python
import functools

import jax
import jax.numpy as jnp
from jax import lax
from jax.experimental import pallas as pl
from jax.experimental.pallas import tpu as pltpu
from jax.sharding import PartitionSpec as P

TILE = 64
HOURS = 2
CT_DEV = 32
PT_DEV = 16
SLOTS = 128
CELLS_DEV = CT_DEV * TILE
PIXELS_DEV = PT_DEV * TILE
LANES = 2 * TILE
MIB = 1 << 20

LIGHT = pl.CostEstimate(flops=1, bytes_accessed=1, transcendentals=0)
MEDIUM = pl.CostEstimate(flops=2_500_000_000, bytes_accessed=1, transcendentals=0)
HEAVY = pl.CostEstimate(flops=10_000_000_000, bytes_accessed=1, transcendentals=0)

NT = (((1,), (1,)), ((), ()))
NN = (((1,), (0,)), ((), ()))


def split(x):
    high = x.astype(jnp.bfloat16)
    return high, (x - high.astype(jnp.float32)).astype(jnp.bfloat16)


def dot(a, b, dims):
    return lax.dot_general(a, b, dims, preferred_element_type=jnp.float32)


GROUP = 8


def place_kernel(rows, columns, count, weights, *refs):
    high, low, total = refs[-3:]
    band = 128

    @pl.loop(0, PIXELS_DEV // band)
    def _(b):
        total[pl.ds(pl.multiple_of(b * band, band), band), :] = jnp.zeros((band, CELLS_DEV), jnp.float32)

    lane_half = lax.broadcasted_iota(jnp.int32, (TILE, LANES), 1) // TILE
    live = count[0]

    @pl.loop(0, (live + GROUP - 1) // GROUP)
    def _(g):
        for pair in range(GROUP // 2):
            lanes = pl.ds(pl.multiple_of((g * (GROUP // 2) + pair) * LANES, LANES), LANES)
            tiles = weights[:, lanes]
            turned = pltpu.roll(tiles, TILE, 1)
            for i in range(2):
                k = g * GROUP + pair * 2 + i
                row, column = rows[k], columns[k]
                side = jnp.where(k < live, column & 1, -1)
                tile = jnp.where(lane_half == i, tiles, turned)
                at = (
                    pl.ds(pl.multiple_of(row * TILE, TILE), TILE),
                    pl.ds(pl.multiple_of((column >> 1) * LANES, LANES), LANES),
                )
                total[at] = total[at] + jnp.where(lane_half == side, tile, 0.0)

    @pl.loop(0, PIXELS_DEV // band)
    def _(b):
        at = pl.ds(pl.multiple_of(b * band, band), band)
        high[at, :], low[at, :] = split(total[at, :])


def place_tiles(rows, columns, count, weights, *after):
    smem = pl.BlockSpec(memory_space=pltpu.SMEM)
    vmem = pl.BlockSpec(memory_space=pltpu.VMEM)
    half = jax.ShapeDtypeStruct((PIXELS_DEV, CELLS_DEV), jnp.bfloat16)
    return pl.pallas_call(
        place_kernel,
        out_shape=(half, half),
        in_specs=[smem, smem, smem, vmem] + [pl.BlockSpec(memory_space=pl.ANY)] * len(after),
        out_specs=(vmem, vmem),
        scratch_shapes=[pltpu.VMEM((PIXELS_DEV, CELLS_DEV), jnp.float32)],
        compiler_params=pltpu.CompilerParams(vmem_limit_bytes=28 * MIB),
        cost_estimate=HEAVY,
        name="place_tiles",
    )(rows, columns, count, weights, *after)


PIXEL_BLOCK = 256


def remap_blocks(x, high, low):
    m = x.shape[0]
    x_high, x_low = split(x)
    both = jnp.concatenate([x_high, x_low], axis=0)
    for start in range(0, PIXELS_DEV, PIXEL_BLOCK):
        at = slice(start, start + PIXEL_BLOCK)
        first = dot(both, high[at, :], NT)
        yield at, first[:m] + first[m:] + dot(x_high, low[at, :], NT)


def remap_call(kernel, inputs, after, out_rows, high, low, cost, name, scratch_rows=()):
    vmem = pl.BlockSpec(memory_space=pltpu.VMEM)
    return pl.pallas_call(
        kernel,
        out_shape=[jax.ShapeDtypeStruct((rows, PIXELS_DEV), jnp.float32) for rows in out_rows],
        in_specs=[vmem] * (len(inputs) + 2) + [pl.BlockSpec(memory_space=pl.ANY)] * len(after),
        out_specs=[vmem] * len(out_rows),
        scratch_shapes=[pltpu.VMEM((rows, PIXELS_DEV), jnp.float32) for rows in scratch_rows],
        compiler_params=pltpu.CompilerParams(vmem_limit_bytes=24 * MIB),
        cost_estimate=cost,
        name=name,
    )(*inputs, high, low, *after)


def remap_rows_kernel(x, high, low, out):
    for at, result in remap_blocks(x[...], high, low):
        out[:, at] = result


def unfold(block):
    levels = block.shape[0] // 2
    return jnp.concatenate([block[:levels], block[levels:]], axis=1)


def far_rows(same_sub, other_sub):
    even = lax.axis_index("sub") == 0
    blocks = [jnp.where(even, same_sub, other_sub), jnp.where(even, other_sub, same_sub)]
    return [unfold(block) for block in blocks]


def keeps_near():
    return lax.axis_index("tm") == lax.axis_index("lev") // 2


def near_rows(same_sub, other_sub):
    even = lax.axis_index("sub") == 0
    return [jnp.where(even, same_sub, other_sub), jnp.where(even, other_sub, same_sub)]


def by_hour(result, levels):
    pieces = [result[start : start + levels] for start in range(0, 2 * HOURS * levels, levels)]
    return jnp.concatenate([pieces[sub * HOURS + hour] for hour in range(HOURS) for sub in range(2)], axis=0)


def sort_out(near_result, far_result, keep, send):
    near = keeps_near()

    @pl.when(near)
    def _():
        keep[...], send[...] = near_result[...], far_result[...]

    @pl.when(jnp.logical_not(near))
    def _():
        keep[...], send[...] = far_result[...], near_result[...]


def remap_both_kernel(own, sibling, plain, high, low, *refs):
    keep, send, near_result, far_result = refs[-4:]
    rows = own.shape[0]
    blocks = near_rows(own[...], sibling[...]) + [plain[...]]
    for at, result in remap_blocks(jnp.concatenate(blocks, axis=0), high, low):
        near_result[:, at] = by_hour(result, rows // HOURS)
        far_result[:rows, at] = result[2 * rows :]
    far_result[rows:] = jnp.zeros((rows, PIXELS_DEV), jnp.float32)
    sort_out(near_result, far_result, keep, send)


def remap_near_kernel(near_same, near_other, far, high, low, *refs):
    keep, send, near_result, far_result = refs[-4:]
    rows = near_same.shape[0]
    blocks = near_rows(near_same[...], near_other[...]) + [far[...]]
    for at, result in remap_blocks(jnp.concatenate(blocks, axis=0), high, low):
        near_result[:, at] = by_hour(result, rows // HOURS)
        far_result[:rows, at] = result[2 * rows :]
    far_result[rows:] = jnp.zeros((rows, PIXELS_DEV), jnp.float32)
    sort_out(near_result, far_result, keep, send)


def remap_last_kernel(block, high, low, *refs):
    out = refs[-1]
    x = unfold(block[...])
    x = jnp.concatenate([x, jnp.zeros((out.shape[0] - x.shape[0], x.shape[1]), jnp.float32)], axis=0)
    for at, result in remap_blocks(x, high, low):
        out[:, at] = result


def hour_weights(step_hour, steps, hours, width):
    row = lax.broadcasted_iota(jnp.int32, (steps, width), 0)
    first = jnp.zeros((steps, width), jnp.float32)
    second = jnp.zeros((steps, width), jnp.float32)
    for step in range(steps):
        first = jnp.where(row == step, jnp.where(step_hour[step] == hours[0], 1.0, 0.0), first)
        second = jnp.where(row == step, jnp.where(step_hour[step] == hours[1], 1.0, 0.0), second)
    upper = row < steps // 2
    return jnp.where(upper, first, second), jnp.where(upper, second, first)


def turn(x, rows):
    return pltpu.roll(x, rows % x.shape[0], 0)


def join(a, b, bit):
    clear = (lax.broadcasted_iota(jnp.int32, a.shape, 0) & bit) == 0
    kept, moved = jnp.where(clear, a, b), jnp.where(clear, b, a)
    return kept + jnp.where(clear, turn(moved, -bit), turn(moved, bit))


def sum_steps(block, weights):
    def halve(x):
        return x * weights[0] + turn(x * weights[1], 4)

    def four(level):
        a, b, c, d = (halve(block(level + i)) for i in range(4))
        return join(join(a, c, 2), join(b, d, 2), 1)

    return four


def pack(pieces):
    upper = lax.broadcasted_iota(jnp.int32, pieces[0][0].shape, 0) < 4
    at_half = [x if half == place % 2 else turn(x, 4) for place, (x, half) in enumerate(pieces)]
    return [jnp.where(upper, a, b) for a, b in zip(at_half[::2], at_half[1::2])]


def peer_shard(k, j):
    subs = lax.axis_size("sub")
    return (lax.axis_index("lev") ^ k) * subs + (lax.axis_index("sub") ^ j)


def field_copies(field, buffer, arrived, peers):
    copies = []
    for place, (k, j) in enumerate(peers):
        start = pl.multiple_of(peer_shard(k, j) * CELLS_DEV, CELLS_DEV)
        copy = pltpu.make_async_copy(
            field.at[:, :, pl.ds(start, CELLS_DEV)], buffer.at[place], arrived.at[place]
        )
        copy.start()
        copies.append(copy)
    return copies


SUM_WIDTH = 512


def sums_kernel(plain, first, second, step_hour, field, *refs):
    *outs, buffer, arrived = refs
    _, levels, steps, cells = buffer.shape
    rows, cut = HOURS * levels, cells // 2
    copies = field_copies(field, buffer, arrived, [*plain, *first, second])
    me = lax.axis_index("tm")
    groups = range(0, levels, 4)

    def summed(place, start, width, weights):
        four = sum_steps(lambda level: buffer[place, level, :, pl.ds(start, width)], weights)
        return [four(level) for level in groups]

    def store(out, offset, start, width, pieces):
        for place, x in enumerate(pack(pieces)):
            out[offset + place * 8 : offset + place * 8 + 8, pl.ds(start, width)] = x

    weights = hour_weights(step_hour, steps, range(HOURS), SUM_WIDTH)
    for place in range(len(plain)):
        copies[place].wait()

        @pl.loop(0, cells // SUM_WIDTH)
        def _(i):
            start = pl.multiple_of(i * SUM_WIDTH, SUM_WIDTH)
            sums = summed(place, start, SUM_WIDTH, weights)
            pieces = [(x, half) for half in range(HOURS) for x in sums]
            store(outs[place], 0, start, SUM_WIDTH, pieces)

    theirs_first, mine_first, theirs_second, mine_second = outs[len(plain) :]
    width = SUM_WIDTH // 2
    weights = hour_weights(step_hour, steps, (1 - me, me), width)
    for j in range(len(first) + 1):
        place = len(plain) + j
        copies[place].wait()
        offset = j * rows if j < len(first) else 0
        theirs, mine = (theirs_first, mine_first) if j < len(first) else (theirs_second, mine_second)

        @pl.loop(0, cut // width)
        def _(i):
            start = pl.multiple_of(i * width, width)
            sums = summed(place, start, width, weights) + summed(place, cut + start, width, weights)
            store(theirs, offset, start, width, [(x, 0) for x in sums])
            store(mine, offset, start, width, [(x, 1) for x in sums])


def hour_sums(plain, first, second, step_hour, field):
    levels, steps, _ = field.shape
    rows, cut = HOURS * levels, CELLS_DEV // 2
    vmem = pl.BlockSpec(memory_space=pltpu.VMEM)
    shapes = [(rows, CELLS_DEV)] * len(plain) + [(len(first) * rows, cut)] * 2 + [(rows, cut)] * 2
    count = len(plain) + len(first) + 1
    outs = pl.pallas_call(
        functools.partial(sums_kernel, plain, first, second),
        out_shape=[jax.ShapeDtypeStruct(shape, jnp.float32) for shape in shapes],
        in_specs=[pl.BlockSpec(memory_space=pltpu.SMEM), pl.BlockSpec(memory_space=pl.ANY)],
        out_specs=[vmem] * len(shapes),
        scratch_shapes=[
            pltpu.VMEM((count, levels, steps, CELLS_DEV), jnp.float32),
            pltpu.SemaphoreType.DMA((count,)),
        ],
        compiler_params=pltpu.CompilerParams(vmem_limit_bytes=52 * MIB),
        cost_estimate=LIGHT,
        name="hour_sums",
    )(step_hour, field)
    return outs[: len(plain)], outs[len(plain) :]


def merge_kernel(mine, got, *refs):
    outs = refs[-(mine.shape[0] // refs[-1].shape[0]) :]
    rows = outs[0].shape[0]
    for place, out in enumerate(outs):
        at = slice(place * rows, (place + 1) * rows)
        out[...] = mine[at] + got[at]


def hold_kernel(x, *refs):
    refs[-1][...] = x[...]


def far_rows_kernel(same_sub, other_sub, out):
    out[...] = jnp.concatenate(far_rows(same_sub[...], other_sub[...]), axis=0)


def small_call(kernel, inputs, after, shapes, cost, name):
    vmem = pl.BlockSpec(memory_space=pltpu.VMEM)
    return pl.pallas_call(
        kernel,
        out_shape=[jax.ShapeDtypeStruct(shape, jnp.float32) for shape in shapes],
        in_specs=[vmem] * len(inputs) + [pl.BlockSpec(memory_space=pl.ANY)] * len(after),
        out_specs=[vmem] * len(shapes),
        compiler_params=pltpu.CompilerParams(vmem_limit_bytes=8 * MIB),
        cost_estimate=cost,
        name=name,
    )(*inputs, *after)


def finish_kernel(divisor, levels, chip, got_chip, one, got_one, last, got_last, out):
    me, lev, even = lax.axis_index("tm"), lax.axis_index("lev") % 2, lax.axis_index("sub") == 0
    rows = 2 * levels
    near = keeps_near()
    for hour in range(HOURS):
        same_at = pl.ds(pl.multiple_of((hour * 2 + lev) * rows, rows), rows)
        other_at = pl.ds(pl.multiple_of((hour * 2 + 1 - lev) * rows, rows), rows)

        @pl.when(near)
        def _():
            here = slice(hour * rows, (hour + 1) * rows)
            out[same_at, :] = (chip[here] + got_chip[here]) / divisor
            out[other_at, :] = (one[here] + got_one[here]) / divisor

        @pl.when(jnp.logical_not(near))
        def _():
            here = slice(hour * levels, (hour + 1) * levels)
            plain = chip[here] + got_chip[here]
            other = jnp.where(me == hour, last[:levels], got_last[:levels])
            pair = [jnp.where(even, plain, other), jnp.where(even, other, plain)]
            out[same_at, :] = jnp.concatenate(pair, axis=0) / divisor
            out[other_at, :] = jnp.where(me == hour, one[:rows], got_one[:rows]) / divisor


def finish(arrays, levels, divisor):
    call = functools.partial(finish_kernel, divisor, levels)
    shape = (2 * arrays[0].shape[0], PIXELS_DEV)
    return small_call(call, arrays, [], [shape], LIGHT, "finish")[0]


def hour_plan(level_field, tile_weight, tile_rows, tile_columns, live_count, step_hour):
    levs, subs, shards_tm = lax.axis_size("lev"), lax.axis_size("sub"), lax.axis_size("tm")
    half = levs // 2
    divisor = float(level_field.shape[0] * shards_tm // HOURS)
    field = jnp.transpose(level_field, (1, 0, 2))

    def to_peer(x, k, j):
        pairs = [(a * subs + b, (a ^ k) * subs + (b ^ j)) for a in range(levs) for b in range(subs)]
        return lax.ppermute(x, ("lev", "sub"), pairs)

    def swap(x):
        return lax.ppermute(x, "tm", [(0, 1), (1, 0)])

    plain = [(half, 0), (1, 0), (1, 1), (0, 1), (0, 0)]
    first, second = [(half + 1, j) for j in range(subs)], (half, 1)
    sums, (theirs_0, mine_0, theirs_1, mine_1) = hour_sums(plain, first, second, step_hour, field)
    rows = 2 * field.shape[0]
    folded = theirs_1.shape
    sibling = to_peer(sums[3], *plain[3])
    near_got = [to_peer(x, *peer) for x, peer in list(zip(sums, plain))[1:3]]
    got_0 = swap(theirs_0)
    plain_got = to_peer(sums[0], *plain[0])
    high, low = place_tiles(tile_rows, tile_columns, live_count, tile_weight, theirs_0)

    merged = small_call(
        merge_kernel, [mine_0, got_0], [high, sibling], [folded] * subs, LIGHT, "merge_first"
    )
    first_got = [to_peer(x, *peer) for x, peer in zip(merged, first)]
    theirs_1 = small_call(hold_kernel, [theirs_1], [plain_got, *merged], [folded], LIGHT, "hold")[0]
    got_1 = swap(theirs_1)
    both, send = remap_call(
        remap_both_kernel,
        [sums[4], sibling, plain_got],
        [theirs_1],
        [2 * rows] * 2,
        high,
        low,
        MEDIUM,
        "remap_both",
        [2 * rows] * 2,
    )
    got_both = swap(send)
    merged = small_call(
        merge_kernel, [mine_1, got_1], [both, near_got[0]], [folded], HEAVY, "merge_last"
    )
    second_got = to_peer(merged[0], *second)
    far = small_call(far_rows_kernel, first_got, [], [(rows, CELLS_DEV)], HEAVY, "far_rows")[0]
    one, send = remap_call(
        remap_near_kernel,
        [*near_got, far],
        [],
        [2 * rows] * 2,
        high,
        low,
        LIGHT,
        "remap_near",
        [2 * rows] * 2,
    )
    got_one = swap(send)
    padded = -(-rows // 32) * 16
    (last,) = remap_call(remap_last_kernel, [second_got], [one], [padded], high, low, HEAVY, "remap_last")
    got_last = swap(last)
    out = finish([both, got_both, one, got_one, last, got_last], rows // 2, divisor)
    return out.reshape(HOURS, out.shape[0] // HOURS, PIXELS_DEV)


def general_plan(level_field, tile_weight, tile_rows, tile_columns, live_count, step_hour):
    steps, levels, cells = level_field.shape
    shards = lax.axis_size("lev") * lax.axis_size("sub")
    divisor = float(steps * lax.axis_size("tm") // HOURS)
    hours = jnp.arange(HOURS, dtype=jnp.int32)
    table = (step_hour[None, :] == hours[:, None]).astype(jnp.float32)
    fields = level_field.reshape(steps, levels, shards, cells // shards)
    partial = jnp.einsum("hs,slgc->ghlc", table, fields, precision=lax.Precision.HIGHEST)
    regrouped = lax.all_to_all(partial, ("lev", "sub"), split_axis=0, concat_axis=0, tiled=True)
    rows = jnp.transpose(regrouped, (1, 0, 2, 3)).reshape(-1, cells // shards)
    high, low = place_tiles(tile_rows, tile_columns, live_count, tile_weight)
    (out,) = remap_call(remap_rows_kernel, [rows], [], [rows.shape[0]], high, low, LIGHT, "remap_rows")
    out = out.reshape(HOURS, shards * levels, PIXELS_DEV) / divisor
    return lax.psum_scatter(out, "tm", scatter_dimension=1, tiled=True)


def solution(mesh):
    sizes = mesh.shape
    paired = sizes["tm"] == HOURS and sizes["lev"] == 4 and sizes["sub"] == 2

    def body(level_field, *others):
        steps, levels, _ = level_field.shape
        suits = paired and steps == 8 and levels % 4 == 0
        return (hour_plan if suits else general_plan)(level_field, *others)

    placed = (
        P(("groups", "tm"), ("lev", "sub"), None),
        P(None, ("lev", "sub")),
        P(("lev", "sub")),
        P(("lev", "sub")),
        P(("lev", "sub")),
        P("tm"),
    )
    return jax.shard_map(
        body,
        mesh=mesh,
        in_specs=placed,
        out_specs=P("groups", "tm", ("lev", "sub")),
        check_vma=False,
    )
```

```python
import functools

import jax
import jax.numpy as jnp
from jax import lax
from jax.experimental import pallas as pl
from jax.experimental.pallas import tpu as pltpu
from jax.sharding import PartitionSpec as P

TILE = 64
HOURS = 2
CT_DEV = 32
PT_DEV = 16
SLOTS = 128
CELLS_DEV = CT_DEV * TILE
PIXELS_DEV = PT_DEV * TILE
LANES = 2 * TILE
MIB = 1 << 20

LIGHT = pl.CostEstimate(flops=1, bytes_accessed=1, transcendentals=0)
MEDIUM = pl.CostEstimate(flops=2_500_000_000, bytes_accessed=1, transcendentals=0)
HEAVY = pl.CostEstimate(flops=10_000_000_000, bytes_accessed=1, transcendentals=0)

NT = (((1,), (1,)), ((), ()))
NN = (((1,), (0,)), ((), ()))


def split(x):
    high = x.astype(jnp.bfloat16)
    return high, (x - high.astype(jnp.float32)).astype(jnp.bfloat16)


def dot(a, b, dims):
    return lax.dot_general(a, b, dims, preferred_element_type=jnp.float32)


GROUP = 8


def place_kernel(rows, columns, count, weights, *refs):
    high, low, total = refs[-3:]
    band = 128

    @pl.loop(0, PIXELS_DEV // band)
    def _(b):
        total[pl.ds(pl.multiple_of(b * band, band), band), :] = jnp.zeros((band, CELLS_DEV), jnp.float32)

    lane_half = lax.broadcasted_iota(jnp.int32, (TILE, LANES), 1) // TILE
    live = count[0]

    @pl.loop(0, (live + GROUP - 1) // GROUP)
    def _(g):
        for pair in range(GROUP // 2):
            lanes = pl.ds(pl.multiple_of((g * (GROUP // 2) + pair) * LANES, LANES), LANES)
            tiles = weights[:, lanes]
            turned = pltpu.roll(tiles, TILE, 1)
            for i in range(2):
                k = g * GROUP + pair * 2 + i
                row, column = rows[k], columns[k]
                side = jnp.where(k < live, column & 1, -1)
                tile = jnp.where(lane_half == i, tiles, turned)
                at = (
                    pl.ds(pl.multiple_of(row * TILE, TILE), TILE),
                    pl.ds(pl.multiple_of((column >> 1) * LANES, LANES), LANES),
                )
                total[at] = total[at] + jnp.where(lane_half == side, tile, 0.0)

    @pl.loop(0, PIXELS_DEV // band)
    def _(b):
        at = pl.ds(pl.multiple_of(b * band, band), band)
        high[at, :], low[at, :] = split(total[at, :])


def place_tiles(rows, columns, count, weights, *after):
    smem = pl.BlockSpec(memory_space=pltpu.SMEM)
    vmem = pl.BlockSpec(memory_space=pltpu.VMEM)
    half = jax.ShapeDtypeStruct((PIXELS_DEV, CELLS_DEV), jnp.bfloat16)
    return pl.pallas_call(
        place_kernel,
        out_shape=(half, half),
        in_specs=[smem, smem, smem, vmem] + [pl.BlockSpec(memory_space=pl.ANY)] * len(after),
        out_specs=(vmem, vmem),
        scratch_shapes=[pltpu.VMEM((PIXELS_DEV, CELLS_DEV), jnp.float32)],
        compiler_params=pltpu.CompilerParams(vmem_limit_bytes=28 * MIB),
        cost_estimate=HEAVY,
        name="place_tiles",
    )(rows, columns, count, weights, *after)


PIXEL_BLOCK = 256


def remap_blocks(x, high, low, cells=slice(None)):
    m = x.shape[0]
    x_high, x_low = split(x)
    both = jnp.concatenate([x_high, x_low], axis=0)
    for start in range(0, PIXELS_DEV, PIXEL_BLOCK):
        at = slice(start, start + PIXEL_BLOCK)
        first = dot(both, high[at, cells], NT)
        yield at, first[:m] + first[m:] + dot(x_high, low[at, cells], NT)


def remap_call(kernel, inputs, after, out_rows, high, low, cost, name, scratch_rows=()):
    vmem = pl.BlockSpec(memory_space=pltpu.VMEM)
    return pl.pallas_call(
        kernel,
        out_shape=[
            jax.ShapeDtypeStruct(rows if isinstance(rows, tuple) else (rows, PIXELS_DEV), jnp.float32)
            for rows in out_rows
        ],
        in_specs=[vmem] * (len(inputs) + 2) + [pl.BlockSpec(memory_space=pl.ANY)] * len(after),
        out_specs=[vmem] * len(out_rows),
        scratch_shapes=[pltpu.VMEM((rows, PIXELS_DEV), jnp.float32) for rows in scratch_rows],
        compiler_params=pltpu.CompilerParams(vmem_limit_bytes=24 * MIB),
        cost_estimate=cost,
        name=name,
    )(*inputs, high, low, *after)


def remap_rows_kernel(x, high, low, out):
    for at, result in remap_blocks(x[...], high, low):
        out[:, at] = result


def unfold(block):
    levels = block.shape[0] // 2
    return jnp.concatenate([block[:levels], block[levels:]], axis=1)


def far_rows(same_sub, other_sub):
    even = lax.axis_index("sub") == 0
    blocks = [jnp.where(even, same_sub, other_sub), jnp.where(even, other_sub, same_sub)]
    return [unfold(block) for block in blocks]


def keeps_near():
    return lax.axis_index("tm") == lax.axis_index("lev") // 2


def near_rows(same_sub, other_sub):
    even = lax.axis_index("sub") == 0
    return [jnp.where(even, same_sub, other_sub), jnp.where(even, other_sub, same_sub)]


def by_hour(result, levels):
    pieces = [result[start : start + levels] for start in range(0, 2 * HOURS * levels, levels)]
    return jnp.concatenate([pieces[sub * HOURS + hour] for hour in range(HOURS) for sub in range(2)], axis=0)


def sort_out(near_result, far_result, keep, send):
    near = keeps_near()

    @pl.when(near)
    def _():
        keep[...], send[...] = near_result[...], far_result[...]

    @pl.when(jnp.logical_not(near))
    def _():
        keep[...], send[...] = far_result[...], near_result[...]


def remap_both_kernel(own, sibling, plain, high, low, *refs):
    keep, send, near_result, far_result = refs[-4:]
    rows = own.shape[0]
    blocks = near_rows(own[...], sibling[...]) + [plain[...]]
    for at, result in remap_blocks(jnp.concatenate(blocks, axis=0), high, low):
        near_result[:, at] = by_hour(result, rows // HOURS)
        far_result[:rows, at] = result[2 * rows :]
    far_result[rows:] = jnp.zeros((rows, PIXELS_DEV), jnp.float32)
    sort_out(near_result, far_result, keep, send)


def remap_near_kernel(near_same, near_other, far, high, low, *refs):
    keep, send, near_result, far_result = refs[-4:]
    rows = near_same.shape[0]
    blocks = near_rows(near_same[...], near_other[...]) + [far[...]]
    for at, result in remap_blocks(jnp.concatenate(blocks, axis=0), high, low):
        near_result[:, at] = by_hour(result, rows // HOURS)
        far_result[:rows, at] = result[2 * rows :]
    far_result[rows:] = jnp.zeros((rows, PIXELS_DEV), jnp.float32)
    sort_out(near_result, far_result, keep, send)


def remap_half(place, block, high, low):
    x = unfold(block[...])
    levels, cells = x.shape
    x = jnp.concatenate([x, jnp.zeros((-levels % 16, cells), jnp.float32)], axis=0)
    yield from remap_blocks(x, high, low, slice(place * cells, (place + 1) * cells))


def remap_early_kernel(block, high, low, *refs):
    for at, result in remap_half(0, block, high, low):
        refs[-1][:, at] = result


def remap_last_kernel(block, early, high, low, *refs):
    out, total = refs[-2:]
    for at, result in remap_half(1, block, high, low):
        total[:, at] = result + early[:, at]
    out[...] = fold(total[: out.shape[0] // 2])


def hour_weights(step_hour, steps, hours, width):
    row = lax.broadcasted_iota(jnp.int32, (steps, width), 0)
    first = jnp.zeros((steps, width), jnp.float32)
    second = jnp.zeros((steps, width), jnp.float32)
    for step in range(steps):
        first = jnp.where(row == step, jnp.where(step_hour[step] == hours[0], 1.0, 0.0), first)
        second = jnp.where(row == step, jnp.where(step_hour[step] == hours[1], 1.0, 0.0), second)
    upper = row < steps // 2
    return jnp.where(upper, first, second), jnp.where(upper, second, first)


def turn(x, rows):
    return pltpu.roll(x, rows % x.shape[0], 0)


def join(a, b, bit):
    clear = (lax.broadcasted_iota(jnp.int32, a.shape, 0) & bit) == 0
    kept, moved = jnp.where(clear, a, b), jnp.where(clear, b, a)
    return kept + jnp.where(clear, turn(moved, -bit), turn(moved, bit))


def sum_steps(block, weights):
    def halve(x):
        return x * weights[0] + turn(x * weights[1], 4)

    def four(level):
        a, b, c, d = (halve(block(level + i)) for i in range(4))
        return join(join(a, c, 2), join(b, d, 2), 1)

    return four


def pack(pieces):
    upper = lax.broadcasted_iota(jnp.int32, pieces[0][0].shape, 0) < 4
    at_half = [x if half == place % 2 else turn(x, 4) for place, (x, half) in enumerate(pieces)]
    return [jnp.where(upper, a, b) for a, b in zip(at_half[::2], at_half[1::2])]


def peer_shard(k, j):
    subs = lax.axis_size("sub")
    return (lax.axis_index("lev") ^ k) * subs + (lax.axis_index("sub") ^ j)


def field_copies(field, buffer, arrived, peers):
    copies = []
    for place, (k, j) in enumerate(peers):
        start = pl.multiple_of(peer_shard(k, j) * CELLS_DEV, CELLS_DEV)
        copy = pltpu.make_async_copy(
            field.at[:, :, pl.ds(start, CELLS_DEV)], buffer.at[place], arrived.at[place]
        )
        copy.start()
        copies.append(copy)
    return copies


SUM_WIDTH = 512


def sums_kernel(plain, first, second, step_hour, field, *refs):
    *outs, buffer, arrived, hours, hours_arrived = refs
    _, levels, steps, cells = buffer.shape
    rows, cut = HOURS * levels, cells // 2
    copies = field_copies(field, buffer, arrived, [*plain, *first, second])
    fetch = pltpu.make_async_copy(step_hour, hours, hours_arrived)
    fetch.start()
    fetch.wait()
    me = lax.axis_index("tm")
    groups = range(0, levels, 4)

    def summed(place, start, width, weights):
        four = sum_steps(lambda level: buffer[place, level, :, pl.ds(start, width)], weights)
        return [four(level) for level in groups]

    def store(out, offset, start, width, pieces):
        for place, x in enumerate(pack(pieces)):
            out[offset + place * 8 : offset + place * 8 + 8, pl.ds(start, width)] = x

    weights = hour_weights(hours, steps, range(HOURS), SUM_WIDTH)
    for place in range(len(plain)):
        copies[place].wait()

        @pl.loop(0, cells // SUM_WIDTH)
        def _(i):
            start = pl.multiple_of(i * SUM_WIDTH, SUM_WIDTH)
            sums = summed(place, start, SUM_WIDTH, weights)
            pieces = [(x, half) for half in range(HOURS) for x in sums]
            store(outs[place], 0, start, SUM_WIDTH, pieces)

    theirs_first, mine_first, theirs_second, mine_second = outs[len(plain) :]
    width = SUM_WIDTH // 2
    weights = hour_weights(hours, steps, (1 - me, me), width)
    for j in range(len(first) + 1):
        place = len(plain) + j
        copies[place].wait()
        offset = j * rows if j < len(first) else 0
        theirs, mine = (theirs_first, mine_first) if j < len(first) else (theirs_second, mine_second)

        @pl.loop(0, cut // width)
        def _(i):
            start = pl.multiple_of(i * width, width)
            sums = summed(place, start, width, weights) + summed(place, cut + start, width, weights)
            store(theirs, offset, start, width, [(x, 0) for x in sums])
            store(mine, offset, start, width, [(x, 1) for x in sums])


def hour_sums(plain, first, second, step_hour, field):
    levels, steps, _ = field.shape
    rows, cut = HOURS * levels, CELLS_DEV // 2
    vmem = pl.BlockSpec(memory_space=pltpu.VMEM)
    shapes = [(rows, CELLS_DEV)] * len(plain) + [(len(first) * rows, cut)] * 2 + [(rows, cut)] * 2
    count = len(plain) + len(first) + 1
    outs = pl.pallas_call(
        functools.partial(sums_kernel, plain, first, second),
        out_shape=[jax.ShapeDtypeStruct(shape, jnp.float32) for shape in shapes],
        in_specs=[pl.BlockSpec(memory_space=pl.ANY)] * 2,
        out_specs=[vmem] * len(shapes),
        scratch_shapes=[
            pltpu.VMEM((count, levels, steps, CELLS_DEV), jnp.float32),
            pltpu.SemaphoreType.DMA((count,)),
            pltpu.SMEM((steps,), jnp.int32),
            pltpu.SemaphoreType.DMA,
        ],
        compiler_params=pltpu.CompilerParams(vmem_limit_bytes=52 * MIB),
        cost_estimate=LIGHT,
        name="hour_sums",
    )(step_hour, field)
    return outs[: len(plain)], outs[len(plain) :]


def merge_kernel(mine, got, *refs):
    outs = refs[-2:]
    rows = outs[0].shape[0]
    for place, out in enumerate(outs):
        at = slice(place * rows, (place + 1) * rows)
        out[...] = mine[at] + got[at]


def fold(x):
    half = x.shape[1] // 2
    return jnp.concatenate([x[:, :half], x[:, half:]], axis=0)


def merge_last_kernel(mine, got, *refs):
    outs = refs[-2:]
    levels = mine.shape[0] // 2
    total = mine[...] + got[...]
    for place, out in enumerate(outs):
        out[...] = fold(total[place * levels : (place + 1) * levels])


def hold_kernel(x, *refs):
    refs[-1][...] = x[...]


def far_rows_kernel(same_sub, other_sub, out):
    out[...] = jnp.concatenate(far_rows(same_sub[...], other_sub[...]), axis=0)


def small_call(kernel, inputs, after, shapes, cost, name):
    vmem = pl.BlockSpec(memory_space=pltpu.VMEM)
    return pl.pallas_call(
        kernel,
        out_shape=[jax.ShapeDtypeStruct(shape, jnp.float32) for shape in shapes],
        in_specs=[vmem] * len(inputs) + [pl.BlockSpec(memory_space=pl.ANY)] * len(after),
        out_specs=[vmem] * len(shapes),
        compiler_params=pltpu.CompilerParams(vmem_limit_bytes=8 * MIB),
        cost_estimate=cost,
        name=name,
    )(*inputs, *after)


def finish_kernel(divisor, levels, chip, got_chip, one, got_one, last, got_last, out):
    me, lev, even = lax.axis_index("tm"), lax.axis_index("lev") % 2, lax.axis_index("sub") == 0
    rows = 2 * levels
    near = keeps_near()
    for hour in range(HOURS):
        same_at = pl.ds(pl.multiple_of((hour * 2 + lev) * rows, rows), rows)
        other_at = pl.ds(pl.multiple_of((hour * 2 + 1 - lev) * rows, rows), rows)

        @pl.when(near)
        def _():
            here = slice(hour * rows, (hour + 1) * rows)
            out[same_at, :] = (chip[here] + got_chip[here]) / divisor
            out[other_at, :] = (one[here] + got_one[here]) / divisor

        @pl.when(jnp.logical_not(near))
        def _():
            here = slice(hour * levels, (hour + 1) * levels)
            plain = chip[here] + got_chip[here]
            other = unfold(jnp.where(me == hour, last[...], got_last[...]))
            pair = [jnp.where(even, plain, other), jnp.where(even, other, plain)]
            out[same_at, :] = jnp.concatenate(pair, axis=0) / divisor
            out[other_at, :] = jnp.where(me == hour, one[:rows], got_one[:rows]) / divisor


def finish(arrays, levels, divisor):
    call = functools.partial(finish_kernel, divisor, levels)
    shape = (2 * arrays[0].shape[0], PIXELS_DEV)
    return small_call(call, arrays, [], [shape], LIGHT, "finish")[0]


def hour_plan(level_field, tile_weight, tile_rows, tile_columns, live_count, step_hour):
    levs, subs, shards_tm = lax.axis_size("lev"), lax.axis_size("sub"), lax.axis_size("tm")
    half = levs // 2
    divisor = float(level_field.shape[0] * shards_tm // HOURS)
    field = jnp.transpose(level_field, (1, 0, 2))

    def to_peer(x, k, j):
        pairs = [(a * subs + b, (a ^ k) * subs + (b ^ j)) for a in range(levs) for b in range(subs)]
        return lax.ppermute(x, ("lev", "sub"), pairs)

    def swap(x):
        return lax.ppermute(x, "tm", [(0, 1), (1, 0)])

    plain = [(half, 0), (1, 0), (1, 1), (0, 1), (0, 0)]
    first, second = [(half + 1, j) for j in range(subs)], (half, 1)
    sums, (theirs_0, mine_0, theirs_1, mine_1) = hour_sums(plain, first, second, step_hour, field)
    rows = 2 * field.shape[0]
    folded = theirs_1.shape
    sibling = to_peer(sums[3], *plain[3])
    near_got = [to_peer(x, *peer) for x, peer in list(zip(sums, plain))[1:3]]
    got_0 = swap(theirs_0)
    plain_got = to_peer(sums[0], *plain[0])
    high, low = place_tiles(tile_rows, tile_columns, live_count, tile_weight, theirs_0)

    merged = small_call(
        merge_kernel, [mine_0, got_0], [high, sibling], [folded] * subs, LIGHT, "merge_first"
    )
    first_got = [to_peer(x, *peer) for x, peer in zip(merged, first)]
    theirs_1 = small_call(hold_kernel, [theirs_1], [plain_got, *merged], [folded], LIGHT, "hold")[0]
    got_1 = swap(theirs_1)
    both, send = remap_call(
        remap_both_kernel,
        [sums[4], sibling, plain_got],
        [theirs_1],
        [2 * rows] * 2,
        high,
        low,
        MEDIUM,
        "remap_both",
        [2 * rows] * 2,
    )
    got_both = swap(send)
    quarter = (folded[0], folded[1] // 2)
    merged = small_call(
        merge_last_kernel, [mine_1, got_1], [both, near_got[0]], [quarter] * 2, HEAVY, "merge_last"
    )
    late = small_call(hold_kernel, [merged[1]], first_got[:1], [quarter], LIGHT, "hold")
    second_got = [to_peer(x, *second) for x in (merged[0], late[0])]
    far = small_call(far_rows_kernel, first_got, [], [(rows, CELLS_DEV)], HEAVY, "far_rows")[0]
    one, send = remap_call(
        remap_near_kernel,
        [*near_got, far],
        [],
        [2 * rows] * 2,
        high,
        low,
        LIGHT,
        "remap_near",
        [2 * rows] * 2,
    )
    got_one = swap(send)
    padded = -(-rows // 32) * 16
    (early,) = remap_call(
        remap_early_kernel, second_got[:1], [one], [padded], high, low, HEAVY, "remap_early"
    )
    (last,) = remap_call(
        remap_last_kernel,
        [second_got[1], early],
        [],
        [(rows, PIXELS_DEV // 2)],
        high,
        low,
        HEAVY,
        "remap_last",
        [padded],
    )
    got_last = swap(last)
    out = finish([both, got_both, one, got_one, last, got_last], rows // 2, divisor)
    return out.reshape(HOURS, out.shape[0] // HOURS, PIXELS_DEV)


def general_plan(level_field, tile_weight, tile_rows, tile_columns, live_count, step_hour):
    steps, levels, cells = level_field.shape
    shards = lax.axis_size("lev") * lax.axis_size("sub")
    divisor = float(steps * lax.axis_size("tm") // HOURS)
    hours = jnp.arange(HOURS, dtype=jnp.int32)
    table = (step_hour[None, :] == hours[:, None]).astype(jnp.float32)
    fields = level_field.reshape(steps, levels, shards, cells // shards)
    partial = jnp.einsum("hs,slgc->ghlc", table, fields, precision=lax.Precision.HIGHEST)
    regrouped = lax.all_to_all(partial, ("lev", "sub"), split_axis=0, concat_axis=0, tiled=True)
    rows = jnp.transpose(regrouped, (1, 0, 2, 3)).reshape(-1, cells // shards)
    high, low = place_tiles(tile_rows, tile_columns, live_count, tile_weight)
    (out,) = remap_call(remap_rows_kernel, [rows], [], [rows.shape[0]], high, low, LIGHT, "remap_rows")
    out = out.reshape(HOURS, shards * levels, PIXELS_DEV) / divisor
    return lax.psum_scatter(out, "tm", scatter_dimension=1, tiled=True)


def solution(mesh):
    sizes = mesh.shape
    paired = sizes["tm"] == HOURS and sizes["lev"] == 4 and sizes["sub"] == 2

    def body(level_field, *others):
        steps, levels, _ = level_field.shape
        suits = paired and steps == 8 and levels % 4 == 0
        return (hour_plan if suits else general_plan)(level_field, *others)

    placed = (
        P(("groups", "tm"), ("lev", "sub"), None),
        P(None, ("lev", "sub")),
        P(("lev", "sub")),
        P(("lev", "sub")),
        P(("lev", "sub")),
        P("tm"),
    )
    return jax.shard_map(
        body,
        mesh=mesh,
        in_specs=placed,
        out_specs=P("groups", "tm", ("lev", "sub")),
        check_vma=False,
    )
```

```python
import functools

import jax
import jax.numpy as jnp
from jax import lax
from jax.experimental import pallas as pl
from jax.experimental.pallas import tpu as pltpu
from jax.sharding import PartitionSpec as P

TILE = 64
HOURS = 2
CT_DEV = 32
PT_DEV = 16
SLOTS = 128
CELLS_DEV = CT_DEV * TILE
PIXELS_DEV = PT_DEV * TILE
LANES = 2 * TILE
MIB = 1 << 20

LIGHT = pl.CostEstimate(flops=1, bytes_accessed=1, transcendentals=0)
MEDIUM = pl.CostEstimate(flops=2_500_000_000, bytes_accessed=1, transcendentals=0)
HEAVY = pl.CostEstimate(flops=10_000_000_000, bytes_accessed=1, transcendentals=0)

NT = (((1,), (1,)), ((), ()))
NN = (((1,), (0,)), ((), ()))


def split(x):
    high = x.astype(jnp.bfloat16)
    return high, (x - high.astype(jnp.float32)).astype(jnp.bfloat16)


def dot(a, b, dims):
    return lax.dot_general(a, b, dims, preferred_element_type=jnp.float32)


GROUP = 8


def place_kernel(rows, columns, count, weights, *refs):
    high, low, total = refs[-3:]
    band = 128

    @pl.loop(0, PIXELS_DEV // band)
    def _(b):
        total[pl.ds(pl.multiple_of(b * band, band), band), :] = jnp.zeros((band, CELLS_DEV), jnp.float32)

    lane_half = lax.broadcasted_iota(jnp.int32, (TILE, LANES), 1) // TILE
    live = count[0]

    @pl.loop(0, (live + GROUP - 1) // GROUP)
    def _(g):
        for pair in range(GROUP // 2):
            lanes = pl.ds(pl.multiple_of((g * (GROUP // 2) + pair) * LANES, LANES), LANES)
            tiles = weights[:, lanes]
            turned = pltpu.roll(tiles, TILE, 1)
            for i in range(2):
                k = g * GROUP + pair * 2 + i
                row, column = rows[k], columns[k]
                side = jnp.where(k < live, column & 1, -1)
                tile = jnp.where(lane_half == i, tiles, turned)
                at = (
                    pl.ds(pl.multiple_of(row * TILE, TILE), TILE),
                    pl.ds(pl.multiple_of((column >> 1) * LANES, LANES), LANES),
                )
                total[at] = total[at] + jnp.where(lane_half == side, tile, 0.0)

    @pl.loop(0, PIXELS_DEV // band)
    def _(b):
        at = pl.ds(pl.multiple_of(b * band, band), band)
        high[at, :], low[at, :] = split(total[at, :])


def place_tiles(rows, columns, count, weights, *after):
    smem = pl.BlockSpec(memory_space=pltpu.SMEM)
    vmem = pl.BlockSpec(memory_space=pltpu.VMEM)
    half = jax.ShapeDtypeStruct((PIXELS_DEV, CELLS_DEV), jnp.bfloat16)
    return pl.pallas_call(
        place_kernel,
        out_shape=(half, half),
        in_specs=[smem, smem, smem, vmem] + [pl.BlockSpec(memory_space=pl.ANY)] * len(after),
        out_specs=(vmem, vmem),
        scratch_shapes=[pltpu.VMEM((PIXELS_DEV, CELLS_DEV), jnp.float32)],
        compiler_params=pltpu.CompilerParams(vmem_limit_bytes=28 * MIB),
        cost_estimate=HEAVY,
        name="place_tiles",
    )(rows, columns, count, weights, *after)


PIXEL_BLOCK = 256


def remap_blocks(x, high, low):
    m = x.shape[0]
    x_high, x_low = split(x)
    both = jnp.concatenate([x_high, x_low], axis=0)
    for start in range(0, PIXELS_DEV, PIXEL_BLOCK):
        at = slice(start, start + PIXEL_BLOCK)
        first = dot(both, high[at, :], NT)
        yield at, first[:m] + first[m:] + dot(x_high, low[at, :], NT)


def remap_call(kernel, inputs, after, out_rows, high, low, cost, name, scratch_rows=()):
    vmem = pl.BlockSpec(memory_space=pltpu.VMEM)
    return pl.pallas_call(
        kernel,
        out_shape=[
            jax.ShapeDtypeStruct(rows if isinstance(rows, tuple) else (rows, PIXELS_DEV), jnp.float32)
            for rows in out_rows
        ],
        in_specs=[vmem] * (len(inputs) + 2) + [pl.BlockSpec(memory_space=pl.ANY)] * len(after),
        out_specs=[vmem] * len(out_rows),
        scratch_shapes=[pltpu.VMEM((rows, PIXELS_DEV), jnp.float32) for rows in scratch_rows],
        compiler_params=pltpu.CompilerParams(vmem_limit_bytes=24 * MIB),
        cost_estimate=cost,
        name=name,
    )(*inputs, high, low, *after)


def remap_rows_kernel(x, high, low, out):
    for at, result in remap_blocks(x[...], high, low):
        out[:, at] = result


def unfold(block):
    levels = block.shape[0] // 2
    return jnp.concatenate([block[:levels], block[levels:]], axis=1)


def far_rows(same_sub, other_sub):
    even = lax.axis_index("sub") == 0
    blocks = [jnp.where(even, same_sub, other_sub), jnp.where(even, other_sub, same_sub)]
    return [unfold(block) for block in blocks]


def keeps_near():
    return lax.axis_index("tm") == lax.axis_index("lev") // 2


def near_rows(same_sub, other_sub):
    even = lax.axis_index("sub") == 0
    return [jnp.where(even, same_sub, other_sub), jnp.where(even, other_sub, same_sub)]


def by_hour(result, levels):
    pieces = [result[start : start + levels] for start in range(0, 2 * HOURS * levels, levels)]
    return jnp.concatenate([pieces[sub * HOURS + hour] for hour in range(HOURS) for sub in range(2)], axis=0)


def sort_out(near_result, far_result, keep, send):
    near = keeps_near()

    @pl.when(near)
    def _():
        keep[...], send[...] = near_result[...], far_result[...]

    @pl.when(jnp.logical_not(near))
    def _():
        keep[...], send[...] = far_result[...], near_result[...]


def remap_both_kernel(own, sibling, plain, high, low, *refs):
    keep, send, near_result, far_result = refs[-4:]
    rows = own.shape[0]
    blocks = near_rows(own[...], sibling[...]) + [plain[...]]
    for at, result in remap_blocks(jnp.concatenate(blocks, axis=0), high, low):
        near_result[:, at] = by_hour(result, rows // HOURS)
        far_result[:rows, at] = result[2 * rows :]
    far_result[rows:] = jnp.zeros((rows, PIXELS_DEV), jnp.float32)
    sort_out(near_result, far_result, keep, send)


def remap_near_kernel(near_same, near_other, far, high, low, *refs):
    keep, send, near_result, far_result = refs[-4:]
    rows = near_same.shape[0]
    blocks = near_rows(near_same[...], near_other[...]) + [far[...]]
    for at, result in remap_blocks(jnp.concatenate(blocks, axis=0), high, low):
        near_result[:, at] = by_hour(result, rows // HOURS)
        far_result[:rows, at] = result[2 * rows :]
    far_result[rows:] = jnp.zeros((rows, PIXELS_DEV), jnp.float32)
    sort_out(near_result, far_result, keep, send)


def remap_last_kernel(block, high, low, *refs):
    out, total = refs[-2:]
    x = unfold(block[...])
    levels, cells = x.shape
    x = jnp.concatenate([x, jnp.zeros((-levels % 16, cells), jnp.float32)], axis=0)
    for at, result in remap_blocks(x, high, low):
        total[:, at] = result
    out[...] = fold(total[:levels])


def hour_weights(step_hour, steps, hours, width):
    row = lax.broadcasted_iota(jnp.int32, (steps, width), 0)
    first = jnp.zeros((steps, width), jnp.float32)
    second = jnp.zeros((steps, width), jnp.float32)
    for step in range(steps):
        first = jnp.where(row == step, jnp.where(step_hour[step] == hours[0], 1.0, 0.0), first)
        second = jnp.where(row == step, jnp.where(step_hour[step] == hours[1], 1.0, 0.0), second)
    upper = row < steps // 2
    return jnp.where(upper, first, second), jnp.where(upper, second, first)


def turn(x, rows):
    return pltpu.roll(x, rows % x.shape[0], 0)


def join(a, b, bit):
    clear = (lax.broadcasted_iota(jnp.int32, a.shape, 0) & bit) == 0
    kept, moved = jnp.where(clear, a, b), jnp.where(clear, b, a)
    return kept + jnp.where(clear, turn(moved, -bit), turn(moved, bit))


def sum_steps(block, weights):
    def halve(x):
        return x * weights[0] + turn(x * weights[1], 4)

    def four(level):
        a, b, c, d = (halve(block(level + i)) for i in range(4))
        return join(join(a, c, 2), join(b, d, 2), 1)

    return four


def pack(pieces):
    upper = lax.broadcasted_iota(jnp.int32, pieces[0][0].shape, 0) < 4
    at_half = [x if half == place % 2 else turn(x, 4) for place, (x, half) in enumerate(pieces)]
    return [jnp.where(upper, a, b) for a, b in zip(at_half[::2], at_half[1::2])]


def peer_shard(k, j):
    subs = lax.axis_size("sub")
    return (lax.axis_index("lev") ^ k) * subs + (lax.axis_index("sub") ^ j)


def field_copies(field, buffer, arrived, peers):
    copies = []
    for place, (k, j) in enumerate(peers):
        start = pl.multiple_of(peer_shard(k, j) * CELLS_DEV, CELLS_DEV)
        copy = pltpu.make_async_copy(
            field.at[:, :, pl.ds(start, CELLS_DEV)], buffer.at[place], arrived.at[place]
        )
        copy.start()
        copies.append(copy)
    return copies


SUM_WIDTH = 512


def sums_kernel(plain, first, second, step_hour, field, *refs):
    *outs, buffer, arrived, hours, hours_arrived = refs
    _, levels, steps, cells = buffer.shape
    rows, cut = HOURS * levels, cells // 2
    copies = field_copies(field, buffer, arrived, [*plain, *first, second])
    fetch = pltpu.make_async_copy(step_hour, hours, hours_arrived)
    fetch.start()
    fetch.wait()
    me = lax.axis_index("tm")
    groups = range(0, levels, 4)

    def summed(place, start, width, weights):
        four = sum_steps(lambda level: buffer[place, level, :, pl.ds(start, width)], weights)
        return [four(level) for level in groups]

    def store(out, offset, start, width, pieces):
        for place, x in enumerate(pack(pieces)):
            out[offset + place * 8 : offset + place * 8 + 8, pl.ds(start, width)] = x

    weights = hour_weights(hours, steps, range(HOURS), SUM_WIDTH)
    for place in range(len(plain)):
        copies[place].wait()

        @pl.loop(0, cells // SUM_WIDTH)
        def _(i):
            start = pl.multiple_of(i * SUM_WIDTH, SUM_WIDTH)
            sums = summed(place, start, SUM_WIDTH, weights)
            pieces = [(x, half) for half in range(HOURS) for x in sums]
            store(outs[place], 0, start, SUM_WIDTH, pieces)

    theirs_first, mine_first, theirs_second, mine_second = outs[len(plain) :]
    width = SUM_WIDTH // 2
    weights = hour_weights(hours, steps, (1 - me, me), width)
    for j in range(len(first) + 1):
        place = len(plain) + j
        copies[place].wait()
        offset = j * rows if j < len(first) else 0
        theirs, mine = (theirs_first, mine_first) if j < len(first) else (theirs_second, mine_second)

        @pl.loop(0, cut // width)
        def _(i):
            start = pl.multiple_of(i * width, width)
            sums = summed(place, start, width, weights) + summed(place, cut + start, width, weights)
            store(theirs, offset, start, width, [(x, 0) for x in sums])
            store(mine, offset, start, width, [(x, 1) for x in sums])


def hour_sums(plain, first, second, step_hour, field):
    levels, steps, _ = field.shape
    rows, cut = HOURS * levels, CELLS_DEV // 2
    vmem = pl.BlockSpec(memory_space=pltpu.VMEM)
    shapes = [(rows, CELLS_DEV)] * len(plain) + [(len(first) * rows, cut)] * 2 + [(rows, cut)] * 2
    count = len(plain) + len(first) + 1
    outs = pl.pallas_call(
        functools.partial(sums_kernel, plain, first, second),
        out_shape=[jax.ShapeDtypeStruct(shape, jnp.float32) for shape in shapes],
        in_specs=[pl.BlockSpec(memory_space=pl.ANY)] * 2,
        out_specs=[vmem] * len(shapes),
        scratch_shapes=[
            pltpu.VMEM((count, levels, steps, CELLS_DEV), jnp.float32),
            pltpu.SemaphoreType.DMA((count,)),
            pltpu.SMEM((steps,), jnp.int32),
            pltpu.SemaphoreType.DMA,
        ],
        compiler_params=pltpu.CompilerParams(vmem_limit_bytes=52 * MIB),
        cost_estimate=LIGHT,
        name="hour_sums",
    )(step_hour, field)
    return outs[: len(plain)], outs[len(plain) :]


def merge_first_kernel(mine, got, *refs):
    rows = refs[-1].shape[0]
    refs[-1][...] = mine[:rows] + got[:rows]


def merge_next_kernel(mine, got, *refs):
    rows = refs[-1].shape[0]
    refs[-1][...] = mine[rows:] + got[rows:]


def merge_last_kernel(mine, got, *refs):
    refs[-1][...] = mine[...] + got[...]


def fold(x):
    half = x.shape[1] // 2
    return jnp.concatenate([x[:, :half], x[:, half:]], axis=0)


def hold_kernel(x, *refs):
    refs[-1][...] = x[...]


def far_rows_kernel(same_sub, other_sub, out):
    out[...] = jnp.concatenate(far_rows(same_sub[...], other_sub[...]), axis=0)


def small_call(kernel, inputs, after, shapes, cost, name):
    vmem = pl.BlockSpec(memory_space=pltpu.VMEM)
    return pl.pallas_call(
        kernel,
        out_shape=[jax.ShapeDtypeStruct(shape, jnp.float32) for shape in shapes],
        in_specs=[vmem] * len(inputs) + [pl.BlockSpec(memory_space=pl.ANY)] * len(after),
        out_specs=[vmem] * len(shapes),
        compiler_params=pltpu.CompilerParams(vmem_limit_bytes=8 * MIB),
        cost_estimate=cost,
        name=name,
    )(*inputs, *after)


def finish_kernel(divisor, levels, chip, got_chip, one, got_one, last, got_last, out):
    me, lev, even = lax.axis_index("tm"), lax.axis_index("lev") % 2, lax.axis_index("sub") == 0
    rows = 2 * levels
    near = keeps_near()
    for hour in range(HOURS):
        same_at = pl.ds(pl.multiple_of((hour * 2 + lev) * rows, rows), rows)
        other_at = pl.ds(pl.multiple_of((hour * 2 + 1 - lev) * rows, rows), rows)

        @pl.when(near)
        def _():
            here = slice(hour * rows, (hour + 1) * rows)
            out[same_at, :] = (chip[here] + got_chip[here]) / divisor
            out[other_at, :] = (one[here] + got_one[here]) / divisor

        @pl.when(jnp.logical_not(near))
        def _():
            here = slice(hour * levels, (hour + 1) * levels)
            plain = chip[here] + got_chip[here]
            other = unfold(jnp.where(me == hour, last[...], got_last[...]))
            pair = [jnp.where(even, plain, other), jnp.where(even, other, plain)]
            out[same_at, :] = jnp.concatenate(pair, axis=0) / divisor
            out[other_at, :] = jnp.where(me == hour, one[:rows], got_one[:rows]) / divisor


def finish(arrays, levels, divisor):
    call = functools.partial(finish_kernel, divisor, levels)
    shape = (2 * arrays[0].shape[0], PIXELS_DEV)
    return small_call(call, arrays, [], [shape], LIGHT, "finish")[0]


def hour_plan(level_field, tile_weight, tile_rows, tile_columns, live_count, step_hour):
    levs, subs, shards_tm = lax.axis_size("lev"), lax.axis_size("sub"), lax.axis_size("tm")
    half = levs // 2
    divisor = float(level_field.shape[0] * shards_tm // HOURS)
    field = jnp.transpose(level_field, (1, 0, 2))

    def to_peer(x, k, j):
        pairs = [(a * subs + b, (a ^ k) * subs + (b ^ j)) for a in range(levs) for b in range(subs)]
        return lax.ppermute(x, ("lev", "sub"), pairs)

    def swap(x):
        return lax.ppermute(x, "tm", [(0, 1), (1, 0)])

    plain = [(half, 0), (1, 0), (1, 1), (0, 1), (0, 0)]
    first, second = [(half + 1, j) for j in range(subs)], (half, 1)
    sums, (theirs_0, mine_0, theirs_1, mine_1) = hour_sums(plain, first, second, step_hour, field)
    rows = 2 * field.shape[0]
    folded = theirs_1.shape
    sibling = to_peer(sums[3], *plain[3])
    near_got = [to_peer(x, *peer) for x, peer in list(zip(sums, plain))[1:3]]
    got_0 = swap(theirs_0)
    plain_got = to_peer(sums[0], *plain[0])
    high, low = place_tiles(tile_rows, tile_columns, live_count, tile_weight, theirs_0)

    merged = small_call(
        merge_first_kernel, [mine_0, got_0], [high, sibling], [folded], LIGHT, "merge_first"
    )
    far_same = to_peer(merged[0], *first[0])
    theirs_1 = small_call(hold_kernel, [theirs_1], [plain_got, *merged], [folded], LIGHT, "hold")[0]
    got_1 = swap(theirs_1)
    merged = small_call(merge_next_kernel, [mine_0, got_0], [theirs_1], [folded], LIGHT, "merge_next")
    far_other = to_peer(merged[0], *first[1])
    both, send = remap_call(
        remap_both_kernel,
        [sums[4], sibling, plain_got],
        merged,
        [2 * rows] * 2,
        high,
        low,
        MEDIUM,
        "remap_both",
        [2 * rows] * 2,
    )
    got_both = swap(send)
    merged = small_call(
        merge_last_kernel, [mine_1, got_1], [both, near_got[0]], [folded], HEAVY, "merge_last"
    )
    second_got = to_peer(merged[0], *second)
    far = small_call(far_rows_kernel, [far_same, far_other], [], [(rows, CELLS_DEV)], HEAVY, "far_rows")[0]
    one, send = remap_call(
        remap_near_kernel,
        [*near_got, far],
        [],
        [2 * rows] * 2,
        high,
        low,
        LIGHT,
        "remap_near",
        [2 * rows] * 2,
    )
    got_one = swap(send)
    padded = -(-rows // 32) * 16
    (last,) = remap_call(
        remap_last_kernel,
        [second_got],
        [one],
        [(rows, PIXELS_DEV // 2)],
        high,
        low,
        HEAVY,
        "remap_last",
        [padded],
    )
    got_last = swap(last)
    out = finish([both, got_both, one, got_one, last, got_last], rows // 2, divisor)
    return out.reshape(HOURS, out.shape[0] // HOURS, PIXELS_DEV)


def general_plan(level_field, tile_weight, tile_rows, tile_columns, live_count, step_hour):
    steps, levels, cells = level_field.shape
    shards = lax.axis_size("lev") * lax.axis_size("sub")
    divisor = float(steps * lax.axis_size("tm") // HOURS)
    hours = jnp.arange(HOURS, dtype=jnp.int32)
    table = (step_hour[None, :] == hours[:, None]).astype(jnp.float32)
    fields = level_field.reshape(steps, levels, shards, cells // shards)
    partial = jnp.einsum("hs,slgc->ghlc", table, fields, precision=lax.Precision.HIGHEST)
    regrouped = lax.all_to_all(partial, ("lev", "sub"), split_axis=0, concat_axis=0, tiled=True)
    rows = jnp.transpose(regrouped, (1, 0, 2, 3)).reshape(-1, cells // shards)
    high, low = place_tiles(tile_rows, tile_columns, live_count, tile_weight)
    (out,) = remap_call(remap_rows_kernel, [rows], [], [rows.shape[0]], high, low, LIGHT, "remap_rows")
    out = out.reshape(HOURS, shards * levels, PIXELS_DEV) / divisor
    return lax.psum_scatter(out, "tm", scatter_dimension=1, tiled=True)


def solution(mesh):
    sizes = mesh.shape
    paired = sizes["tm"] == HOURS and sizes["lev"] == 4 and sizes["sub"] == 2

    def body(level_field, *others):
        steps, levels, _ = level_field.shape
        suits = paired and steps == 8 and levels % 4 == 0
        return (hour_plan if suits else general_plan)(level_field, *others)

    placed = (
        P(("groups", "tm"), ("lev", "sub"), None),
        P(None, ("lev", "sub")),
        P(("lev", "sub")),
        P(("lev", "sub")),
        P(("lev", "sub")),
        P("tm"),
    )
    return jax.shard_map(
        body,
        mesh=mesh,
        in_specs=placed,
        out_specs=P("groups", "tm", ("lev", "sub")),
        check_vma=False,
    )
```

```python
import functools

import jax
import jax.numpy as jnp
from jax import lax
from jax.experimental import pallas as pl
from jax.experimental.pallas import tpu as pltpu
from jax.sharding import PartitionSpec as P

TILE = 64
HOURS = 2
CT_DEV = 32
PT_DEV = 16
SLOTS = 128
CELLS_DEV = CT_DEV * TILE
PIXELS_DEV = PT_DEV * TILE
LANES = 2 * TILE
MIB = 1 << 20

LIGHT = pl.CostEstimate(flops=1, bytes_accessed=1, transcendentals=0)
MEDIUM = pl.CostEstimate(flops=2_500_000_000, bytes_accessed=1, transcendentals=0)
HEAVY = pl.CostEstimate(flops=10_000_000_000, bytes_accessed=1, transcendentals=0)

NT = (((1,), (1,)), ((), ()))
NN = (((1,), (0,)), ((), ()))


def split(x):
    high = x.astype(jnp.bfloat16)
    return high, (x - high.astype(jnp.float32)).astype(jnp.bfloat16)


def dot(a, b, dims):
    return lax.dot_general(a, b, dims, preferred_element_type=jnp.float32)


GROUP = 8


def place_kernel(rows, columns, count, weights, *refs):
    high, low, total = refs[-3:]
    band = 128

    @pl.loop(0, PIXELS_DEV // band)
    def _(b):
        total[pl.ds(pl.multiple_of(b * band, band), band), :] = jnp.zeros((band, CELLS_DEV), jnp.float32)

    lane_half = lax.broadcasted_iota(jnp.int32, (TILE, LANES), 1) // TILE
    live = count[0]

    @pl.loop(0, (live + GROUP - 1) // GROUP)
    def _(g):
        for pair in range(GROUP // 2):
            lanes = pl.ds(pl.multiple_of((g * (GROUP // 2) + pair) * LANES, LANES), LANES)
            tiles = weights[:, lanes]
            turned = pltpu.roll(tiles, TILE, 1)
            for i in range(2):
                k = g * GROUP + pair * 2 + i
                row, column = rows[k], columns[k]
                side = jnp.where(k < live, column & 1, -1)
                tile = jnp.where(lane_half == i, tiles, turned)
                at = (
                    pl.ds(pl.multiple_of(row * TILE, TILE), TILE),
                    pl.ds(pl.multiple_of((column >> 1) * LANES, LANES), LANES),
                )
                total[at] = total[at] + jnp.where(lane_half == side, tile, 0.0)

    @pl.loop(0, PIXELS_DEV // band)
    def _(b):
        at = pl.ds(pl.multiple_of(b * band, band), band)
        high[at, :], low[at, :] = split(total[at, :])


def place_tiles(rows, columns, count, weights, *after):
    smem = pl.BlockSpec(memory_space=pltpu.SMEM)
    vmem = pl.BlockSpec(memory_space=pltpu.VMEM)
    half = jax.ShapeDtypeStruct((PIXELS_DEV, CELLS_DEV), jnp.bfloat16)
    return pl.pallas_call(
        place_kernel,
        out_shape=(half, half),
        in_specs=[smem, smem, smem, vmem] + [pl.BlockSpec(memory_space=pl.ANY)] * len(after),
        out_specs=(vmem, vmem),
        scratch_shapes=[pltpu.VMEM((PIXELS_DEV, CELLS_DEV), jnp.float32)],
        compiler_params=pltpu.CompilerParams(vmem_limit_bytes=28 * MIB),
        cost_estimate=LIGHT,
        name="place_tiles",
    )(rows, columns, count, weights, *after)


PIXEL_BLOCK = 256


def remap_blocks(x, high, low):
    m = x.shape[0]
    x_high, x_low = split(x)
    both = jnp.concatenate([x_high, x_low], axis=0)
    for start in range(0, PIXELS_DEV, PIXEL_BLOCK):
        at = slice(start, start + PIXEL_BLOCK)
        first = dot(both, high[at, :], NT)
        yield at, first[:m] + first[m:] + dot(x_high, low[at, :], NT)


def remap_call(kernel, inputs, after, out_rows, high, low, cost, name, scratch_rows=()):
    vmem = pl.BlockSpec(memory_space=pltpu.VMEM)
    return pl.pallas_call(
        kernel,
        out_shape=[
            jax.ShapeDtypeStruct(rows if isinstance(rows, tuple) else (rows, PIXELS_DEV), jnp.float32)
            for rows in out_rows
        ],
        in_specs=[vmem] * (len(inputs) + 2) + [pl.BlockSpec(memory_space=pl.ANY)] * len(after),
        out_specs=[vmem] * len(out_rows),
        scratch_shapes=[pltpu.VMEM((rows, PIXELS_DEV), jnp.float32) for rows in scratch_rows],
        compiler_params=pltpu.CompilerParams(vmem_limit_bytes=24 * MIB),
        cost_estimate=cost,
        name=name,
    )(*inputs, high, low, *after)


def remap_rows_kernel(x, high, low, out):
    for at, result in remap_blocks(x[...], high, low):
        out[:, at] = result


def unfold(block):
    levels = block.shape[0] // 2
    return jnp.concatenate([block[:levels], block[levels:]], axis=1)


def far_rows(same_sub, other_sub):
    even = lax.axis_index("sub") == 0
    blocks = [jnp.where(even, same_sub, other_sub), jnp.where(even, other_sub, same_sub)]
    return [unfold(block) for block in blocks]


def keeps_near():
    return lax.axis_index("tm") == lax.axis_index("lev") // 2


def near_rows(same_sub, other_sub):
    even = lax.axis_index("sub") == 0
    return [jnp.where(even, same_sub, other_sub), jnp.where(even, other_sub, same_sub)]


def by_hour(result, levels):
    pieces = [result[start : start + levels] for start in range(0, 2 * HOURS * levels, levels)]
    return jnp.concatenate([pieces[sub * HOURS + hour] for hour in range(HOURS) for sub in range(2)], axis=0)


def sort_out(near_result, far_result, keep, send):
    near = keeps_near()

    @pl.when(near)
    def _():
        keep[...], send[...] = near_result[...], far_result[...]

    @pl.when(jnp.logical_not(near))
    def _():
        keep[...], send[...] = far_result[...], near_result[...]


def remap_both_kernel(own, sibling, plain, high, low, *refs):
    keep, send, near_result, far_result = refs[-4:]
    rows = own.shape[0]
    blocks = near_rows(own[...], sibling[...]) + [plain[...]]
    for at, result in remap_blocks(jnp.concatenate(blocks, axis=0), high, low):
        near_result[:, at] = by_hour(result, rows // HOURS)
        far_result[:rows, at] = result[2 * rows :]
    far_result[rows:] = jnp.zeros((rows, PIXELS_DEV), jnp.float32)
    sort_out(near_result, far_result, keep, send)


def remap_near_kernel(near_same, near_other, far, high, low, *refs):
    keep, send, near_result, far_result = refs[-4:]
    rows = near_same.shape[0]
    blocks = near_rows(near_same[...], near_other[...]) + [far[...]]
    for at, result in remap_blocks(jnp.concatenate(blocks, axis=0), high, low):
        near_result[:, at] = by_hour(result, rows // HOURS)
        far_result[:rows, at] = result[2 * rows :]
    far_result[rows:] = jnp.zeros((rows, PIXELS_DEV), jnp.float32)
    sort_out(near_result, far_result, keep, send)


def remap_last_kernel(block, high, low, *refs):
    out, total = refs[-2:]
    x = unfold(block[...])
    levels, cells = x.shape
    x = jnp.concatenate([x, jnp.zeros((-levels % 16, cells), jnp.float32)], axis=0)
    for at, result in remap_blocks(x, high, low):
        total[:, at] = result
    out[...] = fold(total[:levels])


def hour_weights(step_hour, steps, hours, width):
    row = lax.broadcasted_iota(jnp.int32, (steps, width), 0)
    first = jnp.zeros((steps, width), jnp.float32)
    second = jnp.zeros((steps, width), jnp.float32)
    for step in range(steps):
        first = jnp.where(row == step, jnp.where(step_hour[step] == hours[0], 1.0, 0.0), first)
        second = jnp.where(row == step, jnp.where(step_hour[step] == hours[1], 1.0, 0.0), second)
    upper = row < steps // 2
    return jnp.where(upper, first, second), jnp.where(upper, second, first)


def turn(x, rows):
    return pltpu.roll(x, rows % x.shape[0], 0)


def join(a, b, bit):
    clear = (lax.broadcasted_iota(jnp.int32, a.shape, 0) & bit) == 0
    kept, moved = jnp.where(clear, a, b), jnp.where(clear, b, a)
    return kept + jnp.where(clear, turn(moved, -bit), turn(moved, bit))


def sum_steps(block, weights):
    def halve(x):
        return x * weights[0] + turn(x * weights[1], 4)

    def four(level):
        a, b, c, d = (halve(block(level + i)) for i in range(4))
        return join(join(a, c, 2), join(b, d, 2), 1)

    return four


def pack(pieces):
    upper = lax.broadcasted_iota(jnp.int32, pieces[0][0].shape, 0) < 4
    at_half = [x if half == place % 2 else turn(x, 4) for place, (x, half) in enumerate(pieces)]
    return [jnp.where(upper, a, b) for a, b in zip(at_half[::2], at_half[1::2])]


def peer_shard(k, j):
    subs = lax.axis_size("sub")
    return (lax.axis_index("lev") ^ k) * subs + (lax.axis_index("sub") ^ j)


def field_copies(field, buffer, arrived, peers):
    copies = []
    for place, (k, j) in enumerate(peers):
        start = pl.multiple_of(peer_shard(k, j) * CELLS_DEV, CELLS_DEV)
        copy = pltpu.make_async_copy(
            field.at[:, :, pl.ds(start, CELLS_DEV)], buffer.at[place], arrived.at[place]
        )
        copy.start()
        copies.append(copy)
    return copies


SUM_WIDTH = 512


def sums_kernel(plain, first, second, step_hour, field, *refs):
    *outs, buffer, arrived, hours, hours_arrived = refs
    _, levels, steps, cells = buffer.shape
    rows, cut = HOURS * levels, cells // 2
    copies = field_copies(field, buffer, arrived, [*plain, *first, second])
    fetch = pltpu.make_async_copy(step_hour, hours, hours_arrived)
    fetch.start()
    fetch.wait()
    me = lax.axis_index("tm")
    groups = range(0, levels, 4)

    def summed(place, start, width, weights):
        four = sum_steps(lambda level: buffer[place, level, :, pl.ds(start, width)], weights)
        return [four(level) for level in groups]

    def store(out, offset, start, width, pieces):
        for place, x in enumerate(pack(pieces)):
            out[offset + place * 8 : offset + place * 8 + 8, pl.ds(start, width)] = x

    weights = hour_weights(hours, steps, range(HOURS), SUM_WIDTH)
    for place in range(len(plain)):
        copies[place].wait()

        @pl.loop(0, cells // SUM_WIDTH)
        def _(i):
            start = pl.multiple_of(i * SUM_WIDTH, SUM_WIDTH)
            sums = summed(place, start, SUM_WIDTH, weights)
            pieces = [(x, half) for half in range(HOURS) for x in sums]
            store(outs[place], 0, start, SUM_WIDTH, pieces)

    theirs_first, mine_first, theirs_second, mine_second = outs[len(plain) :]
    width = SUM_WIDTH // 2
    weights = hour_weights(hours, steps, (1 - me, me), width)
    for j in range(len(first) + 1):
        place = len(plain) + j
        copies[place].wait()
        offset = j * rows if j < len(first) else 0
        theirs, mine = (theirs_first, mine_first) if j < len(first) else (theirs_second, mine_second)

        @pl.loop(0, cut // width)
        def _(i):
            start = pl.multiple_of(i * width, width)
            sums = summed(place, start, width, weights) + summed(place, cut + start, width, weights)
            store(theirs, offset, start, width, [(x, 0) for x in sums])
            store(mine, offset, start, width, [(x, 1) for x in sums])


def hour_sums(plain, first, second, step_hour, field):
    levels, steps, _ = field.shape
    rows, cut = HOURS * levels, CELLS_DEV // 2
    vmem = pl.BlockSpec(memory_space=pltpu.VMEM)
    shapes = [(rows, CELLS_DEV)] * len(plain) + [(len(first) * rows, cut)] * 2 + [(rows, cut)] * 2
    count = len(plain) + len(first) + 1
    outs = pl.pallas_call(
        functools.partial(sums_kernel, plain, first, second),
        out_shape=[jax.ShapeDtypeStruct(shape, jnp.float32) for shape in shapes],
        in_specs=[pl.BlockSpec(memory_space=pl.ANY)] * 2,
        out_specs=[vmem] * len(shapes),
        scratch_shapes=[
            pltpu.VMEM((count, levels, steps, CELLS_DEV), jnp.float32),
            pltpu.SemaphoreType.DMA((count,)),
            pltpu.SMEM((steps,), jnp.int32),
            pltpu.SemaphoreType.DMA,
        ],
        compiler_params=pltpu.CompilerParams(vmem_limit_bytes=52 * MIB),
        cost_estimate=LIGHT,
        name="hour_sums",
    )(step_hour, field)
    return outs[: len(plain)], outs[len(plain) :]


def merge_first_kernel(mine, got, *refs):
    rows = refs[-1].shape[0]
    refs[-1][...] = mine[:rows] + got[:rows]


def merge_next_kernel(mine, got, *refs):
    rows = refs[-1].shape[0]
    refs[-1][...] = mine[rows:] + got[rows:]


def merge_last_kernel(mine, got, *refs):
    refs[-1][...] = mine[...] + got[...]


def fold(x):
    half = x.shape[1] // 2
    return jnp.concatenate([x[:, :half], x[:, half:]], axis=0)


def hold_kernel(x, *refs):
    refs[-1][...] = x[...]


def far_rows_kernel(same_sub, other_sub, out):
    out[...] = jnp.concatenate(far_rows(same_sub[...], other_sub[...]), axis=0)


def small_call(kernel, inputs, after, shapes, cost, name):
    vmem = pl.BlockSpec(memory_space=pltpu.VMEM)
    return pl.pallas_call(
        kernel,
        out_shape=[jax.ShapeDtypeStruct(shape, jnp.float32) for shape in shapes],
        in_specs=[vmem] * len(inputs) + [pl.BlockSpec(memory_space=pl.ANY)] * len(after),
        out_specs=[vmem] * len(shapes),
        compiler_params=pltpu.CompilerParams(vmem_limit_bytes=8 * MIB),
        cost_estimate=cost,
        name=name,
    )(*inputs, *after)


def finish_kernel(divisor, levels, chip, got_chip, one, got_one, last, got_last, out):
    me, lev, even = lax.axis_index("tm"), lax.axis_index("lev") % 2, lax.axis_index("sub") == 0
    rows = 2 * levels
    near = keeps_near()
    for hour in range(HOURS):
        same_at = pl.ds(pl.multiple_of((hour * 2 + lev) * rows, rows), rows)
        other_at = pl.ds(pl.multiple_of((hour * 2 + 1 - lev) * rows, rows), rows)

        @pl.when(near)
        def _():
            here = slice(hour * rows, (hour + 1) * rows)
            out[same_at, :] = (chip[here] + got_chip[here]) / divisor
            out[other_at, :] = (one[here] + got_one[here]) / divisor

        @pl.when(jnp.logical_not(near))
        def _():
            here = slice(hour * levels, (hour + 1) * levels)
            plain = chip[here] + got_chip[here]
            other = unfold(jnp.where(me == hour, last[...], got_last[...]))
            pair = [jnp.where(even, plain, other), jnp.where(even, other, plain)]
            out[same_at, :] = jnp.concatenate(pair, axis=0) / divisor
            out[other_at, :] = jnp.where(me == hour, one[:rows], got_one[:rows]) / divisor


def finish(arrays, levels, divisor):
    call = functools.partial(finish_kernel, divisor, levels)
    shape = (2 * arrays[0].shape[0], PIXELS_DEV)
    return small_call(call, arrays, [], [shape], LIGHT, "finish")[0]


def hour_plan(level_field, tile_weight, tile_rows, tile_columns, live_count, step_hour):
    levs, subs, shards_tm = lax.axis_size("lev"), lax.axis_size("sub"), lax.axis_size("tm")
    half = levs // 2
    divisor = float(level_field.shape[0] * shards_tm // HOURS)
    field = jnp.transpose(level_field, (1, 0, 2))

    def to_peer(x, k, j):
        pairs = [(a * subs + b, (a ^ k) * subs + (b ^ j)) for a in range(levs) for b in range(subs)]
        return lax.ppermute(x, ("lev", "sub"), pairs)

    def swap(x):
        return lax.ppermute(x, "tm", [(0, 1), (1, 0)])

    plain = [(half, 0), (1, 0), (1, 1), (0, 1), (0, 0)]
    first, second = [(half + 1, j) for j in range(subs)], (half, 1)
    sums, (theirs_0, mine_0, theirs_1, mine_1) = hour_sums(plain, first, second, step_hour, field)
    rows = 2 * field.shape[0]
    folded = theirs_1.shape
    sibling = to_peer(sums[3], *plain[3])
    near_got = [to_peer(x, *peer) for x, peer in list(zip(sums, plain))[1:3]]
    got_0 = swap(theirs_0)
    plain_got = to_peer(sums[0], *plain[0])
    high, low = place_tiles(tile_rows, tile_columns, live_count, tile_weight, theirs_0)

    merged = small_call(
        merge_first_kernel, [mine_0, got_0], [high, sibling], [folded], LIGHT, "merge_first"
    )
    far_same = to_peer(merged[0], *first[0])
    merged = small_call(merge_next_kernel, [mine_0, got_0], merged, [folded], LIGHT, "merge_next")
    far_other = to_peer(merged[0], *first[1])
    theirs_1 = small_call(hold_kernel, [theirs_1], [plain_got, *merged], [folded], LIGHT, "hold")[0]
    got_1 = swap(theirs_1)
    both, send = remap_call(
        remap_both_kernel,
        [sums[4], sibling, plain_got],
        [theirs_1],
        [2 * rows] * 2,
        high,
        low,
        MEDIUM,
        "remap_both",
        [2 * rows] * 2,
    )
    got_both = swap(send)
    merged = small_call(
        merge_last_kernel, [mine_1, got_1], [both, near_got[0]], [folded], HEAVY, "merge_last"
    )
    second_got = to_peer(merged[0], *second)
    far = small_call(far_rows_kernel, [far_same, far_other], [], [(rows, CELLS_DEV)], HEAVY, "far_rows")[0]
    one, send = remap_call(
        remap_near_kernel,
        [*near_got, far],
        [],
        [2 * rows] * 2,
        high,
        low,
        LIGHT,
        "remap_near",
        [2 * rows] * 2,
    )
    got_one = swap(send)
    padded = -(-rows // 32) * 16
    (last,) = remap_call(
        remap_last_kernel,
        [second_got],
        [one],
        [(rows, PIXELS_DEV // 2)],
        high,
        low,
        HEAVY,
        "remap_last",
        [padded],
    )
    got_last = swap(last)
    out = finish([both, got_both, one, got_one, last, got_last], rows // 2, divisor)
    return out.reshape(HOURS, out.shape[0] // HOURS, PIXELS_DEV)


def general_plan(level_field, tile_weight, tile_rows, tile_columns, live_count, step_hour):
    steps, levels, cells = level_field.shape
    shards = lax.axis_size("lev") * lax.axis_size("sub")
    divisor = float(steps * lax.axis_size("tm") // HOURS)
    hours = jnp.arange(HOURS, dtype=jnp.int32)
    table = (step_hour[None, :] == hours[:, None]).astype(jnp.float32)
    fields = level_field.reshape(steps, levels, shards, cells // shards)
    partial = jnp.einsum("hs,slgc->ghlc", table, fields, precision=lax.Precision.HIGHEST)
    regrouped = lax.all_to_all(partial, ("lev", "sub"), split_axis=0, concat_axis=0, tiled=True)
    rows = jnp.transpose(regrouped, (1, 0, 2, 3)).reshape(-1, cells // shards)
    high, low = place_tiles(tile_rows, tile_columns, live_count, tile_weight)
    (out,) = remap_call(remap_rows_kernel, [rows], [], [rows.shape[0]], high, low, LIGHT, "remap_rows")
    out = out.reshape(HOURS, shards * levels, PIXELS_DEV) / divisor
    return lax.psum_scatter(out, "tm", scatter_dimension=1, tiled=True)


def solution(mesh):
    sizes = mesh.shape
    paired = sizes["tm"] == HOURS and sizes["lev"] == 4 and sizes["sub"] == 2

    def body(level_field, *others):
        steps, levels, _ = level_field.shape
        suits = paired and steps == 8 and levels % 4 == 0
        return (hour_plan if suits else general_plan)(level_field, *others)

    placed = (
        P(("groups", "tm"), ("lev", "sub"), None),
        P(None, ("lev", "sub")),
        P(("lev", "sub")),
        P(("lev", "sub")),
        P(("lev", "sub")),
        P("tm"),
    )
    return jax.shard_map(
        body,
        mesh=mesh,
        in_specs=placed,
        out_specs=P("groups", "tm", ("lev", "sub")),
        check_vma=False,
    )
```

```python
import functools

import jax
import jax.numpy as jnp
from jax import lax
from jax.experimental import pallas as pl
from jax.experimental.pallas import tpu as pltpu
from jax.sharding import PartitionSpec as P

TILE = 64
HOURS = 2
CT_DEV = 32
PT_DEV = 16
SLOTS = 128
CELLS_DEV = CT_DEV * TILE
PIXELS_DEV = PT_DEV * TILE
LANES = 2 * TILE
MIB = 1 << 20

LIGHT = pl.CostEstimate(flops=1, bytes_accessed=1, transcendentals=0)
MEDIUM = pl.CostEstimate(flops=2_500_000_000, bytes_accessed=1, transcendentals=0)
HEAVY = pl.CostEstimate(flops=10_000_000_000, bytes_accessed=1, transcendentals=0)

NT = (((1,), (1,)), ((), ()))
NN = (((1,), (0,)), ((), ()))


def split(x):
    high = x.astype(jnp.bfloat16)
    return high, (x - high.astype(jnp.float32)).astype(jnp.bfloat16)


def dot(a, b, dims):
    return lax.dot_general(a, b, dims, preferred_element_type=jnp.float32)


GROUP = 8


def place_kernel(rows, columns, count, weights, *refs):
    high, low, total = refs[-3:]
    band = 128

    @pl.loop(0, PIXELS_DEV // band)
    def _(b):
        total[pl.ds(pl.multiple_of(b * band, band), band), :] = jnp.zeros((band, CELLS_DEV), jnp.float32)

    lane_half = lax.broadcasted_iota(jnp.int32, (TILE, LANES), 1) // TILE
    live = count[0]

    @pl.loop(0, (live + GROUP - 1) // GROUP)
    def _(g):
        for pair in range(GROUP // 2):
            lanes = pl.ds(pl.multiple_of((g * (GROUP // 2) + pair) * LANES, LANES), LANES)
            tiles = weights[:, lanes]
            turned = pltpu.roll(tiles, TILE, 1)
            for i in range(2):
                k = g * GROUP + pair * 2 + i
                row, column = rows[k], columns[k]
                side = jnp.where(k < live, column & 1, -1)
                tile = jnp.where(lane_half == i, tiles, turned)
                at = (
                    pl.ds(pl.multiple_of(row * TILE, TILE), TILE),
                    pl.ds(pl.multiple_of((column >> 1) * LANES, LANES), LANES),
                )
                total[at] = total[at] + jnp.where(lane_half == side, tile, 0.0)

    @pl.loop(0, PIXELS_DEV // band)
    def _(b):
        at = pl.ds(pl.multiple_of(b * band, band), band)
        high[at, :], low[at, :] = split(total[at, :])


def place_tiles(rows, columns, count, weights, *after):
    smem = pl.BlockSpec(memory_space=pltpu.SMEM)
    vmem = pl.BlockSpec(memory_space=pltpu.VMEM)
    half = jax.ShapeDtypeStruct((PIXELS_DEV, CELLS_DEV), jnp.bfloat16)
    return pl.pallas_call(
        place_kernel,
        out_shape=(half, half),
        in_specs=[smem, smem, smem, vmem] + [pl.BlockSpec(memory_space=pl.ANY)] * len(after),
        out_specs=(vmem, vmem),
        scratch_shapes=[pltpu.VMEM((PIXELS_DEV, CELLS_DEV), jnp.float32)],
        compiler_params=pltpu.CompilerParams(vmem_limit_bytes=28 * MIB),
        cost_estimate=LIGHT,
        name="place_tiles",
    )(rows, columns, count, weights, *after)


PIXEL_BLOCK = 256


def remap_blocks(x, high, low):
    m = x.shape[0]
    x_high, x_low = split(x)
    both = jnp.concatenate([x_high, x_low], axis=0)
    for start in range(0, PIXELS_DEV, PIXEL_BLOCK):
        at = slice(start, start + PIXEL_BLOCK)
        first = dot(both, high[at, :], NT)
        yield at, first[:m] + first[m:] + dot(x_high, low[at, :], NT)


def remap_call(kernel, inputs, after, out_rows, high, low, cost, name, scratch_rows=()):
    vmem = pl.BlockSpec(memory_space=pltpu.VMEM)
    return pl.pallas_call(
        kernel,
        out_shape=[
            jax.ShapeDtypeStruct(rows if isinstance(rows, tuple) else (rows, PIXELS_DEV), jnp.float32)
            for rows in out_rows
        ],
        in_specs=[vmem] * (len(inputs) + 2) + [pl.BlockSpec(memory_space=pl.ANY)] * len(after),
        out_specs=[vmem] * len(out_rows),
        scratch_shapes=[pltpu.VMEM((rows, PIXELS_DEV), jnp.float32) for rows in scratch_rows],
        compiler_params=pltpu.CompilerParams(vmem_limit_bytes=24 * MIB),
        cost_estimate=cost,
        name=name,
    )(*inputs, high, low, *after)


def remap_rows_kernel(x, high, low, out):
    for at, result in remap_blocks(x[...], high, low):
        out[:, at] = result


def unfold(block):
    levels = block.shape[0] // 2
    return jnp.concatenate([block[:levels], block[levels:]], axis=1)


def far_rows(same_sub, other_sub):
    even = lax.axis_index("sub") == 0
    blocks = [jnp.where(even, same_sub, other_sub), jnp.where(even, other_sub, same_sub)]
    return [unfold(block) for block in blocks]


def keeps_near():
    return lax.axis_index("tm") == lax.axis_index("lev") // 2


def near_rows(same_sub, other_sub):
    even = lax.axis_index("sub") == 0
    return [jnp.where(even, same_sub, other_sub), jnp.where(even, other_sub, same_sub)]


def by_hour(result, levels):
    pieces = [result[start : start + levels] for start in range(0, 2 * HOURS * levels, levels)]
    return jnp.concatenate([pieces[sub * HOURS + hour] for hour in range(HOURS) for sub in range(2)], axis=0)


def sort_out(near_result, far_result, keep, send):
    near = keeps_near()

    @pl.when(near)
    def _():
        keep[...], send[...] = near_result[...], far_result[...]

    @pl.when(jnp.logical_not(near))
    def _():
        keep[...], send[...] = far_result[...], near_result[...]


def remap_both_kernel(own, sibling, plain, high, low, *refs):
    keep, send, near_result, far_result = refs[-4:]
    rows = own.shape[0]
    blocks = near_rows(own[...], sibling[...]) + [plain[...]]
    for at, result in remap_blocks(jnp.concatenate(blocks, axis=0), high, low):
        near_result[:, at] = by_hour(result, rows // HOURS)
        far_result[:rows, at] = result[2 * rows :]
    far_result[rows:] = jnp.zeros((rows, PIXELS_DEV), jnp.float32)
    sort_out(near_result, far_result, keep, send)


def remap_near_kernel(near_same, near_other, far, high, low, *refs):
    keep, send, near_result, far_result = refs[-4:]
    rows = near_same.shape[0]
    blocks = near_rows(near_same[...], near_other[...]) + [far[...]]
    for at, result in remap_blocks(jnp.concatenate(blocks, axis=0), high, low):
        near_result[:, at] = by_hour(result, rows // HOURS)
        far_result[:rows, at] = result[2 * rows :]
    far_result[rows:] = jnp.zeros((rows, PIXELS_DEV), jnp.float32)
    sort_out(near_result, far_result, keep, send)


def remap_last_kernel(block, high, low, *refs):
    out, total = refs[-2:]
    x = unfold(block[...])
    levels, cells = x.shape
    x = jnp.concatenate([x, jnp.zeros((-levels % 16, cells), jnp.float32)], axis=0)
    for at, result in remap_blocks(x, high, low):
        total[:, at] = result
    out[...] = fold(total[:levels])


def hour_weights(step_hour, steps, hours, width):
    row = lax.broadcasted_iota(jnp.int32, (steps, width), 0)
    first = jnp.zeros((steps, width), jnp.float32)
    second = jnp.zeros((steps, width), jnp.float32)
    for step in range(steps):
        first = jnp.where(row == step, jnp.where(step_hour[step] == hours[0], 1.0, 0.0), first)
        second = jnp.where(row == step, jnp.where(step_hour[step] == hours[1], 1.0, 0.0), second)
    upper = row < steps // 2
    return jnp.where(upper, first, second), jnp.where(upper, second, first)


def turn(x, rows):
    return pltpu.roll(x, rows % x.shape[0], 0)


def join(a, b, bit):
    clear = (lax.broadcasted_iota(jnp.int32, a.shape, 0) & bit) == 0
    kept, moved = jnp.where(clear, a, b), jnp.where(clear, b, a)
    return kept + jnp.where(clear, turn(moved, -bit), turn(moved, bit))


def sum_steps(block, weights):
    def halve(x):
        return x * weights[0] + turn(x * weights[1], 4)

    def four(level):
        a, b, c, d = (halve(block(level + i)) for i in range(4))
        return join(join(a, c, 2), join(b, d, 2), 1)

    return four


def pack(pieces):
    upper = lax.broadcasted_iota(jnp.int32, pieces[0][0].shape, 0) < 4
    at_half = [x if half == place % 2 else turn(x, 4) for place, (x, half) in enumerate(pieces)]
    return [jnp.where(upper, a, b) for a, b in zip(at_half[::2], at_half[1::2])]


def peer_shard(k, j):
    subs = lax.axis_size("sub")
    return (lax.axis_index("lev") ^ k) * subs + (lax.axis_index("sub") ^ j)


def field_copies(field, buffer, arrived, peers):
    copies = []
    for place, (k, j) in enumerate(peers):
        start = pl.multiple_of(peer_shard(k, j) * CELLS_DEV, CELLS_DEV)
        copy = pltpu.make_async_copy(
            field.at[:, :, pl.ds(start, CELLS_DEV)], buffer.at[place], arrived.at[place]
        )
        copy.start()
        copies.append(copy)
    return copies


SUM_WIDTH = 512


def sums_kernel(plain, first, second, step_hour, field, *refs):
    *outs, buffer, arrived, hours, hours_arrived = refs
    _, levels, steps, cells = buffer.shape
    rows, cut = HOURS * levels, cells // 2
    copies = field_copies(field, buffer, arrived, [*plain, *first, second])
    fetch = pltpu.make_async_copy(step_hour, hours, hours_arrived)
    fetch.start()
    fetch.wait()
    me = lax.axis_index("tm")
    groups = range(0, levels, 4)

    def summed(place, start, width, weights):
        four = sum_steps(lambda level: buffer[place, level, :, pl.ds(start, width)], weights)
        return [four(level) for level in groups]

    def store(out, offset, start, width, pieces):
        for place, x in enumerate(pack(pieces)):
            out[offset + place * 8 : offset + place * 8 + 8, pl.ds(start, width)] = x

    weights = hour_weights(hours, steps, range(HOURS), SUM_WIDTH)
    for place in range(len(plain)):
        copies[place].wait()

        @pl.loop(0, cells // SUM_WIDTH)
        def _(i):
            start = pl.multiple_of(i * SUM_WIDTH, SUM_WIDTH)
            sums = summed(place, start, SUM_WIDTH, weights)
            pieces = [(x, half) for half in range(HOURS) for x in sums]
            store(outs[place], 0, start, SUM_WIDTH, pieces)

    theirs_first, mine_first, theirs_second, mine_second = outs[len(plain) :]
    width = SUM_WIDTH // 2
    weights = hour_weights(hours, steps, (1 - me, me), width)
    for j in range(len(first) + 1):
        place = len(plain) + j
        copies[place].wait()
        offset = j * rows if j < len(first) else 0
        theirs, mine = (theirs_first, mine_first) if j < len(first) else (theirs_second, mine_second)

        @pl.loop(0, cut // width)
        def _(i):
            start = pl.multiple_of(i * width, width)
            sums = summed(place, start, width, weights) + summed(place, cut + start, width, weights)
            store(theirs, offset, start, width, [(x, 0) for x in sums])
            store(mine, offset, start, width, [(x, 1) for x in sums])


def hour_sums(plain, first, second, step_hour, field):
    levels, steps, _ = field.shape
    rows, cut = HOURS * levels, CELLS_DEV // 2
    vmem = pl.BlockSpec(memory_space=pltpu.VMEM)
    shapes = [(rows, CELLS_DEV)] * len(plain) + [(len(first) * rows, cut)] * 2 + [(rows, cut)] * 2
    count = len(plain) + len(first) + 1
    outs = pl.pallas_call(
        functools.partial(sums_kernel, plain, first, second),
        out_shape=[jax.ShapeDtypeStruct(shape, jnp.float32) for shape in shapes],
        in_specs=[pl.BlockSpec(memory_space=pl.ANY)] * 2,
        out_specs=[vmem] * len(shapes),
        scratch_shapes=[
            pltpu.VMEM((count, levels, steps, CELLS_DEV), jnp.float32),
            pltpu.SemaphoreType.DMA((count,)),
            pltpu.SMEM((steps,), jnp.int32),
            pltpu.SemaphoreType.DMA,
        ],
        compiler_params=pltpu.CompilerParams(vmem_limit_bytes=52 * MIB),
        cost_estimate=LIGHT,
        name="hour_sums",
    )(step_hour, field)
    return outs[: len(plain)], outs[len(plain) :]


def merge_first_kernel(mine, got, *refs):
    rows = refs[-1].shape[0]
    refs[-1][...] = mine[:rows] + got[:rows]


def merge_next_kernel(mine, got, *refs):
    rows = refs[-1].shape[0]
    refs[-1][...] = mine[rows:] + got[rows:]


def merge_last_kernel(mine, got, *refs):
    refs[-1][...] = mine[...] + got[...]


def fold(x):
    half = x.shape[1] // 2
    return jnp.concatenate([x[:, :half], x[:, half:]], axis=0)


def hold_kernel(x, *refs):
    refs[-1][...] = x[...]


def far_rows_kernel(same_sub, other_sub, out):
    out[...] = jnp.concatenate(far_rows(same_sub[...], other_sub[...]), axis=0)


def small_call(kernel, inputs, after, shapes, cost, name):
    vmem = pl.BlockSpec(memory_space=pltpu.VMEM)
    return pl.pallas_call(
        kernel,
        out_shape=[jax.ShapeDtypeStruct(shape, jnp.float32) for shape in shapes],
        in_specs=[vmem] * len(inputs) + [pl.BlockSpec(memory_space=pl.ANY)] * len(after),
        out_specs=[vmem] * len(shapes),
        compiler_params=pltpu.CompilerParams(vmem_limit_bytes=8 * MIB),
        cost_estimate=cost,
        name=name,
    )(*inputs, *after)


def finish_kernel(divisor, levels, chip, got_chip, one, got_one, last, got_last, out):
    me, lev, even = lax.axis_index("tm"), lax.axis_index("lev") % 2, lax.axis_index("sub") == 0
    rows = 2 * levels
    near = keeps_near()
    for hour in range(HOURS):
        same_at = pl.ds(pl.multiple_of((hour * 2 + lev) * rows, rows), rows)
        other_at = pl.ds(pl.multiple_of((hour * 2 + 1 - lev) * rows, rows), rows)

        @pl.when(near)
        def _():
            here = slice(hour * rows, (hour + 1) * rows)
            out[same_at, :] = (chip[here] + got_chip[here]) / divisor
            out[other_at, :] = (one[here] + got_one[here]) / divisor

        @pl.when(jnp.logical_not(near))
        def _():
            here = slice(hour * levels, (hour + 1) * levels)
            plain = chip[here] + got_chip[here]
            other = unfold(jnp.where(me == hour, last[...], got_last[...]))
            pair = [jnp.where(even, plain, other), jnp.where(even, other, plain)]
            out[same_at, :] = jnp.concatenate(pair, axis=0) / divisor
            out[other_at, :] = jnp.where(me == hour, one[:rows], got_one[:rows]) / divisor


def finish(arrays, levels, divisor):
    call = functools.partial(finish_kernel, divisor, levels)
    shape = (2 * arrays[0].shape[0], PIXELS_DEV)
    return small_call(call, arrays, [], [shape], LIGHT, "finish")[0]


def hour_plan(level_field, tile_weight, tile_rows, tile_columns, live_count, step_hour):
    levs, subs, shards_tm = lax.axis_size("lev"), lax.axis_size("sub"), lax.axis_size("tm")
    half = levs // 2
    divisor = float(level_field.shape[0] * shards_tm // HOURS)
    field = jnp.transpose(level_field, (1, 0, 2))

    def to_peer(x, k, j):
        pairs = [(a * subs + b, (a ^ k) * subs + (b ^ j)) for a in range(levs) for b in range(subs)]
        return lax.ppermute(x, ("lev", "sub"), pairs)

    def hand_over(x):
        pairs = [(a * shards_tm + a // half, a * shards_tm + 1 - a // half) for a in range(levs)]
        return lax.ppermute(x, ("lev", "tm"), pairs)

    def swap(x):
        return lax.ppermute(x, "tm", [(0, 1), (1, 0)])

    plain = [(half, 0), (1, 0), (1, 1), (0, 1), (0, 0)]
    first, second = [(half + 1, j) for j in range(subs)], (half, 1)
    sums, (theirs_0, mine_0, theirs_1, mine_1) = hour_sums(plain, first, second, step_hour, field)
    rows = 2 * field.shape[0]
    folded = theirs_1.shape
    sibling = to_peer(sums[3], *plain[3])
    near_got = [to_peer(x, *peer) for x, peer in list(zip(sums, plain))[1:3]]
    got_0 = swap(theirs_0)
    plain_got = to_peer(sums[0], *plain[0])
    high, low = place_tiles(tile_rows, tile_columns, live_count, tile_weight, theirs_0)

    merged = small_call(
        merge_first_kernel, [mine_0, got_0], [high, sibling], [folded], LIGHT, "merge_first"
    )
    far_same = to_peer(merged[0], *first[0])
    merged = small_call(merge_next_kernel, [mine_0, got_0], merged, [folded], LIGHT, "merge_next")
    far_other = to_peer(merged[0], *first[1])
    theirs_1 = small_call(hold_kernel, [theirs_1], [plain_got, *merged], [folded], LIGHT, "hold")[0]
    got_1 = swap(theirs_1)
    both, send = remap_call(
        remap_both_kernel,
        [sums[4], sibling, plain_got],
        [theirs_1],
        [2 * rows] * 2,
        high,
        low,
        MEDIUM,
        "remap_both",
        [2 * rows] * 2,
    )
    got_both = swap(send)
    merged = small_call(
        merge_last_kernel, [mine_1, got_1], [both, near_got[0]], [folded], HEAVY, "merge_last"
    )
    second_got = to_peer(merged[0], *second)
    far = small_call(far_rows_kernel, [far_same, far_other], [], [(rows, CELLS_DEV)], HEAVY, "far_rows")[0]
    one, send = remap_call(
        remap_near_kernel,
        [*near_got, far],
        [],
        [2 * rows] * 2,
        high,
        low,
        LIGHT,
        "remap_near",
        [2 * rows] * 2,
    )
    got_one = swap(send)
    padded = -(-rows // 32) * 16
    (last,) = remap_call(
        remap_last_kernel,
        [second_got],
        [one],
        [(rows, PIXELS_DEV // 2)],
        high,
        low,
        HEAVY,
        "remap_last",
        [padded],
    )
    got_last = hand_over(last)
    out = finish([both, got_both, one, got_one, last, got_last], rows // 2, divisor)
    return out.reshape(HOURS, out.shape[0] // HOURS, PIXELS_DEV)


def general_plan(level_field, tile_weight, tile_rows, tile_columns, live_count, step_hour):
    steps, levels, cells = level_field.shape
    shards = lax.axis_size("lev") * lax.axis_size("sub")
    divisor = float(steps * lax.axis_size("tm") // HOURS)
    hours = jnp.arange(HOURS, dtype=jnp.int32)
    table = (step_hour[None, :] == hours[:, None]).astype(jnp.float32)
    fields = level_field.reshape(steps, levels, shards, cells // shards)
    partial = jnp.einsum("hs,slgc->ghlc", table, fields, precision=lax.Precision.HIGHEST)
    regrouped = lax.all_to_all(partial, ("lev", "sub"), split_axis=0, concat_axis=0, tiled=True)
    rows = jnp.transpose(regrouped, (1, 0, 2, 3)).reshape(-1, cells // shards)
    high, low = place_tiles(tile_rows, tile_columns, live_count, tile_weight)
    (out,) = remap_call(remap_rows_kernel, [rows], [], [rows.shape[0]], high, low, LIGHT, "remap_rows")
    out = out.reshape(HOURS, shards * levels, PIXELS_DEV) / divisor
    return lax.psum_scatter(out, "tm", scatter_dimension=1, tiled=True)


def solution(mesh):
    sizes = mesh.shape
    paired = sizes["tm"] == HOURS and sizes["lev"] == 4 and sizes["sub"] == 2

    def body(level_field, *others):
        steps, levels, _ = level_field.shape
        suits = paired and steps == 8 and levels % 4 == 0
        return (hour_plan if suits else general_plan)(level_field, *others)

    placed = (
        P(("groups", "tm"), ("lev", "sub"), None),
        P(None, ("lev", "sub")),
        P(("lev", "sub")),
        P(("lev", "sub")),
        P(("lev", "sub")),
        P("tm"),
    )
    return jax.shard_map(
        body,
        mesh=mesh,
        in_specs=placed,
        out_specs=P("groups", "tm", ("lev", "sub")),
        check_vma=False,
    )
```

```python
import functools

import jax
import jax.numpy as jnp
from jax import lax
from jax.experimental import pallas as pl
from jax.experimental.pallas import tpu as pltpu
from jax.sharding import PartitionSpec as P

TILE = 64
HOURS = 2
CT_DEV = 32
PT_DEV = 16
SLOTS = 128
CELLS_DEV = CT_DEV * TILE
PIXELS_DEV = PT_DEV * TILE
LANES = 2 * TILE
MIB = 1 << 20

LIGHT = pl.CostEstimate(flops=1, bytes_accessed=1, transcendentals=0)
MEDIUM = pl.CostEstimate(flops=2_500_000_000, bytes_accessed=1, transcendentals=0)
HEAVY = pl.CostEstimate(flops=10_000_000_000, bytes_accessed=1, transcendentals=0)

NT = (((1,), (1,)), ((), ()))
NN = (((1,), (0,)), ((), ()))


def split(x):
    high = x.astype(jnp.bfloat16)
    return high, (x - high.astype(jnp.float32)).astype(jnp.bfloat16)


def dot(a, b, dims):
    return lax.dot_general(a, b, dims, preferred_element_type=jnp.float32)


GROUP = 8


def place_kernel(rows, columns, count, weights, *refs):
    high, low, total = refs[-3:]
    band = 128

    @pl.loop(0, PIXELS_DEV // band)
    def _(b):
        total[pl.ds(pl.multiple_of(b * band, band), band), :] = jnp.zeros((band, CELLS_DEV), jnp.float32)

    lane_half = lax.broadcasted_iota(jnp.int32, (TILE, LANES), 1) // TILE
    live = count[0]

    @pl.loop(0, (live + GROUP - 1) // GROUP)
    def _(g):
        for pair in range(GROUP // 2):
            lanes = pl.ds(pl.multiple_of((g * (GROUP // 2) + pair) * LANES, LANES), LANES)
            tiles = weights[:, lanes]
            turned = pltpu.roll(tiles, TILE, 1)
            for i in range(2):
                k = g * GROUP + pair * 2 + i
                row, column = rows[k], columns[k]
                side = jnp.where(k < live, column & 1, -1)
                tile = jnp.where(lane_half == i, tiles, turned)
                at = (
                    pl.ds(pl.multiple_of(row * TILE, TILE), TILE),
                    pl.ds(pl.multiple_of((column >> 1) * LANES, LANES), LANES),
                )
                total[at] = total[at] + jnp.where(lane_half == side, tile, 0.0)

    @pl.loop(0, PIXELS_DEV // band)
    def _(b):
        at = pl.ds(pl.multiple_of(b * band, band), band)
        high[at, :], low[at, :] = split(total[at, :])


def place_tiles(rows, columns, count, weights, *after):
    smem = pl.BlockSpec(memory_space=pltpu.SMEM)
    vmem = pl.BlockSpec(memory_space=pltpu.VMEM)
    half = jax.ShapeDtypeStruct((PIXELS_DEV, CELLS_DEV), jnp.bfloat16)
    return pl.pallas_call(
        place_kernel,
        out_shape=(half, half),
        in_specs=[smem, smem, smem, vmem] + [pl.BlockSpec(memory_space=pl.ANY)] * len(after),
        out_specs=(vmem, vmem),
        scratch_shapes=[pltpu.VMEM((PIXELS_DEV, CELLS_DEV), jnp.float32)],
        compiler_params=pltpu.CompilerParams(vmem_limit_bytes=28 * MIB),
        cost_estimate=LIGHT,
        name="place_tiles",
    )(rows, columns, count, weights, *after)


PIXEL_BLOCK = 256


def remap_blocks(x, high, low):
    m = x.shape[0]
    x_high, x_low = split(x)
    both = jnp.concatenate([x_high, x_low], axis=0)
    for start in range(0, PIXELS_DEV, PIXEL_BLOCK):
        at = slice(start, start + PIXEL_BLOCK)
        first = dot(both, high[at, :], NT)
        yield at, first[:m] + first[m:] + dot(x_high, low[at, :], NT)


def remap_call(kernel, inputs, after, out_rows, high, low, cost, name, scratch_rows=()):
    vmem = pl.BlockSpec(memory_space=pltpu.VMEM)
    return pl.pallas_call(
        kernel,
        out_shape=[
            jax.ShapeDtypeStruct(rows if isinstance(rows, tuple) else (rows, PIXELS_DEV), jnp.float32)
            for rows in out_rows
        ],
        in_specs=[vmem] * (len(inputs) + 2) + [pl.BlockSpec(memory_space=pl.ANY)] * len(after),
        out_specs=[vmem] * len(out_rows),
        scratch_shapes=[pltpu.VMEM((rows, PIXELS_DEV), jnp.float32) for rows in scratch_rows],
        compiler_params=pltpu.CompilerParams(vmem_limit_bytes=24 * MIB),
        cost_estimate=cost,
        name=name,
    )(*inputs, high, low, *after)


def remap_rows_kernel(x, high, low, out):
    for at, result in remap_blocks(x[...], high, low):
        out[:, at] = result


def unfold(block):
    levels = block.shape[0] // 2
    return jnp.concatenate([block[:levels], block[levels:]], axis=1)


def far_rows(same_sub, other_sub):
    even = lax.axis_index("sub") == 0
    blocks = [jnp.where(even, same_sub, other_sub), jnp.where(even, other_sub, same_sub)]
    return [unfold(block) for block in blocks]


def keeps_near():
    return lax.axis_index("tm") == lax.axis_index("lev") // 2


def near_rows(same_sub, other_sub):
    even = lax.axis_index("sub") == 0
    return [jnp.where(even, same_sub, other_sub), jnp.where(even, other_sub, same_sub)]


def by_hour(result, levels):
    pieces = [result[start : start + levels] for start in range(0, 2 * HOURS * levels, levels)]
    return jnp.concatenate([pieces[sub * HOURS + hour] for hour in range(HOURS) for sub in range(2)], axis=0)


def sort_out(near_result, far_result, keep, send):
    near = keeps_near()

    @pl.when(near)
    def _():
        keep[...], send[...] = near_result[...], far_result[...]

    @pl.when(jnp.logical_not(near))
    def _():
        keep[...], send[...] = far_result[...], near_result[...]


def remap_both_kernel(own, sibling, plain, high, low, *refs):
    keep, send, near_result, far_result = refs[-4:]
    rows = own.shape[0]
    blocks = near_rows(own[...], sibling[...]) + [plain[...]]
    for at, result in remap_blocks(jnp.concatenate(blocks, axis=0), high, low):
        near_result[:, at] = by_hour(result, rows // HOURS)
        far_result[:rows, at] = result[2 * rows :]
    far_result[rows:] = jnp.zeros((rows, PIXELS_DEV), jnp.float32)
    sort_out(near_result, far_result, keep, send)


def remap_near_kernel(near_same, near_other, far, high, low, *refs):
    keep, send, near_result, far_result = refs[-4:]
    rows = near_same.shape[0]
    blocks = near_rows(near_same[...], near_other[...]) + [far[...]]
    for at, result in remap_blocks(jnp.concatenate(blocks, axis=0), high, low):
        near_result[:, at] = by_hour(result, rows // HOURS)
        far_result[:rows, at] = result[2 * rows :]
    far_result[rows:] = jnp.zeros((rows, PIXELS_DEV), jnp.float32)
    sort_out(near_result, far_result, keep, send)


def remap_last_kernel(block, high, low, *refs):
    out, total = refs[-2:]
    x = unfold(block[...])
    levels, cells = x.shape
    x = jnp.concatenate([x, jnp.zeros((-levels % 16, cells), jnp.float32)], axis=0)
    for at, result in remap_blocks(x, high, low):
        total[:, at] = result
    out[...] = fold(total[:levels])


def hour_weights(step_hour, steps, hours, width):
    row = lax.broadcasted_iota(jnp.int32, (steps, width), 0)
    first = jnp.zeros((steps, width), jnp.float32)
    second = jnp.zeros((steps, width), jnp.float32)
    for step in range(steps):
        first = jnp.where(row == step, jnp.where(step_hour[step] == hours[0], 1.0, 0.0), first)
        second = jnp.where(row == step, jnp.where(step_hour[step] == hours[1], 1.0, 0.0), second)
    upper = row < steps // 2
    return jnp.where(upper, first, second), jnp.where(upper, second, first)


def turn(x, rows):
    return pltpu.roll(x, rows % x.shape[0], 0)


def join(a, b, bit):
    clear = (lax.broadcasted_iota(jnp.int32, a.shape, 0) & bit) == 0
    kept, moved = jnp.where(clear, a, b), jnp.where(clear, b, a)
    return kept + jnp.where(clear, turn(moved, -bit), turn(moved, bit))


def sum_steps(block, weights):
    def halve(x):
        return x * weights[0] + turn(x * weights[1], 4)

    def four(level):
        a, b, c, d = (halve(block(level + i)) for i in range(4))
        return join(join(a, c, 2), join(b, d, 2), 1)

    return four


def pack(pieces):
    upper = lax.broadcasted_iota(jnp.int32, pieces[0][0].shape, 0) < 4
    at_half = [x if half == place % 2 else turn(x, 4) for place, (x, half) in enumerate(pieces)]
    return [jnp.where(upper, a, b) for a, b in zip(at_half[::2], at_half[1::2])]


def peer_shard(k, j):
    subs = lax.axis_size("sub")
    return (lax.axis_index("lev") ^ k) * subs + (lax.axis_index("sub") ^ j)


def field_copies(field, buffer, arrived, peers):
    copies = []
    for place, (k, j) in enumerate(peers):
        start = pl.multiple_of(peer_shard(k, j) * CELLS_DEV, CELLS_DEV)
        copy = pltpu.make_async_copy(
            field.at[:, :, pl.ds(start, CELLS_DEV)], buffer.at[place], arrived.at[place]
        )
        copy.start()
        copies.append(copy)
    return copies


SUM_WIDTH = 512


def sums_kernel(plain, first, second, step_hour, field, *refs):
    *outs, buffer, arrived, hours, hours_arrived = refs
    _, levels, steps, cells = buffer.shape
    rows, cut = HOURS * levels, cells // 2
    copies = field_copies(field, buffer, arrived, [*plain, *first, second])
    fetch = pltpu.make_async_copy(step_hour, hours, hours_arrived)
    fetch.start()
    fetch.wait()
    me = lax.axis_index("tm")
    groups = range(0, levels, 4)

    def summed(place, start, width, weights):
        four = sum_steps(lambda level: buffer[place, level, :, pl.ds(start, width)], weights)
        return [four(level) for level in groups]

    def store(out, offset, start, width, pieces):
        for place, x in enumerate(pack(pieces)):
            out[offset + place * 8 : offset + place * 8 + 8, pl.ds(start, width)] = x

    weights = hour_weights(hours, steps, range(HOURS), SUM_WIDTH)
    for place in range(len(plain)):
        copies[place].wait()

        @pl.loop(0, cells // SUM_WIDTH)
        def _(i):
            start = pl.multiple_of(i * SUM_WIDTH, SUM_WIDTH)
            sums = summed(place, start, SUM_WIDTH, weights)
            pieces = [(x, half) for half in range(HOURS) for x in sums]
            store(outs[place], 0, start, SUM_WIDTH, pieces)

    theirs_first, mine_first, theirs_second, mine_second = outs[len(plain) :]
    width = SUM_WIDTH // 2
    weights = hour_weights(hours, steps, (1 - me, me), width)
    for j in range(len(first) + 1):
        place = len(plain) + j
        copies[place].wait()
        offset = j * rows if j < len(first) else 0
        theirs, mine = (theirs_first, mine_first) if j < len(first) else (theirs_second, mine_second)

        @pl.loop(0, cut // width)
        def _(i):
            start = pl.multiple_of(i * width, width)
            sums = summed(place, start, width, weights) + summed(place, cut + start, width, weights)
            store(theirs, offset, start, width, [(x, 0) for x in sums])
            store(mine, offset, start, width, [(x, 1) for x in sums])


def hour_sums(plain, first, second, step_hour, field):
    levels, steps, _ = field.shape
    rows, cut = HOURS * levels, CELLS_DEV // 2
    vmem = pl.BlockSpec(memory_space=pltpu.VMEM)
    shapes = [(rows, CELLS_DEV)] * len(plain) + [(len(first) * rows, cut)] * 2 + [(rows, cut)] * 2
    count = len(plain) + len(first) + 1
    outs = pl.pallas_call(
        functools.partial(sums_kernel, plain, first, second),
        out_shape=[jax.ShapeDtypeStruct(shape, jnp.float32) for shape in shapes],
        in_specs=[pl.BlockSpec(memory_space=pl.ANY)] * 2,
        out_specs=[vmem] * len(shapes),
        scratch_shapes=[
            pltpu.VMEM((count, levels, steps, CELLS_DEV), jnp.float32),
            pltpu.SemaphoreType.DMA((count,)),
            pltpu.SMEM((steps,), jnp.int32),
            pltpu.SemaphoreType.DMA,
        ],
        compiler_params=pltpu.CompilerParams(vmem_limit_bytes=52 * MIB),
        cost_estimate=LIGHT,
        name="hour_sums",
    )(step_hour, field)
    return outs[: len(plain)], outs[len(plain) :]


def merge_first_kernel(mine, got, *refs):
    rows = refs[-1].shape[0]
    refs[-1][...] = mine[:rows] + got[:rows]


def merge_next_kernel(mine, got, *refs):
    rows = refs[-1].shape[0]
    refs[-1][...] = mine[rows:] + got[rows:]


def merge_last_kernel(mine, got, *refs):
    refs[-1][...] = mine[...] + got[...]


def fold(x):
    half = x.shape[1] // 2
    return jnp.concatenate([x[:, :half], x[:, half:]], axis=0)


def hold_kernel(x, *refs):
    refs[-1][...] = x[...]


def far_rows_kernel(same_sub, other_sub, out):
    out[...] = jnp.concatenate(far_rows(same_sub[...], other_sub[...]), axis=0)


def small_call(kernel, inputs, after, shapes, cost, name):
    vmem = pl.BlockSpec(memory_space=pltpu.VMEM)
    return pl.pallas_call(
        kernel,
        out_shape=[jax.ShapeDtypeStruct(shape, jnp.float32) for shape in shapes],
        in_specs=[vmem] * len(inputs) + [pl.BlockSpec(memory_space=pl.ANY)] * len(after),
        out_specs=[vmem] * len(shapes),
        compiler_params=pltpu.CompilerParams(vmem_limit_bytes=8 * MIB),
        cost_estimate=cost,
        name=name,
    )(*inputs, *after)


def output_rows(same_lev, hour, levels):
    lev = lax.axis_index("lev") % 2
    start = hour * 2 + (lev if same_lev else 1 - lev)
    return pl.ds(pl.multiple_of(start * 2 * levels, 2 * levels), 2 * levels)


def write_first_kernel(divisor, levels, chip, got_chip, one, got_one, out):
    me = lax.axis_index("tm")
    rows = 2 * levels
    near = keeps_near()
    for hour in range(HOURS):
        here = slice(hour * rows, (hour + 1) * rows)

        @pl.when(near)
        def _():
            out[output_rows(True, hour, levels), :] = (chip[here] + got_chip[here]) / divisor
            out[output_rows(False, hour, levels), :] = (one[here] + got_one[here]) / divisor

        @pl.when(jnp.logical_not(near))
        def _():
            out[output_rows(False, hour, levels), :] = jnp.where(me == hour, one[:rows], got_one[:rows]) / divisor


def write_last_kernel(divisor, levels, plain, got_plain, last, got_last, begun, out, stage, written):
    me, even = lax.axis_index("tm"), lax.axis_index("sub") == 0

    @pl.when(jnp.logical_not(keeps_near()))
    def _():
        copies = []
        for hour in range(HOURS):
            here = slice(hour * levels, (hour + 1) * levels)
            first = plain[here] + got_plain[here]
            other = unfold(jnp.where(me == hour, last[...], got_last[...]))
            pair = [jnp.where(even, first, other), jnp.where(even, other, first)]
            stage[hour] = jnp.concatenate(pair, axis=0) / divisor
            target = out.at[output_rows(True, hour, levels), :]
            copies.append(pltpu.make_async_copy(stage.at[hour], target, written.at[hour]))
            copies[-1].start()
        for copy in copies:
            copy.wait()


def write_first(arrays, levels, divisor):
    kernel = functools.partial(write_first_kernel, divisor, levels)
    shape = (2 * arrays[0].shape[0], PIXELS_DEV)
    return small_call(kernel, arrays, [], [shape], LIGHT, "write_first")[0]


def write_last(begun, arrays, levels, divisor):
    vmem, anywhere = pl.BlockSpec(memory_space=pltpu.VMEM), pl.BlockSpec(memory_space=pl.ANY)
    return pl.pallas_call(
        functools.partial(write_last_kernel, divisor, levels),
        out_shape=jax.ShapeDtypeStruct(begun.shape, begun.dtype),
        in_specs=[vmem] * len(arrays) + [anywhere],
        out_specs=anywhere,
        scratch_shapes=[
            pltpu.VMEM((HOURS, 2 * levels, PIXELS_DEV), jnp.float32),
            pltpu.SemaphoreType.DMA((HOURS,)),
        ],
        input_output_aliases={len(arrays): 0},
        compiler_params=pltpu.CompilerParams(vmem_limit_bytes=8 * MIB),
        cost_estimate=LIGHT,
        name="write_last",
    )(*arrays, begun)


def hour_plan(level_field, tile_weight, tile_rows, tile_columns, live_count, step_hour):
    levs, subs, shards_tm = lax.axis_size("lev"), lax.axis_size("sub"), lax.axis_size("tm")
    half = levs // 2
    divisor = float(level_field.shape[0] * shards_tm // HOURS)
    field = jnp.transpose(level_field, (1, 0, 2))

    def to_peer(x, k, j):
        pairs = [(a * subs + b, (a ^ k) * subs + (b ^ j)) for a in range(levs) for b in range(subs)]
        return lax.ppermute(x, ("lev", "sub"), pairs)

    def hand_over(x):
        pairs = [(a * shards_tm + a // half, a * shards_tm + 1 - a // half) for a in range(levs)]
        return lax.ppermute(x, ("lev", "tm"), pairs)

    def swap(x):
        return lax.ppermute(x, "tm", [(0, 1), (1, 0)])

    plain = [(half, 0), (1, 0), (1, 1), (0, 1), (0, 0)]
    first, second = [(half + 1, j) for j in range(subs)], (half, 1)
    sums, (theirs_0, mine_0, theirs_1, mine_1) = hour_sums(plain, first, second, step_hour, field)
    rows = 2 * field.shape[0]
    folded = theirs_1.shape
    sibling = to_peer(sums[3], *plain[3])
    near_got = [to_peer(x, *peer) for x, peer in list(zip(sums, plain))[1:3]]
    got_0 = swap(theirs_0)
    plain_got = to_peer(sums[0], *plain[0])
    high, low = place_tiles(tile_rows, tile_columns, live_count, tile_weight, theirs_0)

    merged = small_call(
        merge_first_kernel, [mine_0, got_0], [high, sibling], [folded], LIGHT, "merge_first"
    )
    far_same = to_peer(merged[0], *first[0])
    merged = small_call(merge_next_kernel, [mine_0, got_0], merged, [folded], LIGHT, "merge_next")
    far_other = to_peer(merged[0], *first[1])
    theirs_1 = small_call(hold_kernel, [theirs_1], [plain_got, *merged], [folded], LIGHT, "hold")[0]
    got_1 = swap(theirs_1)
    both, send = remap_call(
        remap_both_kernel,
        [sums[4], sibling, plain_got],
        [theirs_1],
        [2 * rows] * 2,
        high,
        low,
        MEDIUM,
        "remap_both",
        [2 * rows] * 2,
    )
    got_both = swap(send)
    merged = small_call(
        merge_last_kernel, [mine_1, got_1], [both, near_got[0]], [folded], HEAVY, "merge_last"
    )
    second_got = to_peer(merged[0], *second)
    far = small_call(far_rows_kernel, [far_same, far_other], [], [(rows, CELLS_DEV)], HEAVY, "far_rows")[0]
    one, send = remap_call(
        remap_near_kernel,
        [*near_got, far],
        [],
        [2 * rows] * 2,
        high,
        low,
        LIGHT,
        "remap_near",
        [2 * rows] * 2,
    )
    got_one = swap(send)
    padded = -(-rows // 32) * 16
    (last,) = remap_call(
        remap_last_kernel,
        [second_got],
        [one],
        [(rows, PIXELS_DEV // 2)],
        high,
        low,
        HEAVY,
        "remap_last",
        [padded],
    )
    got_last = hand_over(last)
    levels = rows // 2
    out = write_first([both, got_both, one, got_one], levels, divisor)
    out = write_last(out, [both, got_both, last, got_last], levels, divisor)
    return out.reshape(HOURS, out.shape[0] // HOURS, PIXELS_DEV)


def general_plan(level_field, tile_weight, tile_rows, tile_columns, live_count, step_hour):
    steps, levels, cells = level_field.shape
    shards = lax.axis_size("lev") * lax.axis_size("sub")
    divisor = float(steps * lax.axis_size("tm") // HOURS)
    hours = jnp.arange(HOURS, dtype=jnp.int32)
    table = (step_hour[None, :] == hours[:, None]).astype(jnp.float32)
    fields = level_field.reshape(steps, levels, shards, cells // shards)
    partial = jnp.einsum("hs,slgc->ghlc", table, fields, precision=lax.Precision.HIGHEST)
    regrouped = lax.all_to_all(partial, ("lev", "sub"), split_axis=0, concat_axis=0, tiled=True)
    rows = jnp.transpose(regrouped, (1, 0, 2, 3)).reshape(-1, cells // shards)
    high, low = place_tiles(tile_rows, tile_columns, live_count, tile_weight)
    (out,) = remap_call(remap_rows_kernel, [rows], [], [rows.shape[0]], high, low, LIGHT, "remap_rows")
    out = out.reshape(HOURS, shards * levels, PIXELS_DEV) / divisor
    return lax.psum_scatter(out, "tm", scatter_dimension=1, tiled=True)


def solution(mesh):
    sizes = mesh.shape
    paired = sizes["tm"] == HOURS and sizes["lev"] == 4 and sizes["sub"] == 2

    def body(level_field, *others):
        steps, levels, _ = level_field.shape
        suits = paired and steps == 8 and levels % 4 == 0
        return (hour_plan if suits else general_plan)(level_field, *others)

    placed = (
        P(("groups", "tm"), ("lev", "sub"), None),
        P(None, ("lev", "sub")),
        P(("lev", "sub")),
        P(("lev", "sub")),
        P(("lev", "sub")),
        P("tm"),
    )
    return jax.shard_map(
        body,
        mesh=mesh,
        in_specs=placed,
        out_specs=P("groups", "tm", ("lev", "sub")),
        check_vma=False,
    )
```

```python
import functools

import jax
import jax.numpy as jnp
from jax import lax
from jax.experimental import pallas as pl
from jax.experimental.pallas import tpu as pltpu
from jax.sharding import PartitionSpec as P

TILE = 64
HOURS = 2
CT_DEV = 32
PT_DEV = 16
SLOTS = 128
CELLS_DEV = CT_DEV * TILE
PIXELS_DEV = PT_DEV * TILE
LANES = 2 * TILE
MIB = 1 << 20

LIGHT = pl.CostEstimate(flops=1, bytes_accessed=1, transcendentals=0)
MEDIUM = pl.CostEstimate(flops=2_500_000_000, bytes_accessed=1, transcendentals=0)
HEAVY = pl.CostEstimate(flops=10_000_000_000, bytes_accessed=1, transcendentals=0)

NT = (((1,), (1,)), ((), ()))
NN = (((1,), (0,)), ((), ()))


def split(x):
    high = x.astype(jnp.bfloat16)
    return high, (x - high.astype(jnp.float32)).astype(jnp.bfloat16)


def dot(a, b, dims):
    return lax.dot_general(a, b, dims, preferred_element_type=jnp.float32)


GROUP = 8


def place_kernel(rows, columns, count, weights, *refs):
    high, low, total = refs[-3:]
    band = 128

    @pl.loop(0, PIXELS_DEV // band)
    def _(b):
        total[pl.ds(pl.multiple_of(b * band, band), band), :] = jnp.zeros((band, CELLS_DEV), jnp.float32)

    lane_half = lax.broadcasted_iota(jnp.int32, (TILE, LANES), 1) // TILE
    live = count[0]

    @pl.loop(0, (live + GROUP - 1) // GROUP)
    def _(g):
        for pair in range(GROUP // 2):
            lanes = pl.ds(pl.multiple_of((g * (GROUP // 2) + pair) * LANES, LANES), LANES)
            tiles = weights[:, lanes]
            turned = pltpu.roll(tiles, TILE, 1)
            for i in range(2):
                k = g * GROUP + pair * 2 + i
                row, column = rows[k], columns[k]
                side = jnp.where(k < live, column & 1, -1)
                tile = jnp.where(lane_half == i, tiles, turned)
                at = (
                    pl.ds(pl.multiple_of(row * TILE, TILE), TILE),
                    pl.ds(pl.multiple_of((column >> 1) * LANES, LANES), LANES),
                )
                total[at] = total[at] + jnp.where(lane_half == side, tile, 0.0)

    @pl.loop(0, PIXELS_DEV // band)
    def _(b):
        at = pl.ds(pl.multiple_of(b * band, band), band)
        high[at, :], low[at, :] = split(total[at, :])


def place_tiles(rows, columns, count, weights, *after):
    smem = pl.BlockSpec(memory_space=pltpu.SMEM)
    vmem = pl.BlockSpec(memory_space=pltpu.VMEM)
    half = jax.ShapeDtypeStruct((PIXELS_DEV, CELLS_DEV), jnp.bfloat16)
    return pl.pallas_call(
        place_kernel,
        out_shape=(half, half),
        in_specs=[smem, smem, smem, vmem] + [pl.BlockSpec(memory_space=pl.ANY)] * len(after),
        out_specs=(vmem, vmem),
        scratch_shapes=[pltpu.VMEM((PIXELS_DEV, CELLS_DEV), jnp.float32)],
        compiler_params=pltpu.CompilerParams(vmem_limit_bytes=28 * MIB),
        cost_estimate=LIGHT,
        name="place_tiles",
    )(rows, columns, count, weights, *after)


PIXEL_BLOCK = 256


def remap_blocks(x, high, low, cells=slice(None)):
    m = x.shape[0]
    x_high, x_low = split(x)
    both = jnp.concatenate([x_high, x_low], axis=0)
    for start in range(0, PIXELS_DEV, PIXEL_BLOCK):
        at = slice(start, start + PIXEL_BLOCK)
        first = dot(both, high[at, cells], NT)
        yield at, first[:m] + first[m:] + dot(x_high, low[at, cells], NT)


def remap_call(kernel, inputs, after, out_rows, high, low, cost, name, scratch_rows=()):
    vmem = pl.BlockSpec(memory_space=pltpu.VMEM)
    return pl.pallas_call(
        kernel,
        out_shape=[
            jax.ShapeDtypeStruct(rows if isinstance(rows, tuple) else (rows, PIXELS_DEV), jnp.float32)
            for rows in out_rows
        ],
        in_specs=[vmem] * (len(inputs) + 2) + [pl.BlockSpec(memory_space=pl.ANY)] * len(after),
        out_specs=[vmem] * len(out_rows),
        scratch_shapes=[pltpu.VMEM((rows, PIXELS_DEV), jnp.float32) for rows in scratch_rows],
        compiler_params=pltpu.CompilerParams(vmem_limit_bytes=24 * MIB),
        cost_estimate=cost,
        name=name,
    )(*inputs, high, low, *after)


def remap_rows_kernel(x, high, low, out):
    for at, result in remap_blocks(x[...], high, low):
        out[:, at] = result


def unfold(block):
    levels = block.shape[0] // 2
    return jnp.concatenate([block[:levels], block[levels:]], axis=1)


def far_rows(same_sub, other_sub):
    even = lax.axis_index("sub") == 0
    blocks = [jnp.where(even, same_sub, other_sub), jnp.where(even, other_sub, same_sub)]
    return [unfold(block) for block in blocks]


def keeps_near():
    return lax.axis_index("tm") == lax.axis_index("lev") // 2


def near_rows(same_sub, other_sub):
    even = lax.axis_index("sub") == 0
    return [jnp.where(even, same_sub, other_sub), jnp.where(even, other_sub, same_sub)]


def by_hour(result, levels):
    pieces = [result[start : start + levels] for start in range(0, 2 * HOURS * levels, levels)]
    return jnp.concatenate([pieces[sub * HOURS + hour] for hour in range(HOURS) for sub in range(2)], axis=0)


def sort_out(near_result, far_result, keep, send):
    near = keeps_near()

    @pl.when(near)
    def _():
        keep[...], send[...] = near_result[...], far_result[...]

    @pl.when(jnp.logical_not(near))
    def _():
        keep[...], send[...] = far_result[...], near_result[...]


def remap_both_kernel(own, sibling, plain, high, low, *refs):
    keep, send, near_result, far_result = refs[-4:]
    rows = own.shape[0]
    blocks = near_rows(own[...], sibling[...]) + [plain[...]]
    for at, result in remap_blocks(jnp.concatenate(blocks, axis=0), high, low):
        near_result[:, at] = by_hour(result, rows // HOURS)
        far_result[:rows, at] = result[2 * rows :]
    far_result[rows:] = jnp.zeros((rows, PIXELS_DEV), jnp.float32)
    sort_out(near_result, far_result, keep, send)


def remap_near_kernel(near_same, near_other, far, high, low, *refs):
    keep, send, near_result, far_result = refs[-4:]
    rows = near_same.shape[0]
    blocks = near_rows(near_same[...], near_other[...]) + [far[...]]
    for at, result in remap_blocks(jnp.concatenate(blocks, axis=0), high, low):
        near_result[:, at] = by_hour(result, rows // HOURS)
        far_result[:rows, at] = result[2 * rows :]
    far_result[rows:] = jnp.zeros((rows, PIXELS_DEV), jnp.float32)
    sort_out(near_result, far_result, keep, send)


def remap_half(place, block, high, low):
    x = unfold(block[...])
    levels, cells = x.shape
    x = jnp.concatenate([x, jnp.zeros((-levels % 16, cells), jnp.float32)], axis=0)
    yield from remap_blocks(x, high, low, slice(place * cells, (place + 1) * cells))


def remap_early_kernel(block, high, low, *refs):
    for at, result in remap_half(0, block, high, low):
        refs[-1][:, at] = result


def remap_last_kernel(block, early, high, low, *refs):
    out, total = refs[-2:]
    for at, result in remap_half(1, block, high, low):
        total[:, at] = result + early[:, at]
    out[...] = fold(total[: out.shape[0] // 2])


def hour_weights(step_hour, steps, hours, width):
    row = lax.broadcasted_iota(jnp.int32, (steps, width), 0)
    first = jnp.zeros((steps, width), jnp.float32)
    second = jnp.zeros((steps, width), jnp.float32)
    for step in range(steps):
        first = jnp.where(row == step, jnp.where(step_hour[step] == hours[0], 1.0, 0.0), first)
        second = jnp.where(row == step, jnp.where(step_hour[step] == hours[1], 1.0, 0.0), second)
    upper = row < steps // 2
    return jnp.where(upper, first, second), jnp.where(upper, second, first)


def turn(x, rows):
    return pltpu.roll(x, rows % x.shape[0], 0)


def join(a, b, bit):
    clear = (lax.broadcasted_iota(jnp.int32, a.shape, 0) & bit) == 0
    kept, moved = jnp.where(clear, a, b), jnp.where(clear, b, a)
    return kept + jnp.where(clear, turn(moved, -bit), turn(moved, bit))


def sum_steps(block, weights):
    def halve(x):
        return x * weights[0] + turn(x * weights[1], 4)

    def four(level):
        a, b, c, d = (halve(block(level + i)) for i in range(4))
        return join(join(a, c, 2), join(b, d, 2), 1)

    return four


def pack(pieces):
    upper = lax.broadcasted_iota(jnp.int32, pieces[0][0].shape, 0) < 4
    at_half = [x if half == place % 2 else turn(x, 4) for place, (x, half) in enumerate(pieces)]
    return [jnp.where(upper, a, b) for a, b in zip(at_half[::2], at_half[1::2])]


def peer_shard(k, j):
    subs = lax.axis_size("sub")
    return (lax.axis_index("lev") ^ k) * subs + (lax.axis_index("sub") ^ j)


def field_copies(field, buffer, arrived, peers):
    copies = []
    for place, (k, j) in enumerate(peers):
        start = pl.multiple_of(peer_shard(k, j) * CELLS_DEV, CELLS_DEV)
        copy = pltpu.make_async_copy(
            field.at[:, :, pl.ds(start, CELLS_DEV)], buffer.at[place], arrived.at[place]
        )
        copy.start()
        copies.append(copy)
    return copies


SUM_WIDTH = 512


def sums_kernel(plain, first, second, step_hour, field, *refs):
    *outs, buffer, arrived, hours, hours_arrived = refs
    _, levels, steps, cells = buffer.shape
    rows, cut = HOURS * levels, cells // 2
    copies = field_copies(field, buffer, arrived, [*plain, *first, second])
    fetch = pltpu.make_async_copy(step_hour, hours, hours_arrived)
    fetch.start()
    fetch.wait()
    me = lax.axis_index("tm")
    groups = range(0, levels, 4)

    def summed(place, start, width, weights):
        four = sum_steps(lambda level: buffer[place, level, :, pl.ds(start, width)], weights)
        return [four(level) for level in groups]

    def store(out, offset, start, width, pieces):
        for place, x in enumerate(pack(pieces)):
            out[offset + place * 8 : offset + place * 8 + 8, pl.ds(start, width)] = x

    weights = hour_weights(hours, steps, range(HOURS), SUM_WIDTH)
    for place in range(len(plain)):
        copies[place].wait()

        @pl.loop(0, cells // SUM_WIDTH)
        def _(i):
            start = pl.multiple_of(i * SUM_WIDTH, SUM_WIDTH)
            sums = summed(place, start, SUM_WIDTH, weights)
            pieces = [(x, half) for half in range(HOURS) for x in sums]
            store(outs[place], 0, start, SUM_WIDTH, pieces)

    theirs_first, mine_first, theirs_second, mine_second = outs[len(plain) :]
    width = SUM_WIDTH // 2
    weights = hour_weights(hours, steps, (1 - me, me), width)
    for j in range(len(first) + 1):
        place = len(plain) + j
        copies[place].wait()
        offset = j * rows if j < len(first) else 0
        theirs, mine = (theirs_first, mine_first) if j < len(first) else (theirs_second, mine_second)

        @pl.loop(0, cut // width)
        def _(i):
            start = pl.multiple_of(i * width, width)
            sums = summed(place, start, width, weights) + summed(place, cut + start, width, weights)
            store(theirs, offset, start, width, [(x, 0) for x in sums])
            store(mine, offset, start, width, [(x, 1) for x in sums])


def hour_sums(plain, first, second, step_hour, field):
    levels, steps, _ = field.shape
    rows, cut = HOURS * levels, CELLS_DEV // 2
    vmem = pl.BlockSpec(memory_space=pltpu.VMEM)
    shapes = [(rows, CELLS_DEV)] * len(plain) + [(len(first) * rows, cut)] * 2 + [(rows, cut)] * 2
    count = len(plain) + len(first) + 1
    outs = pl.pallas_call(
        functools.partial(sums_kernel, plain, first, second),
        out_shape=[jax.ShapeDtypeStruct(shape, jnp.float32) for shape in shapes],
        in_specs=[pl.BlockSpec(memory_space=pl.ANY)] * 2,
        out_specs=[vmem] * len(shapes),
        scratch_shapes=[
            pltpu.VMEM((count, levels, steps, CELLS_DEV), jnp.float32),
            pltpu.SemaphoreType.DMA((count,)),
            pltpu.SMEM((steps,), jnp.int32),
            pltpu.SemaphoreType.DMA,
        ],
        compiler_params=pltpu.CompilerParams(vmem_limit_bytes=52 * MIB),
        cost_estimate=LIGHT,
        name="hour_sums",
    )(step_hour, field)
    return outs[: len(plain)], outs[len(plain) :]


def merge_first_kernel(mine, got, *refs):
    rows = refs[-1].shape[0]
    refs[-1][...] = mine[:rows] + got[:rows]


def merge_next_kernel(mine, got, *refs):
    rows = refs[-1].shape[0]
    refs[-1][...] = mine[rows:] + got[rows:]


def fold(x):
    half = x.shape[1] // 2
    return jnp.concatenate([x[:, :half], x[:, half:]], axis=0)


def merge_last_kernel(mine, got, *refs):
    outs = refs[-2:]
    levels = mine.shape[0] // 2
    total = mine[...] + got[...]
    for place, out in enumerate(outs):
        out[...] = fold(total[place * levels : (place + 1) * levels])


def hold_kernel(x, *refs):
    refs[-1][...] = x[...]


def far_rows_kernel(same_sub, other_sub, out):
    out[...] = jnp.concatenate(far_rows(same_sub[...], other_sub[...]), axis=0)


def small_call(kernel, inputs, after, shapes, cost, name):
    vmem = pl.BlockSpec(memory_space=pltpu.VMEM)
    return pl.pallas_call(
        kernel,
        out_shape=[jax.ShapeDtypeStruct(shape, jnp.float32) for shape in shapes],
        in_specs=[vmem] * len(inputs) + [pl.BlockSpec(memory_space=pl.ANY)] * len(after),
        out_specs=[vmem] * len(shapes),
        compiler_params=pltpu.CompilerParams(vmem_limit_bytes=8 * MIB),
        cost_estimate=cost,
        name=name,
    )(*inputs, *after)


def output_rows(same_lev, hour, levels):
    lev = lax.axis_index("lev") % 2
    start = hour * 2 + (lev if same_lev else 1 - lev)
    return pl.ds(pl.multiple_of(start * 2 * levels, 2 * levels), 2 * levels)


def write_first_kernel(divisor, levels, chip, got_chip, one, got_one, out):
    me = lax.axis_index("tm")
    rows = 2 * levels
    near = keeps_near()
    for hour in range(HOURS):
        here = slice(hour * rows, (hour + 1) * rows)

        @pl.when(near)
        def _():
            out[output_rows(True, hour, levels), :] = (chip[here] + got_chip[here]) / divisor
            out[output_rows(False, hour, levels), :] = (one[here] + got_one[here]) / divisor

        @pl.when(jnp.logical_not(near))
        def _():
            out[output_rows(False, hour, levels), :] = jnp.where(me == hour, one[:rows], got_one[:rows]) / divisor


def write_last_kernel(divisor, levels, plain, got_plain, last, got_last, begun, out, stage, written):
    me, even = lax.axis_index("tm"), lax.axis_index("sub") == 0

    @pl.when(jnp.logical_not(keeps_near()))
    def _():
        copies = []
        for hour in range(HOURS):
            here = slice(hour * levels, (hour + 1) * levels)
            first = plain[here] + got_plain[here]
            other = unfold(jnp.where(me == hour, last[...], got_last[...]))
            pair = [jnp.where(even, first, other), jnp.where(even, other, first)]
            stage[hour] = jnp.concatenate(pair, axis=0) / divisor
            target = out.at[output_rows(True, hour, levels), :]
            copies.append(pltpu.make_async_copy(stage.at[hour], target, written.at[hour]))
            copies[-1].start()
        for copy in copies:
            copy.wait()


def write_first(arrays, levels, divisor):
    kernel = functools.partial(write_first_kernel, divisor, levels)
    shape = (2 * arrays[0].shape[0], PIXELS_DEV)
    return small_call(kernel, arrays, [], [shape], LIGHT, "write_first")[0]


def write_last(begun, arrays, levels, divisor):
    vmem, anywhere = pl.BlockSpec(memory_space=pltpu.VMEM), pl.BlockSpec(memory_space=pl.ANY)
    return pl.pallas_call(
        functools.partial(write_last_kernel, divisor, levels),
        out_shape=jax.ShapeDtypeStruct(begun.shape, begun.dtype),
        in_specs=[vmem] * len(arrays) + [anywhere],
        out_specs=anywhere,
        scratch_shapes=[
            pltpu.VMEM((HOURS, 2 * levels, PIXELS_DEV), jnp.float32),
            pltpu.SemaphoreType.DMA((HOURS,)),
        ],
        input_output_aliases={len(arrays): 0},
        compiler_params=pltpu.CompilerParams(vmem_limit_bytes=8 * MIB),
        cost_estimate=LIGHT,
        name="write_last",
    )(*arrays, begun)


def hour_plan(level_field, tile_weight, tile_rows, tile_columns, live_count, step_hour):
    levs, subs, shards_tm = lax.axis_size("lev"), lax.axis_size("sub"), lax.axis_size("tm")
    half = levs // 2
    divisor = float(level_field.shape[0] * shards_tm // HOURS)
    field = jnp.transpose(level_field, (1, 0, 2))

    def to_peer(x, k, j):
        pairs = [(a * subs + b, (a ^ k) * subs + (b ^ j)) for a in range(levs) for b in range(subs)]
        return lax.ppermute(x, ("lev", "sub"), pairs)

    def hand_over(x):
        pairs = [(a * shards_tm + a // half, a * shards_tm + 1 - a // half) for a in range(levs)]
        return lax.ppermute(x, ("lev", "tm"), pairs)

    def swap(x):
        return lax.ppermute(x, "tm", [(0, 1), (1, 0)])

    plain = [(half, 0), (1, 0), (1, 1), (0, 1), (0, 0)]
    first, second = [(half + 1, j) for j in range(subs)], (half, 1)
    sums, (theirs_0, mine_0, theirs_1, mine_1) = hour_sums(plain, first, second, step_hour, field)
    rows = 2 * field.shape[0]
    folded = theirs_1.shape
    sibling = to_peer(sums[3], *plain[3])
    near_got = [to_peer(x, *peer) for x, peer in list(zip(sums, plain))[1:3]]
    got_0 = swap(theirs_0)
    plain_got = to_peer(sums[0], *plain[0])
    high, low = place_tiles(tile_rows, tile_columns, live_count, tile_weight, theirs_0)

    merged = small_call(
        merge_first_kernel, [mine_0, got_0], [high, sibling], [folded], LIGHT, "merge_first"
    )
    far_same = to_peer(merged[0], *first[0])
    merged = small_call(merge_next_kernel, [mine_0, got_0], merged, [folded], LIGHT, "merge_next")
    far_other = to_peer(merged[0], *first[1])
    theirs_1 = small_call(hold_kernel, [theirs_1], [plain_got, *merged], [folded], LIGHT, "hold")[0]
    got_1 = swap(theirs_1)
    both, send = remap_call(
        remap_both_kernel,
        [sums[4], sibling, plain_got],
        [theirs_1],
        [2 * rows] * 2,
        high,
        low,
        MEDIUM,
        "remap_both",
        [2 * rows] * 2,
    )
    got_both = swap(send)
    quarter = (folded[0], folded[1] // 2)
    merged = small_call(
        merge_last_kernel, [mine_1, got_1], [both, *near_got], [quarter] * 2, HEAVY, "merge_last"
    )
    late = small_call(hold_kernel, [merged[1]], [merged[0]], [quarter], LIGHT, "hold")
    second_got = [to_peer(x, *second) for x in (merged[0], late[0])]
    far = small_call(far_rows_kernel, [far_same, far_other], [], [(rows, CELLS_DEV)], HEAVY, "far_rows")[0]
    one, send = remap_call(
        remap_near_kernel,
        [*near_got, far],
        [],
        [2 * rows] * 2,
        high,
        low,
        LIGHT,
        "remap_near",
        [2 * rows] * 2,
    )
    got_one = swap(send)
    padded = -(-rows // 32) * 16
    (early,) = remap_call(
        remap_early_kernel, second_got[:1], [one, got_both], [padded], high, low, LIGHT, "remap_early"
    )
    (last,) = remap_call(
        remap_last_kernel,
        [second_got[1], early],
        [],
        [(rows, PIXELS_DEV // 2)],
        high,
        low,
        HEAVY,
        "remap_last",
        [padded],
    )
    got_last = hand_over(last)
    levels = rows // 2
    out = write_first([both, got_both, one, got_one], levels, divisor)
    out = write_last(out, [both, got_both, last, got_last], levels, divisor)
    return out.reshape(HOURS, out.shape[0] // HOURS, PIXELS_DEV)


def general_plan(level_field, tile_weight, tile_rows, tile_columns, live_count, step_hour):
    steps, levels, cells = level_field.shape
    shards = lax.axis_size("lev") * lax.axis_size("sub")
    divisor = float(steps * lax.axis_size("tm") // HOURS)
    hours = jnp.arange(HOURS, dtype=jnp.int32)
    table = (step_hour[None, :] == hours[:, None]).astype(jnp.float32)
    fields = level_field.reshape(steps, levels, shards, cells // shards)
    partial = jnp.einsum("hs,slgc->ghlc", table, fields, precision=lax.Precision.HIGHEST)
    regrouped = lax.all_to_all(partial, ("lev", "sub"), split_axis=0, concat_axis=0, tiled=True)
    rows = jnp.transpose(regrouped, (1, 0, 2, 3)).reshape(-1, cells // shards)
    high, low = place_tiles(tile_rows, tile_columns, live_count, tile_weight)
    (out,) = remap_call(remap_rows_kernel, [rows], [], [rows.shape[0]], high, low, LIGHT, "remap_rows")
    out = out.reshape(HOURS, shards * levels, PIXELS_DEV) / divisor
    return lax.psum_scatter(out, "tm", scatter_dimension=1, tiled=True)


def solution(mesh):
    sizes = mesh.shape
    paired = sizes["tm"] == HOURS and sizes["lev"] == 4 and sizes["sub"] == 2

    def body(level_field, *others):
        steps, levels, _ = level_field.shape
        suits = paired and steps == 8 and levels % 4 == 0
        return (hour_plan if suits else general_plan)(level_field, *others)

    placed = (
        P(("groups", "tm"), ("lev", "sub"), None),
        P(None, ("lev", "sub")),
        P(("lev", "sub")),
        P(("lev", "sub")),
        P(("lev", "sub")),
        P("tm"),
    )
    return jax.shard_map(
        body,
        mesh=mesh,
        in_specs=placed,
        out_specs=P("groups", "tm", ("lev", "sub")),
        check_vma=False,
    )
```

```python
import functools

import jax
import jax.numpy as jnp
from jax import lax
from jax.experimental import pallas as pl
from jax.experimental.pallas import tpu as pltpu
from jax.sharding import PartitionSpec as P

TILE = 64
HOURS = 2
CT_DEV = 32
PT_DEV = 16
SLOTS = 128
CELLS_DEV = CT_DEV * TILE
PIXELS_DEV = PT_DEV * TILE
LANES = 2 * TILE
MIB = 1 << 20

LIGHT = pl.CostEstimate(flops=1, bytes_accessed=1, transcendentals=0)
MEDIUM = pl.CostEstimate(flops=2_500_000_000, bytes_accessed=1, transcendentals=0)
HEAVY = pl.CostEstimate(flops=10_000_000_000, bytes_accessed=1, transcendentals=0)

NT = (((1,), (1,)), ((), ()))
NN = (((1,), (0,)), ((), ()))


def split(x):
    high = x.astype(jnp.bfloat16)
    return high, (x - high.astype(jnp.float32)).astype(jnp.bfloat16)


def dot(a, b, dims):
    return lax.dot_general(a, b, dims, preferred_element_type=jnp.float32)


GROUP = 8


def place_kernel(rows, columns, count, weights, *refs):
    high, low, total = refs[-3:]
    band = 128

    @pl.loop(0, PIXELS_DEV // band)
    def _(b):
        total[pl.ds(pl.multiple_of(b * band, band), band), :] = jnp.zeros((band, CELLS_DEV), jnp.float32)

    lane_half = lax.broadcasted_iota(jnp.int32, (TILE, LANES), 1) // TILE
    live = count[0]

    @pl.loop(0, (live + GROUP - 1) // GROUP)
    def _(g):
        for pair in range(GROUP // 2):
            lanes = pl.ds(pl.multiple_of((g * (GROUP // 2) + pair) * LANES, LANES), LANES)
            tiles = weights[:, lanes]
            turned = pltpu.roll(tiles, TILE, 1)
            for i in range(2):
                k = g * GROUP + pair * 2 + i
                row, column = rows[k], columns[k]
                side = jnp.where(k < live, column & 1, -1)
                tile = jnp.where(lane_half == i, tiles, turned)
                at = (
                    pl.ds(pl.multiple_of(row * TILE, TILE), TILE),
                    pl.ds(pl.multiple_of((column >> 1) * LANES, LANES), LANES),
                )
                total[at] = total[at] + jnp.where(lane_half == side, tile, 0.0)

    @pl.loop(0, PIXELS_DEV // band)
    def _(b):
        at = pl.ds(pl.multiple_of(b * band, band), band)
        high[at, :], low[at, :] = split(total[at, :])


def place_tiles(rows, columns, count, weights, *after):
    smem = pl.BlockSpec(memory_space=pltpu.SMEM)
    vmem = pl.BlockSpec(memory_space=pltpu.VMEM)
    half = jax.ShapeDtypeStruct((PIXELS_DEV, CELLS_DEV), jnp.bfloat16)
    return pl.pallas_call(
        place_kernel,
        out_shape=(half, half),
        in_specs=[smem, smem, smem, vmem] + [pl.BlockSpec(memory_space=pl.ANY)] * len(after),
        out_specs=(vmem, vmem),
        scratch_shapes=[pltpu.VMEM((PIXELS_DEV, CELLS_DEV), jnp.float32)],
        compiler_params=pltpu.CompilerParams(vmem_limit_bytes=28 * MIB),
        cost_estimate=LIGHT,
        name="place_tiles",
    )(rows, columns, count, weights, *after)


PIXEL_BLOCK = 256


def remap_blocks(x, high, low):
    m = x.shape[0]
    x_high, x_low = split(x)
    both = jnp.concatenate([x_high, x_low], axis=0)
    for start in range(0, PIXELS_DEV, PIXEL_BLOCK):
        at = slice(start, start + PIXEL_BLOCK)
        first = dot(both, high[at, :], NT)
        yield at, first[:m] + first[m:] + dot(x_high, low[at, :], NT)


def remap_call(kernel, inputs, after, out_rows, high, low, cost, name, scratch_rows=()):
    vmem = pl.BlockSpec(memory_space=pltpu.VMEM)
    return pl.pallas_call(
        kernel,
        out_shape=[
            jax.ShapeDtypeStruct(rows if isinstance(rows, tuple) else (rows, PIXELS_DEV), jnp.float32)
            for rows in out_rows
        ],
        in_specs=[vmem] * (len(inputs) + 2) + [pl.BlockSpec(memory_space=pl.ANY)] * len(after),
        out_specs=[vmem] * len(out_rows),
        scratch_shapes=[pltpu.VMEM((rows, PIXELS_DEV), jnp.float32) for rows in scratch_rows],
        compiler_params=pltpu.CompilerParams(vmem_limit_bytes=24 * MIB),
        cost_estimate=cost,
        name=name,
    )(*inputs, high, low, *after)


def remap_rows_kernel(x, high, low, out):
    for at, result in remap_blocks(x[...], high, low):
        out[:, at] = result


def unfold(block):
    levels = block.shape[0] // 2
    return jnp.concatenate([block[:levels], block[levels:]], axis=1)


def far_rows(same_sub, other_sub):
    even = lax.axis_index("sub") == 0
    blocks = [jnp.where(even, same_sub, other_sub), jnp.where(even, other_sub, same_sub)]
    return [unfold(block) for block in blocks]


def keeps_near():
    return lax.axis_index("tm") == lax.axis_index("lev") // 2


def near_rows(same_sub, other_sub):
    even = lax.axis_index("sub") == 0
    return [jnp.where(even, same_sub, other_sub), jnp.where(even, other_sub, same_sub)]


def by_hour(result, levels):
    pieces = [result[start : start + levels] for start in range(0, 2 * HOURS * levels, levels)]
    return jnp.concatenate([pieces[sub * HOURS + hour] for hour in range(HOURS) for sub in range(2)], axis=0)


def sort_out(near_result, far_result, keep, send):
    near = keeps_near()

    @pl.when(near)
    def _():
        keep[...], send[...] = near_result[...], far_result[...]

    @pl.when(jnp.logical_not(near))
    def _():
        keep[...], send[...] = far_result[...], near_result[...]


def remap_both_kernel(own, sibling, plain, high, low, *refs):
    keep, send, near_result, far_result = refs[-4:]
    rows = own.shape[0]
    blocks = near_rows(own[...], sibling[...]) + [plain[...]]
    for at, result in remap_blocks(jnp.concatenate(blocks, axis=0), high, low):
        near_result[:, at] = by_hour(result, rows // HOURS)
        far_result[:rows, at] = result[2 * rows :]
    far_result[rows:] = jnp.zeros((rows, PIXELS_DEV), jnp.float32)
    sort_out(near_result, far_result, keep, send)


def remap_near_kernel(near_same, near_other, high, low, *refs):
    rows = near_same.shape[0]
    x = jnp.concatenate(near_rows(near_same[...], near_other[...]), axis=0)
    for at, result in remap_blocks(x, high, low):
        refs[-1][:, at] = by_hour(result, rows // HOURS)


def remap_far_kernel(same, other, high, low, *refs):
    x = jnp.concatenate(far_rows(same[...], other[...]), axis=0)
    for at, result in remap_blocks(x, high, low):
        refs[-1][:, at] = result


def remap_last_kernel(block, high, low, *refs):
    out, total = refs[-2:]
    x = unfold(block[...])
    levels, cells = x.shape
    x = jnp.concatenate([x, jnp.zeros((-levels % 16, cells), jnp.float32)], axis=0)
    for at, result in remap_blocks(x, high, low):
        total[:, at] = result
    out[...] = fold(total[:levels])


def hour_weights(step_hour, steps, hours, width):
    row = lax.broadcasted_iota(jnp.int32, (steps, width), 0)
    first = jnp.zeros((steps, width), jnp.float32)
    second = jnp.zeros((steps, width), jnp.float32)
    for step in range(steps):
        first = jnp.where(row == step, jnp.where(step_hour[step] == hours[0], 1.0, 0.0), first)
        second = jnp.where(row == step, jnp.where(step_hour[step] == hours[1], 1.0, 0.0), second)
    upper = row < steps // 2
    return jnp.where(upper, first, second), jnp.where(upper, second, first)


def turn(x, rows):
    return pltpu.roll(x, rows % x.shape[0], 0)


def join(a, b, bit):
    clear = (lax.broadcasted_iota(jnp.int32, a.shape, 0) & bit) == 0
    kept, moved = jnp.where(clear, a, b), jnp.where(clear, b, a)
    return kept + jnp.where(clear, turn(moved, -bit), turn(moved, bit))


def sum_steps(block, weights):
    def halve(x):
        return x * weights[0] + turn(x * weights[1], 4)

    def four(level):
        a, b, c, d = (halve(block(level + i)) for i in range(4))
        return join(join(a, c, 2), join(b, d, 2), 1)

    return four


def pack(pieces):
    upper = lax.broadcasted_iota(jnp.int32, pieces[0][0].shape, 0) < 4
    at_half = [x if half == place % 2 else turn(x, 4) for place, (x, half) in enumerate(pieces)]
    return [jnp.where(upper, a, b) for a, b in zip(at_half[::2], at_half[1::2])]


def peer_shard(k, j):
    subs = lax.axis_size("sub")
    return (lax.axis_index("lev") ^ k) * subs + (lax.axis_index("sub") ^ j)


def field_copies(field, buffer, arrived, peers):
    copies = []
    for place, (k, j) in enumerate(peers):
        start = pl.multiple_of(peer_shard(k, j) * CELLS_DEV, CELLS_DEV)
        copy = pltpu.make_async_copy(
            field.at[:, :, pl.ds(start, CELLS_DEV)], buffer.at[place], arrived.at[place]
        )
        copy.start()
        copies.append(copy)
    return copies


SUM_WIDTH = 512


def sums_kernel(plain, first, second, step_hour, field, *refs):
    *outs, buffer, arrived, hours, hours_arrived = refs
    _, levels, steps, cells = buffer.shape
    rows, cut = HOURS * levels, cells // 2
    copies = field_copies(field, buffer, arrived, [*plain, *first, second])
    fetch = pltpu.make_async_copy(step_hour, hours, hours_arrived)
    fetch.start()
    fetch.wait()
    me = lax.axis_index("tm")
    groups = range(0, levels, 4)

    def summed(place, start, width, weights):
        four = sum_steps(lambda level: buffer[place, level, :, pl.ds(start, width)], weights)
        return [four(level) for level in groups]

    def store(out, offset, start, width, pieces):
        for place, x in enumerate(pack(pieces)):
            out[offset + place * 8 : offset + place * 8 + 8, pl.ds(start, width)] = x

    weights = hour_weights(hours, steps, range(HOURS), SUM_WIDTH)
    for place in range(len(plain)):
        copies[place].wait()

        @pl.loop(0, cells // SUM_WIDTH)
        def _(i):
            start = pl.multiple_of(i * SUM_WIDTH, SUM_WIDTH)
            sums = summed(place, start, SUM_WIDTH, weights)
            pieces = [(x, half) for half in range(HOURS) for x in sums]
            store(outs[place], 0, start, SUM_WIDTH, pieces)

    theirs_first, mine_first, theirs_second, mine_second = outs[len(plain) :]
    width = SUM_WIDTH // 2
    weights = hour_weights(hours, steps, (1 - me, me), width)
    for j in range(len(first) + 1):
        place = len(plain) + j
        copies[place].wait()
        offset = j * rows if j < len(first) else 0
        theirs, mine = (theirs_first, mine_first) if j < len(first) else (theirs_second, mine_second)

        @pl.loop(0, cut // width)
        def _(i):
            start = pl.multiple_of(i * width, width)
            sums = summed(place, start, width, weights) + summed(place, cut + start, width, weights)
            store(theirs, offset, start, width, [(x, 0) for x in sums])
            store(mine, offset, start, width, [(x, 1) for x in sums])


def hour_sums(plain, first, second, step_hour, field):
    levels, steps, _ = field.shape
    rows, cut = HOURS * levels, CELLS_DEV // 2
    vmem = pl.BlockSpec(memory_space=pltpu.VMEM)
    shapes = [(rows, CELLS_DEV)] * len(plain) + [(len(first) * rows, cut)] * 2 + [(rows, cut)] * 2
    count = len(plain) + len(first) + 1
    outs = pl.pallas_call(
        functools.partial(sums_kernel, plain, first, second),
        out_shape=[jax.ShapeDtypeStruct(shape, jnp.float32) for shape in shapes],
        in_specs=[pl.BlockSpec(memory_space=pl.ANY)] * 2,
        out_specs=[vmem] * len(shapes),
        scratch_shapes=[
            pltpu.VMEM((count, levels, steps, CELLS_DEV), jnp.float32),
            pltpu.SemaphoreType.DMA((count,)),
            pltpu.SMEM((steps,), jnp.int32),
            pltpu.SemaphoreType.DMA,
        ],
        compiler_params=pltpu.CompilerParams(vmem_limit_bytes=52 * MIB),
        cost_estimate=LIGHT,
        name="hour_sums",
    )(step_hour, field)
    return outs[: len(plain)], outs[len(plain) :]


def merge_first_kernel(mine, got, *refs):
    rows = refs[-1].shape[0]
    refs[-1][...] = mine[:rows] + got[:rows]


def merge_next_kernel(mine, got, *refs):
    rows = refs[-1].shape[0]
    refs[-1][...] = mine[rows:] + got[rows:]


def merge_last_kernel(mine, got, *refs):
    refs[-1][...] = mine[...] + got[...]


def fold(x):
    half = x.shape[1] // 2
    return jnp.concatenate([x[:, :half], x[:, half:]], axis=0)


def hold_kernel(x, *refs):
    refs[-1][...] = x[...]


def small_call(kernel, inputs, after, shapes, cost, name):
    vmem = pl.BlockSpec(memory_space=pltpu.VMEM)
    return pl.pallas_call(
        kernel,
        out_shape=[jax.ShapeDtypeStruct(shape, jnp.float32) for shape in shapes],
        in_specs=[vmem] * len(inputs) + [pl.BlockSpec(memory_space=pl.ANY)] * len(after),
        out_specs=[vmem] * len(shapes),
        compiler_params=pltpu.CompilerParams(vmem_limit_bytes=8 * MIB),
        cost_estimate=cost,
        name=name,
    )(*inputs, *after)


def output_rows(same_lev, hour, levels):
    lev = lax.axis_index("lev") % 2
    start = hour * 2 + (lev if same_lev else 1 - lev)
    return pl.ds(pl.multiple_of(start * 2 * levels, 2 * levels), 2 * levels)


def write_first_kernel(divisor, levels, chip, got_chip, lev_near, got_near, far, got_far, out):
    me = lax.axis_index("tm")
    rows = 2 * levels
    near = keeps_near()
    for hour in range(HOURS):
        here = slice(hour * rows, (hour + 1) * rows)

        @pl.when(near)
        def _():
            out[output_rows(True, hour, levels), :] = (chip[here] + got_chip[here]) / divisor
            out[output_rows(False, hour, levels), :] = (lev_near[here] + got_near[here]) / divisor

        @pl.when(jnp.logical_not(near))
        def _():
            out[output_rows(False, hour, levels), :] = jnp.where(me == hour, far[...], got_far[...]) / divisor


def write_last_kernel(divisor, levels, plain, got_plain, last, got_last, begun, out, stage, written):
    me, even = lax.axis_index("tm"), lax.axis_index("sub") == 0

    @pl.when(jnp.logical_not(keeps_near()))
    def _():
        copies = []
        for hour in range(HOURS):
            here = slice(hour * levels, (hour + 1) * levels)
            first = plain[here] + got_plain[here]
            other = unfold(jnp.where(me == hour, last[...], got_last[...]))
            pair = [jnp.where(even, first, other), jnp.where(even, other, first)]
            stage[hour] = jnp.concatenate(pair, axis=0) / divisor
            target = out.at[output_rows(True, hour, levels), :]
            copies.append(pltpu.make_async_copy(stage.at[hour], target, written.at[hour]))
            copies[-1].start()
        for copy in copies:
            copy.wait()


def write_first(arrays, levels, divisor):
    kernel = functools.partial(write_first_kernel, divisor, levels)
    shape = (2 * arrays[0].shape[0], PIXELS_DEV)
    return small_call(kernel, arrays, [], [shape], LIGHT, "write_first")[0]


def write_last(begun, arrays, levels, divisor):
    vmem, anywhere = pl.BlockSpec(memory_space=pltpu.VMEM), pl.BlockSpec(memory_space=pl.ANY)
    return pl.pallas_call(
        functools.partial(write_last_kernel, divisor, levels),
        out_shape=jax.ShapeDtypeStruct(begun.shape, begun.dtype),
        in_specs=[vmem] * len(arrays) + [anywhere],
        out_specs=anywhere,
        scratch_shapes=[
            pltpu.VMEM((HOURS, 2 * levels, PIXELS_DEV), jnp.float32),
            pltpu.SemaphoreType.DMA((HOURS,)),
        ],
        input_output_aliases={len(arrays): 0},
        compiler_params=pltpu.CompilerParams(vmem_limit_bytes=8 * MIB),
        cost_estimate=LIGHT,
        name="write_last",
    )(*arrays, begun)


def hour_plan(level_field, tile_weight, tile_rows, tile_columns, live_count, step_hour):
    levs, subs, shards_tm = lax.axis_size("lev"), lax.axis_size("sub"), lax.axis_size("tm")
    half = levs // 2
    divisor = float(level_field.shape[0] * shards_tm // HOURS)
    field = jnp.transpose(level_field, (1, 0, 2))

    def to_peer(x, k, j):
        pairs = [(a * subs + b, (a ^ k) * subs + (b ^ j)) for a in range(levs) for b in range(subs)]
        return lax.ppermute(x, ("lev", "sub"), pairs)

    def hand_over(x):
        pairs = [(a * shards_tm + a // half, a * shards_tm + 1 - a // half) for a in range(levs)]
        return lax.ppermute(x, ("lev", "tm"), pairs)

    def swap(x):
        return lax.ppermute(x, "tm", [(0, 1), (1, 0)])

    plain = [(half, 0), (1, 0), (1, 1), (0, 1), (0, 0)]
    first, second = [(half + 1, j) for j in range(subs)], (half, 1)
    sums, (theirs_0, mine_0, theirs_1, mine_1) = hour_sums(plain, first, second, step_hour, field)
    rows = 2 * field.shape[0]
    folded = theirs_1.shape
    sibling = to_peer(sums[3], *plain[3])
    near_got = [to_peer(x, *peer) for x, peer in list(zip(sums, plain))[1:3]]
    got_0 = swap(theirs_0)
    plain_got = to_peer(sums[0], *plain[0])
    high, low = place_tiles(tile_rows, tile_columns, live_count, tile_weight, theirs_0)

    merged = small_call(
        merge_first_kernel, [mine_0, got_0], [high, sibling], [folded], LIGHT, "merge_first"
    )
    far_same = to_peer(merged[0], *first[0])
    merged = small_call(merge_next_kernel, [mine_0, got_0], merged, [folded], LIGHT, "merge_next")
    far_other = to_peer(merged[0], *first[1])
    theirs_1 = small_call(hold_kernel, [theirs_1], [plain_got, *merged], [folded], LIGHT, "hold")[0]
    got_1 = swap(theirs_1)
    both, send = remap_call(
        remap_both_kernel,
        [sums[4], sibling, plain_got],
        [theirs_1],
        [2 * rows] * 2,
        high,
        low,
        MEDIUM,
        "remap_both",
        [2 * rows] * 2,
    )
    got_both = swap(send)
    merged = small_call(
        merge_last_kernel, [mine_1, got_1], [both, near_got[0]], [folded], HEAVY, "merge_last"
    )
    second_got = to_peer(merged[0], *second)
    (near,) = remap_call(
        remap_near_kernel, near_got, merged, [2 * rows], high, low, LIGHT, "remap_near"
    )
    got_near = swap(near)
    (far,) = remap_call(remap_far_kernel, [far_same, far_other], [near], [rows], high, low, HEAVY, "remap_far")
    got_far = swap(far)
    padded = -(-rows // 32) * 16
    (last,) = remap_call(
        remap_last_kernel,
        [second_got],
        [far],
        [(rows, PIXELS_DEV // 2)],
        high,
        low,
        HEAVY,
        "remap_last",
        [padded],
    )
    got_last = hand_over(last)
    levels = rows // 2
    out = write_first([both, got_both, near, got_near, far, got_far], levels, divisor)
    out = write_last(out, [both, got_both, last, got_last], levels, divisor)
    return out.reshape(HOURS, out.shape[0] // HOURS, PIXELS_DEV)


def general_plan(level_field, tile_weight, tile_rows, tile_columns, live_count, step_hour):
    steps, levels, cells = level_field.shape
    shards = lax.axis_size("lev") * lax.axis_size("sub")
    divisor = float(steps * lax.axis_size("tm") // HOURS)
    hours = jnp.arange(HOURS, dtype=jnp.int32)
    table = (step_hour[None, :] == hours[:, None]).astype(jnp.float32)
    fields = level_field.reshape(steps, levels, shards, cells // shards)
    partial = jnp.einsum("hs,slgc->ghlc", table, fields, precision=lax.Precision.HIGHEST)
    regrouped = lax.all_to_all(partial, ("lev", "sub"), split_axis=0, concat_axis=0, tiled=True)
    rows = jnp.transpose(regrouped, (1, 0, 2, 3)).reshape(-1, cells // shards)
    high, low = place_tiles(tile_rows, tile_columns, live_count, tile_weight)
    (out,) = remap_call(remap_rows_kernel, [rows], [], [rows.shape[0]], high, low, LIGHT, "remap_rows")
    out = out.reshape(HOURS, shards * levels, PIXELS_DEV) / divisor
    return lax.psum_scatter(out, "tm", scatter_dimension=1, tiled=True)


def solution(mesh):
    sizes = mesh.shape
    paired = sizes["tm"] == HOURS and sizes["lev"] == 4 and sizes["sub"] == 2

    def body(level_field, *others):
        steps, levels, _ = level_field.shape
        suits = paired and steps == 8 and levels % 4 == 0
        return (hour_plan if suits else general_plan)(level_field, *others)

    placed = (
        P(("groups", "tm"), ("lev", "sub"), None),
        P(None, ("lev", "sub")),
        P(("lev", "sub")),
        P(("lev", "sub")),
        P(("lev", "sub")),
        P("tm"),
    )
    return jax.shard_map(
        body,
        mesh=mesh,
        in_specs=placed,
        out_specs=P("groups", "tm", ("lev", "sub")),
        check_vma=False,
    )
```

```python
import functools

import jax
import jax.numpy as jnp
from jax import lax
from jax.experimental import pallas as pl
from jax.experimental.pallas import tpu as pltpu
from jax.sharding import PartitionSpec as P

TILE = 64
HOURS = 2
CT_DEV = 32
PT_DEV = 16
SLOTS = 128
CELLS_DEV = CT_DEV * TILE
PIXELS_DEV = PT_DEV * TILE
LANES = 2 * TILE
MIB = 1 << 20

LIGHT = pl.CostEstimate(flops=1, bytes_accessed=1, transcendentals=0)
MEDIUM = pl.CostEstimate(flops=2_500_000_000, bytes_accessed=1, transcendentals=0)
HEAVY = pl.CostEstimate(flops=10_000_000_000, bytes_accessed=1, transcendentals=0)

NT = (((1,), (1,)), ((), ()))
NN = (((1,), (0,)), ((), ()))


def split(x):
    high = x.astype(jnp.bfloat16)
    return high, (x - high.astype(jnp.float32)).astype(jnp.bfloat16)


def dot(a, b, dims):
    return lax.dot_general(a, b, dims, preferred_element_type=jnp.float32)


GROUP = 8


def place_kernel(rows, columns, count, weights, *refs):
    high, low, total = refs[-3:]
    band = 128

    @pl.loop(0, PIXELS_DEV // band)
    def _(b):
        total[pl.ds(pl.multiple_of(b * band, band), band), :] = jnp.zeros((band, CELLS_DEV), jnp.float32)

    lane_half = lax.broadcasted_iota(jnp.int32, (TILE, LANES), 1) // TILE
    live = count[0]

    @pl.loop(0, (live + GROUP - 1) // GROUP)
    def _(g):
        for pair in range(GROUP // 2):
            lanes = pl.ds(pl.multiple_of((g * (GROUP // 2) + pair) * LANES, LANES), LANES)
            tiles = weights[:, lanes]
            turned = pltpu.roll(tiles, TILE, 1)
            for i in range(2):
                k = g * GROUP + pair * 2 + i
                row, column = rows[k], columns[k]
                side = jnp.where(k < live, column & 1, -1)
                tile = jnp.where(lane_half == i, tiles, turned)
                at = (
                    pl.ds(pl.multiple_of(row * TILE, TILE), TILE),
                    pl.ds(pl.multiple_of((column >> 1) * LANES, LANES), LANES),
                )
                total[at] = total[at] + jnp.where(lane_half == side, tile, 0.0)

    @pl.loop(0, PIXELS_DEV // band)
    def _(b):
        at = pl.ds(pl.multiple_of(b * band, band), band)
        high[at, :], low[at, :] = split(total[at, :])


def place_tiles(rows, columns, count, weights, *after):
    smem = pl.BlockSpec(memory_space=pltpu.SMEM)
    vmem = pl.BlockSpec(memory_space=pltpu.VMEM)
    half = jax.ShapeDtypeStruct((PIXELS_DEV, CELLS_DEV), jnp.bfloat16)
    return pl.pallas_call(
        place_kernel,
        out_shape=(half, half),
        in_specs=[smem, smem, smem, vmem] + [pl.BlockSpec(memory_space=pl.ANY)] * len(after),
        out_specs=(vmem, vmem),
        scratch_shapes=[pltpu.VMEM((PIXELS_DEV, CELLS_DEV), jnp.float32)],
        compiler_params=pltpu.CompilerParams(vmem_limit_bytes=28 * MIB),
        cost_estimate=LIGHT,
        name="place_tiles",
    )(rows, columns, count, weights, *after)


PIXEL_BLOCK = 256


def remap_blocks(x, high, low):
    m = x.shape[0]
    x_high, x_low = split(x)
    both = jnp.concatenate([x_high, x_low], axis=0)
    for start in range(0, PIXELS_DEV, PIXEL_BLOCK):
        at = slice(start, start + PIXEL_BLOCK)
        first = dot(both, high[at, :], NT)
        yield at, first[:m] + first[m:] + dot(x_high, low[at, :], NT)


def remap_call(kernel, inputs, after, out_rows, high, low, cost, name, scratch_rows=()):
    vmem = pl.BlockSpec(memory_space=pltpu.VMEM)
    return pl.pallas_call(
        kernel,
        out_shape=[
            jax.ShapeDtypeStruct(rows if isinstance(rows, tuple) else (rows, PIXELS_DEV), jnp.float32)
            for rows in out_rows
        ],
        in_specs=[vmem] * (len(inputs) + 2) + [pl.BlockSpec(memory_space=pl.ANY)] * len(after),
        out_specs=[vmem] * len(out_rows),
        scratch_shapes=[pltpu.VMEM((rows, PIXELS_DEV), jnp.float32) for rows in scratch_rows],
        compiler_params=pltpu.CompilerParams(vmem_limit_bytes=24 * MIB),
        cost_estimate=cost,
        name=name,
    )(*inputs, high, low, *after)


def remap_rows_kernel(x, high, low, out):
    for at, result in remap_blocks(x[...], high, low):
        out[:, at] = result


def unfold(block):
    levels = block.shape[0] // 2
    return jnp.concatenate([block[:levels], block[levels:]], axis=1)


def far_rows(same_sub, other_sub):
    even = lax.axis_index("sub") == 0
    blocks = [jnp.where(even, same_sub, other_sub), jnp.where(even, other_sub, same_sub)]
    return [unfold(block) for block in blocks]


def keeps_near():
    return lax.axis_index("tm") == lax.axis_index("lev") // 2


def near_rows(same_sub, other_sub):
    even = lax.axis_index("sub") == 0
    return [jnp.where(even, same_sub, other_sub), jnp.where(even, other_sub, same_sub)]


def by_hour(result, levels):
    pieces = [result[start : start + levels] for start in range(0, 2 * HOURS * levels, levels)]
    return jnp.concatenate([pieces[sub * HOURS + hour] for hour in range(HOURS) for sub in range(2)], axis=0)


def sort_out(near_result, far_result, keep, send):
    near = keeps_near()

    @pl.when(near)
    def _():
        keep[...], send[...] = near_result[...], far_result[...]

    @pl.when(jnp.logical_not(near))
    def _():
        keep[...], send[...] = far_result[...], near_result[...]


def remap_both_kernel(own, sibling, plain, high, low, *refs):
    keep, send, near_result, far_result = refs[-4:]
    rows = own.shape[0]
    blocks = near_rows(own[...], sibling[...]) + [plain[...]]
    for at, result in remap_blocks(jnp.concatenate(blocks, axis=0), high, low):
        near_result[:, at] = by_hour(result, rows // HOURS)
        far_result[:rows, at] = result[2 * rows :]
    far_result[rows:] = jnp.zeros((rows, PIXELS_DEV), jnp.float32)
    sort_out(near_result, far_result, keep, send)


def remap_near_kernel(near_same, near_other, high, low, *refs):
    rows = near_same.shape[0]
    x = jnp.concatenate(near_rows(near_same[...], near_other[...]), axis=0)
    for at, result in remap_blocks(x, high, low):
        refs[-1][:, at] = by_hour(result, rows // HOURS)


def remap_far_kernel(same, other, high, low, *refs):
    x = jnp.concatenate(far_rows(same[...], other[...]), axis=0)
    for at, result in remap_blocks(x, high, low):
        refs[-1][:, at] = result


def remap_last_kernel(block, high, low, *refs):
    out, total = refs[-2:]
    x = unfold(block[...])
    levels, cells = x.shape
    x = jnp.concatenate([x, jnp.zeros((-levels % 16, cells), jnp.float32)], axis=0)
    for at, result in remap_blocks(x, high, low):
        total[:, at] = result
    out[...] = fold(total[:levels])


def hour_weights(step_hour, steps, hours, width):
    row = lax.broadcasted_iota(jnp.int32, (steps, width), 0)
    first = jnp.zeros((steps, width), jnp.float32)
    second = jnp.zeros((steps, width), jnp.float32)
    for step in range(steps):
        first = jnp.where(row == step, jnp.where(step_hour[step] == hours[0], 1.0, 0.0), first)
        second = jnp.where(row == step, jnp.where(step_hour[step] == hours[1], 1.0, 0.0), second)
    upper = row < steps // 2
    return jnp.where(upper, first, second), jnp.where(upper, second, first)


def turn(x, rows):
    return pltpu.roll(x, rows % x.shape[0], 0)


def join(a, b, bit):
    clear = (lax.broadcasted_iota(jnp.int32, a.shape, 0) & bit) == 0
    kept, moved = jnp.where(clear, a, b), jnp.where(clear, b, a)
    return kept + jnp.where(clear, turn(moved, -bit), turn(moved, bit))


def sum_steps(block, weights):
    def halve(x):
        return x * weights[0] + turn(x * weights[1], 4)

    def four(level):
        a, b, c, d = (halve(block(level + i)) for i in range(4))
        return join(join(a, c, 2), join(b, d, 2), 1)

    return four


def pack(pieces):
    upper = lax.broadcasted_iota(jnp.int32, pieces[0][0].shape, 0) < 4
    at_half = [x if half == place % 2 else turn(x, 4) for place, (x, half) in enumerate(pieces)]
    return [jnp.where(upper, a, b) for a, b in zip(at_half[::2], at_half[1::2])]


def peer_shard(k, j):
    subs = lax.axis_size("sub")
    return (lax.axis_index("lev") ^ k) * subs + (lax.axis_index("sub") ^ j)


def field_copies(field, buffer, arrived, peers):
    copies = []
    for place, (k, j) in enumerate(peers):
        start = pl.multiple_of(peer_shard(k, j) * CELLS_DEV, CELLS_DEV)
        copy = pltpu.make_async_copy(
            field.at[:, :, pl.ds(start, CELLS_DEV)], buffer.at[place], arrived.at[place]
        )
        copy.start()
        copies.append(copy)
    return copies


SUM_WIDTH = 512


def sums_kernel(plain, first, second, step_hour, field, *refs):
    *outs, buffer, arrived, hours, hours_arrived = refs
    _, levels, steps, cells = buffer.shape
    rows, cut = HOURS * levels, cells // 2
    copies = field_copies(field, buffer, arrived, [*plain, *first, second])
    fetch = pltpu.make_async_copy(step_hour, hours, hours_arrived)
    fetch.start()
    fetch.wait()
    me = lax.axis_index("tm")
    groups = range(0, levels, 4)

    def summed(place, start, width, weights):
        four = sum_steps(lambda level: buffer[place, level, :, pl.ds(start, width)], weights)
        return [four(level) for level in groups]

    def store(out, offset, start, width, pieces):
        for place, x in enumerate(pack(pieces)):
            out[offset + place * 8 : offset + place * 8 + 8, pl.ds(start, width)] = x

    weights = hour_weights(hours, steps, range(HOURS), SUM_WIDTH)
    for place in range(len(plain)):
        copies[place].wait()

        @pl.loop(0, cells // SUM_WIDTH)
        def _(i):
            start = pl.multiple_of(i * SUM_WIDTH, SUM_WIDTH)
            sums = summed(place, start, SUM_WIDTH, weights)
            pieces = [(x, half) for half in range(HOURS) for x in sums]
            store(outs[place], 0, start, SUM_WIDTH, pieces)

    theirs_first, mine_first, theirs_second, mine_second = outs[len(plain) :]
    width = SUM_WIDTH // 2
    weights = hour_weights(hours, steps, (1 - me, me), width)
    for j in range(len(first) + 1):
        place = len(plain) + j
        copies[place].wait()
        offset = j * rows if j < len(first) else 0
        theirs, mine = (theirs_first, mine_first) if j < len(first) else (theirs_second, mine_second)

        @pl.loop(0, cut // width)
        def _(i):
            start = pl.multiple_of(i * width, width)
            sums = summed(place, start, width, weights) + summed(place, cut + start, width, weights)
            store(theirs, offset, start, width, [(x, 0) for x in sums])
            store(mine, offset, start, width, [(x, 1) for x in sums])


def hour_sums(plain, first, second, step_hour, field):
    levels, steps, _ = field.shape
    rows, cut = HOURS * levels, CELLS_DEV // 2
    vmem = pl.BlockSpec(memory_space=pltpu.VMEM)
    shapes = [(rows, CELLS_DEV)] * len(plain) + [(len(first) * rows, cut)] * 2 + [(rows, cut)] * 2
    count = len(plain) + len(first) + 1
    outs = pl.pallas_call(
        functools.partial(sums_kernel, plain, first, second),
        out_shape=[jax.ShapeDtypeStruct(shape, jnp.float32) for shape in shapes],
        in_specs=[pl.BlockSpec(memory_space=pl.ANY)] * 2,
        out_specs=[vmem] * len(shapes),
        scratch_shapes=[
            pltpu.VMEM((count, levels, steps, CELLS_DEV), jnp.float32),
            pltpu.SemaphoreType.DMA((count,)),
            pltpu.SMEM((steps,), jnp.int32),
            pltpu.SemaphoreType.DMA,
        ],
        compiler_params=pltpu.CompilerParams(vmem_limit_bytes=52 * MIB),
        cost_estimate=LIGHT,
        name="hour_sums",
    )(step_hour, field)
    return outs[: len(plain)], outs[len(plain) :]


def merge_first_kernel(mine, got, *refs):
    rows = refs[-1].shape[0]
    refs[-1][...] = mine[:rows] + got[:rows]


def merge_next_kernel(mine, got, *refs):
    rows = refs[-1].shape[0]
    refs[-1][...] = mine[rows:] + got[rows:]


def merge_last_kernel(mine, got, *refs):
    refs[-1][...] = mine[...] + got[...]


def fold(x):
    half = x.shape[1] // 2
    return jnp.concatenate([x[:, :half], x[:, half:]], axis=0)


def hold_kernel(x, *refs):
    refs[-1][...] = x[...]


def small_call(kernel, inputs, after, shapes, cost, name):
    vmem = pl.BlockSpec(memory_space=pltpu.VMEM)
    return pl.pallas_call(
        kernel,
        out_shape=[jax.ShapeDtypeStruct(shape, jnp.float32) for shape in shapes],
        in_specs=[vmem] * len(inputs) + [pl.BlockSpec(memory_space=pl.ANY)] * len(after),
        out_specs=[vmem] * len(shapes),
        compiler_params=pltpu.CompilerParams(vmem_limit_bytes=8 * MIB),
        cost_estimate=cost,
        name=name,
    )(*inputs, *after)


def output_rows(same_lev, hour, levels):
    lev = lax.axis_index("lev") % 2
    start = hour * 2 + (lev if same_lev else 1 - lev)
    return pl.ds(pl.multiple_of(start * 2 * levels, 2 * levels), 2 * levels)


def write_first_kernel(divisor, levels, chip, got_chip, lev_near, got_near, far, got_far, out):
    me = lax.axis_index("tm")
    rows = 2 * levels
    near = keeps_near()
    for hour in range(HOURS):
        here = slice(hour * rows, (hour + 1) * rows)

        @pl.when(near)
        def _():
            out[output_rows(True, hour, levels), :] = (chip[here] + got_chip[here]) / divisor
            out[output_rows(False, hour, levels), :] = (lev_near[here] + got_near[here]) / divisor

        @pl.when(jnp.logical_not(near))
        def _():
            out[output_rows(False, hour, levels), :] = jnp.where(me == hour, far[...], got_far[...]) / divisor


def write_last_kernel(divisor, levels, plain, got_plain, last, got_last, begun, out, stage, written):
    me, even = lax.axis_index("tm"), lax.axis_index("sub") == 0

    @pl.when(jnp.logical_not(keeps_near()))
    def _():
        copies = []
        for hour in range(HOURS):
            here = slice(hour * levels, (hour + 1) * levels)
            first = plain[here] + got_plain[here]
            other = unfold(jnp.where(me == hour, last[...], got_last[...]))
            pair = [jnp.where(even, first, other), jnp.where(even, other, first)]
            stage[hour] = jnp.concatenate(pair, axis=0) / divisor
            target = out.at[output_rows(True, hour, levels), :]
            copies.append(pltpu.make_async_copy(stage.at[hour], target, written.at[hour]))
            copies[-1].start()
        for copy in copies:
            copy.wait()


def write_first(arrays, levels, divisor):
    kernel = functools.partial(write_first_kernel, divisor, levels)
    shape = (2 * arrays[0].shape[0], PIXELS_DEV)
    return small_call(kernel, arrays, [], [shape], LIGHT, "write_first")[0]


def write_last(begun, arrays, levels, divisor):
    vmem, anywhere = pl.BlockSpec(memory_space=pltpu.VMEM), pl.BlockSpec(memory_space=pl.ANY)
    return pl.pallas_call(
        functools.partial(write_last_kernel, divisor, levels),
        out_shape=jax.ShapeDtypeStruct(begun.shape, begun.dtype),
        in_specs=[vmem] * len(arrays) + [anywhere],
        out_specs=anywhere,
        scratch_shapes=[
            pltpu.VMEM((HOURS, 2 * levels, PIXELS_DEV), jnp.float32),
            pltpu.SemaphoreType.DMA((HOURS,)),
        ],
        input_output_aliases={len(arrays): 0},
        compiler_params=pltpu.CompilerParams(vmem_limit_bytes=8 * MIB),
        cost_estimate=LIGHT,
        name="write_last",
    )(*arrays, begun)


def hour_plan(level_field, tile_weight, tile_rows, tile_columns, live_count, step_hour):
    levs, subs, shards_tm = lax.axis_size("lev"), lax.axis_size("sub"), lax.axis_size("tm")
    half = levs // 2
    divisor = float(level_field.shape[0] * shards_tm // HOURS)
    field = jnp.transpose(level_field, (1, 0, 2))

    def to_peer(x, k, j):
        pairs = [(a * subs + b, (a ^ k) * subs + (b ^ j)) for a in range(levs) for b in range(subs)]
        return lax.ppermute(x, ("lev", "sub"), pairs)

    def swap(x):
        return lax.ppermute(x, "tm", [(0, 1), (1, 0)])

    plain = [(half, 0), (1, 0), (1, 1), (0, 1), (0, 0)]
    first, second = [(half + 1, j) for j in range(subs)], (half, 1)
    sums, (theirs_0, mine_0, theirs_1, mine_1) = hour_sums(plain, first, second, step_hour, field)
    rows = 2 * field.shape[0]
    folded = theirs_1.shape
    sibling = to_peer(sums[3], *plain[3])
    near_got = [to_peer(x, *peer) for x, peer in list(zip(sums, plain))[1:3]]
    got_0 = swap(theirs_0)
    plain_got = to_peer(sums[0], *plain[0])
    high, low = place_tiles(tile_rows, tile_columns, live_count, tile_weight, theirs_0)

    merged = small_call(
        merge_first_kernel, [mine_0, got_0], [high, sibling], [folded], LIGHT, "merge_first"
    )
    far_same = to_peer(merged[0], *first[0])
    merged = small_call(merge_next_kernel, [mine_0, got_0], merged, [folded], LIGHT, "merge_next")
    far_other = to_peer(merged[0], *first[1])
    theirs_1 = small_call(hold_kernel, [theirs_1], [plain_got, *merged], [folded], LIGHT, "hold")[0]
    got_1 = swap(theirs_1)
    both, send = remap_call(
        remap_both_kernel,
        [sums[4], sibling, plain_got],
        [theirs_1],
        [2 * rows] * 2,
        high,
        low,
        MEDIUM,
        "remap_both",
        [2 * rows] * 2,
    )
    got_both = swap(send)
    merged = small_call(
        merge_last_kernel, [mine_1, got_1], [both, near_got[0]], [folded], HEAVY, "merge_last"
    )
    second_got = to_peer(merged[0], *second)
    (near,) = remap_call(
        remap_near_kernel, near_got, merged, [2 * rows], high, low, LIGHT, "remap_near"
    )
    got_near = swap(near)
    (far,) = remap_call(remap_far_kernel, [far_same, far_other], [near], [rows], high, low, HEAVY, "remap_far")
    got_far = swap(far)
    padded = -(-rows // 32) * 16
    (last,) = remap_call(
        remap_last_kernel,
        [second_got],
        [far],
        [(rows, PIXELS_DEV // 2)],
        high,
        low,
        HEAVY,
        "remap_last",
        [padded],
    )
    got_last = swap(last)
    levels = rows // 2
    out = write_first([both, got_both, near, got_near, far, got_far], levels, divisor)
    out = write_last(out, [both, got_both, last, got_last], levels, divisor)
    return out.reshape(HOURS, out.shape[0] // HOURS, PIXELS_DEV)


def general_plan(level_field, tile_weight, tile_rows, tile_columns, live_count, step_hour):
    steps, levels, cells = level_field.shape
    shards = lax.axis_size("lev") * lax.axis_size("sub")
    divisor = float(steps * lax.axis_size("tm") // HOURS)
    hours = jnp.arange(HOURS, dtype=jnp.int32)
    table = (step_hour[None, :] == hours[:, None]).astype(jnp.float32)
    fields = level_field.reshape(steps, levels, shards, cells // shards)
    partial = jnp.einsum("hs,slgc->ghlc", table, fields, precision=lax.Precision.HIGHEST)
    regrouped = lax.all_to_all(partial, ("lev", "sub"), split_axis=0, concat_axis=0, tiled=True)
    rows = jnp.transpose(regrouped, (1, 0, 2, 3)).reshape(-1, cells // shards)
    high, low = place_tiles(tile_rows, tile_columns, live_count, tile_weight)
    (out,) = remap_call(remap_rows_kernel, [rows], [], [rows.shape[0]], high, low, LIGHT, "remap_rows")
    out = out.reshape(HOURS, shards * levels, PIXELS_DEV) / divisor
    return lax.psum_scatter(out, "tm", scatter_dimension=1, tiled=True)


def solution(mesh):
    sizes = mesh.shape
    paired = sizes["tm"] == HOURS and sizes["lev"] == 4 and sizes["sub"] == 2

    def body(level_field, *others):
        steps, levels, _ = level_field.shape
        suits = paired and steps == 8 and levels % 4 == 0
        return (hour_plan if suits else general_plan)(level_field, *others)

    placed = (
        P(("groups", "tm"), ("lev", "sub"), None),
        P(None, ("lev", "sub")),
        P(("lev", "sub")),
        P(("lev", "sub")),
        P(("lev", "sub")),
        P("tm"),
    )
    return jax.shard_map(
        body,
        mesh=mesh,
        in_specs=placed,
        out_specs=P("groups", "tm", ("lev", "sub")),
        check_vma=False,
    )
```

```python
import functools

import jax
import jax.numpy as jnp
from jax import lax
from jax.experimental import pallas as pl
from jax.experimental.pallas import tpu as pltpu
from jax.sharding import PartitionSpec as P

TILE = 64
HOURS = 2
CT_DEV = 32
PT_DEV = 16
SLOTS = 128
CELLS_DEV = CT_DEV * TILE
PIXELS_DEV = PT_DEV * TILE
LANES = 2 * TILE
MIB = 1 << 20

LIGHT = pl.CostEstimate(flops=1, bytes_accessed=1, transcendentals=0)
MEDIUM = pl.CostEstimate(flops=2_500_000_000, bytes_accessed=1, transcendentals=0)
HEAVY = pl.CostEstimate(flops=10_000_000_000, bytes_accessed=1, transcendentals=0)

NT = (((1,), (1,)), ((), ()))
NN = (((1,), (0,)), ((), ()))


def split(x):
    high = x.astype(jnp.bfloat16)
    return high, (x - high.astype(jnp.float32)).astype(jnp.bfloat16)


def dot(a, b, dims):
    return lax.dot_general(a, b, dims, preferred_element_type=jnp.float32)


GROUP = 8


def place_kernel(rows, columns, count, weights, *refs):
    high, low, total = refs[-3:]
    band = 128

    @pl.loop(0, PIXELS_DEV // band)
    def _(b):
        total[pl.ds(pl.multiple_of(b * band, band), band), :] = jnp.zeros((band, CELLS_DEV), jnp.float32)

    lane_half = lax.broadcasted_iota(jnp.int32, (TILE, LANES), 1) // TILE
    live = count[0]

    @pl.loop(0, (live + GROUP - 1) // GROUP)
    def _(g):
        for pair in range(GROUP // 2):
            lanes = pl.ds(pl.multiple_of((g * (GROUP // 2) + pair) * LANES, LANES), LANES)
            tiles = weights[:, lanes]
            turned = pltpu.roll(tiles, TILE, 1)
            for i in range(2):
                k = g * GROUP + pair * 2 + i
                row, column = rows[k], columns[k]
                side = jnp.where(k < live, column & 1, -1)
                tile = jnp.where(lane_half == i, tiles, turned)
                at = (
                    pl.ds(pl.multiple_of(row * TILE, TILE), TILE),
                    pl.ds(pl.multiple_of((column >> 1) * LANES, LANES), LANES),
                )
                total[at] = total[at] + jnp.where(lane_half == side, tile, 0.0)

    @pl.loop(0, PIXELS_DEV // band)
    def _(b):
        at = pl.ds(pl.multiple_of(b * band, band), band)
        high[at, :], low[at, :] = split(total[at, :])


def place_tiles(rows, columns, count, weights, *after):
    smem = pl.BlockSpec(memory_space=pltpu.SMEM)
    vmem = pl.BlockSpec(memory_space=pltpu.VMEM)
    half = jax.ShapeDtypeStruct((PIXELS_DEV, CELLS_DEV), jnp.bfloat16)
    return pl.pallas_call(
        place_kernel,
        out_shape=(half, half),
        in_specs=[smem, smem, smem, vmem] + [pl.BlockSpec(memory_space=pl.ANY)] * len(after),
        out_specs=(vmem, vmem),
        scratch_shapes=[pltpu.VMEM((PIXELS_DEV, CELLS_DEV), jnp.float32)],
        compiler_params=pltpu.CompilerParams(vmem_limit_bytes=28 * MIB),
        cost_estimate=LIGHT,
        name="place_tiles",
    )(rows, columns, count, weights, *after)


PIXEL_BLOCK = 256


def remap_blocks(x, high, low):
    m = x.shape[0]
    x_high, x_low = split(x)
    both = jnp.concatenate([x_high, x_low], axis=0)
    for start in range(0, PIXELS_DEV, PIXEL_BLOCK):
        at = slice(start, start + PIXEL_BLOCK)
        first = dot(both, high[at, :], NT)
        yield at, first[:m] + first[m:] + dot(x_high, low[at, :], NT)


def remap_call(kernel, inputs, after, out_rows, high, low, cost, name, scratch_rows=()):
    vmem = pl.BlockSpec(memory_space=pltpu.VMEM)
    return pl.pallas_call(
        kernel,
        out_shape=[
            jax.ShapeDtypeStruct(rows if isinstance(rows, tuple) else (rows, PIXELS_DEV), jnp.float32)
            for rows in out_rows
        ],
        in_specs=[vmem] * (len(inputs) + 2) + [pl.BlockSpec(memory_space=pl.ANY)] * len(after),
        out_specs=[vmem] * len(out_rows),
        scratch_shapes=[pltpu.VMEM((rows, PIXELS_DEV), jnp.float32) for rows in scratch_rows],
        compiler_params=pltpu.CompilerParams(vmem_limit_bytes=24 * MIB),
        cost_estimate=cost,
        name=name,
    )(*inputs, high, low, *after)


def remap_rows_kernel(x, high, low, out):
    for at, result in remap_blocks(x[...], high, low):
        out[:, at] = result


def unfold(block):
    levels = block.shape[0] // 2
    return jnp.concatenate([block[:levels], block[levels:]], axis=1)


def far_rows(same_sub, other_sub):
    even = lax.axis_index("sub") == 0
    blocks = [jnp.where(even, same_sub, other_sub), jnp.where(even, other_sub, same_sub)]
    return [unfold(block) for block in blocks]


def keeps_near():
    return lax.axis_index("tm") == lax.axis_index("lev") // 2


def near_rows(same_sub, other_sub):
    even = lax.axis_index("sub") == 0
    return [jnp.where(even, same_sub, other_sub), jnp.where(even, other_sub, same_sub)]


def by_hour(result, levels):
    pieces = [result[start : start + levels] for start in range(0, 2 * HOURS * levels, levels)]
    return jnp.concatenate([pieces[sub * HOURS + hour] for hour in range(HOURS) for sub in range(2)], axis=0)


def sort_out(near_result, far_result, keep, send):
    near = keeps_near()

    @pl.when(near)
    def _():
        keep[...], send[...] = near_result[...], far_result[...]

    @pl.when(jnp.logical_not(near))
    def _():
        keep[...], send[...] = far_result[...], near_result[...]


def remap_both_kernel(own, sibling, plain, high, low, *refs):
    keep, send, near_result, far_result = refs[-4:]
    rows = own.shape[0]
    blocks = near_rows(own[...], sibling[...]) + [plain[...]]
    for at, result in remap_blocks(jnp.concatenate(blocks, axis=0), high, low):
        near_result[:, at] = by_hour(result, rows // HOURS)
        far_result[:rows, at] = result[2 * rows :]
    far_result[rows:] = jnp.zeros((rows, PIXELS_DEV), jnp.float32)
    sort_out(near_result, far_result, keep, send)


def remap_near_kernel(near_same, near_other, high, low, *refs):
    outs = refs[-HOURS:]
    rows = near_same.shape[0]
    x = jnp.concatenate(near_rows(near_same[...], near_other[...]), axis=0)
    for at, result in remap_blocks(x, high, low):
        result = by_hour(result, rows // HOURS)
        for hour, out in enumerate(outs):
            out[:, at] = result[hour * rows : (hour + 1) * rows]


def remap_far_kernel(same, other, near, high, low, *refs):
    far, send = refs[-2:]
    x = jnp.concatenate(far_rows(same[...], other[...]), axis=0)
    for at, result in remap_blocks(x, high, low):
        far[:, at] = result
        send[:, at] = jnp.where(keeps_near(), result, near[:, at])


def remap_last_kernel(block, high, low, *refs):
    out, total = refs[-2:]
    x = unfold(block[...])
    levels, cells = x.shape
    x = jnp.concatenate([x, jnp.zeros((-levels % 16, cells), jnp.float32)], axis=0)
    for at, result in remap_blocks(x, high, low):
        total[:, at] = result
    out[...] = fold(total[:levels])


def hour_weights(step_hour, steps, hours, width):
    row = lax.broadcasted_iota(jnp.int32, (steps, width), 0)
    first = jnp.zeros((steps, width), jnp.float32)
    second = jnp.zeros((steps, width), jnp.float32)
    for step in range(steps):
        first = jnp.where(row == step, jnp.where(step_hour[step] == hours[0], 1.0, 0.0), first)
        second = jnp.where(row == step, jnp.where(step_hour[step] == hours[1], 1.0, 0.0), second)
    upper = row < steps // 2
    return jnp.where(upper, first, second), jnp.where(upper, second, first)


def turn(x, rows):
    return pltpu.roll(x, rows % x.shape[0], 0)


def join(a, b, bit):
    clear = (lax.broadcasted_iota(jnp.int32, a.shape, 0) & bit) == 0
    kept, moved = jnp.where(clear, a, b), jnp.where(clear, b, a)
    return kept + jnp.where(clear, turn(moved, -bit), turn(moved, bit))


def sum_steps(block, weights):
    def halve(x):
        return x * weights[0] + turn(x * weights[1], 4)

    def four(level):
        a, b, c, d = (halve(block(level + i)) for i in range(4))
        return join(join(a, c, 2), join(b, d, 2), 1)

    return four


def pack(pieces):
    upper = lax.broadcasted_iota(jnp.int32, pieces[0][0].shape, 0) < 4
    at_half = [x if half == place % 2 else turn(x, 4) for place, (x, half) in enumerate(pieces)]
    return [jnp.where(upper, a, b) for a, b in zip(at_half[::2], at_half[1::2])]


def peer_shard(k, j):
    subs = lax.axis_size("sub")
    return (lax.axis_index("lev") ^ k) * subs + (lax.axis_index("sub") ^ j)


def field_copies(field, buffer, arrived, peers):
    copies = []
    for place, (k, j) in enumerate(peers):
        start = pl.multiple_of(peer_shard(k, j) * CELLS_DEV, CELLS_DEV)
        copy = pltpu.make_async_copy(
            field.at[:, :, pl.ds(start, CELLS_DEV)], buffer.at[place], arrived.at[place]
        )
        copy.start()
        copies.append(copy)
    return copies


SUM_WIDTH = 512


def sums_kernel(plain, first, second, step_hour, field, *refs):
    *outs, buffer, arrived, hours, hours_arrived = refs
    _, levels, steps, cells = buffer.shape
    rows, cut = HOURS * levels, cells // 2
    copies = field_copies(field, buffer, arrived, [*plain, *first, second])
    fetch = pltpu.make_async_copy(step_hour, hours, hours_arrived)
    fetch.start()
    fetch.wait()
    me = lax.axis_index("tm")
    groups = range(0, levels, 4)

    def summed(place, start, width, weights):
        four = sum_steps(lambda level: buffer[place, level, :, pl.ds(start, width)], weights)
        return [four(level) for level in groups]

    def store(out, offset, start, width, pieces):
        for place, x in enumerate(pack(pieces)):
            out[offset + place * 8 : offset + place * 8 + 8, pl.ds(start, width)] = x

    weights = hour_weights(hours, steps, range(HOURS), SUM_WIDTH)
    for place in range(len(plain)):
        copies[place].wait()

        @pl.loop(0, cells // SUM_WIDTH)
        def _(i):
            start = pl.multiple_of(i * SUM_WIDTH, SUM_WIDTH)
            sums = summed(place, start, SUM_WIDTH, weights)
            pieces = [(x, half) for half in range(HOURS) for x in sums]
            store(outs[place], 0, start, SUM_WIDTH, pieces)

    theirs_first, mine_first, theirs_second, mine_second = outs[len(plain) :]
    width = SUM_WIDTH // 2
    weights = hour_weights(hours, steps, (1 - me, me), width)
    for j in range(len(first) + 1):
        place = len(plain) + j
        copies[place].wait()
        offset = j * rows if j < len(first) else 0
        theirs, mine = (theirs_first, mine_first) if j < len(first) else (theirs_second, mine_second)

        @pl.loop(0, cut // width)
        def _(i):
            start = pl.multiple_of(i * width, width)
            sums = summed(place, start, width, weights) + summed(place, cut + start, width, weights)
            store(theirs, offset, start, width, [(x, 0) for x in sums])
            store(mine, offset, start, width, [(x, 1) for x in sums])


def hour_sums(plain, first, second, step_hour, field):
    levels, steps, _ = field.shape
    rows, cut = HOURS * levels, CELLS_DEV // 2
    vmem = pl.BlockSpec(memory_space=pltpu.VMEM)
    shapes = [(rows, CELLS_DEV)] * len(plain) + [(len(first) * rows, cut)] * 2 + [(rows, cut)] * 2
    count = len(plain) + len(first) + 1
    outs = pl.pallas_call(
        functools.partial(sums_kernel, plain, first, second),
        out_shape=[jax.ShapeDtypeStruct(shape, jnp.float32) for shape in shapes],
        in_specs=[pl.BlockSpec(memory_space=pl.ANY)] * 2,
        out_specs=[vmem] * len(shapes),
        scratch_shapes=[
            pltpu.VMEM((count, levels, steps, CELLS_DEV), jnp.float32),
            pltpu.SemaphoreType.DMA((count,)),
            pltpu.SMEM((steps,), jnp.int32),
            pltpu.SemaphoreType.DMA,
        ],
        compiler_params=pltpu.CompilerParams(vmem_limit_bytes=52 * MIB),
        cost_estimate=LIGHT,
        name="hour_sums",
    )(step_hour, field)
    return outs[: len(plain)], outs[len(plain) :]


def merge_first_kernel(mine, got, *refs):
    rows = refs[-1].shape[0]
    refs[-1][...] = mine[:rows] + got[:rows]


def merge_next_kernel(mine, got, *refs):
    rows = refs[-1].shape[0]
    refs[-1][...] = mine[rows:] + got[rows:]


def merge_last_kernel(mine, got, *refs):
    refs[-1][...] = mine[...] + got[...]


def fold(x):
    half = x.shape[1] // 2
    return jnp.concatenate([x[:, :half], x[:, half:]], axis=0)


def hold_kernel(x, *refs):
    refs[-1][...] = x[...]


def small_call(kernel, inputs, after, shapes, cost, name):
    vmem = pl.BlockSpec(memory_space=pltpu.VMEM)
    return pl.pallas_call(
        kernel,
        out_shape=[jax.ShapeDtypeStruct(shape, jnp.float32) for shape in shapes],
        in_specs=[vmem] * len(inputs) + [pl.BlockSpec(memory_space=pl.ANY)] * len(after),
        out_specs=[vmem] * len(shapes),
        compiler_params=pltpu.CompilerParams(vmem_limit_bytes=8 * MIB),
        cost_estimate=cost,
        name=name,
    )(*inputs, *after)


def output_rows(same_lev, hour, levels):
    lev = lax.axis_index("lev") % 2
    start = hour * 2 + (lev if same_lev else 1 - lev)
    return pl.ds(pl.multiple_of(start * 2 * levels, 2 * levels), 2 * levels)


def write_first_kernel(divisor, levels, chip, got_chip, first_hour, got_first, second_hour, far, got, out):
    me = lax.axis_index("tm")
    rows = 2 * levels
    near = keeps_near()
    sums = [(first_hour, got_first), (second_hour, got)]
    for hour in range(HOURS):
        here = slice(hour * rows, (hour + 1) * rows)

        @pl.when(near)
        def _():
            out[output_rows(True, hour, levels), :] = (chip[here] + got_chip[here]) / divisor
            out[output_rows(False, hour, levels), :] = (sums[hour][0][...] + sums[hour][1][...]) / divisor

        @pl.when(jnp.logical_not(near))
        def _():
            out[output_rows(False, hour, levels), :] = jnp.where(me == hour, far[...], got[...]) / divisor


def write_last_kernel(divisor, levels, plain, got_plain, last, got_last, begun, out, stage, written):
    me, even = lax.axis_index("tm"), lax.axis_index("sub") == 0

    @pl.when(jnp.logical_not(keeps_near()))
    def _():
        copies = []
        for hour in range(HOURS):
            here = slice(hour * levels, (hour + 1) * levels)
            first = plain[here] + got_plain[here]
            other = unfold(jnp.where(me == hour, last[...], got_last[...]))
            pair = [jnp.where(even, first, other), jnp.where(even, other, first)]
            stage[hour] = jnp.concatenate(pair, axis=0) / divisor
            target = out.at[output_rows(True, hour, levels), :]
            copies.append(pltpu.make_async_copy(stage.at[hour], target, written.at[hour]))
            copies[-1].start()
        for copy in copies:
            copy.wait()


def write_first(arrays, levels, divisor):
    kernel = functools.partial(write_first_kernel, divisor, levels)
    shape = (2 * arrays[0].shape[0], PIXELS_DEV)
    return small_call(kernel, arrays, [], [shape], LIGHT, "write_first")[0]


def write_last(begun, arrays, levels, divisor):
    vmem, anywhere = pl.BlockSpec(memory_space=pltpu.VMEM), pl.BlockSpec(memory_space=pl.ANY)
    return pl.pallas_call(
        functools.partial(write_last_kernel, divisor, levels),
        out_shape=jax.ShapeDtypeStruct(begun.shape, begun.dtype),
        in_specs=[vmem] * len(arrays) + [anywhere],
        out_specs=anywhere,
        scratch_shapes=[
            pltpu.VMEM((HOURS, 2 * levels, PIXELS_DEV), jnp.float32),
            pltpu.SemaphoreType.DMA((HOURS,)),
        ],
        input_output_aliases={len(arrays): 0},
        compiler_params=pltpu.CompilerParams(vmem_limit_bytes=8 * MIB),
        cost_estimate=LIGHT,
        name="write_last",
    )(*arrays, begun)


def hour_plan(level_field, tile_weight, tile_rows, tile_columns, live_count, step_hour):
    levs, subs, shards_tm = lax.axis_size("lev"), lax.axis_size("sub"), lax.axis_size("tm")
    half = levs // 2
    divisor = float(level_field.shape[0] * shards_tm // HOURS)
    field = jnp.transpose(level_field, (1, 0, 2))

    def to_peer(x, k, j):
        pairs = [(a * subs + b, (a ^ k) * subs + (b ^ j)) for a in range(levs) for b in range(subs)]
        return lax.ppermute(x, ("lev", "sub"), pairs)

    def swap(x):
        return lax.ppermute(x, "tm", [(0, 1), (1, 0)])

    plain = [(half, 0), (1, 0), (1, 1), (0, 1), (0, 0)]
    first, second = [(half + 1, j) for j in range(subs)], (half, 1)
    sums, (theirs_0, mine_0, theirs_1, mine_1) = hour_sums(plain, first, second, step_hour, field)
    rows = 2 * field.shape[0]
    folded = theirs_1.shape
    sibling = to_peer(sums[3], *plain[3])
    near_got = [to_peer(x, *peer) for x, peer in list(zip(sums, plain))[1:3]]
    got_0 = swap(theirs_0)
    plain_got = to_peer(sums[0], *plain[0])
    high, low = place_tiles(tile_rows, tile_columns, live_count, tile_weight, theirs_0)

    merged = small_call(
        merge_first_kernel, [mine_0, got_0], [high, sibling], [folded], LIGHT, "merge_first"
    )
    far_same = to_peer(merged[0], *first[0])
    merged = small_call(merge_next_kernel, [mine_0, got_0], merged, [folded], LIGHT, "merge_next")
    far_other = to_peer(merged[0], *first[1])
    theirs_1 = small_call(hold_kernel, [theirs_1], [plain_got, *merged], [folded], LIGHT, "hold")[0]
    got_1 = swap(theirs_1)
    both, send = remap_call(
        remap_both_kernel,
        [sums[4], sibling, plain_got],
        [theirs_1],
        [2 * rows] * 2,
        high,
        low,
        MEDIUM,
        "remap_both",
        [2 * rows] * 2,
    )
    got_both = swap(send)
    merged = small_call(
        merge_last_kernel, [mine_1, got_1], [both, near_got[0]], [folded], HEAVY, "merge_last"
    )
    second_got = to_peer(merged[0], *second)
    first_hour, second_hour = remap_call(
        remap_near_kernel, near_got, merged, [rows] * HOURS, high, low, LIGHT, "remap_near"
    )
    got_first = swap(first_hour)
    far, send = remap_call(
        remap_far_kernel, [far_same, far_other, second_hour], [], [rows] * 2, high, low, HEAVY, "remap_far"
    )
    got = swap(send)
    padded = -(-rows // 32) * 16
    (last,) = remap_call(
        remap_last_kernel,
        [second_got],
        [far],
        [(rows, PIXELS_DEV // 2)],
        high,
        low,
        HEAVY,
        "remap_last",
        [padded],
    )
    got_last = swap(last)
    levels = rows // 2
    out = write_first([both, got_both, first_hour, got_first, second_hour, far, got], levels, divisor)
    out = write_last(out, [both, got_both, last, got_last], levels, divisor)
    return out.reshape(HOURS, out.shape[0] // HOURS, PIXELS_DEV)


def general_plan(level_field, tile_weight, tile_rows, tile_columns, live_count, step_hour):
    steps, levels, cells = level_field.shape
    shards = lax.axis_size("lev") * lax.axis_size("sub")
    divisor = float(steps * lax.axis_size("tm") // HOURS)
    hours = jnp.arange(HOURS, dtype=jnp.int32)
    table = (step_hour[None, :] == hours[:, None]).astype(jnp.float32)
    fields = level_field.reshape(steps, levels, shards, cells // shards)
    partial = jnp.einsum("hs,slgc->ghlc", table, fields, precision=lax.Precision.HIGHEST)
    regrouped = lax.all_to_all(partial, ("lev", "sub"), split_axis=0, concat_axis=0, tiled=True)
    rows = jnp.transpose(regrouped, (1, 0, 2, 3)).reshape(-1, cells // shards)
    high, low = place_tiles(tile_rows, tile_columns, live_count, tile_weight)
    (out,) = remap_call(remap_rows_kernel, [rows], [], [rows.shape[0]], high, low, LIGHT, "remap_rows")
    out = out.reshape(HOURS, shards * levels, PIXELS_DEV) / divisor
    return lax.psum_scatter(out, "tm", scatter_dimension=1, tiled=True)


def solution(mesh):
    sizes = mesh.shape
    paired = sizes["tm"] == HOURS and sizes["lev"] == 4 and sizes["sub"] == 2

    def body(level_field, *others):
        steps, levels, _ = level_field.shape
        suits = paired and steps == 8 and levels % 4 == 0
        return (hour_plan if suits else general_plan)(level_field, *others)

    placed = (
        P(("groups", "tm"), ("lev", "sub"), None),
        P(None, ("lev", "sub")),
        P(("lev", "sub")),
        P(("lev", "sub")),
        P(("lev", "sub")),
        P("tm"),
    )
    return jax.shard_map(
        body,
        mesh=mesh,
        in_specs=placed,
        out_specs=P("groups", "tm", ("lev", "sub")),
        check_vma=False,
    )
```

```python
import functools

import jax
import jax.numpy as jnp
from jax import lax
from jax.experimental import pallas as pl
from jax.experimental.pallas import tpu as pltpu
from jax.sharding import PartitionSpec as P

TILE = 64
HOURS = 2
CT_DEV = 32
PT_DEV = 16
SLOTS = 128
CELLS_DEV = CT_DEV * TILE
PIXELS_DEV = PT_DEV * TILE
LANES = 2 * TILE
MIB = 1 << 20

LIGHT = pl.CostEstimate(flops=1, bytes_accessed=1, transcendentals=0)
MEDIUM = pl.CostEstimate(flops=2_500_000_000, bytes_accessed=1, transcendentals=0)
HEAVY = pl.CostEstimate(flops=10_000_000_000, bytes_accessed=1, transcendentals=0)

NT = (((1,), (1,)), ((), ()))
NN = (((1,), (0,)), ((), ()))


def split(x):
    high = x.astype(jnp.bfloat16)
    return high, (x - high.astype(jnp.float32)).astype(jnp.bfloat16)


def dot(a, b, dims):
    return lax.dot_general(a, b, dims, preferred_element_type=jnp.float32)


GROUP = 8


def place_kernel(rows, columns, count, weights, *refs):
    high, low, total = refs[-3:]
    band = 128

    @pl.loop(0, PIXELS_DEV // band)
    def _(b):
        total[pl.ds(pl.multiple_of(b * band, band), band), :] = jnp.zeros((band, CELLS_DEV), jnp.float32)

    lane_half = lax.broadcasted_iota(jnp.int32, (TILE, LANES), 1) // TILE
    live = count[0]

    @pl.loop(0, (live + GROUP - 1) // GROUP)
    def _(g):
        for pair in range(GROUP // 2):
            lanes = pl.ds(pl.multiple_of((g * (GROUP // 2) + pair) * LANES, LANES), LANES)
            tiles = weights[:, lanes]
            turned = pltpu.roll(tiles, TILE, 1)
            for i in range(2):
                k = g * GROUP + pair * 2 + i
                row, column = rows[k], columns[k]
                side = jnp.where(k < live, column & 1, -1)
                tile = jnp.where(lane_half == i, tiles, turned)
                at = (
                    pl.ds(pl.multiple_of(row * TILE, TILE), TILE),
                    pl.ds(pl.multiple_of((column >> 1) * LANES, LANES), LANES),
                )
                total[at] = total[at] + jnp.where(lane_half == side, tile, 0.0)

    @pl.loop(0, PIXELS_DEV // band)
    def _(b):
        at = pl.ds(pl.multiple_of(b * band, band), band)
        high[at, :], low[at, :] = split(total[at, :])


def place_tiles(rows, columns, count, weights, *after):
    smem = pl.BlockSpec(memory_space=pltpu.SMEM)
    vmem = pl.BlockSpec(memory_space=pltpu.VMEM)
    half = jax.ShapeDtypeStruct((PIXELS_DEV, CELLS_DEV), jnp.bfloat16)
    return pl.pallas_call(
        place_kernel,
        out_shape=(half, half),
        in_specs=[smem, smem, smem, vmem] + [pl.BlockSpec(memory_space=pl.ANY)] * len(after),
        out_specs=(vmem, vmem),
        scratch_shapes=[pltpu.VMEM((PIXELS_DEV, CELLS_DEV), jnp.float32)],
        compiler_params=pltpu.CompilerParams(vmem_limit_bytes=28 * MIB),
        cost_estimate=LIGHT,
        name="place_tiles",
    )(rows, columns, count, weights, *after)


PIXEL_BLOCK = 256


def remap_blocks(x, high, low):
    m = x.shape[0]
    x_high, x_low = split(x)
    both = jnp.concatenate([x_high, x_low], axis=0)
    for start in range(0, PIXELS_DEV, PIXEL_BLOCK):
        at = slice(start, start + PIXEL_BLOCK)
        first = dot(both, high[at, :], NT)
        yield at, first[:m] + first[m:] + dot(x_high, low[at, :], NT)


def remap_call(kernel, inputs, after, out_rows, high, low, cost, name, scratch_rows=()):
    vmem = pl.BlockSpec(memory_space=pltpu.VMEM)
    return pl.pallas_call(
        kernel,
        out_shape=[
            jax.ShapeDtypeStruct(rows if isinstance(rows, tuple) else (rows, PIXELS_DEV), jnp.float32)
            for rows in out_rows
        ],
        in_specs=[vmem] * (len(inputs) + 2) + [pl.BlockSpec(memory_space=pl.ANY)] * len(after),
        out_specs=[vmem] * len(out_rows),
        scratch_shapes=[pltpu.VMEM((rows, PIXELS_DEV), jnp.float32) for rows in scratch_rows],
        compiler_params=pltpu.CompilerParams(vmem_limit_bytes=24 * MIB),
        cost_estimate=cost,
        name=name,
    )(*inputs, high, low, *after)


def remap_rows_kernel(x, high, low, out):
    for at, result in remap_blocks(x[...], high, low):
        out[:, at] = result


def unfold(block):
    levels = block.shape[0] // 2
    return jnp.concatenate([block[:levels], block[levels:]], axis=1)


def far_rows(same_sub, other_sub):
    even = lax.axis_index("sub") == 0
    blocks = [jnp.where(even, same_sub, other_sub), jnp.where(even, other_sub, same_sub)]
    return [unfold(block) for block in blocks]


def keeps_near():
    return lax.axis_index("tm") == lax.axis_index("lev") // 2


def near_rows(same_sub, other_sub):
    even = lax.axis_index("sub") == 0
    return [jnp.where(even, same_sub, other_sub), jnp.where(even, other_sub, same_sub)]


def by_hour(result, levels):
    pieces = [result[start : start + levels] for start in range(0, 2 * HOURS * levels, levels)]
    return jnp.concatenate([pieces[sub * HOURS + hour] for hour in range(HOURS) for sub in range(2)], axis=0)


def sort_out(near_result, far_result, keep, send):
    near = keeps_near()

    @pl.when(near)
    def _():
        keep[...], send[...] = near_result[...], far_result[...]

    @pl.when(jnp.logical_not(near))
    def _():
        keep[...], send[...] = far_result[...], near_result[...]


def remap_both_kernel(own, sibling, plain, high, low, *refs):
    keep, send, near_result, far_result = refs[-4:]
    rows = own.shape[0]
    blocks = near_rows(own[...], sibling[...]) + [plain[...]]
    for at, result in remap_blocks(jnp.concatenate(blocks, axis=0), high, low):
        near_result[:, at] = by_hour(result, rows // HOURS)
        far_result[:rows, at] = result[2 * rows :]
    far_result[rows:] = jnp.zeros((rows, PIXELS_DEV), jnp.float32)
    sort_out(near_result, far_result, keep, send)


def remap_near_kernel(near_same, near_other, high, low, *refs):
    outs = refs[-HOURS:]
    rows = near_same.shape[0]
    x = jnp.concatenate(near_rows(near_same[...], near_other[...]), axis=0)
    for at, result in remap_blocks(x, high, low):
        result = by_hour(result, rows // HOURS)
        for hour, out in enumerate(outs):
            out[:, at] = result[hour * rows : (hour + 1) * rows]


def remap_far_kernel(same, other, near, high, low, *refs):
    far, send = refs[-2:]
    x = jnp.concatenate(far_rows(same[...], other[...]), axis=0)
    for at, result in remap_blocks(x, high, low):
        far[:, at] = result
        send[:, at] = jnp.where(keeps_near(), result, near[:, at])


def remap_last_kernel(block, high, low, *refs):
    out, total = refs[-2:]
    x = unfold(block[...])
    levels, cells = x.shape
    x = jnp.concatenate([x, jnp.zeros((-levels % 16, cells), jnp.float32)], axis=0)
    for at, result in remap_blocks(x, high, low):
        total[:, at] = result
    out[...] = fold(total[:levels])


def hour_weights(step_hour, steps, hours, width):
    row = lax.broadcasted_iota(jnp.int32, (steps, width), 0)
    first = jnp.zeros((steps, width), jnp.float32)
    second = jnp.zeros((steps, width), jnp.float32)
    for step in range(steps):
        first = jnp.where(row == step, jnp.where(step_hour[step] == hours[0], 1.0, 0.0), first)
        second = jnp.where(row == step, jnp.where(step_hour[step] == hours[1], 1.0, 0.0), second)
    upper = row < steps // 2
    return jnp.where(upper, first, second), jnp.where(upper, second, first)


def turn(x, rows):
    return pltpu.roll(x, rows % x.shape[0], 0)


def join(a, b, bit):
    clear = (lax.broadcasted_iota(jnp.int32, a.shape, 0) & bit) == 0
    kept, moved = jnp.where(clear, a, b), jnp.where(clear, b, a)
    return kept + jnp.where(clear, turn(moved, -bit), turn(moved, bit))


def sum_steps(block, weights):
    def halve(x):
        return x * weights[0] + turn(x * weights[1], 4)

    def four(level):
        a, b, c, d = (halve(block(level + i)) for i in range(4))
        return join(join(a, c, 2), join(b, d, 2), 1)

    return four


def pack(pieces):
    upper = lax.broadcasted_iota(jnp.int32, pieces[0][0].shape, 0) < 4
    at_half = [x if half == place % 2 else turn(x, 4) for place, (x, half) in enumerate(pieces)]
    return [jnp.where(upper, a, b) for a, b in zip(at_half[::2], at_half[1::2])]


def peer_shard(k, j):
    subs = lax.axis_size("sub")
    return (lax.axis_index("lev") ^ k) * subs + (lax.axis_index("sub") ^ j)


def field_copies(field, buffer, arrived, peers):
    copies = []
    for place, (k, j) in enumerate(peers):
        start = pl.multiple_of(peer_shard(k, j) * CELLS_DEV, CELLS_DEV)
        copy = pltpu.make_async_copy(
            field.at[:, :, pl.ds(start, CELLS_DEV)], buffer.at[place], arrived.at[place]
        )
        copy.start()
        copies.append(copy)
    return copies


SUM_WIDTH = 512


def sums_kernel(plain, chunks, step_hour, field, *refs):
    buffer, arrived, hours, hours_arrived = refs[-4:]
    outs = refs[-4 - len(plain) - 2 * len(chunks) : -4]
    _, levels, steps, cells = buffer.shape
    rows, cut = HOURS * levels, cells // 2
    copies = field_copies(field, buffer, arrived, [*plain, *sum(chunks, [])])
    fetch = pltpu.make_async_copy(step_hour, hours, hours_arrived)
    fetch.start()
    fetch.wait()
    me = lax.axis_index("tm")
    groups = range(0, levels, 4)

    def summed(place, start, width, weights):
        four = sum_steps(lambda level: buffer[place, level, :, pl.ds(start, width)], weights)
        return [four(level) for level in groups]

    def store(out, offset, start, width, pieces):
        for place, x in enumerate(pack(pieces)):
            out[offset + place * 8 : offset + place * 8 + 8, pl.ds(start, width)] = x

    weights = hour_weights(hours, steps, range(HOURS), SUM_WIDTH)
    for place in range(len(plain)):
        copies[place].wait()

        @pl.loop(0, cells // SUM_WIDTH)
        def _(i):
            start = pl.multiple_of(i * SUM_WIDTH, SUM_WIDTH)
            sums = summed(place, start, SUM_WIDTH, weights)
            pieces = [(x, half) for half in range(HOURS) for x in sums]
            store(outs[place], 0, start, SUM_WIDTH, pieces)

    width = SUM_WIDTH // 2
    weights = hour_weights(hours, steps, (1 - me, me), width)
    place = len(plain)
    for chunk, members in enumerate(chunks):
        theirs, mine = outs[len(plain) + 2 * chunk], outs[len(plain) + 2 * chunk + 1]
        for j in range(len(members)):
            copies[place].wait()

            @pl.loop(0, cut // width)
            def _(i):
                start = pl.multiple_of(i * width, width)
                sums = summed(place, start, width, weights) + summed(place, cut + start, width, weights)
                store(theirs, j * rows, start, width, [(x, 0) for x in sums])
                store(mine, j * rows, start, width, [(x, 1) for x in sums])

            place += 1


def hour_sums(plain, chunks, step_hour, field, *after):
    levels, steps, _ = field.shape
    rows, cut = HOURS * levels, CELLS_DEV // 2
    vmem = pl.BlockSpec(memory_space=pltpu.VMEM)
    shapes = [(rows, CELLS_DEV)] * len(plain)
    for members in chunks:
        shapes += [(len(members) * rows, cut)] * 2
    count = len(plain) + sum(map(len, chunks))
    outs = pl.pallas_call(
        functools.partial(sums_kernel, plain, chunks),
        out_shape=[jax.ShapeDtypeStruct(shape, jnp.float32) for shape in shapes],
        in_specs=[pl.BlockSpec(memory_space=pl.ANY)] * (2 + len(after)),
        out_specs=[vmem] * len(shapes),
        scratch_shapes=[
            pltpu.VMEM((count, levels, steps, CELLS_DEV), jnp.float32),
            pltpu.SemaphoreType.DMA((count,)),
            pltpu.SMEM((steps,), jnp.int32),
            pltpu.SemaphoreType.DMA,
        ],
        compiler_params=pltpu.CompilerParams(vmem_limit_bytes=52 * MIB),
        cost_estimate=LIGHT,
        name="hour_sums",
    )(step_hour, field, *after)
    return outs[: len(plain)], outs[len(plain) :]


def merge_first_kernel(mine, got, *refs):
    rows = refs[-1].shape[0]
    refs[-1][...] = mine[:rows] + got[:rows]


def merge_next_kernel(mine, got, *refs):
    rows = refs[-1].shape[0]
    refs[-1][...] = mine[rows:] + got[rows:]


def merge_last_kernel(mine, got, *refs):
    refs[-1][...] = mine[...] + got[...]


def fold(x):
    half = x.shape[1] // 2
    return jnp.concatenate([x[:, :half], x[:, half:]], axis=0)


def hold_kernel(x, *refs):
    refs[-1][...] = x[...]


def small_call(kernel, inputs, after, shapes, cost, name):
    vmem = pl.BlockSpec(memory_space=pltpu.VMEM)
    return pl.pallas_call(
        kernel,
        out_shape=[jax.ShapeDtypeStruct(shape, jnp.float32) for shape in shapes],
        in_specs=[vmem] * len(inputs) + [pl.BlockSpec(memory_space=pl.ANY)] * len(after),
        out_specs=[vmem] * len(shapes),
        compiler_params=pltpu.CompilerParams(vmem_limit_bytes=8 * MIB),
        cost_estimate=cost,
        name=name,
    )(*inputs, *after)


def output_rows(same_lev, hour, levels):
    lev = lax.axis_index("lev") % 2
    start = hour * 2 + (lev if same_lev else 1 - lev)
    return pl.ds(pl.multiple_of(start * 2 * levels, 2 * levels), 2 * levels)


def write_first_kernel(divisor, levels, chip, got_chip, first_hour, got_first, second_hour, far, got, out):
    me = lax.axis_index("tm")
    rows = 2 * levels
    near = keeps_near()
    sums = [(first_hour, got_first), (second_hour, got)]
    for hour in range(HOURS):
        here = slice(hour * rows, (hour + 1) * rows)

        @pl.when(near)
        def _():
            out[output_rows(True, hour, levels), :] = (chip[here] + got_chip[here]) / divisor
            out[output_rows(False, hour, levels), :] = (sums[hour][0][...] + sums[hour][1][...]) / divisor

        @pl.when(jnp.logical_not(near))
        def _():
            out[output_rows(False, hour, levels), :] = jnp.where(me == hour, far[...], got[...]) / divisor


def write_last_kernel(divisor, levels, plain, got_plain, last, got_last, begun, out, stage, written):
    me, even = lax.axis_index("tm"), lax.axis_index("sub") == 0

    @pl.when(jnp.logical_not(keeps_near()))
    def _():
        copies = []
        for hour in range(HOURS):
            here = slice(hour * levels, (hour + 1) * levels)
            first = plain[here] + got_plain[here]
            other = unfold(jnp.where(me == hour, last[...], got_last[...]))
            pair = [jnp.where(even, first, other), jnp.where(even, other, first)]
            stage[hour] = jnp.concatenate(pair, axis=0) / divisor
            target = out.at[output_rows(True, hour, levels), :]
            copies.append(pltpu.make_async_copy(stage.at[hour], target, written.at[hour]))
            copies[-1].start()
        for copy in copies:
            copy.wait()


def write_first(arrays, levels, divisor):
    kernel = functools.partial(write_first_kernel, divisor, levels)
    shape = (2 * arrays[0].shape[0], PIXELS_DEV)
    return small_call(kernel, arrays, [], [shape], LIGHT, "write_first")[0]


def write_last(begun, arrays, levels, divisor):
    vmem, anywhere = pl.BlockSpec(memory_space=pltpu.VMEM), pl.BlockSpec(memory_space=pl.ANY)
    return pl.pallas_call(
        functools.partial(write_last_kernel, divisor, levels),
        out_shape=jax.ShapeDtypeStruct(begun.shape, begun.dtype),
        in_specs=[vmem] * len(arrays) + [anywhere],
        out_specs=anywhere,
        scratch_shapes=[
            pltpu.VMEM((HOURS, 2 * levels, PIXELS_DEV), jnp.float32),
            pltpu.SemaphoreType.DMA((HOURS,)),
        ],
        input_output_aliases={len(arrays): 0},
        compiler_params=pltpu.CompilerParams(vmem_limit_bytes=8 * MIB),
        cost_estimate=LIGHT,
        name="write_last",
    )(*arrays, begun)


def hour_plan(level_field, tile_weight, tile_rows, tile_columns, live_count, step_hour):
    levs, subs, shards_tm = lax.axis_size("lev"), lax.axis_size("sub"), lax.axis_size("tm")
    half = levs // 2
    divisor = float(level_field.shape[0] * shards_tm // HOURS)
    field = jnp.transpose(level_field, (1, 0, 2))

    def to_peer(x, k, j):
        pairs = [(a * subs + b, (a ^ k) * subs + (b ^ j)) for a in range(levs) for b in range(subs)]
        return lax.ppermute(x, ("lev", "sub"), pairs)

    def swap(x):
        return lax.ppermute(x, "tm", [(0, 1), (1, 0)])

    plain, lev_near = (half, 0), [(1, j) for j in range(subs)]
    first, second = [(half + 1, j) for j in range(subs)], (half, 1)
    (plain_sums, sibling), (theirs_0, mine_0) = hour_sums([plain, (0, 1)], [first], step_hour, field)
    rows = 2 * field.shape[0]
    sibling = to_peer(sibling, 0, 1)
    got_0 = swap(theirs_0)
    plain_got = to_peer(plain_sums, *plain)
    (*near_sums, own), (theirs_1, mine_1) = hour_sums(
        [*lev_near, (0, 0)], [[second]], step_hour, field, theirs_0
    )
    folded = theirs_1.shape
    near_got = [to_peer(x, *peer) for x, peer in zip(near_sums, lev_near)]

    merged = small_call(
        merge_first_kernel, [mine_0, got_0], [sibling, theirs_1], [folded], LIGHT, "merge_first"
    )
    far_same = to_peer(merged[0], *first[0])
    merged = small_call(merge_next_kernel, [mine_0, got_0], merged, [folded], LIGHT, "merge_next")
    far_other = to_peer(merged[0], *first[1])
    high, low = place_tiles(tile_rows, tile_columns, live_count, tile_weight, *merged)
    theirs_1 = small_call(hold_kernel, [theirs_1], [plain_got, high], [folded], LIGHT, "hold")[0]
    got_1 = swap(theirs_1)
    both, send = remap_call(
        remap_both_kernel,
        [own, sibling, plain_got],
        [theirs_1],
        [2 * rows] * 2,
        high,
        low,
        MEDIUM,
        "remap_both",
        [2 * rows] * 2,
    )
    got_both = swap(send)
    merged = small_call(
        merge_last_kernel, [mine_1, got_1], [both, near_got[0]], [folded], HEAVY, "merge_last"
    )
    second_got = to_peer(merged[0], *second)
    first_hour, second_hour = remap_call(
        remap_near_kernel, near_got, merged, [rows] * HOURS, high, low, LIGHT, "remap_near"
    )
    got_first = swap(first_hour)
    far, send = remap_call(
        remap_far_kernel, [far_same, far_other, second_hour], [], [rows] * 2, high, low, HEAVY, "remap_far"
    )
    got = swap(send)
    padded = -(-rows // 32) * 16
    (last,) = remap_call(
        remap_last_kernel,
        [second_got],
        [far],
        [(rows, PIXELS_DEV // 2)],
        high,
        low,
        HEAVY,
        "remap_last",
        [padded],
    )
    got_last = swap(last)
    levels = rows // 2
    out = write_first([both, got_both, first_hour, got_first, second_hour, far, got], levels, divisor)
    out = write_last(out, [both, got_both, last, got_last], levels, divisor)
    return out.reshape(HOURS, out.shape[0] // HOURS, PIXELS_DEV)


def general_plan(level_field, tile_weight, tile_rows, tile_columns, live_count, step_hour):
    steps, levels, cells = level_field.shape
    shards = lax.axis_size("lev") * lax.axis_size("sub")
    divisor = float(steps * lax.axis_size("tm") // HOURS)
    hours = jnp.arange(HOURS, dtype=jnp.int32)
    table = (step_hour[None, :] == hours[:, None]).astype(jnp.float32)
    fields = level_field.reshape(steps, levels, shards, cells // shards)
    partial = jnp.einsum("hs,slgc->ghlc", table, fields, precision=lax.Precision.HIGHEST)
    regrouped = lax.all_to_all(partial, ("lev", "sub"), split_axis=0, concat_axis=0, tiled=True)
    rows = jnp.transpose(regrouped, (1, 0, 2, 3)).reshape(-1, cells // shards)
    high, low = place_tiles(tile_rows, tile_columns, live_count, tile_weight)
    (out,) = remap_call(remap_rows_kernel, [rows], [], [rows.shape[0]], high, low, LIGHT, "remap_rows")
    out = out.reshape(HOURS, shards * levels, PIXELS_DEV) / divisor
    return lax.psum_scatter(out, "tm", scatter_dimension=1, tiled=True)


def solution(mesh):
    sizes = mesh.shape
    paired = sizes["tm"] == HOURS and sizes["lev"] == 4 and sizes["sub"] == 2

    def body(level_field, *others):
        steps, levels, _ = level_field.shape
        suits = paired and steps == 8 and levels % 4 == 0
        return (hour_plan if suits else general_plan)(level_field, *others)

    placed = (
        P(("groups", "tm"), ("lev", "sub"), None),
        P(None, ("lev", "sub")),
        P(("lev", "sub")),
        P(("lev", "sub")),
        P(("lev", "sub")),
        P("tm"),
    )
    return jax.shard_map(
        body,
        mesh=mesh,
        in_specs=placed,
        out_specs=P("groups", "tm", ("lev", "sub")),
        check_vma=False,
    )
```

```python
import functools

import jax
import jax.numpy as jnp
from jax import lax
from jax.experimental import pallas as pl
from jax.experimental.pallas import tpu as pltpu
from jax.sharding import PartitionSpec as P

TILE = 64
HOURS = 2
CT_DEV = 32
PT_DEV = 16
SLOTS = 128
CELLS_DEV = CT_DEV * TILE
PIXELS_DEV = PT_DEV * TILE
LANES = 2 * TILE
MIB = 1 << 20

LIGHT = pl.CostEstimate(flops=1, bytes_accessed=1, transcendentals=0)
MEDIUM = pl.CostEstimate(flops=2_500_000_000, bytes_accessed=1, transcendentals=0)
HEAVY = pl.CostEstimate(flops=10_000_000_000, bytes_accessed=1, transcendentals=0)

NT = (((1,), (1,)), ((), ()))
NN = (((1,), (0,)), ((), ()))


def split(x):
    high = x.astype(jnp.bfloat16)
    return high, (x - high.astype(jnp.float32)).astype(jnp.bfloat16)


def dot(a, b, dims):
    return lax.dot_general(a, b, dims, preferred_element_type=jnp.float32)


GROUP = 8


def place_kernel(rows, columns, count, weights, *refs):
    high, low, total = refs[-3:]
    band = 128

    @pl.loop(0, PIXELS_DEV // band)
    def _(b):
        total[pl.ds(pl.multiple_of(b * band, band), band), :] = jnp.zeros((band, CELLS_DEV), jnp.float32)

    lane_half = lax.broadcasted_iota(jnp.int32, (TILE, LANES), 1) // TILE
    live = count[0]

    @pl.loop(0, (live + GROUP - 1) // GROUP)
    def _(g):
        for pair in range(GROUP // 2):
            lanes = pl.ds(pl.multiple_of((g * (GROUP // 2) + pair) * LANES, LANES), LANES)
            tiles = weights[:, lanes]
            turned = pltpu.roll(tiles, TILE, 1)
            for i in range(2):
                k = g * GROUP + pair * 2 + i
                row, column = rows[k], columns[k]
                side = jnp.where(k < live, column & 1, -1)
                tile = jnp.where(lane_half == i, tiles, turned)
                at = (
                    pl.ds(pl.multiple_of(row * TILE, TILE), TILE),
                    pl.ds(pl.multiple_of((column >> 1) * LANES, LANES), LANES),
                )
                total[at] = total[at] + jnp.where(lane_half == side, tile, 0.0)

    @pl.loop(0, PIXELS_DEV // band)
    def _(b):
        at = pl.ds(pl.multiple_of(b * band, band), band)
        high[at, :], low[at, :] = split(total[at, :])


def place_tiles(rows, columns, count, weights, *after):
    smem = pl.BlockSpec(memory_space=pltpu.SMEM)
    vmem = pl.BlockSpec(memory_space=pltpu.VMEM)
    half = jax.ShapeDtypeStruct((PIXELS_DEV, CELLS_DEV), jnp.bfloat16)
    return pl.pallas_call(
        place_kernel,
        out_shape=(half, half),
        in_specs=[smem, smem, smem, vmem] + [pl.BlockSpec(memory_space=pl.ANY)] * len(after),
        out_specs=(vmem, vmem),
        scratch_shapes=[pltpu.VMEM((PIXELS_DEV, CELLS_DEV), jnp.float32)],
        compiler_params=pltpu.CompilerParams(vmem_limit_bytes=28 * MIB),
        cost_estimate=LIGHT,
        name="place_tiles",
    )(rows, columns, count, weights, *after)


PIXEL_BLOCK = 1024


def remap_blocks(x, high, low):
    m = x.shape[0]
    x_high, x_low = split(x)
    both = jnp.concatenate([x_high, x_low], axis=0)
    for start in range(0, PIXELS_DEV, PIXEL_BLOCK):
        at = slice(start, start + PIXEL_BLOCK)
        first = dot(both, high[at, :], NT)
        yield at, first[:m] + first[m:] + dot(x_high, low[at, :], NT)


def remap_call(kernel, inputs, after, out_rows, high, low, cost, name, scratch_rows=()):
    vmem = pl.BlockSpec(memory_space=pltpu.VMEM)
    return pl.pallas_call(
        kernel,
        out_shape=[
            jax.ShapeDtypeStruct(rows if isinstance(rows, tuple) else (rows, PIXELS_DEV), jnp.float32)
            for rows in out_rows
        ],
        in_specs=[vmem] * (len(inputs) + 2) + [pl.BlockSpec(memory_space=pl.ANY)] * len(after),
        out_specs=[vmem] * len(out_rows),
        scratch_shapes=[pltpu.VMEM((rows, PIXELS_DEV), jnp.float32) for rows in scratch_rows],
        compiler_params=pltpu.CompilerParams(vmem_limit_bytes=24 * MIB),
        cost_estimate=cost,
        name=name,
    )(*inputs, high, low, *after)


def remap_rows_kernel(x, high, low, out):
    for at, result in remap_blocks(x[...], high, low):
        out[:, at] = result


def unfold(block):
    levels = block.shape[0] // 2
    return jnp.concatenate([block[:levels], block[levels:]], axis=1)


def far_rows(same_sub, other_sub):
    even = lax.axis_index("sub") == 0
    blocks = [jnp.where(even, same_sub, other_sub), jnp.where(even, other_sub, same_sub)]
    return [unfold(block) for block in blocks]


def keeps_near():
    return lax.axis_index("tm") == lax.axis_index("lev") // 2


def near_rows(same_sub, other_sub):
    even = lax.axis_index("sub") == 0
    return [jnp.where(even, same_sub, other_sub), jnp.where(even, other_sub, same_sub)]


def by_hour(result, levels):
    pieces = [result[start : start + levels] for start in range(0, 2 * HOURS * levels, levels)]
    return jnp.concatenate([pieces[sub * HOURS + hour] for hour in range(HOURS) for sub in range(2)], axis=0)


def sort_out(near_result, far_result, keep, send):
    near = keeps_near()

    @pl.when(near)
    def _():
        keep[...], send[...] = near_result[...], far_result[...]

    @pl.when(jnp.logical_not(near))
    def _():
        keep[...], send[...] = far_result[...], near_result[...]


def remap_both_kernel(own, sibling, plain, high, low, *refs):
    keep, send, near_result, far_result = refs[-4:]
    rows = own.shape[0]
    blocks = near_rows(own[...], sibling[...]) + [plain[...]]
    for at, result in remap_blocks(jnp.concatenate(blocks, axis=0), high, low):
        near_result[:, at] = by_hour(result, rows // HOURS)
        far_result[:rows, at] = result[2 * rows :]
    far_result[rows:] = jnp.zeros((rows, PIXELS_DEV), jnp.float32)
    sort_out(near_result, far_result, keep, send)


def remap_near_kernel(near_same, near_other, high, low, *refs):
    outs = refs[-HOURS:]
    rows = near_same.shape[0]
    x = jnp.concatenate(near_rows(near_same[...], near_other[...]), axis=0)
    for at, result in remap_blocks(x, high, low):
        result = by_hour(result, rows // HOURS)
        for hour, out in enumerate(outs):
            out[:, at] = result[hour * rows : (hour + 1) * rows]


def remap_far_kernel(same, other, near, high, low, *refs):
    far, send = refs[-2:]
    x = jnp.concatenate(far_rows(same[...], other[...]), axis=0)
    for at, result in remap_blocks(x, high, low):
        far[:, at] = result
        send[:, at] = jnp.where(keeps_near(), result, near[:, at])


def remap_last_kernel(block, high, low, *refs):
    out, total = refs[-2:]
    x = unfold(block[...])
    levels, cells = x.shape
    x = jnp.concatenate([x, jnp.zeros((-levels % 16, cells), jnp.float32)], axis=0)
    for at, result in remap_blocks(x, high, low):
        total[:, at] = result
    out[...] = fold(total[:levels])


def hour_weights(step_hour, steps, hours, width):
    row = lax.broadcasted_iota(jnp.int32, (steps, width), 0)
    first = jnp.zeros((steps, width), jnp.float32)
    second = jnp.zeros((steps, width), jnp.float32)
    for step in range(steps):
        first = jnp.where(row == step, jnp.where(step_hour[step] == hours[0], 1.0, 0.0), first)
        second = jnp.where(row == step, jnp.where(step_hour[step] == hours[1], 1.0, 0.0), second)
    upper = row < steps // 2
    return jnp.where(upper, first, second), jnp.where(upper, second, first)


def turn(x, rows):
    return pltpu.roll(x, rows % x.shape[0], 0)


def join(a, b, bit):
    clear = (lax.broadcasted_iota(jnp.int32, a.shape, 0) & bit) == 0
    kept, moved = jnp.where(clear, a, b), jnp.where(clear, b, a)
    return kept + jnp.where(clear, turn(moved, -bit), turn(moved, bit))


def sum_steps(block, weights):
    def halve(x):
        return x * weights[0] + turn(x * weights[1], 4)

    def four(level):
        a, b, c, d = (halve(block(level + i)) for i in range(4))
        return join(join(a, c, 2), join(b, d, 2), 1)

    return four


def pack(pieces):
    upper = lax.broadcasted_iota(jnp.int32, pieces[0][0].shape, 0) < 4
    at_half = [x if half == place % 2 else turn(x, 4) for place, (x, half) in enumerate(pieces)]
    return [jnp.where(upper, a, b) for a, b in zip(at_half[::2], at_half[1::2])]


def peer_shard(k, j):
    subs = lax.axis_size("sub")
    return (lax.axis_index("lev") ^ k) * subs + (lax.axis_index("sub") ^ j)


def field_copies(field, buffer, arrived, peers):
    copies = []
    for place, (k, j) in enumerate(peers):
        start = pl.multiple_of(peer_shard(k, j) * CELLS_DEV, CELLS_DEV)
        copy = pltpu.make_async_copy(
            field.at[:, :, pl.ds(start, CELLS_DEV)], buffer.at[place], arrived.at[place]
        )
        copy.start()
        copies.append(copy)
    return copies


SUM_WIDTH = 512


def sums_kernel(plain, first, second, step_hour, field, *refs):
    *outs, buffer, arrived, hours, hours_arrived = refs
    _, levels, steps, cells = buffer.shape
    rows, cut = HOURS * levels, cells // 2
    copies = field_copies(field, buffer, arrived, [*plain, *first, second])
    fetch = pltpu.make_async_copy(step_hour, hours, hours_arrived)
    fetch.start()
    fetch.wait()
    me = lax.axis_index("tm")
    groups = range(0, levels, 4)

    def summed(place, start, width, weights):
        four = sum_steps(lambda level: buffer[place, level, :, pl.ds(start, width)], weights)
        return [four(level) for level in groups]

    def store(out, offset, start, width, pieces):
        for place, x in enumerate(pack(pieces)):
            out[offset + place * 8 : offset + place * 8 + 8, pl.ds(start, width)] = x

    weights = hour_weights(hours, steps, range(HOURS), SUM_WIDTH)
    for place in range(len(plain)):
        copies[place].wait()

        @pl.loop(0, cells // SUM_WIDTH)
        def _(i):
            start = pl.multiple_of(i * SUM_WIDTH, SUM_WIDTH)
            sums = summed(place, start, SUM_WIDTH, weights)
            pieces = [(x, half) for half in range(HOURS) for x in sums]
            store(outs[place], 0, start, SUM_WIDTH, pieces)

    theirs_first, mine_first, theirs_second, mine_second = outs[len(plain) :]
    width = SUM_WIDTH // 2
    weights = hour_weights(hours, steps, (1 - me, me), width)
    for j in range(len(first) + 1):
        place = len(plain) + j
        copies[place].wait()
        offset = j * rows if j < len(first) else 0
        theirs, mine = (theirs_first, mine_first) if j < len(first) else (theirs_second, mine_second)

        @pl.loop(0, cut // width)
        def _(i):
            start = pl.multiple_of(i * width, width)
            sums = summed(place, start, width, weights) + summed(place, cut + start, width, weights)
            store(theirs, offset, start, width, [(x, 0) for x in sums])
            store(mine, offset, start, width, [(x, 1) for x in sums])


def hour_sums(plain, first, second, step_hour, field):
    levels, steps, _ = field.shape
    rows, cut = HOURS * levels, CELLS_DEV // 2
    vmem = pl.BlockSpec(memory_space=pltpu.VMEM)
    shapes = [(rows, CELLS_DEV)] * len(plain) + [(len(first) * rows, cut)] * 2 + [(rows, cut)] * 2
    count = len(plain) + len(first) + 1
    outs = pl.pallas_call(
        functools.partial(sums_kernel, plain, first, second),
        out_shape=[jax.ShapeDtypeStruct(shape, jnp.float32) for shape in shapes],
        in_specs=[pl.BlockSpec(memory_space=pl.ANY)] * 2,
        out_specs=[vmem] * len(shapes),
        scratch_shapes=[
            pltpu.VMEM((count, levels, steps, CELLS_DEV), jnp.float32),
            pltpu.SemaphoreType.DMA((count,)),
            pltpu.SMEM((steps,), jnp.int32),
            pltpu.SemaphoreType.DMA,
        ],
        compiler_params=pltpu.CompilerParams(vmem_limit_bytes=52 * MIB),
        cost_estimate=LIGHT,
        name="hour_sums",
    )(step_hour, field)
    return outs[: len(plain)], outs[len(plain) :]


def merge_first_kernel(mine, got, *refs):
    rows = refs[-1].shape[0]
    refs[-1][...] = mine[:rows] + got[:rows]


def merge_next_kernel(mine, got, *refs):
    rows = refs[-1].shape[0]
    refs[-1][...] = mine[rows:] + got[rows:]


def merge_last_kernel(mine, got, *refs):
    refs[-1][...] = mine[...] + got[...]


def fold(x):
    half = x.shape[1] // 2
    return jnp.concatenate([x[:, :half], x[:, half:]], axis=0)


def hold_kernel(x, *refs):
    refs[-1][...] = x[...]


def small_call(kernel, inputs, after, shapes, cost, name):
    vmem = pl.BlockSpec(memory_space=pltpu.VMEM)
    return pl.pallas_call(
        kernel,
        out_shape=[jax.ShapeDtypeStruct(shape, jnp.float32) for shape in shapes],
        in_specs=[vmem] * len(inputs) + [pl.BlockSpec(memory_space=pl.ANY)] * len(after),
        out_specs=[vmem] * len(shapes),
        compiler_params=pltpu.CompilerParams(vmem_limit_bytes=8 * MIB),
        cost_estimate=cost,
        name=name,
    )(*inputs, *after)


def output_rows(same_lev, hour, levels):
    lev = lax.axis_index("lev") % 2
    start = hour * 2 + (lev if same_lev else 1 - lev)
    return pl.ds(pl.multiple_of(start * 2 * levels, 2 * levels), 2 * levels)


def write_first_kernel(divisor, levels, chip, got_chip, first_hour, got_first, second_hour, far, got, out):
    me = lax.axis_index("tm")
    rows = 2 * levels
    near = keeps_near()
    sums = [(first_hour, got_first), (second_hour, got)]
    for hour in range(HOURS):
        here = slice(hour * rows, (hour + 1) * rows)

        @pl.when(near)
        def _():
            out[output_rows(True, hour, levels), :] = (chip[here] + got_chip[here]) / divisor
            out[output_rows(False, hour, levels), :] = (sums[hour][0][...] + sums[hour][1][...]) / divisor

        @pl.when(jnp.logical_not(near))
        def _():
            out[output_rows(False, hour, levels), :] = jnp.where(me == hour, far[...], got[...]) / divisor


def write_last_kernel(divisor, levels, plain, got_plain, last, got_last, begun, out, stage, written):
    me, even = lax.axis_index("tm"), lax.axis_index("sub") == 0

    @pl.when(jnp.logical_not(keeps_near()))
    def _():
        copies = []
        for hour in range(HOURS):
            here = slice(hour * levels, (hour + 1) * levels)
            first = plain[here] + got_plain[here]
            other = unfold(jnp.where(me == hour, last[...], got_last[...]))
            pair = [jnp.where(even, first, other), jnp.where(even, other, first)]
            stage[hour] = jnp.concatenate(pair, axis=0) / divisor
            target = out.at[output_rows(True, hour, levels), :]
            copies.append(pltpu.make_async_copy(stage.at[hour], target, written.at[hour]))
            copies[-1].start()
        for copy in copies:
            copy.wait()


def write_first(arrays, levels, divisor):
    kernel = functools.partial(write_first_kernel, divisor, levels)
    shape = (2 * arrays[0].shape[0], PIXELS_DEV)
    return small_call(kernel, arrays, [], [shape], LIGHT, "write_first")[0]


def write_last(begun, arrays, levels, divisor):
    vmem, anywhere = pl.BlockSpec(memory_space=pltpu.VMEM), pl.BlockSpec(memory_space=pl.ANY)
    return pl.pallas_call(
        functools.partial(write_last_kernel, divisor, levels),
        out_shape=jax.ShapeDtypeStruct(begun.shape, begun.dtype),
        in_specs=[vmem] * len(arrays) + [anywhere],
        out_specs=anywhere,
        scratch_shapes=[
            pltpu.VMEM((HOURS, 2 * levels, PIXELS_DEV), jnp.float32),
            pltpu.SemaphoreType.DMA((HOURS,)),
        ],
        input_output_aliases={len(arrays): 0},
        compiler_params=pltpu.CompilerParams(vmem_limit_bytes=8 * MIB),
        cost_estimate=LIGHT,
        name="write_last",
    )(*arrays, begun)


def hour_plan(level_field, tile_weight, tile_rows, tile_columns, live_count, step_hour):
    levs, subs, shards_tm = lax.axis_size("lev"), lax.axis_size("sub"), lax.axis_size("tm")
    half = levs // 2
    divisor = float(level_field.shape[0] * shards_tm // HOURS)
    field = jnp.transpose(level_field, (1, 0, 2))

    def to_peer(x, k, j):
        pairs = [(a * subs + b, (a ^ k) * subs + (b ^ j)) for a in range(levs) for b in range(subs)]
        return lax.ppermute(x, ("lev", "sub"), pairs)

    def swap(x):
        return lax.ppermute(x, "tm", [(0, 1), (1, 0)])

    plain = [(half, 0), (1, 0), (1, 1), (0, 1), (0, 0)]
    first, second = [(half + 1, j) for j in range(subs)], (half, 1)
    sums, (theirs_0, mine_0, theirs_1, mine_1) = hour_sums(plain, first, second, step_hour, field)
    rows = 2 * field.shape[0]
    folded = theirs_1.shape
    sibling = to_peer(sums[3], *plain[3])
    near_got = [to_peer(x, *peer) for x, peer in list(zip(sums, plain))[1:3]]
    got_0 = swap(theirs_0)
    plain_got = to_peer(sums[0], *plain[0])
    high, low = place_tiles(tile_rows, tile_columns, live_count, tile_weight, theirs_0)

    merged = small_call(
        merge_first_kernel, [mine_0, got_0], [high, sibling], [folded], LIGHT, "merge_first"
    )
    far_same = to_peer(merged[0], *first[0])
    merged = small_call(merge_next_kernel, [mine_0, got_0], merged, [folded], LIGHT, "merge_next")
    far_other = to_peer(merged[0], *first[1])
    theirs_1 = small_call(hold_kernel, [theirs_1], [plain_got, *merged], [folded], LIGHT, "hold")[0]
    got_1 = swap(theirs_1)
    both, send = remap_call(
        remap_both_kernel,
        [sums[4], sibling, plain_got],
        [theirs_1],
        [2 * rows] * 2,
        high,
        low,
        MEDIUM,
        "remap_both",
        [2 * rows] * 2,
    )
    got_both = swap(send)
    merged = small_call(
        merge_last_kernel, [mine_1, got_1], [both, near_got[0]], [folded], HEAVY, "merge_last"
    )
    second_got = to_peer(merged[0], *second)
    first_hour, second_hour = remap_call(
        remap_near_kernel, near_got, merged, [rows] * HOURS, high, low, LIGHT, "remap_near"
    )
    got_first = swap(first_hour)
    far, send = remap_call(
        remap_far_kernel, [far_same, far_other, second_hour], [], [rows] * 2, high, low, HEAVY, "remap_far"
    )
    got = swap(send)
    padded = -(-rows // 32) * 16
    (last,) = remap_call(
        remap_last_kernel,
        [second_got],
        [far],
        [(rows, PIXELS_DEV // 2)],
        high,
        low,
        HEAVY,
        "remap_last",
        [padded],
    )
    got_last = swap(last)
    levels = rows // 2
    out = write_first([both, got_both, first_hour, got_first, second_hour, far, got], levels, divisor)
    out = write_last(out, [both, got_both, last, got_last], levels, divisor)
    return out.reshape(HOURS, out.shape[0] // HOURS, PIXELS_DEV)


def general_plan(level_field, tile_weight, tile_rows, tile_columns, live_count, step_hour):
    steps, levels, cells = level_field.shape
    shards = lax.axis_size("lev") * lax.axis_size("sub")
    divisor = float(steps * lax.axis_size("tm") // HOURS)
    hours = jnp.arange(HOURS, dtype=jnp.int32)
    table = (step_hour[None, :] == hours[:, None]).astype(jnp.float32)
    fields = level_field.reshape(steps, levels, shards, cells // shards)
    partial = jnp.einsum("hs,slgc->ghlc", table, fields, precision=lax.Precision.HIGHEST)
    regrouped = lax.all_to_all(partial, ("lev", "sub"), split_axis=0, concat_axis=0, tiled=True)
    rows = jnp.transpose(regrouped, (1, 0, 2, 3)).reshape(-1, cells // shards)
    high, low = place_tiles(tile_rows, tile_columns, live_count, tile_weight)
    (out,) = remap_call(remap_rows_kernel, [rows], [], [rows.shape[0]], high, low, LIGHT, "remap_rows")
    out = out.reshape(HOURS, shards * levels, PIXELS_DEV) / divisor
    return lax.psum_scatter(out, "tm", scatter_dimension=1, tiled=True)


def solution(mesh):
    sizes = mesh.shape
    paired = sizes["tm"] == HOURS and sizes["lev"] == 4 and sizes["sub"] == 2

    def body(level_field, *others):
        steps, levels, _ = level_field.shape
        suits = paired and steps == 8 and levels % 4 == 0
        return (hour_plan if suits else general_plan)(level_field, *others)

    placed = (
        P(("groups", "tm"), ("lev", "sub"), None),
        P(None, ("lev", "sub")),
        P(("lev", "sub")),
        P(("lev", "sub")),
        P(("lev", "sub")),
        P("tm"),
    )
    return jax.shard_map(
        body,
        mesh=mesh,
        in_specs=placed,
        out_specs=P("groups", "tm", ("lev", "sub")),
        check_vma=False,
    )
```

```python
import functools

import jax
import jax.numpy as jnp
from jax import lax
from jax.experimental import pallas as pl
from jax.experimental.pallas import tpu as pltpu
from jax.sharding import PartitionSpec as P

TILE = 64
HOURS = 2
CT_DEV = 32
PT_DEV = 16
SLOTS = 128
CELLS_DEV = CT_DEV * TILE
PIXELS_DEV = PT_DEV * TILE
LANES = 2 * TILE
MIB = 1 << 20

LIGHT = pl.CostEstimate(flops=1, bytes_accessed=1, transcendentals=0)
MEDIUM = pl.CostEstimate(flops=2_500_000_000, bytes_accessed=1, transcendentals=0)
HEAVY = pl.CostEstimate(flops=10_000_000_000, bytes_accessed=1, transcendentals=0)

NN = (((1,), (0,)), ((), ()))


def split(x):
    high = x.astype(jnp.bfloat16)
    return high, (x - high.astype(jnp.float32)).astype(jnp.bfloat16)


def dot(a, b, dims):
    return lax.dot_general(a, b, dims, preferred_element_type=jnp.float32)


GROUP = 8


def place_kernel(rows, columns, count, weights, *refs):
    high, low, total = refs[-3:]
    band = 256

    @pl.loop(0, CELLS_DEV // band)
    def _(b):
        total[pl.ds(pl.multiple_of(b * band, band), band), :] = jnp.zeros((band, PIXELS_DEV), jnp.float32)

    lane_half = lax.broadcasted_iota(jnp.int32, (TILE, LANES), 1) // TILE
    live = count[0]

    @pl.loop(0, (live + GROUP - 1) // GROUP)
    def _(g):
        for pair in range(GROUP // 2):
            lanes = pl.ds(pl.multiple_of((g * (GROUP // 2) + pair) * LANES, LANES), LANES)
            tiles = weights[:, lanes]
            turned = jnp.transpose(jnp.concatenate([tiles, tiles], axis=0))
            for i in range(2):
                k = g * GROUP + pair * 2 + i
                row, column = rows[k], columns[k]
                side = jnp.where(k < live, row & 1, -1)
                at = (
                    pl.ds(pl.multiple_of(column * TILE, TILE), TILE),
                    pl.ds(pl.multiple_of((row >> 1) * LANES, LANES), LANES),
                )
                tile = turned[i * TILE : (i + 1) * TILE]
                total[at] = total[at] + jnp.where(lane_half == side, tile, 0.0)

    @pl.loop(0, CELLS_DEV // band)
    def _(b):
        at = pl.ds(pl.multiple_of(b * band, band), band)
        high[at, :], low[at, :] = split(total[at, :])


def place_tiles(rows, columns, count, weights, *after):
    smem = pl.BlockSpec(memory_space=pltpu.SMEM)
    vmem = pl.BlockSpec(memory_space=pltpu.VMEM)
    half = jax.ShapeDtypeStruct((CELLS_DEV, PIXELS_DEV), jnp.bfloat16)
    return pl.pallas_call(
        place_kernel,
        out_shape=(half, half),
        in_specs=[smem, smem, smem, vmem] + [pl.BlockSpec(memory_space=pl.ANY)] * len(after),
        out_specs=(vmem, vmem),
        scratch_shapes=[pltpu.VMEM((CELLS_DEV, PIXELS_DEV), jnp.float32)],
        compiler_params=pltpu.CompilerParams(vmem_limit_bytes=28 * MIB),
        cost_estimate=LIGHT,
        name="place_tiles",
    )(rows, columns, count, weights, *after)


PIXEL_BLOCK = 256


def remap_blocks(x, high, low):
    m = x.shape[0]
    x_high, x_low = split(x)
    both = jnp.concatenate([x_high, x_low], axis=0)
    for start in range(0, PIXELS_DEV, PIXEL_BLOCK):
        at = slice(start, start + PIXEL_BLOCK)
        first = dot(both, high[:, at], NN)
        yield at, first[:m] + first[m:] + dot(x_high, low[:, at], NN)


def remap_call(kernel, inputs, after, out_rows, high, low, cost, name, scratch_rows=()):
    vmem = pl.BlockSpec(memory_space=pltpu.VMEM)
    return pl.pallas_call(
        kernel,
        out_shape=[
            jax.ShapeDtypeStruct(rows if isinstance(rows, tuple) else (rows, PIXELS_DEV), jnp.float32)
            for rows in out_rows
        ],
        in_specs=[vmem] * (len(inputs) + 2) + [pl.BlockSpec(memory_space=pl.ANY)] * len(after),
        out_specs=[vmem] * len(out_rows),
        scratch_shapes=[pltpu.VMEM((rows, PIXELS_DEV), jnp.float32) for rows in scratch_rows],
        compiler_params=pltpu.CompilerParams(vmem_limit_bytes=24 * MIB),
        cost_estimate=cost,
        name=name,
    )(*inputs, high, low, *after)


def remap_rows_kernel(x, high, low, out):
    for at, result in remap_blocks(x[...], high, low):
        out[:, at] = result


def unfold(block):
    levels = block.shape[0] // 2
    return jnp.concatenate([block[:levels], block[levels:]], axis=1)


def far_rows(same_sub, other_sub):
    even = lax.axis_index("sub") == 0
    blocks = [jnp.where(even, same_sub, other_sub), jnp.where(even, other_sub, same_sub)]
    return [unfold(block) for block in blocks]


def keeps_near():
    return lax.axis_index("tm") == lax.axis_index("lev") // 2


def near_rows(same_sub, other_sub):
    even = lax.axis_index("sub") == 0
    return [jnp.where(even, same_sub, other_sub), jnp.where(even, other_sub, same_sub)]


def by_hour(result, levels):
    pieces = [result[start : start + levels] for start in range(0, 2 * HOURS * levels, levels)]
    return jnp.concatenate([pieces[sub * HOURS + hour] for hour in range(HOURS) for sub in range(2)], axis=0)


def sort_out(near_result, far_result, keep, send):
    near = keeps_near()

    @pl.when(near)
    def _():
        keep[...], send[...] = near_result[...], far_result[...]

    @pl.when(jnp.logical_not(near))
    def _():
        keep[...], send[...] = far_result[...], near_result[...]


def remap_both_kernel(own, sibling, plain, high, low, *refs):
    keep, send, near_result, far_result = refs[-4:]
    rows = own.shape[0]
    blocks = near_rows(own[...], sibling[...]) + [plain[...]]
    for at, result in remap_blocks(jnp.concatenate(blocks, axis=0), high, low):
        near_result[:, at] = by_hour(result, rows // HOURS)
        far_result[:rows, at] = result[2 * rows :]
    far_result[rows:] = jnp.zeros((rows, PIXELS_DEV), jnp.float32)
    sort_out(near_result, far_result, keep, send)


def remap_near_kernel(near_same, near_other, high, low, *refs):
    outs = refs[-HOURS:]
    rows = near_same.shape[0]
    x = jnp.concatenate(near_rows(near_same[...], near_other[...]), axis=0)
    for at, result in remap_blocks(x, high, low):
        result = by_hour(result, rows // HOURS)
        for hour, out in enumerate(outs):
            out[:, at] = result[hour * rows : (hour + 1) * rows]


def remap_far_kernel(same, other, near, high, low, *refs):
    far, send = refs[-2:]
    x = jnp.concatenate(far_rows(same[...], other[...]), axis=0)
    for at, result in remap_blocks(x, high, low):
        far[:, at] = result
        send[:, at] = jnp.where(keeps_near(), result, near[:, at])


def remap_last_kernel(block, high, low, *refs):
    out, total = refs[-2:]
    x = unfold(block[...])
    levels, cells = x.shape
    x = jnp.concatenate([x, jnp.zeros((-levels % 16, cells), jnp.float32)], axis=0)
    for at, result in remap_blocks(x, high, low):
        total[:, at] = result
    out[...] = fold(total[:levels])


def hour_weights(step_hour, steps, hours, width):
    row = lax.broadcasted_iota(jnp.int32, (steps, width), 0)
    first = jnp.zeros((steps, width), jnp.float32)
    second = jnp.zeros((steps, width), jnp.float32)
    for step in range(steps):
        first = jnp.where(row == step, jnp.where(step_hour[step] == hours[0], 1.0, 0.0), first)
        second = jnp.where(row == step, jnp.where(step_hour[step] == hours[1], 1.0, 0.0), second)
    upper = row < steps // 2
    return jnp.where(upper, first, second), jnp.where(upper, second, first)


def turn(x, rows):
    return pltpu.roll(x, rows % x.shape[0], 0)


def join(a, b, bit):
    clear = (lax.broadcasted_iota(jnp.int32, a.shape, 0) & bit) == 0
    kept, moved = jnp.where(clear, a, b), jnp.where(clear, b, a)
    return kept + jnp.where(clear, turn(moved, -bit), turn(moved, bit))


def sum_steps(block, weights):
    def halve(x):
        return x * weights[0] + turn(x * weights[1], 4)

    def four(level):
        a, b, c, d = (halve(block(level + i)) for i in range(4))
        return join(join(a, c, 2), join(b, d, 2), 1)

    return four


def pack(pieces):
    upper = lax.broadcasted_iota(jnp.int32, pieces[0][0].shape, 0) < 4
    at_half = [x if half == place % 2 else turn(x, 4) for place, (x, half) in enumerate(pieces)]
    return [jnp.where(upper, a, b) for a, b in zip(at_half[::2], at_half[1::2])]


def peer_shard(k, j):
    subs = lax.axis_size("sub")
    return (lax.axis_index("lev") ^ k) * subs + (lax.axis_index("sub") ^ j)


def field_copies(field, buffer, arrived, peers):
    copies = []
    for place, (k, j) in enumerate(peers):
        start = pl.multiple_of(peer_shard(k, j) * CELLS_DEV, CELLS_DEV)
        copy = pltpu.make_async_copy(
            field.at[:, :, pl.ds(start, CELLS_DEV)], buffer.at[place], arrived.at[place]
        )
        copy.start()
        copies.append(copy)
    return copies


SUM_WIDTH = 512


def sums_kernel(plain, first, second, step_hour, field, *refs):
    *outs, buffer, arrived, hours, hours_arrived = refs
    _, levels, steps, cells = buffer.shape
    rows, cut = HOURS * levels, cells // 2
    copies = field_copies(field, buffer, arrived, [*plain, *first, second])
    fetch = pltpu.make_async_copy(step_hour, hours, hours_arrived)
    fetch.start()
    fetch.wait()
    me = lax.axis_index("tm")
    groups = range(0, levels, 4)

    def summed(place, start, width, weights):
        four = sum_steps(lambda level: buffer[place, level, :, pl.ds(start, width)], weights)
        return [four(level) for level in groups]

    def store(out, offset, start, width, pieces):
        for place, x in enumerate(pack(pieces)):
            out[offset + place * 8 : offset + place * 8 + 8, pl.ds(start, width)] = x

    weights = hour_weights(hours, steps, range(HOURS), SUM_WIDTH)
    for place in range(len(plain)):
        copies[place].wait()

        @pl.loop(0, cells // SUM_WIDTH)
        def _(i):
            start = pl.multiple_of(i * SUM_WIDTH, SUM_WIDTH)
            sums = summed(place, start, SUM_WIDTH, weights)
            pieces = [(x, half) for half in range(HOURS) for x in sums]
            store(outs[place], 0, start, SUM_WIDTH, pieces)

    theirs_first, mine_first, theirs_second, mine_second = outs[len(plain) :]
    width = SUM_WIDTH // 2
    weights = hour_weights(hours, steps, (1 - me, me), width)
    for j in range(len(first) + 1):
        place = len(plain) + j
        copies[place].wait()
        offset = j * rows if j < len(first) else 0
        theirs, mine = (theirs_first, mine_first) if j < len(first) else (theirs_second, mine_second)

        @pl.loop(0, cut // width)
        def _(i):
            start = pl.multiple_of(i * width, width)
            sums = summed(place, start, width, weights) + summed(place, cut + start, width, weights)
            store(theirs, offset, start, width, [(x, 0) for x in sums])
            store(mine, offset, start, width, [(x, 1) for x in sums])


def hour_sums(plain, first, second, step_hour, field):
    levels, steps, _ = field.shape
    rows, cut = HOURS * levels, CELLS_DEV // 2
    vmem = pl.BlockSpec(memory_space=pltpu.VMEM)
    shapes = [(rows, CELLS_DEV)] * len(plain) + [(len(first) * rows, cut)] * 2 + [(rows, cut)] * 2
    count = len(plain) + len(first) + 1
    outs = pl.pallas_call(
        functools.partial(sums_kernel, plain, first, second),
        out_shape=[jax.ShapeDtypeStruct(shape, jnp.float32) for shape in shapes],
        in_specs=[pl.BlockSpec(memory_space=pl.ANY)] * 2,
        out_specs=[vmem] * len(shapes),
        scratch_shapes=[
            pltpu.VMEM((count, levels, steps, CELLS_DEV), jnp.float32),
            pltpu.SemaphoreType.DMA((count,)),
            pltpu.SMEM((steps,), jnp.int32),
            pltpu.SemaphoreType.DMA,
        ],
        compiler_params=pltpu.CompilerParams(vmem_limit_bytes=52 * MIB),
        cost_estimate=LIGHT,
        name="hour_sums",
    )(step_hour, field)
    return outs[: len(plain)], outs[len(plain) :]


def merge_first_kernel(mine, got, *refs):
    rows = refs[-1].shape[0]
    refs[-1][...] = mine[:rows] + got[:rows]


def merge_next_kernel(mine, got, *refs):
    rows = refs[-1].shape[0]
    refs[-1][...] = mine[rows:] + got[rows:]


def merge_last_kernel(mine, got, *refs):
    refs[-1][...] = mine[...] + got[...]


def fold(x):
    half = x.shape[1] // 2
    return jnp.concatenate([x[:, :half], x[:, half:]], axis=0)


def hold_kernel(x, *refs):
    refs[-1][...] = x[...]


def small_call(kernel, inputs, after, shapes, cost, name):
    vmem = pl.BlockSpec(memory_space=pltpu.VMEM)
    return pl.pallas_call(
        kernel,
        out_shape=[jax.ShapeDtypeStruct(shape, jnp.float32) for shape in shapes],
        in_specs=[vmem] * len(inputs) + [pl.BlockSpec(memory_space=pl.ANY)] * len(after),
        out_specs=[vmem] * len(shapes),
        compiler_params=pltpu.CompilerParams(vmem_limit_bytes=8 * MIB),
        cost_estimate=cost,
        name=name,
    )(*inputs, *after)


def output_rows(same_lev, hour, levels):
    lev = lax.axis_index("lev") % 2
    start = hour * 2 + (lev if same_lev else 1 - lev)
    return pl.ds(pl.multiple_of(start * 2 * levels, 2 * levels), 2 * levels)


def write_first_kernel(divisor, levels, chip, got_chip, first_hour, got_first, second_hour, far, got, out):
    me = lax.axis_index("tm")
    rows = 2 * levels
    near = keeps_near()
    sums = [(first_hour, got_first), (second_hour, got)]
    for hour in range(HOURS):
        here = slice(hour * rows, (hour + 1) * rows)

        @pl.when(near)
        def _():
            out[output_rows(True, hour, levels), :] = (chip[here] + got_chip[here]) / divisor
            out[output_rows(False, hour, levels), :] = (sums[hour][0][...] + sums[hour][1][...]) / divisor

        @pl.when(jnp.logical_not(near))
        def _():
            out[output_rows(False, hour, levels), :] = jnp.where(me == hour, far[...], got[...]) / divisor


def write_last_kernel(divisor, levels, plain, got_plain, last, got_last, begun, out, stage, written):
    me, even = lax.axis_index("tm"), lax.axis_index("sub") == 0

    @pl.when(jnp.logical_not(keeps_near()))
    def _():
        copies = []
        for hour in range(HOURS):
            here = slice(hour * levels, (hour + 1) * levels)
            first = plain[here] + got_plain[here]
            other = unfold(jnp.where(me == hour, last[...], got_last[...]))
            pair = [jnp.where(even, first, other), jnp.where(even, other, first)]
            stage[hour] = jnp.concatenate(pair, axis=0) / divisor
            target = out.at[output_rows(True, hour, levels), :]
            copies.append(pltpu.make_async_copy(stage.at[hour], target, written.at[hour]))
            copies[-1].start()
        for copy in copies:
            copy.wait()


def write_first(arrays, levels, divisor):
    kernel = functools.partial(write_first_kernel, divisor, levels)
    shape = (2 * arrays[0].shape[0], PIXELS_DEV)
    return small_call(kernel, arrays, [], [shape], LIGHT, "write_first")[0]


def write_last(begun, arrays, levels, divisor):
    vmem, anywhere = pl.BlockSpec(memory_space=pltpu.VMEM), pl.BlockSpec(memory_space=pl.ANY)
    return pl.pallas_call(
        functools.partial(write_last_kernel, divisor, levels),
        out_shape=jax.ShapeDtypeStruct(begun.shape, begun.dtype),
        in_specs=[vmem] * len(arrays) + [anywhere],
        out_specs=anywhere,
        scratch_shapes=[
            pltpu.VMEM((HOURS, 2 * levels, PIXELS_DEV), jnp.float32),
            pltpu.SemaphoreType.DMA((HOURS,)),
        ],
        input_output_aliases={len(arrays): 0},
        compiler_params=pltpu.CompilerParams(vmem_limit_bytes=8 * MIB),
        cost_estimate=LIGHT,
        name="write_last",
    )(*arrays, begun)


def hour_plan(level_field, tile_weight, tile_rows, tile_columns, live_count, step_hour):
    levs, subs, shards_tm = lax.axis_size("lev"), lax.axis_size("sub"), lax.axis_size("tm")
    half = levs // 2
    divisor = float(level_field.shape[0] * shards_tm // HOURS)
    field = jnp.transpose(level_field, (1, 0, 2))

    def to_peer(x, k, j):
        pairs = [(a * subs + b, (a ^ k) * subs + (b ^ j)) for a in range(levs) for b in range(subs)]
        return lax.ppermute(x, ("lev", "sub"), pairs)

    def swap(x):
        return lax.ppermute(x, "tm", [(0, 1), (1, 0)])

    plain = [(half, 0), (1, 0), (1, 1), (0, 1), (0, 0)]
    first, second = [(half + 1, j) for j in range(subs)], (half, 1)
    sums, (theirs_0, mine_0, theirs_1, mine_1) = hour_sums(plain, first, second, step_hour, field)
    rows = 2 * field.shape[0]
    folded = theirs_1.shape
    sibling = to_peer(sums[3], *plain[3])
    near_got = [to_peer(x, *peer) for x, peer in list(zip(sums, plain))[1:3]]
    got_0 = swap(theirs_0)
    plain_got = to_peer(sums[0], *plain[0])
    high, low = place_tiles(tile_rows, tile_columns, live_count, tile_weight, theirs_0)

    merged = small_call(
        merge_first_kernel, [mine_0, got_0], [high, sibling], [folded], LIGHT, "merge_first"
    )
    far_same = to_peer(merged[0], *first[0])
    merged = small_call(merge_next_kernel, [mine_0, got_0], merged, [folded], LIGHT, "merge_next")
    far_other = to_peer(merged[0], *first[1])
    theirs_1 = small_call(hold_kernel, [theirs_1], [plain_got, *merged], [folded], LIGHT, "hold")[0]
    got_1 = swap(theirs_1)
    both, send = remap_call(
        remap_both_kernel,
        [sums[4], sibling, plain_got],
        [theirs_1],
        [2 * rows] * 2,
        high,
        low,
        MEDIUM,
        "remap_both",
        [2 * rows] * 2,
    )
    got_both = swap(send)
    merged = small_call(
        merge_last_kernel, [mine_1, got_1], [both, near_got[0]], [folded], HEAVY, "merge_last"
    )
    second_got = to_peer(merged[0], *second)
    first_hour, second_hour = remap_call(
        remap_near_kernel, near_got, merged, [rows] * HOURS, high, low, LIGHT, "remap_near"
    )
    got_first = swap(first_hour)
    far, send = remap_call(
        remap_far_kernel, [far_same, far_other, second_hour], [], [rows] * 2, high, low, HEAVY, "remap_far"
    )
    got = swap(send)
    padded = -(-rows // 32) * 16
    (last,) = remap_call(
        remap_last_kernel,
        [second_got],
        [far],
        [(rows, PIXELS_DEV // 2)],
        high,
        low,
        HEAVY,
        "remap_last",
        [padded],
    )
    got_last = swap(last)
    levels = rows // 2
    out = write_first([both, got_both, first_hour, got_first, second_hour, far, got], levels, divisor)
    out = write_last(out, [both, got_both, last, got_last], levels, divisor)
    return out.reshape(HOURS, out.shape[0] // HOURS, PIXELS_DEV)


def general_plan(level_field, tile_weight, tile_rows, tile_columns, live_count, step_hour):
    steps, levels, cells = level_field.shape
    shards = lax.axis_size("lev") * lax.axis_size("sub")
    divisor = float(steps * lax.axis_size("tm") // HOURS)
    hours = jnp.arange(HOURS, dtype=jnp.int32)
    table = (step_hour[None, :] == hours[:, None]).astype(jnp.float32)
    fields = level_field.reshape(steps, levels, shards, cells // shards)
    partial = jnp.einsum("hs,slgc->ghlc", table, fields, precision=lax.Precision.HIGHEST)
    regrouped = lax.all_to_all(partial, ("lev", "sub"), split_axis=0, concat_axis=0, tiled=True)
    rows = jnp.transpose(regrouped, (1, 0, 2, 3)).reshape(-1, cells // shards)
    high, low = place_tiles(tile_rows, tile_columns, live_count, tile_weight)
    (out,) = remap_call(remap_rows_kernel, [rows], [], [rows.shape[0]], high, low, LIGHT, "remap_rows")
    out = out.reshape(HOURS, shards * levels, PIXELS_DEV) / divisor
    return lax.psum_scatter(out, "tm", scatter_dimension=1, tiled=True)


def solution(mesh):
    sizes = mesh.shape
    paired = sizes["tm"] == HOURS and sizes["lev"] == 4 and sizes["sub"] == 2

    def body(level_field, *others):
        steps, levels, _ = level_field.shape
        suits = paired and steps == 8 and levels % 4 == 0
        return (hour_plan if suits else general_plan)(level_field, *others)

    placed = (
        P(("groups", "tm"), ("lev", "sub"), None),
        P(None, ("lev", "sub")),
        P(("lev", "sub")),
        P(("lev", "sub")),
        P(("lev", "sub")),
        P("tm"),
    )
    return jax.shard_map(
        body,
        mesh=mesh,
        in_specs=placed,
        out_specs=P("groups", "tm", ("lev", "sub")),
        check_vma=False,
    )
```

```python
import functools

import jax
import jax.numpy as jnp
from jax import lax
from jax.experimental import pallas as pl
from jax.experimental.pallas import tpu as pltpu
from jax.sharding import PartitionSpec as P

TILE = 64
HOURS = 2
CT_DEV = 32
PT_DEV = 16
SLOTS = 128
CELLS_DEV = CT_DEV * TILE
PIXELS_DEV = PT_DEV * TILE
LANES = 2 * TILE
MIB = 1 << 20

LIGHT = pl.CostEstimate(flops=1, bytes_accessed=1, transcendentals=0)
MEDIUM = pl.CostEstimate(flops=2_500_000_000, bytes_accessed=1, transcendentals=0)
HEAVY = pl.CostEstimate(flops=10_000_000_000, bytes_accessed=1, transcendentals=0)

NN = (((1,), (0,)), ((), ()))


def split(x):
    high = x.astype(jnp.bfloat16)
    return high, (x - high.astype(jnp.float32)).astype(jnp.bfloat16)


def dot(a, b, dims):
    return lax.dot_general(a, b, dims, preferred_element_type=jnp.float32)


GROUP = 8


def place_kernel(rows, columns, count, weights, *refs):
    high, low, total = refs[-3:]
    band = 256

    @pl.loop(0, CELLS_DEV // band)
    def _(b):
        total[pl.ds(pl.multiple_of(b * band, band), band), :] = jnp.zeros((band, PIXELS_DEV), jnp.float32)

    lane_half = lax.broadcasted_iota(jnp.int32, (TILE, LANES), 1) // TILE
    live = count[0]

    @pl.loop(0, (live + GROUP - 1) // GROUP)
    def _(g):
        for pair in range(GROUP // 2):
            lanes = pl.ds(pl.multiple_of((g * (GROUP // 2) + pair) * LANES, LANES), LANES)
            tiles = weights[:, lanes]
            turned = jnp.transpose(jnp.concatenate([tiles, tiles], axis=0))
            for i in range(2):
                k = g * GROUP + pair * 2 + i
                row, column = rows[k], columns[k]
                side = jnp.where(k < live, row & 1, -1)
                at = (
                    pl.ds(pl.multiple_of(column * TILE, TILE), TILE),
                    pl.ds(pl.multiple_of((row >> 1) * LANES, LANES), LANES),
                )
                tile = turned[i * TILE : (i + 1) * TILE]
                total[at] = total[at] + jnp.where(lane_half == side, tile, 0.0)

    @pl.loop(0, CELLS_DEV // band)
    def _(b):
        at = pl.ds(pl.multiple_of(b * band, band), band)
        high[at, :], low[at, :] = split(total[at, :])


def place_tiles(rows, columns, count, weights, *after):
    smem = pl.BlockSpec(memory_space=pltpu.SMEM)
    vmem = pl.BlockSpec(memory_space=pltpu.VMEM)
    half = jax.ShapeDtypeStruct((CELLS_DEV, PIXELS_DEV), jnp.bfloat16)
    return pl.pallas_call(
        place_kernel,
        out_shape=(half, half),
        in_specs=[smem, smem, smem, vmem] + [pl.BlockSpec(memory_space=pl.ANY)] * len(after),
        out_specs=(vmem, vmem),
        scratch_shapes=[pltpu.VMEM((CELLS_DEV, PIXELS_DEV), jnp.float32)],
        compiler_params=pltpu.CompilerParams(vmem_limit_bytes=28 * MIB),
        cost_estimate=LIGHT,
        name="place_tiles",
    )(rows, columns, count, weights, *after)


PIXEL_BLOCK = 256


def remap_blocks(x, high, low):
    m = x.shape[0]
    x_high, x_low = split(x)
    both = jnp.concatenate([x_high, x_low], axis=0)
    for start in range(0, PIXELS_DEV, PIXEL_BLOCK):
        at = slice(start, start + PIXEL_BLOCK)
        first = dot(both, high[:, at], NN)
        yield at, first[:m] + first[m:] + dot(x_high, low[:, at], NN)


def remap_call(kernel, inputs, after, out_rows, high, low, cost, name, scratch_rows=()):
    vmem = pl.BlockSpec(memory_space=pltpu.VMEM)
    return pl.pallas_call(
        kernel,
        out_shape=[
            jax.ShapeDtypeStruct(rows if isinstance(rows, tuple) else (rows, PIXELS_DEV), jnp.float32)
            for rows in out_rows
        ],
        in_specs=[vmem] * (len(inputs) + 2) + [pl.BlockSpec(memory_space=pl.ANY)] * len(after),
        out_specs=[vmem] * len(out_rows),
        scratch_shapes=[pltpu.VMEM((rows, PIXELS_DEV), jnp.float32) for rows in scratch_rows],
        compiler_params=pltpu.CompilerParams(vmem_limit_bytes=24 * MIB),
        cost_estimate=cost,
        name=name,
    )(*inputs, high, low, *after)


def remap_rows_kernel(x, high, low, out):
    for at, result in remap_blocks(x[...], high, low):
        out[:, at] = result


def unfold(block):
    levels = block.shape[0] // 2
    return jnp.concatenate([block[:levels], block[levels:]], axis=1)


def far_rows(same_sub, other_sub):
    even = lax.axis_index("sub") == 0
    blocks = [jnp.where(even, same_sub, other_sub), jnp.where(even, other_sub, same_sub)]
    return [unfold(block) for block in blocks]


def keeps_near():
    return lax.axis_index("tm") == lax.axis_index("lev") // 2


def near_rows(same_sub, other_sub):
    even = lax.axis_index("sub") == 0
    return [jnp.where(even, same_sub, other_sub), jnp.where(even, other_sub, same_sub)]


def by_hour(result, levels):
    pieces = [result[start : start + levels] for start in range(0, 2 * HOURS * levels, levels)]
    return jnp.concatenate([pieces[sub * HOURS + hour] for hour in range(HOURS) for sub in range(2)], axis=0)


def sort_out(near_result, far_result, keep, send):
    near = keeps_near()

    @pl.when(near)
    def _():
        keep[...], send[...] = near_result[...], far_result[...]

    @pl.when(jnp.logical_not(near))
    def _():
        keep[...], send[...] = far_result[...], near_result[...]


def remap_both_kernel(own, sibling, plain, high, low, *refs):
    keep, send, near_result, far_result = refs[-4:]
    rows = own.shape[0]
    blocks = near_rows(own[...], sibling[...]) + [plain[...]]
    for at, result in remap_blocks(jnp.concatenate(blocks, axis=0), high, low):
        near_result[:, at] = by_hour(result, rows // HOURS)
        far_result[:rows, at] = result[2 * rows :]
    far_result[rows:] = jnp.zeros((rows, PIXELS_DEV), jnp.float32)
    sort_out(near_result, far_result, keep, send)


def remap_near_kernel(near_same, near_other, high, low, *refs):
    outs = refs[-HOURS:]
    rows = near_same.shape[0]
    x = jnp.concatenate(near_rows(near_same[...], near_other[...]), axis=0)
    for at, result in remap_blocks(x, high, low):
        result = by_hour(result, rows // HOURS)
        for hour, out in enumerate(outs):
            out[:, at] = result[hour * rows : (hour + 1) * rows]


def remap_far_kernel(same, other, near, high, low, *refs):
    far, send = refs[-2:]
    x = jnp.concatenate(far_rows(same[...], other[...]), axis=0)
    for at, result in remap_blocks(x, high, low):
        far[:, at] = result
        send[:, at] = jnp.where(keeps_near(), result, near[:, at])


def remap_last_kernel(block, high, low, *refs):
    out, total = refs[-2:]
    x = unfold(block[...])
    levels, cells = x.shape
    x = jnp.concatenate([x, jnp.zeros((-levels % 16, cells), jnp.float32)], axis=0)
    for at, result in remap_blocks(x, high, low):
        total[:, at] = result
    out[...] = fold(total[:levels])


def hour_weights(step_hour, steps, hours, width):
    row = lax.broadcasted_iota(jnp.int32, (steps, width), 0)
    first = jnp.zeros((steps, width), jnp.float32)
    second = jnp.zeros((steps, width), jnp.float32)
    for step in range(steps):
        first = jnp.where(row == step, jnp.where(step_hour[step] == hours[0], 1.0, 0.0), first)
        second = jnp.where(row == step, jnp.where(step_hour[step] == hours[1], 1.0, 0.0), second)
    upper = row < steps // 2
    return jnp.where(upper, first, second), jnp.where(upper, second, first)


def turn(x, rows):
    return pltpu.roll(x, rows % x.shape[0], 0)


def join(a, b, bit):
    clear = (lax.broadcasted_iota(jnp.int32, a.shape, 0) & bit) == 0
    kept, moved = jnp.where(clear, a, b), jnp.where(clear, b, a)
    return kept + jnp.where(clear, turn(moved, -bit), turn(moved, bit))


def sum_steps(block, weights):
    def halve(x):
        return x * weights[0] + turn(x * weights[1], 4)

    def four(level):
        a, b, c, d = (halve(block(level + i)) for i in range(4))
        return join(join(a, c, 2), join(b, d, 2), 1)

    return four


def pack(pieces):
    upper = lax.broadcasted_iota(jnp.int32, pieces[0][0].shape, 0) < 4
    at_half = [x if half == place % 2 else turn(x, 4) for place, (x, half) in enumerate(pieces)]
    return [jnp.where(upper, a, b) for a, b in zip(at_half[::2], at_half[1::2])]


def peer_shard(k, j):
    subs = lax.axis_size("sub")
    return (lax.axis_index("lev") ^ k) * subs + (lax.axis_index("sub") ^ j)


def field_copies(field, buffer, arrived, peers):
    copies = []
    for place, (k, j) in enumerate(peers):
        start = pl.multiple_of(peer_shard(k, j) * CELLS_DEV, CELLS_DEV)
        copy = pltpu.make_async_copy(
            field.at[:, :, pl.ds(start, CELLS_DEV)], buffer.at[place], arrived.at[place]
        )
        copy.start()
        copies.append(copy)
    return copies


SUM_WIDTH = 512


def sums_kernel(plain, first, second, step_hour, field, *refs):
    *outs, buffer, arrived, hours, hours_arrived = refs
    _, levels, steps, cells = buffer.shape
    rows, cut = HOURS * levels, cells // 2
    copies = field_copies(field, buffer, arrived, [*plain, *first, second])
    fetch = pltpu.make_async_copy(step_hour, hours, hours_arrived)
    fetch.start()
    fetch.wait()
    me = lax.axis_index("tm")
    groups = range(0, levels, 4)

    def summed(place, start, width, weights):
        four = sum_steps(lambda level: buffer[place, level, :, pl.ds(start, width)], weights)
        return [four(level) for level in groups]

    def store(out, offset, start, width, pieces):
        for place, x in enumerate(pack(pieces)):
            out[offset + place * 8 : offset + place * 8 + 8, pl.ds(start, width)] = x

    weights = hour_weights(hours, steps, range(HOURS), SUM_WIDTH)
    for place in range(len(plain)):
        copies[place].wait()

        @pl.loop(0, cells // SUM_WIDTH)
        def _(i):
            start = pl.multiple_of(i * SUM_WIDTH, SUM_WIDTH)
            sums = summed(place, start, SUM_WIDTH, weights)
            pieces = [(x, half) for half in range(HOURS) for x in sums]
            store(outs[place], 0, start, SUM_WIDTH, pieces)

    theirs_first, mine_first, theirs_second, mine_second = outs[len(plain) :]
    width = SUM_WIDTH // 2
    weights = hour_weights(hours, steps, (1 - me, me), width)
    for j in range(len(first) + 1):
        place = len(plain) + j
        copies[place].wait()
        offset = j * rows if j < len(first) else 0
        theirs, mine = (theirs_first, mine_first) if j < len(first) else (theirs_second, mine_second)

        @pl.loop(0, cut // width)
        def _(i):
            start = pl.multiple_of(i * width, width)
            sums = summed(place, start, width, weights) + summed(place, cut + start, width, weights)
            store(theirs, offset, start, width, [(x, 0) for x in sums])
            store(mine, offset, start, width, [(x, 1) for x in sums])


def hour_sums(plain, first, second, step_hour, field):
    levels, steps, _ = field.shape
    rows, cut = HOURS * levels, CELLS_DEV // 2
    vmem = pl.BlockSpec(memory_space=pltpu.VMEM)
    shapes = [(rows, CELLS_DEV)] * len(plain) + [(len(first) * rows, cut)] * 2 + [(rows, cut)] * 2
    count = len(plain) + len(first) + 1
    outs = pl.pallas_call(
        functools.partial(sums_kernel, plain, first, second),
        out_shape=[jax.ShapeDtypeStruct(shape, jnp.float32) for shape in shapes],
        in_specs=[pl.BlockSpec(memory_space=pl.ANY)] * 2,
        out_specs=[vmem] * len(shapes),
        scratch_shapes=[
            pltpu.VMEM((count, levels, steps, CELLS_DEV), jnp.float32),
            pltpu.SemaphoreType.DMA((count,)),
            pltpu.SMEM((steps,), jnp.int32),
            pltpu.SemaphoreType.DMA,
        ],
        compiler_params=pltpu.CompilerParams(vmem_limit_bytes=52 * MIB),
        cost_estimate=LIGHT,
        name="hour_sums",
    )(step_hour, field)
    return outs[: len(plain)], outs[len(plain) :]


def merge_first_kernel(mine, got, *refs):
    rows = refs[-1].shape[0]
    refs[-1][...] = mine[:rows] + got[:rows]


def merge_next_kernel(mine, got, *refs):
    rows = refs[-1].shape[0]
    refs[-1][...] = mine[rows:] + got[rows:]


def merge_last_kernel(mine, got, *refs):
    refs[-1][...] = mine[...] + got[...]


def fold(x):
    half = x.shape[1] // 2
    return jnp.concatenate([x[:, :half], x[:, half:]], axis=0)


def hold_kernel(x, *refs):
    refs[-1][...] = x[...]


def small_call(kernel, inputs, after, shapes, cost, name):
    vmem = pl.BlockSpec(memory_space=pltpu.VMEM)
    return pl.pallas_call(
        kernel,
        out_shape=[jax.ShapeDtypeStruct(shape, jnp.float32) for shape in shapes],
        in_specs=[vmem] * len(inputs) + [pl.BlockSpec(memory_space=pl.ANY)] * len(after),
        out_specs=[vmem] * len(shapes),
        compiler_params=pltpu.CompilerParams(vmem_limit_bytes=8 * MIB),
        cost_estimate=cost,
        name=name,
    )(*inputs, *after)


def output_rows(same_lev, hour, levels):
    lev = lax.axis_index("lev") % 2
    start = hour * 2 + (lev if same_lev else 1 - lev)
    return pl.ds(pl.multiple_of(start * 2 * levels, 2 * levels), 2 * levels)


def write_first_kernel(divisor, levels, chip, got_chip, first_hour, got_first, second_hour, far, got, out):
    me = lax.axis_index("tm")
    rows = 2 * levels
    near = keeps_near()
    sums = [(first_hour, got_first), (second_hour, got)]
    for hour in range(HOURS):
        here = slice(hour * rows, (hour + 1) * rows)

        @pl.when(near)
        def _():
            out[output_rows(True, hour, levels), :] = (chip[here] + got_chip[here]) / divisor
            out[output_rows(False, hour, levels), :] = (sums[hour][0][...] + sums[hour][1][...]) / divisor

        @pl.when(jnp.logical_not(near))
        def _():
            out[output_rows(False, hour, levels), :] = jnp.where(me == hour, far[...], got[...]) / divisor


def write_last_kernel(divisor, levels, plain, got_plain, last, got_last, begun, out, stage, written):
    me, even = lax.axis_index("tm"), lax.axis_index("sub") == 0

    @pl.when(jnp.logical_not(keeps_near()))
    def _():
        copies = []
        for hour in range(HOURS):
            here = slice(hour * levels, (hour + 1) * levels)
            first = plain[here] + got_plain[here]
            other = unfold(jnp.where(me == hour, last[...], got_last[...]))
            pair = [jnp.where(even, first, other), jnp.where(even, other, first)]
            stage[hour] = jnp.concatenate(pair, axis=0) / divisor
            target = out.at[output_rows(True, hour, levels), :]
            copies.append(pltpu.make_async_copy(stage.at[hour], target, written.at[hour]))
            copies[-1].start()
        for copy in copies:
            copy.wait()


def write_first(arrays, levels, divisor):
    kernel = functools.partial(write_first_kernel, divisor, levels)
    shape = (2 * arrays[0].shape[0], PIXELS_DEV)
    return small_call(kernel, arrays, [], [shape], LIGHT, "write_first")[0]


def write_last(begun, arrays, levels, divisor):
    vmem, anywhere = pl.BlockSpec(memory_space=pltpu.VMEM), pl.BlockSpec(memory_space=pl.ANY)
    return pl.pallas_call(
        functools.partial(write_last_kernel, divisor, levels),
        out_shape=jax.ShapeDtypeStruct(begun.shape, begun.dtype),
        in_specs=[vmem] * len(arrays) + [anywhere],
        out_specs=anywhere,
        scratch_shapes=[
            pltpu.VMEM((HOURS, 2 * levels, PIXELS_DEV), jnp.float32),
            pltpu.SemaphoreType.DMA((HOURS,)),
        ],
        input_output_aliases={len(arrays): 0},
        compiler_params=pltpu.CompilerParams(vmem_limit_bytes=8 * MIB),
        cost_estimate=LIGHT,
        name="write_last",
    )(*arrays, begun)


def hour_plan(level_field, tile_weight, tile_rows, tile_columns, live_count, step_hour):
    levs, subs, shards_tm = lax.axis_size("lev"), lax.axis_size("sub"), lax.axis_size("tm")
    half = levs // 2
    divisor = float(level_field.shape[0] * shards_tm // HOURS)
    field = jnp.transpose(level_field, (1, 0, 2))

    def to_peer(x, k, j):
        pairs = [(a * subs + b, (a ^ k) * subs + (b ^ j)) for a in range(levs) for b in range(subs)]
        return lax.ppermute(x, ("lev", "sub"), pairs)

    def hand_over(x):
        pairs = [(a * shards_tm + a // half, a * shards_tm + 1 - a // half) for a in range(levs)]
        return lax.ppermute(x, ("lev", "tm"), pairs)

    def swap(x):
        return lax.ppermute(x, "tm", [(0, 1), (1, 0)])

    plain = [(half, 0), (1, 0), (1, 1), (0, 1), (0, 0)]
    first, second = [(half + 1, j) for j in range(subs)], (half, 1)
    sums, (theirs_0, mine_0, theirs_1, mine_1) = hour_sums(plain, first, second, step_hour, field)
    rows = 2 * field.shape[0]
    folded = theirs_1.shape
    sibling = to_peer(sums[3], *plain[3])
    near_got = [to_peer(x, *peer) for x, peer in list(zip(sums, plain))[1:3]]
    got_0 = swap(theirs_0)
    plain_got = to_peer(sums[0], *plain[0])
    high, low = place_tiles(tile_rows, tile_columns, live_count, tile_weight, theirs_0)

    merged = small_call(
        merge_first_kernel, [mine_0, got_0], [high, sibling], [folded], LIGHT, "merge_first"
    )
    far_same = to_peer(merged[0], *first[0])
    merged = small_call(merge_next_kernel, [mine_0, got_0], merged, [folded], LIGHT, "merge_next")
    far_other = to_peer(merged[0], *first[1])
    theirs_1 = small_call(hold_kernel, [theirs_1], [plain_got, *merged], [folded], LIGHT, "hold")[0]
    got_1 = swap(theirs_1)
    both, send = remap_call(
        remap_both_kernel,
        [sums[4], sibling, plain_got],
        [theirs_1],
        [2 * rows] * 2,
        high,
        low,
        MEDIUM,
        "remap_both",
        [2 * rows] * 2,
    )
    got_both = swap(send)
    merged = small_call(
        merge_last_kernel, [mine_1, got_1], [both, near_got[0]], [folded], HEAVY, "merge_last"
    )
    second_got = to_peer(merged[0], *second)
    first_hour, second_hour = remap_call(
        remap_near_kernel, near_got, merged, [rows] * HOURS, high, low, LIGHT, "remap_near"
    )
    got_first = swap(first_hour)
    far, send = remap_call(
        remap_far_kernel, [far_same, far_other, second_hour], [], [rows] * 2, high, low, HEAVY, "remap_far"
    )
    got = swap(send)
    padded = -(-rows // 32) * 16
    (last,) = remap_call(
        remap_last_kernel,
        [second_got],
        [far],
        [(rows, PIXELS_DEV // 2)],
        high,
        low,
        HEAVY,
        "remap_last",
        [padded],
    )
    got_last = hand_over(last)
    levels = rows // 2
    out = write_first([both, got_both, first_hour, got_first, second_hour, far, got], levels, divisor)
    out = write_last(out, [both, got_both, last, got_last], levels, divisor)
    return out.reshape(HOURS, out.shape[0] // HOURS, PIXELS_DEV)


def general_plan(level_field, tile_weight, tile_rows, tile_columns, live_count, step_hour):
    steps, levels, cells = level_field.shape
    shards = lax.axis_size("lev") * lax.axis_size("sub")
    divisor = float(steps * lax.axis_size("tm") // HOURS)
    hours = jnp.arange(HOURS, dtype=jnp.int32)
    table = (step_hour[None, :] == hours[:, None]).astype(jnp.float32)
    fields = level_field.reshape(steps, levels, shards, cells // shards)
    partial = jnp.einsum("hs,slgc->ghlc", table, fields, precision=lax.Precision.HIGHEST)
    regrouped = lax.all_to_all(partial, ("lev", "sub"), split_axis=0, concat_axis=0, tiled=True)
    rows = jnp.transpose(regrouped, (1, 0, 2, 3)).reshape(-1, cells // shards)
    high, low = place_tiles(tile_rows, tile_columns, live_count, tile_weight)
    (out,) = remap_call(remap_rows_kernel, [rows], [], [rows.shape[0]], high, low, LIGHT, "remap_rows")
    out = out.reshape(HOURS, shards * levels, PIXELS_DEV) / divisor
    return lax.psum_scatter(out, "tm", scatter_dimension=1, tiled=True)


def solution(mesh):
    sizes = mesh.shape
    paired = sizes["tm"] == HOURS and sizes["lev"] == 4 and sizes["sub"] == 2

    def body(level_field, *others):
        steps, levels, _ = level_field.shape
        suits = paired and steps == 8 and levels % 4 == 0
        return (hour_plan if suits else general_plan)(level_field, *others)

    placed = (
        P(("groups", "tm"), ("lev", "sub"), None),
        P(None, ("lev", "sub")),
        P(("lev", "sub")),
        P(("lev", "sub")),
        P(("lev", "sub")),
        P("tm"),
    )
    return jax.shard_map(
        body,
        mesh=mesh,
        in_specs=placed,
        out_specs=P("groups", "tm", ("lev", "sub")),
        check_vma=False,
    )
```

```python
import functools

import jax
import jax.numpy as jnp
from jax import lax
from jax.experimental import pallas as pl
from jax.experimental.pallas import tpu as pltpu
from jax.sharding import PartitionSpec as P

TILE = 64
HOURS = 2
CT_DEV = 32
PT_DEV = 16
SLOTS = 128
CELLS_DEV = CT_DEV * TILE
PIXELS_DEV = PT_DEV * TILE
LANES = 2 * TILE
MIB = 1 << 20

LIGHT = pl.CostEstimate(flops=1, bytes_accessed=1, transcendentals=0)
MEDIUM = pl.CostEstimate(flops=2_500_000_000, bytes_accessed=1, transcendentals=0)
HEAVY = pl.CostEstimate(flops=10_000_000_000, bytes_accessed=1, transcendentals=0)

NN = (((1,), (0,)), ((), ()))


def split(x):
    high = x.astype(jnp.bfloat16)
    return high, (x - high.astype(jnp.float32)).astype(jnp.bfloat16)


def dot(a, b, dims):
    return lax.dot_general(a, b, dims, preferred_element_type=jnp.float32)


GROUP = 8


def place_kernel(rows, columns, count, weights, *refs):
    high, low, total = refs[-3:]
    band = 256

    @pl.loop(0, CELLS_DEV // band)
    def _(b):
        total[pl.ds(pl.multiple_of(b * band, band), band), :] = jnp.zeros((band, PIXELS_DEV), jnp.float32)

    lane_half = lax.broadcasted_iota(jnp.int32, (TILE, LANES), 1) // TILE
    live = count[0]

    @pl.loop(0, (live + GROUP - 1) // GROUP)
    def _(g):
        for pair in range(GROUP // 2):
            lanes = pl.ds(pl.multiple_of((g * (GROUP // 2) + pair) * LANES, LANES), LANES)
            tiles = weights[:, lanes]
            turned = jnp.transpose(jnp.concatenate([tiles, tiles], axis=0))
            for i in range(2):
                k = g * GROUP + pair * 2 + i
                row, column = rows[k], columns[k]
                side = jnp.where(k < live, row & 1, -1)
                at = (
                    pl.ds(pl.multiple_of(column * TILE, TILE), TILE),
                    pl.ds(pl.multiple_of((row >> 1) * LANES, LANES), LANES),
                )
                tile = turned[i * TILE : (i + 1) * TILE]
                total[at] = total[at] + jnp.where(lane_half == side, tile, 0.0)

    @pl.loop(0, CELLS_DEV // band)
    def _(b):
        at = pl.ds(pl.multiple_of(b * band, band), band)
        high[at, :], low[at, :] = split(total[at, :])


def place_tiles(rows, columns, count, weights, *after):
    smem = pl.BlockSpec(memory_space=pltpu.SMEM)
    vmem = pl.BlockSpec(memory_space=pltpu.VMEM)
    half = jax.ShapeDtypeStruct((CELLS_DEV, PIXELS_DEV), jnp.bfloat16)
    return pl.pallas_call(
        place_kernel,
        out_shape=(half, half),
        in_specs=[smem, smem, smem, vmem] + [pl.BlockSpec(memory_space=pl.ANY)] * len(after),
        out_specs=(vmem, vmem),
        scratch_shapes=[pltpu.VMEM((CELLS_DEV, PIXELS_DEV), jnp.float32)],
        compiler_params=pltpu.CompilerParams(vmem_limit_bytes=28 * MIB),
        cost_estimate=LIGHT,
        name="place_tiles",
    )(rows, columns, count, weights, *after)


PIXEL_BLOCK = 256


def remap_blocks(x, high, low):
    m = x.shape[0]
    x_high, x_low = split(x)
    both = jnp.concatenate([x_high, x_low], axis=0)
    for start in range(0, PIXELS_DEV, PIXEL_BLOCK):
        at = slice(start, start + PIXEL_BLOCK)
        first = dot(both, high[:, at], NN)
        yield at, first[:m] + first[m:] + dot(x_high, low[:, at], NN)


def remap_call(kernel, inputs, after, out_rows, high, low, cost, name, scratch_rows=()):
    vmem = pl.BlockSpec(memory_space=pltpu.VMEM)
    return pl.pallas_call(
        kernel,
        out_shape=[
            jax.ShapeDtypeStruct(rows if isinstance(rows, tuple) else (rows, PIXELS_DEV), jnp.float32)
            for rows in out_rows
        ],
        in_specs=[vmem] * (len(inputs) + 2) + [pl.BlockSpec(memory_space=pl.ANY)] * len(after),
        out_specs=[vmem] * len(out_rows),
        scratch_shapes=[pltpu.VMEM((rows, PIXELS_DEV), jnp.float32) for rows in scratch_rows],
        compiler_params=pltpu.CompilerParams(vmem_limit_bytes=24 * MIB),
        cost_estimate=cost,
        name=name,
    )(*inputs, high, low, *after)


def remap_rows_kernel(x, high, low, out):
    for at, result in remap_blocks(x[...], high, low):
        out[:, at] = result


def unfold(block):
    levels = block.shape[0] // 2
    return jnp.concatenate([block[:levels], block[levels:]], axis=1)


def far_rows(same_sub, other_sub):
    even = lax.axis_index("sub") == 0
    blocks = [jnp.where(even, same_sub, other_sub), jnp.where(even, other_sub, same_sub)]
    return [unfold(block) for block in blocks]


def keeps_near():
    return lax.axis_index("tm") == lax.axis_index("lev") // 2


def near_rows(same_sub, other_sub):
    even = lax.axis_index("sub") == 0
    return [jnp.where(even, same_sub, other_sub), jnp.where(even, other_sub, same_sub)]


def by_hour(result, levels):
    pieces = [result[start : start + levels] for start in range(0, 2 * HOURS * levels, levels)]
    return jnp.concatenate([pieces[sub * HOURS + hour] for hour in range(HOURS) for sub in range(2)], axis=0)


def sort_out(near_result, far_result, keep, send):
    near = keeps_near()

    @pl.when(near)
    def _():
        keep[...], send[...] = near_result[...], far_result[...]

    @pl.when(jnp.logical_not(near))
    def _():
        keep[...], send[...] = far_result[...], near_result[...]


def remap_both_kernel(own, sibling, plain, high, low, *refs):
    keep, send, near_result, far_result = refs[-4:]
    rows = own.shape[0]
    blocks = near_rows(own[...], sibling[...]) + [plain[...]]
    for at, result in remap_blocks(jnp.concatenate(blocks, axis=0), high, low):
        near_result[:, at] = by_hour(result, rows // HOURS)
        far_result[:rows, at] = result[2 * rows :]
    far_result[rows:] = jnp.zeros((rows, PIXELS_DEV), jnp.float32)
    sort_out(near_result, far_result, keep, send)


def remap_near_kernel(near_same, near_other, high, low, *refs):
    rows = near_same.shape[0]
    x = jnp.concatenate(near_rows(near_same[...], near_other[...]), axis=0)
    for at, result in remap_blocks(x, high, low):
        refs[-1][:, at] = by_hour(result, rows // HOURS)


def remap_far_kernel(same, other, high, low, *refs):
    x = jnp.concatenate(far_rows(same[...], other[...]), axis=0)
    for at, result in remap_blocks(x, high, low):
        refs[-1][:, at] = result


def remap_last_kernel(block, high, low, *refs):
    out, total = refs[-2:]
    x = unfold(block[...])
    levels, cells = x.shape
    x = jnp.concatenate([x, jnp.zeros((-levels % 16, cells), jnp.float32)], axis=0)
    for at, result in remap_blocks(x, high, low):
        total[:, at] = result
    out[...] = fold(total[:levels])


def hour_weights(step_hour, steps, hours, width):
    row = lax.broadcasted_iota(jnp.int32, (steps, width), 0)
    first = jnp.zeros((steps, width), jnp.float32)
    second = jnp.zeros((steps, width), jnp.float32)
    for step in range(steps):
        first = jnp.where(row == step, jnp.where(step_hour[step] == hours[0], 1.0, 0.0), first)
        second = jnp.where(row == step, jnp.where(step_hour[step] == hours[1], 1.0, 0.0), second)
    upper = row < steps // 2
    return jnp.where(upper, first, second), jnp.where(upper, second, first)


def turn(x, rows):
    return pltpu.roll(x, rows % x.shape[0], 0)


def join(a, b, bit):
    clear = (lax.broadcasted_iota(jnp.int32, a.shape, 0) & bit) == 0
    kept, moved = jnp.where(clear, a, b), jnp.where(clear, b, a)
    return kept + jnp.where(clear, turn(moved, -bit), turn(moved, bit))


def sum_steps(block, weights):
    def halve(x):
        return x * weights[0] + turn(x * weights[1], 4)

    def four(level):
        a, b, c, d = (halve(block(level + i)) for i in range(4))
        return join(join(a, c, 2), join(b, d, 2), 1)

    return four


def pack(pieces):
    upper = lax.broadcasted_iota(jnp.int32, pieces[0][0].shape, 0) < 4
    at_half = [x if half == place % 2 else turn(x, 4) for place, (x, half) in enumerate(pieces)]
    return [jnp.where(upper, a, b) for a, b in zip(at_half[::2], at_half[1::2])]


def peer_shard(k, j):
    subs = lax.axis_size("sub")
    return (lax.axis_index("lev") ^ k) * subs + (lax.axis_index("sub") ^ j)


def field_copies(field, buffer, arrived, peers):
    copies = []
    for place, (k, j) in enumerate(peers):
        start = pl.multiple_of(peer_shard(k, j) * CELLS_DEV, CELLS_DEV)
        copy = pltpu.make_async_copy(
            field.at[:, :, pl.ds(start, CELLS_DEV)], buffer.at[place], arrived.at[place]
        )
        copy.start()
        copies.append(copy)
    return copies


SUM_WIDTH = 512


def sums_kernel(plain, first, second, step_hour, field, *refs):
    *outs, buffer, arrived, hours, hours_arrived = refs
    _, levels, steps, cells = buffer.shape
    rows, cut = HOURS * levels, cells // 2
    copies = field_copies(field, buffer, arrived, [*plain, *first, second])
    fetch = pltpu.make_async_copy(step_hour, hours, hours_arrived)
    fetch.start()
    fetch.wait()
    me = lax.axis_index("tm")
    groups = range(0, levels, 4)

    def summed(place, start, width, weights):
        four = sum_steps(lambda level: buffer[place, level, :, pl.ds(start, width)], weights)
        return [four(level) for level in groups]

    def store(out, offset, start, width, pieces):
        for place, x in enumerate(pack(pieces)):
            out[offset + place * 8 : offset + place * 8 + 8, pl.ds(start, width)] = x

    weights = hour_weights(hours, steps, range(HOURS), SUM_WIDTH)
    for place in range(len(plain)):
        copies[place].wait()

        @pl.loop(0, cells // SUM_WIDTH)
        def _(i):
            start = pl.multiple_of(i * SUM_WIDTH, SUM_WIDTH)
            sums = summed(place, start, SUM_WIDTH, weights)
            pieces = [(x, half) for half in range(HOURS) for x in sums]
            store(outs[place], 0, start, SUM_WIDTH, pieces)

    theirs_first, mine_first, theirs_second, mine_second = outs[len(plain) :]
    width = SUM_WIDTH // 2
    weights = hour_weights(hours, steps, (1 - me, me), width)
    for j in range(len(first) + 1):
        place = len(plain) + j
        copies[place].wait()
        offset = j * rows if j < len(first) else 0
        theirs, mine = (theirs_first, mine_first) if j < len(first) else (theirs_second, mine_second)

        @pl.loop(0, cut // width)
        def _(i):
            start = pl.multiple_of(i * width, width)
            sums = summed(place, start, width, weights) + summed(place, cut + start, width, weights)
            store(theirs, offset, start, width, [(x, 0) for x in sums])
            store(mine, offset, start, width, [(x, 1) for x in sums])


def hour_sums(plain, first, second, step_hour, field):
    levels, steps, _ = field.shape
    rows, cut = HOURS * levels, CELLS_DEV // 2
    vmem = pl.BlockSpec(memory_space=pltpu.VMEM)
    shapes = [(rows, CELLS_DEV)] * len(plain) + [(len(first) * rows, cut)] * 2 + [(rows, cut)] * 2
    count = len(plain) + len(first) + 1
    outs = pl.pallas_call(
        functools.partial(sums_kernel, plain, first, second),
        out_shape=[jax.ShapeDtypeStruct(shape, jnp.float32) for shape in shapes],
        in_specs=[pl.BlockSpec(memory_space=pl.ANY)] * 2,
        out_specs=[vmem] * len(shapes),
        scratch_shapes=[
            pltpu.VMEM((count, levels, steps, CELLS_DEV), jnp.float32),
            pltpu.SemaphoreType.DMA((count,)),
            pltpu.SMEM((steps,), jnp.int32),
            pltpu.SemaphoreType.DMA,
        ],
        compiler_params=pltpu.CompilerParams(vmem_limit_bytes=52 * MIB),
        cost_estimate=LIGHT,
        name="hour_sums",
    )(step_hour, field)
    return outs[: len(plain)], outs[len(plain) :]


def merge_first_kernel(mine, got, *refs):
    rows = refs[-1].shape[0]
    refs[-1][...] = mine[:rows] + got[:rows]


def merge_next_kernel(mine, got, *refs):
    rows = refs[-1].shape[0]
    refs[-1][...] = mine[rows:] + got[rows:]


def merge_last_kernel(mine, got, *refs):
    refs[-1][...] = mine[...] + got[...]


def fold(x):
    half = x.shape[1] // 2
    return jnp.concatenate([x[:, :half], x[:, half:]], axis=0)


def hold_kernel(x, *refs):
    refs[-1][...] = x[...]


def small_call(kernel, inputs, after, shapes, cost, name):
    vmem = pl.BlockSpec(memory_space=pltpu.VMEM)
    return pl.pallas_call(
        kernel,
        out_shape=[jax.ShapeDtypeStruct(shape, jnp.float32) for shape in shapes],
        in_specs=[vmem] * len(inputs) + [pl.BlockSpec(memory_space=pl.ANY)] * len(after),
        out_specs=[vmem] * len(shapes),
        compiler_params=pltpu.CompilerParams(vmem_limit_bytes=8 * MIB),
        cost_estimate=cost,
        name=name,
    )(*inputs, *after)


def output_rows(same_lev, hour, levels):
    lev = lax.axis_index("lev") % 2
    start = hour * 2 + (lev if same_lev else 1 - lev)
    return pl.ds(pl.multiple_of(start * 2 * levels, 2 * levels), 2 * levels)


def write_first_kernel(divisor, levels, chip, got_chip, lev_near, got_near, far, got_far, out):
    me = lax.axis_index("tm")
    rows = 2 * levels
    near = keeps_near()
    for hour in range(HOURS):
        here = slice(hour * rows, (hour + 1) * rows)

        @pl.when(near)
        def _():
            out[output_rows(True, hour, levels), :] = (chip[here] + got_chip[here]) / divisor
            out[output_rows(False, hour, levels), :] = (lev_near[here] + got_near[here]) / divisor

        @pl.when(jnp.logical_not(near))
        def _():
            out[output_rows(False, hour, levels), :] = jnp.where(me == hour, far[...], got_far[...]) / divisor


def write_last_kernel(divisor, levels, plain, got_plain, last, got_last, begun, out, stage, written):
    me, even = lax.axis_index("tm"), lax.axis_index("sub") == 0

    @pl.when(jnp.logical_not(keeps_near()))
    def _():
        copies = []
        for hour in range(HOURS):
            here = slice(hour * levels, (hour + 1) * levels)
            first = plain[here] + got_plain[here]
            other = unfold(jnp.where(me == hour, last[...], got_last[...]))
            pair = [jnp.where(even, first, other), jnp.where(even, other, first)]
            stage[hour] = jnp.concatenate(pair, axis=0) / divisor
            target = out.at[output_rows(True, hour, levels), :]
            copies.append(pltpu.make_async_copy(stage.at[hour], target, written.at[hour]))
            copies[-1].start()
        for copy in copies:
            copy.wait()


def write_first(arrays, levels, divisor):
    kernel = functools.partial(write_first_kernel, divisor, levels)
    shape = (2 * arrays[0].shape[0], PIXELS_DEV)
    return small_call(kernel, arrays, [], [shape], LIGHT, "write_first")[0]


def write_last(begun, arrays, levels, divisor):
    vmem, anywhere = pl.BlockSpec(memory_space=pltpu.VMEM), pl.BlockSpec(memory_space=pl.ANY)
    return pl.pallas_call(
        functools.partial(write_last_kernel, divisor, levels),
        out_shape=jax.ShapeDtypeStruct(begun.shape, begun.dtype),
        in_specs=[vmem] * len(arrays) + [anywhere],
        out_specs=anywhere,
        scratch_shapes=[
            pltpu.VMEM((HOURS, 2 * levels, PIXELS_DEV), jnp.float32),
            pltpu.SemaphoreType.DMA((HOURS,)),
        ],
        input_output_aliases={len(arrays): 0},
        compiler_params=pltpu.CompilerParams(vmem_limit_bytes=8 * MIB),
        cost_estimate=LIGHT,
        name="write_last",
    )(*arrays, begun)


def hour_plan(level_field, tile_weight, tile_rows, tile_columns, live_count, step_hour):
    levs, subs, shards_tm = lax.axis_size("lev"), lax.axis_size("sub"), lax.axis_size("tm")
    half = levs // 2
    divisor = float(level_field.shape[0] * shards_tm // HOURS)
    field = jnp.transpose(level_field, (1, 0, 2))

    def to_peer(x, k, j):
        pairs = [(a * subs + b, (a ^ k) * subs + (b ^ j)) for a in range(levs) for b in range(subs)]
        return lax.ppermute(x, ("lev", "sub"), pairs)

    def hand_over(x):
        pairs = [(a * shards_tm + a // half, a * shards_tm + 1 - a // half) for a in range(levs)]
        return lax.ppermute(x, ("lev", "tm"), pairs)

    def swap(x):
        return lax.ppermute(x, "tm", [(0, 1), (1, 0)])

    plain = [(half, 0), (1, 0), (1, 1), (0, 1), (0, 0)]
    first, second = [(half + 1, j) for j in range(subs)], (half, 1)
    sums, (theirs_0, mine_0, theirs_1, mine_1) = hour_sums(plain, first, second, step_hour, field)
    rows = 2 * field.shape[0]
    folded = theirs_1.shape
    sibling = to_peer(sums[3], *plain[3])
    near_got = [to_peer(x, *peer) for x, peer in list(zip(sums, plain))[1:3]]
    got_0 = swap(theirs_0)
    plain_got = to_peer(sums[0], *plain[0])
    high, low = place_tiles(tile_rows, tile_columns, live_count, tile_weight, theirs_0)

    merged = small_call(
        merge_first_kernel, [mine_0, got_0], [high, sibling], [folded], LIGHT, "merge_first"
    )
    far_same = to_peer(merged[0], *first[0])
    merged = small_call(merge_next_kernel, [mine_0, got_0], merged, [folded], LIGHT, "merge_next")
    far_other = to_peer(merged[0], *first[1])
    theirs_1 = small_call(hold_kernel, [theirs_1], [plain_got, *merged], [folded], LIGHT, "hold")[0]
    got_1 = swap(theirs_1)
    both, send = remap_call(
        remap_both_kernel,
        [sums[4], sibling, plain_got],
        [theirs_1],
        [2 * rows] * 2,
        high,
        low,
        MEDIUM,
        "remap_both",
        [2 * rows] * 2,
    )
    got_both = swap(send)
    merged = small_call(
        merge_last_kernel, [mine_1, got_1], [both, near_got[0]], [folded], HEAVY, "merge_last"
    )
    second_got = to_peer(merged[0], *second)
    (near,) = remap_call(
        remap_near_kernel, near_got, merged, [2 * rows], high, low, LIGHT, "remap_near"
    )
    got_near = swap(near)
    (far,) = remap_call(remap_far_kernel, [far_same, far_other], [near], [rows], high, low, HEAVY, "remap_far")
    got_far = hand_over(far)
    padded = -(-rows // 32) * 16
    (last,) = remap_call(
        remap_last_kernel,
        [second_got],
        [far],
        [(rows, PIXELS_DEV // 2)],
        high,
        low,
        HEAVY,
        "remap_last",
        [padded],
    )
    got_last = swap(last)
    levels = rows // 2
    out = write_first([both, got_both, near, got_near, far, got_far], levels, divisor)
    out = write_last(out, [both, got_both, last, got_last], levels, divisor)
    return out.reshape(HOURS, out.shape[0] // HOURS, PIXELS_DEV)


def general_plan(level_field, tile_weight, tile_rows, tile_columns, live_count, step_hour):
    steps, levels, cells = level_field.shape
    shards = lax.axis_size("lev") * lax.axis_size("sub")
    divisor = float(steps * lax.axis_size("tm") // HOURS)
    hours = jnp.arange(HOURS, dtype=jnp.int32)
    table = (step_hour[None, :] == hours[:, None]).astype(jnp.float32)
    fields = level_field.reshape(steps, levels, shards, cells // shards)
    partial = jnp.einsum("hs,slgc->ghlc", table, fields, precision=lax.Precision.HIGHEST)
    regrouped = lax.all_to_all(partial, ("lev", "sub"), split_axis=0, concat_axis=0, tiled=True)
    rows = jnp.transpose(regrouped, (1, 0, 2, 3)).reshape(-1, cells // shards)
    high, low = place_tiles(tile_rows, tile_columns, live_count, tile_weight)
    (out,) = remap_call(remap_rows_kernel, [rows], [], [rows.shape[0]], high, low, LIGHT, "remap_rows")
    out = out.reshape(HOURS, shards * levels, PIXELS_DEV) / divisor
    return lax.psum_scatter(out, "tm", scatter_dimension=1, tiled=True)


def solution(mesh):
    sizes = mesh.shape
    paired = sizes["tm"] == HOURS and sizes["lev"] == 4 and sizes["sub"] == 2

    def body(level_field, *others):
        steps, levels, _ = level_field.shape
        suits = paired and steps == 8 and levels % 4 == 0
        return (hour_plan if suits else general_plan)(level_field, *others)

    placed = (
        P(("groups", "tm"), ("lev", "sub"), None),
        P(None, ("lev", "sub")),
        P(("lev", "sub")),
        P(("lev", "sub")),
        P(("lev", "sub")),
        P("tm"),
    )
    return jax.shard_map(
        body,
        mesh=mesh,
        in_specs=placed,
        out_specs=P("groups", "tm", ("lev", "sub")),
        check_vma=False,
    )
```

```python
import functools

import jax
import jax.numpy as jnp
from jax import lax
from jax.experimental import pallas as pl
from jax.experimental.pallas import tpu as pltpu
from jax.sharding import PartitionSpec as P

TILE = 64
HOURS = 2
CT_DEV = 32
PT_DEV = 16
SLOTS = 128
CELLS_DEV = CT_DEV * TILE
PIXELS_DEV = PT_DEV * TILE
LANES = 2 * TILE
MIB = 1 << 20

LIGHT = pl.CostEstimate(flops=1, bytes_accessed=1, transcendentals=0)
MEDIUM = pl.CostEstimate(flops=2_500_000_000, bytes_accessed=1, transcendentals=0)
HEAVY = pl.CostEstimate(flops=10_000_000_000, bytes_accessed=1, transcendentals=0)

NN = (((1,), (0,)), ((), ()))


def split(x):
    high = x.astype(jnp.bfloat16)
    return high, (x - high.astype(jnp.float32)).astype(jnp.bfloat16)


def dot(a, b, dims):
    return lax.dot_general(a, b, dims, preferred_element_type=jnp.float32)


GROUP = 8


def place_kernel(rows, columns, count, weights, *refs):
    high, low, total = refs[-3:]
    band = 256

    @pl.loop(0, CELLS_DEV // band)
    def _(b):
        total[pl.ds(pl.multiple_of(b * band, band), band), :] = jnp.zeros((band, PIXELS_DEV), jnp.float32)

    lane_half = lax.broadcasted_iota(jnp.int32, (TILE, LANES), 1) // TILE
    live = count[0]

    @pl.loop(0, (live + GROUP - 1) // GROUP)
    def _(g):
        for pair in range(GROUP // 2):
            lanes = pl.ds(pl.multiple_of((g * (GROUP // 2) + pair) * LANES, LANES), LANES)
            tiles = weights[:, lanes]
            turned = jnp.transpose(jnp.concatenate([tiles, tiles], axis=0))
            for i in range(2):
                k = g * GROUP + pair * 2 + i
                row, column = rows[k], columns[k]
                side = jnp.where(k < live, row & 1, -1)
                at = (
                    pl.ds(pl.multiple_of(column * TILE, TILE), TILE),
                    pl.ds(pl.multiple_of((row >> 1) * LANES, LANES), LANES),
                )
                tile = turned[i * TILE : (i + 1) * TILE]
                total[at] = total[at] + jnp.where(lane_half == side, tile, 0.0)

    @pl.loop(0, CELLS_DEV // band)
    def _(b):
        at = pl.ds(pl.multiple_of(b * band, band), band)
        high[at, :], low[at, :] = split(total[at, :])


def place_tiles(rows, columns, count, weights, *after):
    smem = pl.BlockSpec(memory_space=pltpu.SMEM)
    vmem = pl.BlockSpec(memory_space=pltpu.VMEM)
    half = jax.ShapeDtypeStruct((CELLS_DEV, PIXELS_DEV), jnp.bfloat16)
    return pl.pallas_call(
        place_kernel,
        out_shape=(half, half),
        in_specs=[smem, smem, smem, vmem] + [pl.BlockSpec(memory_space=pl.ANY)] * len(after),
        out_specs=(vmem, vmem),
        scratch_shapes=[pltpu.VMEM((CELLS_DEV, PIXELS_DEV), jnp.float32)],
        compiler_params=pltpu.CompilerParams(vmem_limit_bytes=28 * MIB),
        cost_estimate=LIGHT,
        name="place_tiles",
    )(rows, columns, count, weights, *after)


PIXEL_BLOCK = 256


def remap_blocks(x, high, low):
    m = x.shape[0]
    x_high, x_low = split(x)
    both = jnp.concatenate([x_high, x_low], axis=0)
    for start in range(0, PIXELS_DEV, PIXEL_BLOCK):
        at = slice(start, start + PIXEL_BLOCK)
        first = dot(both, high[:, at], NN)
        yield at, first[:m] + first[m:] + dot(x_high, low[:, at], NN)


def remap_call(kernel, inputs, after, out_rows, high, low, cost, name, scratch_rows=()):
    vmem = pl.BlockSpec(memory_space=pltpu.VMEM)
    return pl.pallas_call(
        kernel,
        out_shape=[
            jax.ShapeDtypeStruct(rows if isinstance(rows, tuple) else (rows, PIXELS_DEV), jnp.float32)
            for rows in out_rows
        ],
        in_specs=[vmem] * (len(inputs) + 2) + [pl.BlockSpec(memory_space=pl.ANY)] * len(after),
        out_specs=[vmem] * len(out_rows),
        scratch_shapes=[pltpu.VMEM((rows, PIXELS_DEV), jnp.float32) for rows in scratch_rows],
        compiler_params=pltpu.CompilerParams(vmem_limit_bytes=24 * MIB),
        cost_estimate=cost,
        name=name,
    )(*inputs, high, low, *after)


def remap_rows_kernel(x, high, low, out):
    for at, result in remap_blocks(x[...], high, low):
        out[:, at] = result


def unfold(block):
    levels = block.shape[0] // 2
    return jnp.concatenate([block[:levels], block[levels:]], axis=1)


def far_rows(same_sub, other_sub):
    even = lax.axis_index("sub") == 0
    blocks = [jnp.where(even, same_sub, other_sub), jnp.where(even, other_sub, same_sub)]
    return [unfold(block) for block in blocks]


def keeps_near():
    return lax.axis_index("tm") == lax.axis_index("lev") // 2


def near_rows(same_sub, other_sub):
    even = lax.axis_index("sub") == 0
    return [jnp.where(even, same_sub, other_sub), jnp.where(even, other_sub, same_sub)]


def by_hour(result, levels):
    pieces = [result[start : start + levels] for start in range(0, 2 * HOURS * levels, levels)]
    return jnp.concatenate([pieces[sub * HOURS + hour] for hour in range(HOURS) for sub in range(2)], axis=0)


def sort_out(near_result, far_result, keep, send):
    near = keeps_near()

    @pl.when(near)
    def _():
        keep[...], send[...] = near_result[...], far_result[...]

    @pl.when(jnp.logical_not(near))
    def _():
        keep[...], send[...] = far_result[...], near_result[...]


def remap_both_kernel(own, sibling, plain, high, low, *refs):
    keep, send, near_result, far_result = refs[-4:]
    rows = own.shape[0]
    blocks = near_rows(own[...], sibling[...]) + [plain[...]]
    for at, result in remap_blocks(jnp.concatenate(blocks, axis=0), high, low):
        near_result[:, at] = by_hour(result, rows // HOURS)
        far_result[:rows, at] = result[2 * rows :]
    far_result[rows:] = jnp.zeros((rows, PIXELS_DEV), jnp.float32)
    sort_out(near_result, far_result, keep, send)


def remap_near_kernel(near_same, near_other, high, low, *refs):
    outs = refs[-HOURS:]
    rows = near_same.shape[0]
    x = jnp.concatenate(near_rows(near_same[...], near_other[...]), axis=0)
    for at, result in remap_blocks(x, high, low):
        result = by_hour(result, rows // HOURS)
        for hour, out in enumerate(outs):
            out[:, at] = result[hour * rows : (hour + 1) * rows]


def remap_far_kernel(same, other, near, high, low, *refs):
    far, send = refs[-2:]
    x = jnp.concatenate(far_rows(same[...], other[...]), axis=0)
    for at, result in remap_blocks(x, high, low):
        far[:, at] = result
        send[:, at] = jnp.where(keeps_near(), result, near[:, at])


def remap_last_kernel(block, high, low, *refs):
    out, total = refs[-2:]
    x = unfold(block[...])
    levels, cells = x.shape
    x = jnp.concatenate([x, jnp.zeros((-levels % 16, cells), jnp.float32)], axis=0)
    for at, result in remap_blocks(x, high, low):
        total[:, at] = result
    out[...] = fold(total[:levels])


def hour_weights(step_hour, steps, hours, width):
    row = lax.broadcasted_iota(jnp.int32, (steps, width), 0)
    first = jnp.zeros((steps, width), jnp.float32)
    second = jnp.zeros((steps, width), jnp.float32)
    for step in range(steps):
        first = jnp.where(row == step, jnp.where(step_hour[step] == hours[0], 1.0, 0.0), first)
        second = jnp.where(row == step, jnp.where(step_hour[step] == hours[1], 1.0, 0.0), second)
    upper = row < steps // 2
    return jnp.where(upper, first, second), jnp.where(upper, second, first)


def turn(x, rows):
    return pltpu.roll(x, rows % x.shape[0], 0)


def join(a, b, bit):
    clear = (lax.broadcasted_iota(jnp.int32, a.shape, 0) & bit) == 0
    kept, moved = jnp.where(clear, a, b), jnp.where(clear, b, a)
    return kept + jnp.where(clear, turn(moved, -bit), turn(moved, bit))


def sum_steps(block, weights):
    def halve(x):
        return x * weights[0] + turn(x * weights[1], 4)

    def four(level):
        a, b, c, d = (halve(block(level + i)) for i in range(4))
        return join(join(a, c, 2), join(b, d, 2), 1)

    return four


def pack(pieces):
    upper = lax.broadcasted_iota(jnp.int32, pieces[0][0].shape, 0) < 4
    at_half = [x if half == place % 2 else turn(x, 4) for place, (x, half) in enumerate(pieces)]
    return [jnp.where(upper, a, b) for a, b in zip(at_half[::2], at_half[1::2])]


def peer_shard(k, j):
    subs = lax.axis_size("sub")
    return (lax.axis_index("lev") ^ k) * subs + (lax.axis_index("sub") ^ j)


def field_copies(field, buffer, arrived, peers):
    copies = []
    for place, (k, j) in enumerate(peers):
        start = pl.multiple_of(peer_shard(k, j) * CELLS_DEV, CELLS_DEV)
        copy = pltpu.make_async_copy(
            field.at[:, :, pl.ds(start, CELLS_DEV)], buffer.at[place], arrived.at[place]
        )
        copy.start()
        copies.append(copy)
    return copies


SUM_WIDTH = 512


def sums_kernel(plain, first, second, step_hour, field, *refs):
    *outs, buffer, arrived, hours, hours_arrived = refs
    _, levels, steps, cells = buffer.shape
    rows, cut = HOURS * levels, cells // 2
    copies = field_copies(field, buffer, arrived, [*plain, *first, second])
    fetch = pltpu.make_async_copy(step_hour, hours, hours_arrived)
    fetch.start()
    fetch.wait()
    me = lax.axis_index("tm")
    groups = range(0, levels, 4)

    def summed(place, start, width, weights):
        four = sum_steps(lambda level: buffer[place, level, :, pl.ds(start, width)], weights)
        return [four(level) for level in groups]

    def store(out, offset, start, width, pieces):
        for place, x in enumerate(pack(pieces)):
            out[offset + place * 8 : offset + place * 8 + 8, pl.ds(start, width)] = x

    weights = hour_weights(hours, steps, range(HOURS), SUM_WIDTH)
    for place in range(len(plain)):
        copies[place].wait()

        @pl.loop(0, cells // SUM_WIDTH)
        def _(i):
            start = pl.multiple_of(i * SUM_WIDTH, SUM_WIDTH)
            sums = summed(place, start, SUM_WIDTH, weights)
            pieces = [(x, half) for half in range(HOURS) for x in sums]
            store(outs[place], 0, start, SUM_WIDTH, pieces)

    theirs_first, mine_first, theirs_second, mine_second = outs[len(plain) :]
    width = SUM_WIDTH // 2
    weights = hour_weights(hours, steps, (1 - me, me), width)
    for j in range(len(first) + 1):
        place = len(plain) + j
        copies[place].wait()
        offset = j * rows if j < len(first) else 0
        theirs, mine = (theirs_first, mine_first) if j < len(first) else (theirs_second, mine_second)

        @pl.loop(0, cut // width)
        def _(i):
            start = pl.multiple_of(i * width, width)
            sums = summed(place, start, width, weights) + summed(place, cut + start, width, weights)
            store(theirs, offset, start, width, [(x, 0) for x in sums])
            store(mine, offset, start, width, [(x, 1) for x in sums])


def hour_sums(plain, first, second, step_hour, field):
    levels, steps, _ = field.shape
    rows, cut = HOURS * levels, CELLS_DEV // 2
    vmem = pl.BlockSpec(memory_space=pltpu.VMEM)
    shapes = [(rows, CELLS_DEV)] * len(plain) + [(len(first) * rows, cut)] * 2 + [(rows, cut)] * 2
    count = len(plain) + len(first) + 1
    outs = pl.pallas_call(
        functools.partial(sums_kernel, plain, first, second),
        out_shape=[jax.ShapeDtypeStruct(shape, jnp.float32) for shape in shapes],
        in_specs=[pl.BlockSpec(memory_space=pl.ANY)] * 2,
        out_specs=[vmem] * len(shapes),
        scratch_shapes=[
            pltpu.VMEM((count, levels, steps, CELLS_DEV), jnp.float32),
            pltpu.SemaphoreType.DMA((count,)),
            pltpu.SMEM((steps,), jnp.int32),
            pltpu.SemaphoreType.DMA,
        ],
        compiler_params=pltpu.CompilerParams(vmem_limit_bytes=52 * MIB),
        cost_estimate=LIGHT,
        name="hour_sums",
    )(step_hour, field)
    return outs[: len(plain)], outs[len(plain) :]


def merge_first_kernel(mine, got, *refs):
    rows = refs[-1].shape[0]
    refs[-1][...] = mine[:rows] + got[:rows]


def merge_next_kernel(mine, got, *refs):
    rows = refs[-1].shape[0]
    refs[-1][...] = mine[rows:] + got[rows:]


def merge_last_kernel(mine, got, *refs):
    refs[-1][...] = mine[...] + got[...]


def fold(x):
    half = x.shape[1] // 2
    return jnp.concatenate([x[:, :half], x[:, half:]], axis=0)


def hold_kernel(x, *refs):
    refs[-1][...] = x[...]


def small_call(kernel, inputs, after, shapes, cost, name):
    vmem = pl.BlockSpec(memory_space=pltpu.VMEM)
    return pl.pallas_call(
        kernel,
        out_shape=[jax.ShapeDtypeStruct(shape, jnp.float32) for shape in shapes],
        in_specs=[vmem] * len(inputs) + [pl.BlockSpec(memory_space=pl.ANY)] * len(after),
        out_specs=[vmem] * len(shapes),
        compiler_params=pltpu.CompilerParams(vmem_limit_bytes=8 * MIB),
        cost_estimate=cost,
        name=name,
    )(*inputs, *after)


def output_rows(same_lev, hour, levels):
    lev = lax.axis_index("lev") % 2
    start = hour * 2 + (lev if same_lev else 1 - lev)
    return pl.ds(pl.multiple_of(start * 2 * levels, 2 * levels), 2 * levels)


def write_first_kernel(divisor, levels, chip, got_chip, first_hour, got_first, second_hour, far, got, out):
    me = lax.axis_index("tm")
    rows = 2 * levels
    near = keeps_near()
    sums = [(first_hour, got_first), (second_hour, got)]
    for hour in range(HOURS):
        here = slice(hour * rows, (hour + 1) * rows)

        @pl.when(near)
        def _():
            out[output_rows(True, hour, levels), :] = (chip[here] + got_chip[here]) / divisor
            out[output_rows(False, hour, levels), :] = (sums[hour][0][...] + sums[hour][1][...]) / divisor

        @pl.when(jnp.logical_not(near))
        def _():
            out[output_rows(False, hour, levels), :] = jnp.where(me == hour, far[...], got[...]) / divisor


def write_last_kernel(divisor, levels, plain, got_plain, last, got_last, begun, out, stage, written):
    me, even = lax.axis_index("tm"), lax.axis_index("sub") == 0

    @pl.when(jnp.logical_not(keeps_near()))
    def _():
        copies = []
        for hour in range(HOURS):
            here = slice(hour * levels, (hour + 1) * levels)
            first = plain[here] + got_plain[here]
            other = unfold(jnp.where(me == hour, last[...], got_last[...]))
            pair = [jnp.where(even, first, other), jnp.where(even, other, first)]
            stage[hour] = jnp.concatenate(pair, axis=0) / divisor
            target = out.at[output_rows(True, hour, levels), :]
            copies.append(pltpu.make_async_copy(stage.at[hour], target, written.at[hour]))
            copies[-1].start()
        for copy in copies:
            copy.wait()


def write_first(arrays, levels, divisor):
    kernel = functools.partial(write_first_kernel, divisor, levels)
    shape = (2 * arrays[0].shape[0], PIXELS_DEV)
    return small_call(kernel, arrays, [], [shape], LIGHT, "write_first")[0]


def write_last(begun, arrays, levels, divisor):
    vmem, anywhere = pl.BlockSpec(memory_space=pltpu.VMEM), pl.BlockSpec(memory_space=pl.ANY)
    return pl.pallas_call(
        functools.partial(write_last_kernel, divisor, levels),
        out_shape=jax.ShapeDtypeStruct(begun.shape, begun.dtype),
        in_specs=[vmem] * len(arrays) + [anywhere],
        out_specs=anywhere,
        scratch_shapes=[
            pltpu.VMEM((HOURS, 2 * levels, PIXELS_DEV), jnp.float32),
            pltpu.SemaphoreType.DMA((HOURS,)),
        ],
        input_output_aliases={len(arrays): 0},
        compiler_params=pltpu.CompilerParams(vmem_limit_bytes=8 * MIB),
        cost_estimate=LIGHT,
        name="write_last",
    )(*arrays, begun)


def hour_plan(level_field, tile_weight, tile_rows, tile_columns, live_count, step_hour):
    levs, subs, shards_tm = lax.axis_size("lev"), lax.axis_size("sub"), lax.axis_size("tm")
    half = levs // 2
    divisor = float(level_field.shape[0] * shards_tm // HOURS)
    field = jnp.transpose(level_field, (1, 0, 2))

    def to_peer(x, k, j):
        pairs = [(a * subs + b, (a ^ k) * subs + (b ^ j)) for a in range(levs) for b in range(subs)]
        return lax.ppermute(x, ("lev", "sub"), pairs)

    def swap(x):
        return lax.ppermute(x, "tm", [(0, 1), (1, 0)])

    plain = [(half, 0), (1, 0), (1, 1), (0, 1), (0, 0)]
    first, second = [(half + 1, j) for j in range(subs)], (half, 1)
    sums, (theirs_0, mine_0, theirs_1, mine_1) = hour_sums(plain, first, second, step_hour, field)
    rows = 2 * field.shape[0]
    folded = theirs_1.shape
    sibling = to_peer(sums[3], *plain[3])
    near_got = [to_peer(x, *peer) for x, peer in list(zip(sums, plain))[1:3]]
    got_0 = swap(theirs_0)
    plain_got = to_peer(sums[0], *plain[0])
    merged = small_call(
        merge_first_kernel, [mine_0, got_0], [sibling], [folded], LIGHT, "merge_first"
    )
    far_same = to_peer(merged[0], *first[0])
    merged = small_call(merge_next_kernel, [mine_0, got_0], merged, [folded], LIGHT, "merge_next")
    far_other = to_peer(merged[0], *first[1])
    high, low = place_tiles(tile_rows, tile_columns, live_count, tile_weight, *merged)
    theirs_1 = small_call(hold_kernel, [theirs_1], [plain_got, high], [folded], LIGHT, "hold")[0]
    got_1 = swap(theirs_1)
    both, send = remap_call(
        remap_both_kernel,
        [sums[4], sibling, plain_got],
        [theirs_1],
        [2 * rows] * 2,
        high,
        low,
        MEDIUM,
        "remap_both",
        [2 * rows] * 2,
    )
    got_both = swap(send)
    merged = small_call(
        merge_last_kernel, [mine_1, got_1], [both, near_got[0]], [folded], HEAVY, "merge_last"
    )
    second_got = to_peer(merged[0], *second)
    first_hour, second_hour = remap_call(
        remap_near_kernel, near_got, merged, [rows] * HOURS, high, low, LIGHT, "remap_near"
    )
    got_first = swap(first_hour)
    far, send = remap_call(
        remap_far_kernel, [far_same, far_other, second_hour], [], [rows] * 2, high, low, HEAVY, "remap_far"
    )
    got = swap(send)
    padded = -(-rows // 32) * 16
    (last,) = remap_call(
        remap_last_kernel,
        [second_got],
        [far],
        [(rows, PIXELS_DEV // 2)],
        high,
        low,
        HEAVY,
        "remap_last",
        [padded],
    )
    got_last = swap(last)
    levels = rows // 2
    out = write_first([both, got_both, first_hour, got_first, second_hour, far, got], levels, divisor)
    out = write_last(out, [both, got_both, last, got_last], levels, divisor)
    return out.reshape(HOURS, out.shape[0] // HOURS, PIXELS_DEV)


def general_plan(level_field, tile_weight, tile_rows, tile_columns, live_count, step_hour):
    steps, levels, cells = level_field.shape
    shards = lax.axis_size("lev") * lax.axis_size("sub")
    divisor = float(steps * lax.axis_size("tm") // HOURS)
    hours = jnp.arange(HOURS, dtype=jnp.int32)
    table = (step_hour[None, :] == hours[:, None]).astype(jnp.float32)
    fields = level_field.reshape(steps, levels, shards, cells // shards)
    partial = jnp.einsum("hs,slgc->ghlc", table, fields, precision=lax.Precision.HIGHEST)
    regrouped = lax.all_to_all(partial, ("lev", "sub"), split_axis=0, concat_axis=0, tiled=True)
    rows = jnp.transpose(regrouped, (1, 0, 2, 3)).reshape(-1, cells // shards)
    high, low = place_tiles(tile_rows, tile_columns, live_count, tile_weight)
    (out,) = remap_call(remap_rows_kernel, [rows], [], [rows.shape[0]], high, low, LIGHT, "remap_rows")
    out = out.reshape(HOURS, shards * levels, PIXELS_DEV) / divisor
    return lax.psum_scatter(out, "tm", scatter_dimension=1, tiled=True)


def solution(mesh):
    sizes = mesh.shape
    paired = sizes["tm"] == HOURS and sizes["lev"] == 4 and sizes["sub"] == 2

    def body(level_field, *others):
        steps, levels, _ = level_field.shape
        suits = paired and steps == 8 and levels % 4 == 0
        return (hour_plan if suits else general_plan)(level_field, *others)

    placed = (
        P(("groups", "tm"), ("lev", "sub"), None),
        P(None, ("lev", "sub")),
        P(("lev", "sub")),
        P(("lev", "sub")),
        P(("lev", "sub")),
        P("tm"),
    )
    return jax.shard_map(
        body,
        mesh=mesh,
        in_specs=placed,
        out_specs=P("groups", "tm", ("lev", "sub")),
        check_vma=False,
    )
```

```python
import functools

import jax
import jax.numpy as jnp
from jax import lax
from jax.experimental import pallas as pl
from jax.experimental.pallas import tpu as pltpu
from jax.sharding import PartitionSpec as P

TILE = 64
HOURS = 2
CT_DEV = 32
PT_DEV = 16
SLOTS = 128
CELLS_DEV = CT_DEV * TILE
PIXELS_DEV = PT_DEV * TILE
LANES = 2 * TILE
MIB = 1 << 20

LIGHT = pl.CostEstimate(flops=1, bytes_accessed=1, transcendentals=0)
MEDIUM = pl.CostEstimate(flops=2_500_000_000, bytes_accessed=1, transcendentals=0)
HEAVY = pl.CostEstimate(flops=10_000_000_000, bytes_accessed=1, transcendentals=0)

NN = (((1,), (0,)), ((), ()))


def split(x):
    high = x.astype(jnp.bfloat16)
    return high, (x - high.astype(jnp.float32)).astype(jnp.bfloat16)


def dot(a, b, dims):
    return lax.dot_general(a, b, dims, preferred_element_type=jnp.float32)


GROUP = 8


def place_kernel(rows, columns, count, weights, *refs):
    high, low, total = refs[-3:]
    band = 256

    @pl.loop(0, CELLS_DEV // band)
    def _(b):
        total[pl.ds(pl.multiple_of(b * band, band), band), :] = jnp.zeros((band, PIXELS_DEV), jnp.float32)

    lane_half = lax.broadcasted_iota(jnp.int32, (TILE, LANES), 1) // TILE
    live = count[0]

    @pl.loop(0, (live + GROUP - 1) // GROUP)
    def _(g):
        for pair in range(GROUP // 2):
            lanes = pl.ds(pl.multiple_of((g * (GROUP // 2) + pair) * LANES, LANES), LANES)
            tiles = weights[:, lanes]
            turned = jnp.transpose(jnp.concatenate([tiles, tiles], axis=0))
            for i in range(2):
                k = g * GROUP + pair * 2 + i
                row, column = rows[k], columns[k]
                side = jnp.where(k < live, row & 1, -1)
                at = (
                    pl.ds(pl.multiple_of(column * TILE, TILE), TILE),
                    pl.ds(pl.multiple_of((row >> 1) * LANES, LANES), LANES),
                )
                tile = turned[i * TILE : (i + 1) * TILE]
                total[at] = total[at] + jnp.where(lane_half == side, tile, 0.0)

    @pl.loop(0, CELLS_DEV // band)
    def _(b):
        at = pl.ds(pl.multiple_of(b * band, band), band)
        high[at, :], low[at, :] = split(total[at, :])


def place_tiles(rows, columns, count, weights, *after):
    smem = pl.BlockSpec(memory_space=pltpu.SMEM)
    vmem = pl.BlockSpec(memory_space=pltpu.VMEM)
    half = jax.ShapeDtypeStruct((CELLS_DEV, PIXELS_DEV), jnp.bfloat16)
    return pl.pallas_call(
        place_kernel,
        out_shape=(half, half),
        in_specs=[smem, smem, smem, vmem] + [pl.BlockSpec(memory_space=pl.ANY)] * len(after),
        out_specs=(vmem, vmem),
        scratch_shapes=[pltpu.VMEM((CELLS_DEV, PIXELS_DEV), jnp.float32)],
        compiler_params=pltpu.CompilerParams(vmem_limit_bytes=28 * MIB),
        cost_estimate=LIGHT,
        name="place_tiles",
    )(rows, columns, count, weights, *after)


PIXEL_BLOCK = 256


def remap_blocks(x, high, low):
    m = x.shape[0]
    x_high, x_low = split(x)
    both = jnp.concatenate([x_high, x_low], axis=0)
    for start in range(0, PIXELS_DEV, PIXEL_BLOCK):
        at = slice(start, start + PIXEL_BLOCK)
        first = dot(both, high[:, at], NN)
        yield at, first[:m] + first[m:] + dot(x_high, low[:, at], NN)


def remap_call(kernel, inputs, after, out_rows, high, low, cost, name, scratch_rows=()):
    vmem = pl.BlockSpec(memory_space=pltpu.VMEM)
    return pl.pallas_call(
        kernel,
        out_shape=[
            jax.ShapeDtypeStruct(rows if isinstance(rows, tuple) else (rows, PIXELS_DEV), jnp.float32)
            for rows in out_rows
        ],
        in_specs=[vmem] * (len(inputs) + 2) + [pl.BlockSpec(memory_space=pl.ANY)] * len(after),
        out_specs=[vmem] * len(out_rows),
        scratch_shapes=[pltpu.VMEM((rows, PIXELS_DEV), jnp.float32) for rows in scratch_rows],
        compiler_params=pltpu.CompilerParams(vmem_limit_bytes=24 * MIB),
        cost_estimate=cost,
        name=name,
    )(*inputs, high, low, *after)


def remap_rows_kernel(x, high, low, out):
    for at, result in remap_blocks(x[...], high, low):
        out[:, at] = result


def unfold(block):
    levels = block.shape[0] // 2
    return jnp.concatenate([block[:levels], block[levels:]], axis=1)


def far_rows(same_sub, other_sub):
    even = lax.axis_index("sub") == 0
    blocks = [jnp.where(even, same_sub, other_sub), jnp.where(even, other_sub, same_sub)]
    return [unfold(block) for block in blocks]


def keeps_near():
    return lax.axis_index("tm") == lax.axis_index("lev") // 2


def near_rows(same_sub, other_sub):
    even = lax.axis_index("sub") == 0
    return [jnp.where(even, same_sub, other_sub), jnp.where(even, other_sub, same_sub)]


def by_hour(result, levels):
    pieces = [result[start : start + levels] for start in range(0, 2 * HOURS * levels, levels)]
    return jnp.concatenate([pieces[sub * HOURS + hour] for hour in range(HOURS) for sub in range(2)], axis=0)


def sort_out(near_result, far_result, keep, send):
    near = keeps_near()

    @pl.when(near)
    def _():
        keep[...], send[...] = near_result[...], far_result[...]

    @pl.when(jnp.logical_not(near))
    def _():
        keep[...], send[...] = far_result[...], near_result[...]


def remap_both_kernel(own, sibling, plain, high, low, *refs):
    keep, send, near_result, far_result = refs[-4:]
    rows = own.shape[0]
    blocks = near_rows(own[...], sibling[...]) + [plain[...]]
    for at, result in remap_blocks(jnp.concatenate(blocks, axis=0), high, low):
        near_result[:, at] = by_hour(result, rows // HOURS)
        far_result[:rows, at] = result[2 * rows :]
    far_result[rows:] = jnp.zeros((rows, PIXELS_DEV), jnp.float32)
    sort_out(near_result, far_result, keep, send)


def remap_near_kernel(near_same, near_other, high, low, *refs):
    rows = near_same.shape[0]
    x = jnp.concatenate(near_rows(near_same[...], near_other[...]), axis=0)
    for at, result in remap_blocks(x, high, low):
        refs[-1][:, at] = by_hour(result, rows // HOURS)


def remap_far_kernel(same, other, high, low, *refs):
    x = jnp.concatenate(far_rows(same[...], other[...]), axis=0)
    for at, result in remap_blocks(x, high, low):
        refs[-1][:, at] = result


def remap_last_kernel(block, high, low, *refs):
    out, total = refs[-2:]
    x = unfold(block[...])
    levels, cells = x.shape
    x = jnp.concatenate([x, jnp.zeros((-levels % 16, cells), jnp.float32)], axis=0)
    for at, result in remap_blocks(x, high, low):
        total[:, at] = result
    out[...] = fold(total[:levels])


def hour_weights(step_hour, steps, hours, width):
    row = lax.broadcasted_iota(jnp.int32, (steps, width), 0)
    first = jnp.zeros((steps, width), jnp.float32)
    second = jnp.zeros((steps, width), jnp.float32)
    for step in range(steps):
        first = jnp.where(row == step, jnp.where(step_hour[step] == hours[0], 1.0, 0.0), first)
        second = jnp.where(row == step, jnp.where(step_hour[step] == hours[1], 1.0, 0.0), second)
    upper = row < steps // 2
    return jnp.where(upper, first, second), jnp.where(upper, second, first)


def turn(x, rows):
    return pltpu.roll(x, rows % x.shape[0], 0)


def join(a, b, bit):
    clear = (lax.broadcasted_iota(jnp.int32, a.shape, 0) & bit) == 0
    kept, moved = jnp.where(clear, a, b), jnp.where(clear, b, a)
    return kept + jnp.where(clear, turn(moved, -bit), turn(moved, bit))


def sum_steps(block, weights):
    def halve(x):
        return x * weights[0] + turn(x * weights[1], 4)

    def four(level):
        a, b, c, d = (halve(block(level + i)) for i in range(4))
        return join(join(a, c, 2), join(b, d, 2), 1)

    return four


def pack(pieces):
    upper = lax.broadcasted_iota(jnp.int32, pieces[0][0].shape, 0) < 4
    at_half = [x if half == place % 2 else turn(x, 4) for place, (x, half) in enumerate(pieces)]
    return [jnp.where(upper, a, b) for a, b in zip(at_half[::2], at_half[1::2])]


def peer_shard(k, j):
    subs = lax.axis_size("sub")
    return (lax.axis_index("lev") ^ k) * subs + (lax.axis_index("sub") ^ j)


def field_copies(field, buffer, arrived, peers):
    copies = []
    for place, (k, j) in enumerate(peers):
        start = pl.multiple_of(peer_shard(k, j) * CELLS_DEV, CELLS_DEV)
        copy = pltpu.make_async_copy(
            field.at[:, :, pl.ds(start, CELLS_DEV)], buffer.at[place], arrived.at[place]
        )
        copy.start()
        copies.append(copy)
    return copies


SUM_WIDTH = 512


def sums_kernel(plain, first, second, step_hour, field, *refs):
    *outs, buffer, arrived, hours, hours_arrived = refs
    _, levels, steps, cells = buffer.shape
    rows, cut = HOURS * levels, cells // 2
    copies = field_copies(field, buffer, arrived, [*plain, *first, second])
    fetch = pltpu.make_async_copy(step_hour, hours, hours_arrived)
    fetch.start()
    fetch.wait()
    me = lax.axis_index("tm")
    groups = range(0, levels, 4)

    def summed(place, start, width, weights):
        four = sum_steps(lambda level: buffer[place, level, :, pl.ds(start, width)], weights)
        return [four(level) for level in groups]

    def store(out, offset, start, width, pieces):
        for place, x in enumerate(pack(pieces)):
            out[offset + place * 8 : offset + place * 8 + 8, pl.ds(start, width)] = x

    weights = hour_weights(hours, steps, range(HOURS), SUM_WIDTH)
    for place in range(len(plain)):
        copies[place].wait()

        @pl.loop(0, cells // SUM_WIDTH)
        def _(i):
            start = pl.multiple_of(i * SUM_WIDTH, SUM_WIDTH)
            sums = summed(place, start, SUM_WIDTH, weights)
            pieces = [(x, half) for half in range(HOURS) for x in sums]
            store(outs[place], 0, start, SUM_WIDTH, pieces)

    theirs_first, mine_first, theirs_second, mine_second = outs[len(plain) :]
    width = SUM_WIDTH // 2
    weights = hour_weights(hours, steps, (1 - me, me), width)
    for j in range(len(first) + 1):
        place = len(plain) + j
        copies[place].wait()
        offset = j * rows if j < len(first) else 0
        theirs, mine = (theirs_first, mine_first) if j < len(first) else (theirs_second, mine_second)

        @pl.loop(0, cut // width)
        def _(i):
            start = pl.multiple_of(i * width, width)
            sums = summed(place, start, width, weights) + summed(place, cut + start, width, weights)
            store(theirs, offset, start, width, [(x, 0) for x in sums])
            store(mine, offset, start, width, [(x, 1) for x in sums])


def hour_sums(plain, first, second, step_hour, field):
    levels, steps, _ = field.shape
    rows, cut = HOURS * levels, CELLS_DEV // 2
    vmem = pl.BlockSpec(memory_space=pltpu.VMEM)
    shapes = [(rows, CELLS_DEV)] * len(plain) + [(len(first) * rows, cut)] * 2 + [(rows, cut)] * 2
    count = len(plain) + len(first) + 1
    outs = pl.pallas_call(
        functools.partial(sums_kernel, plain, first, second),
        out_shape=[jax.ShapeDtypeStruct(shape, jnp.float32) for shape in shapes],
        in_specs=[pl.BlockSpec(memory_space=pl.ANY)] * 2,
        out_specs=[vmem] * len(shapes),
        scratch_shapes=[
            pltpu.VMEM((count, levels, steps, CELLS_DEV), jnp.float32),
            pltpu.SemaphoreType.DMA((count,)),
            pltpu.SMEM((steps,), jnp.int32),
            pltpu.SemaphoreType.DMA,
        ],
        compiler_params=pltpu.CompilerParams(vmem_limit_bytes=52 * MIB),
        cost_estimate=LIGHT,
        name="hour_sums",
    )(step_hour, field)
    return outs[: len(plain)], outs[len(plain) :]


def merge_first_kernel(mine, got, *refs):
    rows = refs[-1].shape[0]
    refs[-1][...] = mine[:rows] + got[:rows]


def merge_next_kernel(mine, got, *refs):
    rows = refs[-1].shape[0]
    refs[-1][...] = mine[rows:] + got[rows:]


def merge_last_kernel(mine, got, *refs):
    refs[-1][...] = mine[...] + got[...]


def fold(x):
    half = x.shape[1] // 2
    return jnp.concatenate([x[:, :half], x[:, half:]], axis=0)


def hold_kernel(x, *refs):
    refs[-1][...] = x[...]


def small_call(kernel, inputs, after, shapes, cost, name):
    vmem = pl.BlockSpec(memory_space=pltpu.VMEM)
    return pl.pallas_call(
        kernel,
        out_shape=[jax.ShapeDtypeStruct(shape, jnp.float32) for shape in shapes],
        in_specs=[vmem] * len(inputs) + [pl.BlockSpec(memory_space=pl.ANY)] * len(after),
        out_specs=[vmem] * len(shapes),
        compiler_params=pltpu.CompilerParams(vmem_limit_bytes=8 * MIB),
        cost_estimate=cost,
        name=name,
    )(*inputs, *after)


def output_rows(same_lev, hour, levels):
    lev = lax.axis_index("lev") % 2
    start = hour * 2 + (lev if same_lev else 1 - lev)
    return pl.ds(pl.multiple_of(start * 2 * levels, 2 * levels), 2 * levels)


def write_first_kernel(divisor, levels, chip, got_chip, lev_near, got_near, far, got_far, out):
    me = lax.axis_index("tm")
    rows = 2 * levels
    near = keeps_near()
    for hour in range(HOURS):
        here = slice(hour * rows, (hour + 1) * rows)

        @pl.when(near)
        def _():
            out[output_rows(True, hour, levels), :] = (chip[here] + got_chip[here]) / divisor
            out[output_rows(False, hour, levels), :] = (lev_near[here] + got_near[here]) / divisor

        @pl.when(jnp.logical_not(near))
        def _():
            out[output_rows(False, hour, levels), :] = jnp.where(me == hour, far[...], got_far[...]) / divisor


def write_last_kernel(divisor, levels, plain, got_plain, last, got_last, begun, out, stage, written):
    me, even = lax.axis_index("tm"), lax.axis_index("sub") == 0

    @pl.when(jnp.logical_not(keeps_near()))
    def _():
        copies = []
        for hour in range(HOURS):
            here = slice(hour * levels, (hour + 1) * levels)
            first = plain[here] + got_plain[here]
            other = unfold(jnp.where(me == hour, last[...], got_last[...]))
            pair = [jnp.where(even, first, other), jnp.where(even, other, first)]
            stage[hour] = jnp.concatenate(pair, axis=0) / divisor
            target = out.at[output_rows(True, hour, levels), :]
            copies.append(pltpu.make_async_copy(stage.at[hour], target, written.at[hour]))
            copies[-1].start()
        for copy in copies:
            copy.wait()


def write_first(arrays, levels, divisor):
    kernel = functools.partial(write_first_kernel, divisor, levels)
    shape = (2 * arrays[0].shape[0], PIXELS_DEV)
    return small_call(kernel, arrays, [], [shape], LIGHT, "write_first")[0]


def write_last(begun, arrays, levels, divisor):
    vmem, anywhere = pl.BlockSpec(memory_space=pltpu.VMEM), pl.BlockSpec(memory_space=pl.ANY)
    return pl.pallas_call(
        functools.partial(write_last_kernel, divisor, levels),
        out_shape=jax.ShapeDtypeStruct(begun.shape, begun.dtype),
        in_specs=[vmem] * len(arrays) + [anywhere],
        out_specs=anywhere,
        scratch_shapes=[
            pltpu.VMEM((HOURS, 2 * levels, PIXELS_DEV), jnp.float32),
            pltpu.SemaphoreType.DMA((HOURS,)),
        ],
        input_output_aliases={len(arrays): 0},
        compiler_params=pltpu.CompilerParams(vmem_limit_bytes=8 * MIB),
        cost_estimate=LIGHT,
        name="write_last",
    )(*arrays, begun)


def hour_plan(level_field, tile_weight, tile_rows, tile_columns, live_count, step_hour):
    levs, subs, shards_tm = lax.axis_size("lev"), lax.axis_size("sub"), lax.axis_size("tm")
    half = levs // 2
    divisor = float(level_field.shape[0] * shards_tm // HOURS)
    field = jnp.transpose(level_field, (1, 0, 2))

    def to_peer(x, k, j):
        pairs = [(a * subs + b, (a ^ k) * subs + (b ^ j)) for a in range(levs) for b in range(subs)]
        return lax.ppermute(x, ("lev", "sub"), pairs)

    def swap(x):
        return lax.ppermute(x, "tm", [(0, 1), (1, 0)])

    plain = [(half, 0), (1, 0), (1, 1), (0, 1), (0, 0)]
    first, second = [(half + 1, j) for j in range(subs)], (half, 1)
    sums, (theirs_0, mine_0, theirs_1, mine_1) = hour_sums(plain, first, second, step_hour, field)
    rows = 2 * field.shape[0]
    folded = theirs_1.shape
    sibling = to_peer(sums[3], *plain[3])
    near_got = [to_peer(x, *peer) for x, peer in list(zip(sums, plain))[1:3]]
    got_0 = swap(theirs_0)
    plain_got = to_peer(sums[0], *plain[0])
    merged = small_call(
        merge_first_kernel, [mine_0, got_0], [sibling], [folded], LIGHT, "merge_first"
    )
    far_same = to_peer(merged[0], *first[0])
    merged = small_call(merge_next_kernel, [mine_0, got_0], merged, [folded], LIGHT, "merge_next")
    far_other = to_peer(merged[0], *first[1])
    high, low = place_tiles(tile_rows, tile_columns, live_count, tile_weight, *merged)
    theirs_1 = small_call(hold_kernel, [theirs_1], [plain_got, high], [folded], LIGHT, "hold")[0]
    got_1 = swap(theirs_1)
    both, send = remap_call(
        remap_both_kernel,
        [sums[4], sibling, plain_got],
        [theirs_1],
        [2 * rows] * 2,
        high,
        low,
        MEDIUM,
        "remap_both",
        [2 * rows] * 2,
    )
    got_both = swap(send)
    merged = small_call(
        merge_last_kernel, [mine_1, got_1], [both, near_got[0]], [folded], HEAVY, "merge_last"
    )
    second_got = to_peer(merged[0], *second)
    (near,) = remap_call(
        remap_near_kernel, near_got, merged, [2 * rows], high, low, LIGHT, "remap_near"
    )
    got_near = swap(near)
    (far,) = remap_call(remap_far_kernel, [far_same, far_other], [near], [rows], high, low, HEAVY, "remap_far")
    got_far = swap(far)
    padded = -(-rows // 32) * 16
    (last,) = remap_call(
        remap_last_kernel,
        [second_got],
        [far],
        [(rows, PIXELS_DEV // 2)],
        high,
        low,
        HEAVY,
        "remap_last",
        [padded],
    )
    got_last = swap(last)
    levels = rows // 2
    out = write_first([both, got_both, near, got_near, far, got_far], levels, divisor)
    out = write_last(out, [both, got_both, last, got_last], levels, divisor)
    return out.reshape(HOURS, out.shape[0] // HOURS, PIXELS_DEV)


def general_plan(level_field, tile_weight, tile_rows, tile_columns, live_count, step_hour):
    steps, levels, cells = level_field.shape
    shards = lax.axis_size("lev") * lax.axis_size("sub")
    divisor = float(steps * lax.axis_size("tm") // HOURS)
    hours = jnp.arange(HOURS, dtype=jnp.int32)
    table = (step_hour[None, :] == hours[:, None]).astype(jnp.float32)
    fields = level_field.reshape(steps, levels, shards, cells // shards)
    partial = jnp.einsum("hs,slgc->ghlc", table, fields, precision=lax.Precision.HIGHEST)
    regrouped = lax.all_to_all(partial, ("lev", "sub"), split_axis=0, concat_axis=0, tiled=True)
    rows = jnp.transpose(regrouped, (1, 0, 2, 3)).reshape(-1, cells // shards)
    high, low = place_tiles(tile_rows, tile_columns, live_count, tile_weight)
    (out,) = remap_call(remap_rows_kernel, [rows], [], [rows.shape[0]], high, low, LIGHT, "remap_rows")
    out = out.reshape(HOURS, shards * levels, PIXELS_DEV) / divisor
    return lax.psum_scatter(out, "tm", scatter_dimension=1, tiled=True)


def solution(mesh):
    sizes = mesh.shape
    paired = sizes["tm"] == HOURS and sizes["lev"] == 4 and sizes["sub"] == 2

    def body(level_field, *others):
        steps, levels, _ = level_field.shape
        suits = paired and steps == 8 and levels % 4 == 0
        return (hour_plan if suits else general_plan)(level_field, *others)

    placed = (
        P(("groups", "tm"), ("lev", "sub"), None),
        P(None, ("lev", "sub")),
        P(("lev", "sub")),
        P(("lev", "sub")),
        P(("lev", "sub")),
        P("tm"),
    )
    return jax.shard_map(
        body,
        mesh=mesh,
        in_specs=placed,
        out_specs=P("groups", "tm", ("lev", "sub")),
        check_vma=False,
    )
```
